32 devices in a mesh: dp: 8 (over y, x, core), fsdp: 4 (over z).
Axes of the slice: x: 2, y: 2, z: 4, core: 2. Of those that a mesh axis runs over, the one named last changes fastest.
Arguments:
- inputs: bfloat16 [32, 128, 1024], P(('dp', 'fsdp')), may hold values from -6 to 6
- cotangent: bfloat16 [32, 128, 1024], P(('dp', 'fsdp')), may hold values from -6 to 6
- segment_ids: int32 [32, 128], P(('dp', 'fsdp')), may hold values from 0 to 2, never falling along the last dimension, each value on 1 to 80 neighbouring positions
- section_ids: int32 [32], P(('dp', 'fsdp')), may hold values from 0 to 7
- w_big: bfloat16 [2, 1024, 8192], P(None, ('dp', 'fsdp')), may hold values from -0.9375 to 0.9375
- w_down: bfloat16 [2, 4096, 1024], P(None, ('dp', 'fsdp')), may hold values from -0.09375 to 0.09375
- norm_table: bfloat16 [9, 4096], P(None, ('dp', 'fsdp')), may hold values from -1.5 to 1.6
- m_big: float32 [2, 1024, 8192], P(None, ('dp', 'fsdp')), may hold values from -48 to 48
- m_down: float32 [2, 4096, 1024], P(None, ('dp', 'fsdp')), may hold values from -48 to 48
- m_table: float32 [9, 4096], P(None, ('dp', 'fsdp')), may hold values from -48 to 48
- v_big: float32 [2, 1024, 8192], P(None, ('dp', 'fsdp')), may hold values from 64 to 16384
- v_down: float32 [2, 4096, 1024], P(None, ('dp', 'fsdp')), may hold values from 64 to 16384
- v_table: float32 [9, 4096], P(None, ('dp', 'fsdp')), may hold values from 64 to 16384
Outputs:
- out_act: bfloat16 [32, 128, 1024], P(('dp', 'fsdp'))
- grad_input: bfloat16 [32, 128, 1024], P(('dp', 'fsdp'))
- grad_big: float32 [2, 1024, 8192], P(None, ('dp', 'fsdp'))
- grad_down: float32 [2, 4096, 1024], P(None, ('dp', 'fsdp'))
- grad_table: float32 [9, 4096], P(None, ('dp', 'fsdp'))
- new_m_big: float32 [2, 1024, 8192], P(None, ('dp', 'fsdp'))
- new_m_down: float32 [2, 4096, 1024], P(None, ('dp', 'fsdp'))
- new_m_table: float32 [9, 4096], P(None, ('dp', 'fsdp'))
- step_big: float32 [2, 1024, 8192], P(None, ('dp', 'fsdp'))
- step_down: float32 [2, 4096, 1024], P(None, ('dp', 'fsdp'))
- step_table: float32 [9, 4096], P(None, ('dp', 'fsdp'))
The draws below stay inside these ranges and needn't reach their ends.
Inputs may be any that keep to these rules, and one draw needn't show every extreme that they name: `segment_ids`: in each row the numbers never fall, every one of the 3 utterances has 1 to 80 frames, and one has exactly 80.
All inputs are finite; a program needn't handle non-finite values.
Results may differ from the reference program's by a relative error of at most 0.015.
Values may be sent and summed in bfloat16 or wider, within the bound.
No kernel may reach another device: no remote copies, remote signals or barrier semaphores. Data moves between devices by JAX's collectives and lax.ppermute only.
A program may use at most 384 MiB of HBM per device.

```python
import math
import jax
import jax.numpy as jnp
import numpy as np
from jax import lax

D = 1024
HEADS = 16
FF = 4096
SECTIONS = 8
ROW = 128
SEGS = 3
SEG_MOST = 80
ROWS = 32
TOKENS = 4096


def draw_w_big(key, part):
    key = jax.random.fold_in(key, 11)
    columns = 4 * D + FF
    sample_noise = jnp.clip(jax.random.normal(key, (2, D, columns), jnp.float32), -6.0, 6.0)
    column_index = jnp.arange(columns)
    factor = jnp.where((column_index >= 3 * D) & (column_index < 4 * D), 5.0, 1.0) / math.sqrt(D)
    return (sample_noise * factor[None, None, :]).astype(jnp.bfloat16)


def draw_norm_table(key, part):
    key = jax.random.fold_in(key, 12)
    first_key, second_key = jax.random.split(key)
    shape_pair = (SECTIONS + 1, 4 * D)
    scales = jax.random.uniform(first_key, shape_pair, jnp.float32, 0.5, 1.5)
    shifts = jnp.clip(0.3 * jax.random.normal(second_key, shape_pair, jnp.float32), -1.5, 1.5)
    member_kind = jnp.arange(4 * D) // D % 2
    return jnp.where(member_kind[None, :] == 0, scales, shifts).astype(jnp.bfloat16)


def with_ends(values, key, low, top_value):
    shape = values.shape
    place = [jax.random.randint(jax.random.fold_in(key, axis), (), 0, shape[axis]) for axis in range(len(shape))]
    values = values.at[tuple(place)].set(low)
    longest = shape.index(max(shape))
    place[longest] = (place[longest] + 1) % shape[longest]
    return values.at[tuple(place)].set(top_value)


def block_scale(own_key, shape, pieces, least, largest):
    factor_of, own = 1.0, jax.random.fold_in(own_key, 6)
    for dim, parts in pieces:
        steps = jnp.exp(jax.random.uniform(jax.random.fold_in(own, dim), (parts,), jnp.float32, least / len(pieces), largest / len(pieces)))
        factor_of = factor_of * jnp.repeat(steps, shape[dim] // parts).reshape([-1 if axis == dim else 1 for axis in range(len(shape))])
    return factor_of


def profile(amount, total, limit, skew):
    loads = [(1 << 20) // math.isqrt(grade ** skew) + 1 for grade in range(2, amount + 1)]
    spare, holding = total - limit - (amount - 1), [1] * (amount - 1)
    while spare > 0:
        free = [i for i in range(amount - 1) if holding[i] < limit]
        whole, left = sum([loads[i] for i in free]), spare
        for i in free:
            addition = min(limit - holding[i], max(1, left * loads[i] // whole), spare)
            holding[i] = holding[i] + addition
            spare = spare - addition
    return np.array([limit] + holding)


def uneven_parts(rng, amount, total, reach, lean):
    if amount == 2:
        one = jax.random.randint(rng, (), max(1, total - reach), min(reach, total - 1) + 1)
        return jnp.stack([one, total - one])
    lengths = jnp.asarray(profile(amount, total, reach, lean), jnp.int32)
    twos = (amount - 1) // 2
    source_of, taker = lengths[1:1 + 2 * twos:2], lengths[2:2 + 2 * twos:2]
    margin = jnp.minimum(source_of - 1, reach - taker)
    passed = jax.random.randint(jax.random.fold_in(rng, 1), (twos,), 0, 1 << 20) % (margin + 1)
    lengths = lengths.at[1:1 + 2 * twos:2].set(source_of - passed).at[2:2 + 2 * twos:2].set(taker + passed)
    return lengths[jax.random.permutation(jax.random.fold_in(rng, 2), amount)]


def noise(stream_key, dims, spread, bound, pieces=(), kind=jnp.bfloat16):
    loudness = block_scale(stream_key, dims, pieces, -0.22, 0.18) if pieces else 1.0
    array = jax.random.normal(stream_key, dims, jnp.float32) * spread * loudness
    return jnp.minimum(jnp.maximum(array, -bound), bound).astype(kind)


def setup_inputs(seed: int = 0) -> dict:
    key_of = jax.random.split(jax.random.key(seed), 14)
    return {
        "inputs": noise(key_of[0], (ROWS, ROW, D), 1.0, 6.0, ((0, 32),)),
        "cotangent": noise(key_of[1], (ROWS, ROW, D), 1.0, 6.0, ((0, 32),)),
        "segment_ids": jax.vmap(lambda own: jnp.searchsorted(jnp.cumsum(uneven_parts(own, SEGS, ROW, SEG_MOST, 1)), jnp.arange(ROW), side="right"))(jax.random.split(key_of[2], ROWS)).reshape((ROWS, ROW)).astype(jnp.int32),
        "section_ids": with_ends(jax.random.randint(key_of[3], (ROWS,), 0, SECTIONS), jax.random.fold_in(key_of[3], 1), 0, SECTIONS - 1).astype(jnp.int32),
        "w_big": draw_w_big(jax.random.fold_in(key_of[13], 71), 0),
        "w_down": noise(key_of[5], (2, FF, D), FF ** -0.5, 0.09375, ((1, 32),)),
        "norm_table": draw_norm_table(jax.random.fold_in(key_of[13], 71), 0),
        "m_big": noise(key_of[7], (2, D, 4 * D + FF), ((TOKENS // 64) ** 0.5), 48.0, ((1, 32),), jnp.float32),
        "m_down": noise(key_of[8], (2, FF, D), ((TOKENS // 64) ** 0.5), 48.0, ((1, 32),), jnp.float32),
        "m_table": noise(key_of[9], (SECTIONS + 1, 4 * D), ((TOKENS // 64) ** 0.5), 48.0, ((1, 32),), jnp.float32),
        "v_big": jnp.clip(jnp.exp(math.log(16384.0) - 5.5451774 * jax.random.uniform(key_of[10], (2, D, 4 * D + FF), jnp.float32) ** block_scale(key_of[10], (2, D, 4 * D + FF), ((1, 32),), -0.2, 0.2)), 64.0, 16384.0),
        "v_down": jnp.clip(jnp.exp(math.log(16384.0) - 5.5451774 * jax.random.uniform(key_of[11], (2, FF, D), jnp.float32) ** block_scale(key_of[11], (2, FF, D), ((1, 32),), -0.2, 0.2)), 64.0, 16384.0),
        "v_table": jnp.clip(jnp.exp(math.log(16384.0) - 5.5451774 * jax.random.uniform(key_of[12], (SECTIONS + 1, 4 * D), jnp.float32) ** block_scale(key_of[12], (SECTIONS + 1, 4 * D), ((1, 32),), -0.2, 0.2)), 64.0, 16384.0),
    }


@jax.custom_vjp
def low(v):
    return lax.optimization_barrier(v.astype(jnp.bfloat16)).astype(jnp.float32)

@jax.custom_vjp
def low_back(v):
    return v

def low_keep(v):
    return (low(v), None)

def low_pass(kept, grad):
    return (grad,)

def back_keep(v):
    return (v, None)

def back_low(kept, grad):
    return (low(grad),)
low.defvjp(low_keep, low_pass)
low_back.defvjp(back_keep, back_low)
beta_one = 0.9
beta_two = 0.999
first_fix = 1.0 - 0.9 ** 10
second_fix = 1.0 - 0.999 ** 10

def layer_norm(hidden):
    centred = hidden - lax.optimization_barrier(jnp.mean(hidden, axis=-1, keepdims=True))
    return centred * lax.rsqrt(lax.optimization_barrier(jnp.mean(centred * centred, axis=-1, keepdims=True)) + 1e-05)

def attention(normed, weights, segments, causal):
    row_count, row_length, model_width = normed.shape
    head_size = model_width // HEADS
    projected = jnp.einsum('rld,dc->rlc', normed, weights[:, :3 * model_width], precision=lax.Precision.HIGHEST)
    queries = low(low_back(projected[..., :model_width])).reshape(row_count, row_length, HEADS, head_size)
    key_vecs = low(low_back(projected[..., model_width:2 * model_width])).reshape(row_count, row_length, HEADS, head_size)
    values = low(low_back(projected[..., 2 * model_width:])).reshape(row_count, row_length, HEADS, head_size)
    scores = jnp.einsum('rqhe,rkhe->rhqk', queries, key_vecs, precision=lax.Precision.HIGHEST)
    scores = low_back(scores * (1.0 / math.sqrt(head_size)))
    allowed = segments[:, :, None] == segments[:, None, :]
    if causal:
        position = jnp.arange(row_length)
        allowed = allowed & (position[:, None] >= position[None, :])
    scores = jnp.where(allowed[:, None], scores, -1e+30)
    row_top = lax.optimization_barrier(jnp.max(scores, axis=-1, keepdims=True))
    exponent = jnp.exp(scores - row_top)
    shares = exponent / lax.optimization_barrier(jnp.sum(exponent, axis=-1, keepdims=True))
    mixed = jnp.einsum('rhqk,rkhe->rqhe', low(shares), values, precision=lax.Precision.HIGHEST)
    mixed = low(low_back(mixed.reshape(row_count, row_length, model_width)))
    return low_back(jnp.einsum('rld,dc->rlc', mixed, weights[:, 3 * model_width:4 * model_width], precision=lax.Precision.HIGHEST))

def block(hidden, weights, w_down, gain_rows, segments, causal):
    model_width = hidden.shape[-1]
    normed_one = low(layer_norm(hidden) * gain_rows[:, :, :model_width] + gain_rows[:, :, model_width:2 * model_width])
    hidden = hidden + attention(normed_one, weights, segments, causal)
    normed_two = low(layer_norm(hidden) * gain_rows[:, :, 2 * model_width:3 * model_width] + gain_rows[:, :, 3 * model_width:])
    pre_active = low_back(jnp.einsum('rld,df->rlf', normed_two, weights[:, 4 * model_width:], precision=lax.Precision.HIGHEST))
    active = low(jax.nn.gelu(pre_active))
    return hidden + low_back(jnp.einsum('rlf,fd->rld', active, w_down, precision=lax.Precision.HIGHEST))

def forward(values, w_big, w_down, norm_table, segments, sections):
    row_count = values.shape[0]
    first_rows = jnp.broadcast_to(norm_table[0][None, None, :], (row_count, 1, norm_table.shape[1]))
    second_rows = norm_table[1 + sections][:, None, :]
    middle = block(values, w_big[0], w_down[0], first_rows, segments, True)
    return block(middle, w_big[1], w_down[1], second_rows, segments, False)

def adam_update(moment, square, gradient):
    moment = beta_one * moment + (1.0 - beta_one) * gradient
    square = beta_two * square + (1.0 - beta_two) * gradient * gradient
    update = moment / first_fix / (jnp.sqrt(square / second_fix) + 1e-08)
    return (moment, update)

def reference(inputs, cotangent, segment_ids, section_ids, w_big, w_down, norm_table, m_big, m_down, m_table, v_big, v_down, v_table):
    group_rows = math.gcd(ROWS, max(1, 4096 // ROW))
    group_count = ROWS // group_rows
    masters = (w_big.astype(jnp.float32), w_down.astype(jnp.float32), norm_table.astype(jnp.float32))

    def advance(totals, sliced):
        group_in, group_cot, group_seg, group_section = sliced

        def forward_group(values, big_part, down_part, table_part):
            return forward(values, big_part, down_part, table_part, group_seg, group_section)
        result, pullback = jax.vjp(forward_group, group_in.astype(jnp.float32), *masters)
        gradient = pullback(group_cot.astype(jnp.float32))
        totals = tuple((total + piece for total, piece in zip(totals, gradient[1:])))
        return (totals, (result.astype(jnp.bfloat16), gradient[0].astype(jnp.bfloat16)))
    zeros = tuple((jnp.zeros(master.shape, jnp.float32) for master in masters))
    sliced = (inputs.reshape(group_count, group_rows, ROW, D), cotangent.reshape(group_count, group_rows, ROW, D), segment_ids.reshape(group_count, group_rows, ROW), section_ids.reshape(group_count, group_rows))
    totals, (outputs, grad_inputs) = lax.scan(advance, zeros, sliced)
    grad_big, grad_down, grad_table = totals
    new_m_big, step_big = adam_update(m_big, v_big, grad_big)
    new_m_down, step_down = adam_update(m_down, v_down, grad_down)
    new_m_table, step_table = adam_update(m_table, v_table, grad_table)
    return (outputs.reshape(ROWS, ROW, D), grad_inputs.reshape(ROWS, ROW, D), grad_big, grad_down, grad_table, new_m_big, new_m_down, new_m_table, step_big, step_down, step_table)
```

```python
from functools import partial

import jax
import jax.numpy as jnp
from jax import lax
from jax.sharding import PartitionSpec as P

HEADS = 16

beta_one = 0.9
beta_two = 0.999
first_fix = 1.0 - 0.9**10
second_fix = 1.0 - 0.999**10

f32 = jnp.float32
bf16 = jnp.bfloat16

CORE = ("dp", 1)
SIDE = ("dp", 2)


def masks(size):
    return [1 << k for k in reversed(range(size.bit_length() - 1))]


class Slice:
    def __init__(self, dp, fsdp):
        self.dp, self.fsdp = dp, fsdp
        self.high = [("dp", m) for m in masks(dp) if m > 2]
        self.deep = [("fsdp", m) for m in masks(fsdp)]
        self.order = self.high + [SIDE, CORE] + self.deep
        self.size = {"dp": dp, "fsdp": fsdp}

    def flip(self, value, bit):
        axis, mask = bit
        return lax.ppermute(value, axis, [(i, i ^ mask) for i in range(self.size[axis])])

    def place(self, bit, have):
        return sum(self.order.index(b) < self.order.index(bit) for b in have)


def mine(bit):
    axis, mask = bit
    return (lax.axis_index(axis) // mask) % 2


def merge(own, other, bit, pos):
    side = mine(bit)
    return jnp.where(side == 0, jnp.stack([own, other], pos), jnp.stack([other, own], pos))


def gather(sl, value, bits, have=()):
    have = list(have)
    for bit in bits:
        value = merge(value, sl.flip(value, bit), bit, sl.place(bit, have))
        have.append(bit)
    return value


def split(value, bit, pos):
    side = mine(bit)
    keep = lax.dynamic_index_in_dim(value, side, pos, keepdims=False)
    send = lax.dynamic_index_in_dim(value, 1 - side, pos, keepdims=False)
    return keep, send


def scatter(sl, value, bits, have):
    have, kind = list(have), value.dtype
    for n, bit in enumerate(bits):
        keep, send = split(value, bit, sl.place(bit, have))
        have.remove(bit)
        value = keep.astype(f32) + sl.flip(send, bit).astype(f32)
        if n < len(bits) - 1:
            value = value.astype(kind)
    return value


def dot(left, right):
    return jnp.dot(left, right, preferred_element_type=f32)


def contract_rows(left, right):
    return lax.dot_general(left, right, (((0,), (0,)), ((), ())), preferred_element_type=f32)


def times_transposed(left, right):
    return lax.dot_general(left, right, (((1,), (1,)), ((), ())), preferred_element_type=f32)


def norm(hidden):
    centred = hidden - jnp.mean(hidden, axis=-1, keepdims=True)
    scale = lax.rsqrt(jnp.mean(centred * centred, axis=-1, keepdims=True) + 1e-05)
    return centred * scale, scale


def norm_back(hidden, grad, gain):
    normed, scale = norm(hidden)
    e = grad * gain
    part = scale * (
        e
        - jnp.mean(e, axis=-1, keepdims=True)
        - normed * jnp.mean(e * normed, axis=-1, keepdims=True)
    )
    return part, jnp.sum(grad * normed, axis=0), jnp.sum(grad, axis=0)


def rows_of_pair(sl, value):
    return jnp.concatenate([value, sl.flip(value, CORE)], 0)


def rows_of_four(sl, value):
    two = jnp.concatenate([value, sl.flip(value, SIDE)], 0)
    return jnp.concatenate([two, sl.flip(two, CORE)], 0)


def sum_pair(sl, value):
    n = value.shape[0] // 2
    return value[:n] + sl.flip(value[n:], CORE)


def sum_four(sl, value):
    two = sum_pair(sl, value)
    n = two.shape[0] // 2
    return two[:n] + sl.flip(two[n:].astype(bf16), SIDE).astype(f32)


def allowed_of(segments, causal):
    allowed = segments[:, :, None] == segments[:, None, :]
    if causal:
        position = jnp.arange(segments.shape[1])
        allowed = allowed & (position[:, None] >= position[None, :])
    return allowed


def probs_of(q, k, allowed):
    scores = jnp.einsum("rqhe,rkhe->rhqk", q, k, preferred_element_type=f32) * (
        q.shape[-1] ** -0.5
    )
    scores = jnp.where(allowed[:, None], scores, -1e30)
    exponent = jnp.exp(scores - jnp.max(scores, axis=-1, keepdims=True))
    return exponent / jnp.sum(exponent, axis=-1, keepdims=True)


def heads_of(projected, length):
    tokens, width = projected.shape
    parts = projected.reshape(tokens // length, length, 3, HEADS // 2, width // 3 // (HEADS // 2))
    return parts[:, :, 0], parts[:, :, 1], parts[:, :, 2]


def attend(projected, allowed):
    q, k, v = heads_of(projected, allowed.shape[1])
    probs = probs_of(q, k, allowed)
    mixed = jnp.einsum("rhqk,rkhe->rqhe", probs.astype(bf16), v, preferred_element_type=f32)
    return mixed.astype(bf16).reshape(projected.shape[0], -1)


def attend_back(projected, allowed, d_mixed):
    q, k, v = heads_of(projected, allowed.shape[1])
    d_mixed = d_mixed.reshape(q.shape)
    probs = probs_of(q, k, allowed)
    d_probs = jnp.einsum("rqhe,rkhe->rhqk", d_mixed, v, preferred_element_type=f32)
    d_v = jnp.einsum("rhqk,rqhe->rkhe", probs.astype(bf16), d_mixed, preferred_element_type=f32)
    d_scores = probs * (d_probs - jnp.sum(probs * d_probs, axis=-1, keepdims=True))
    d_scores = d_scores.astype(bf16)
    size = q.shape[-1] ** -0.5
    d_q = jnp.einsum("rhqk,rkhe->rqhe", d_scores, k, preferred_element_type=f32) * size
    d_k = jnp.einsum("rhqk,rqhe->rkhe", d_scores, q, preferred_element_type=f32) * size
    out = jnp.stack([d_q, d_k, d_v], 2).astype(bf16)
    return out.reshape(projected.shape)


def forward(sl, hidden, weights, gains, allowed):
    w_qkv, w_out, w_up, w_down = weights
    first = (norm(hidden)[0] * gains[0] + gains[1]).astype(bf16)
    first = rows_of_pair(sl, first)
    projected = dot(first, w_qkv).astype(bf16)
    mixed = attend(projected, allowed)
    attended = hidden + sum_pair(sl, dot(mixed, w_out))
    second = (norm(attended)[0] * gains[2] + gains[3]).astype(bf16)
    second = rows_of_four(sl, second)
    pre = dot(second, w_up)
    active = jax.nn.gelu(pre).astype(bf16)
    output = attended + sum_four(sl, dot(active, w_down))
    return output, (hidden, first, projected, mixed, attended, second, pre, active)


def backward(sl, d_out, weights, gains, allowed, stored):
    w_qkv, w_out, w_up, w_down = weights
    hidden, first, projected, mixed, attended, second, pre, active = stored
    d_branch = rows_of_four(sl, d_out.astype(bf16))
    g_down = contract_rows(active, d_branch).astype(bf16)
    d_active = times_transposed(d_branch, w_down)
    d_pre = jax.vjp(jax.nn.gelu, pre)[1](d_active)[0].astype(bf16)
    g_up = contract_rows(second, d_pre).astype(bf16)
    d_second = sum_four(sl, times_transposed(d_pre, w_up))
    part, d_gain2, d_shift2 = norm_back(attended, d_second, gains[2])
    d_attended = d_out + part
    d_mix_in = rows_of_pair(sl, d_attended.astype(bf16))
    g_out = contract_rows(mixed, d_mix_in).astype(bf16)
    d_mixed = times_transposed(d_mix_in, w_out).astype(bf16)
    d_projected = attend_back(projected, allowed, d_mixed)
    g_qkv = contract_rows(first, d_projected).astype(bf16)
    d_first = sum_pair(sl, times_transposed(d_projected, w_qkv))
    part, d_gain1, d_shift1 = norm_back(hidden, d_first, gains[0])
    g_table = jnp.concatenate([d_gain1, d_shift1, d_gain2, d_shift2])
    return d_attended + part, (g_qkv, g_out, g_up, g_down, g_table)


def adam_update(moment, square, gradient):
    moment = beta_one * moment + (1.0 - beta_one) * gradient
    square = beta_two * square + (1.0 - beta_two) * gradient * gradient
    update = moment / first_fix / (jnp.sqrt(square / second_fix) + 1e-08)
    return (moment, update)


def body(
    dp,
    fsdp,
    inputs,
    cotangent,
    segment_ids,
    section_ids,
    w_big,
    w_down,
    norm_table,
    m_big,
    m_down,
    m_table,
    v_big,
    v_down,
    v_table,
):
    sl = Slice(dp, fsdp)
    width = inputs.shape[-1]
    rows = w_big.shape[1]
    feeds = w_down.shape[1]
    feed = w_big.shape[2] - 4 * width
    high = dp // 4
    two = 2 * [2]

    qkv = w_big[:, :, : 3 * width].reshape(2, rows, 3, 2 * high, 2, fsdp * rows)
    up = w_big[:, :, 4 * width :].reshape(2, rows, high, 2, 2, fsdp * feeds)
    qkv_keep, qkv_send = split(qkv, CORE, 4)
    up_keep, up_send = split(up, CORE, 4)
    half = 3 * width // 2

    def side_by_side(a, b):
        return jnp.concatenate([a.reshape(2, rows, half), b.reshape(2, rows, feed // 2)], 2)

    pair = merge(
        side_by_side(qkv_keep, up_keep),
        sl.flip(side_by_side(qkv_send, up_send), CORE),
        CORE,
        1,
    )
    out_proj = w_big[:, :, 3 * width : 4 * width].reshape(2, rows, 2, width // 2)
    attn_own = jnp.concatenate([pair[..., :half], jnp.swapaxes(out_proj, 1, 2)], -1)
    up_pair = pair[..., half:].reshape(2, 2, rows, high, 2, fsdp * feeds)
    up_keep, up_send = split(up_pair, SIDE, 4)
    up_own = merge(up_keep, sl.flip(up_send, SIDE), SIDE, 1).reshape(2, *two, rows, feed // 4)

    table = gather(sl, norm_table, [CORE] + sl.deep + sl.high + [SIDE])
    table = table.reshape(dp * fsdp, *norm_table.shape)
    table = jnp.swapaxes(table, 0, 1).reshape(norm_table.shape[0], 4, width).astype(f32)
    section = section_ids[0]
    gains_all = (table[0], lax.dynamic_index_in_dim(table, 1 + section, 0, keepdims=False))

    attn_orders = (sl.deep + sl.high + [SIDE], sl.high + sl.deep + [SIDE])
    feed_order = sl.deep + sl.high

    def fetch(layer):
        attn = gather(sl, attn_own[layer], attn_orders[layer], [CORE])
        attn = attn.reshape(2 * high, 2, fsdp * rows, 2 * width)
        w_qkv = attn[..., :half].reshape(width, half)
        w_out = jnp.swapaxes(attn[..., half:], 1, 2).reshape(width // 2, width)
        w_up = gather(sl, up_own[layer], feed_order, [SIDE, CORE]).reshape(width, feed // 4)
        w_dn = gather(sl, w_down[layer], feed_order).reshape(feed // 4, width)
        return w_qkv, w_out, w_up, w_dn

    weights = [fetch(0), fetch(1)]
    segments = rows_of_pair(sl, segment_ids.astype(f32))
    hidden = inputs[0].astype(f32)
    stored = [None, None]
    allowed = [allowed_of(segments, layer == 0) for layer in range(2)]
    for layer in range(2):
        hidden, stored[layer] = forward(
            sl, hidden, weights[layer], gains_all[layer], allowed[layer]
        )
    out_act = hidden.astype(bf16)
    grad = cotangent[0].astype(f32)
    big, down, tables = [None, None], [None, None], [None, None]
    bits = sl.high + [SIDE]
    for layer in (1, 0):
        grad, (g_qkv, g_out, g_up, g_down, g_table) = backward(
            sl, grad, weights[layer], gains_all[layer], allowed[layer], stored[layer]
        )
        nh, nz = len(sl.high), len(sl.deep)
        feed_back = feed_order[::-1]
        attn_back = attn_orders[layer][::-1]
        g_down = g_down.reshape(*(nh + nz) * [2], feeds, width)
        down[layer] = scatter(sl, g_down, feed_back, feed_order)
        g_up = g_up.reshape(*(nh + 2 + nz) * [2], rows, feed // 4)
        g_up = scatter(sl, g_up, feed_back, sl.order)
        g_up = g_up.reshape(*two, rows, high, fsdp * feeds)
        keep, send = split(g_up, SIDE, 0)
        g_up = merge(keep, sl.flip(send, SIDE), SIDE, 3)
        keep, send = split(g_up, CORE, 0)
        g_up = merge(keep, sl.flip(send, CORE), CORE, 3).reshape(rows, feed)
        g_out = g_out.reshape(*(nh + 1 + nz) * [2], rows, width)
        g_out = scatter(sl, g_out, attn_back, attn_back)
        g_qkv = g_qkv.reshape(*(nh + 2 + nz) * [2], rows, half)
        g_qkv = scatter(sl, g_qkv, attn_back, sl.order)
        g_qkv = g_qkv.reshape(2, rows, 3, 2 * high, fsdp * rows)
        keep, send = split(g_qkv, CORE, 0)
        g_qkv = merge(keep, sl.flip(send, CORE), CORE, 3).reshape(rows, 3 * width)
        big[layer] = jnp.concatenate([g_qkv, g_out, g_up], 1)
        if layer == 0:
            g_table = g_table[None]
        else:
            count = norm_table.shape[0] - 1
            g_table = jnp.where((jnp.arange(count) == section)[:, None], g_table[None], 0.0)
        g_table = jnp.swapaxes(g_table.reshape(-1, dp * fsdp, norm_table.shape[1]), 0, 1)
        g_table = g_table.reshape(*(nh + 2 + nz) * [2], *g_table.shape[1:])
        tables[layer] = scatter(sl, g_table, [CORE] + attn_back, sl.order)
    grad_big = jnp.stack(big)
    grad_down = jnp.stack(down)
    grad_table = jnp.concatenate(tables, 0)
    new_m_big, step_big = adam_update(m_big, v_big, grad_big)
    new_m_down, step_down = adam_update(m_down, v_down, grad_down)
    new_m_table, step_table = adam_update(m_table, v_table, grad_table)
    return (
        out_act[None],
        grad.astype(bf16)[None],
        grad_big,
        grad_down,
        grad_table,
        new_m_big,
        new_m_down,
        new_m_table,
        step_big,
        step_down,
        step_table,
    )


def solution(mesh):
    both = ("dp", "fsdp")
    rows, middle, last = P(both, None, None), P(None, both, None), P(None, both)
    return jax.shard_map(
        partial(body, mesh.shape["dp"], mesh.shape["fsdp"]),
        mesh=mesh,
        in_specs=(rows, rows, P(both, None), P(both), middle, middle, last)
        + 2 * (middle, middle, last),
        out_specs=(rows, rows) + 3 * (middle, middle, last),
        check_vma=False,
    )
```

```python
import math
from functools import partial

import jax
import jax.numpy as jnp
from jax import lax
from jax.experimental import pallas as pl
from jax.experimental.pallas import tpu as pltpu
from jax.sharding import PartitionSpec as P

HEADS = 16

beta_one = 0.9
beta_two = 0.999
first_fix = 1.0 - 0.9**10
second_fix = 1.0 - 0.999**10

f32 = jnp.float32
bf16 = jnp.bfloat16

VMEM = pl.BlockSpec(memory_space=pltpu.VMEM)
SMEM = pl.BlockSpec(memory_space=pltpu.SMEM)
ANY = pl.BlockSpec(memory_space=pl.ANY)

CORE = ("dp", 1)
SIDE = ("dp", 2)


def masks(size):
    return [1 << k for k in reversed(range(size.bit_length() - 1))]


class Slice:
    def __init__(self, dp, fsdp):
        self.high = [("dp", m) for m in masks(dp) if m > 2]
        self.deep = [("fsdp", m) for m in masks(fsdp)]
        self.size = {"dp": dp, "fsdp": fsdp}

    def flip(self, value, bit):
        axis, mask = bit
        return lax.ppermute(value, axis, [(i, i ^ mask) for i in range(self.size[axis])])


def mine(bit):
    axis, mask = bit
    return (lax.axis_index(axis) // mask) % 2


def call(kernel, outs, operands, specs, scratch=(), flops=0, name=None):
    held = [(v.shape, v.dtype) for v, spec in zip(operands, specs) if spec is VMEM] + list(outs)
    held += [(s.shape, s.dtype) for s in scratch if hasattr(s, "memory_space") and s.memory_space == pltpu.VMEM]
    held = sum(math.prod(shape) * jnp.dtype(kind).itemsize for shape, kind in held)
    return pl.pallas_call(
        kernel,
        out_shape=[jax.ShapeDtypeStruct(shape, kind) for shape, kind in outs],
        in_specs=specs,
        out_specs=[VMEM] * len(outs),
        scratch_shapes=list(scratch),
        compiler_params=pltpu.CompilerParams(vmem_limit_bytes=held + (8 << 20)),
        name=name,
    )(*operands)


def merge(own, other, bit, pos):
    side = mine(bit)
    return jnp.where(side == 0, jnp.stack([own, other], pos), jnp.stack([other, own], pos))


def split(value, bit, pos):
    side = mine(bit)
    keep = lax.dynamic_index_in_dim(value, side, pos, keepdims=False)
    send = lax.dynamic_index_in_dim(value, 1 - side, pos, keepdims=False)
    return keep, send


def interleave_kernel(side, own, other, *outs):
    each = own.shape[0] // len(outs)
    for n, out in enumerate(outs):
        part = pl.ds(n * each, each)
        out[:, pl.ds(side[0], 1)] = own[part][:, None]
        out[:, pl.ds(1 - side[0], 1)] = other[part][:, None]


def interleave(own, other, bit, before, outs=1):
    rows, n = own.shape
    shape = (before, rows // before, n)
    whole = (before // outs, 2, rows // before, n)
    result = call(
        interleave_kernel,
        outs * [(whole, own.dtype)],
        [mine(bit)[None], own.reshape(shape), other.reshape(shape)],
        [SMEM, VMEM, VMEM],
        name="interleave",
    )
    return [part.reshape(-1, n) for part in result]


class Gather:
    def __init__(self, sl, own, lead, top_first=False):
        self.sl, self.value, self.lead, self.top_first = sl, own, lead, top_first
        self.have, self.air, self.quarters = [], None, None
        near = sl.high[:0:-1]
        if top_first:
            self.steps = [sl.high[:1], near + sl.deep[:-1], sl.deep[-1:]]
        else:
            self.steps = [sl.deep[:-1], sl.deep[-1:] + near]
        core = mine(CORE)
        self.place = jnp.stack([jnp.zeros_like(core) if top_first else mine(sl.high[0]), core])

    def before(self, bit):
        order = self.sl.high + self.sl.deep
        count = sum(order.index(b) < order.index(bit) for b in self.have)
        return (1 << count) * (1 if bit in self.sl.high else self.lead)

    def start(self):
        if not self.steps:
            self.air = self.sl.flip(self.value, self.sl.high[0]), self.sl.flip(self.value, CORE)
            return
        *others, self.bit = self.steps.pop(0)
        for bit in others:
            other = self.sl.flip(self.value, bit)
            self.value = interleave(self.value, other, bit, self.before(bit))[0]
            self.have.append(bit)
        self.air = self.sl.flip(self.value, self.bit)

    def land(self):
        air, self.air = self.air, None
        if isinstance(air, tuple):
            self.quarters, self.value = [self.value, *air], None
            return
        last = self.top_first and not self.steps
        halves = interleave(self.value, air, self.bit, self.before(self.bit), 1 + last)
        self.have.append(self.bit)
        if last:
            self.quarters = [*halves, self.sl.flip(halves[0], CORE)]
            self.value = None
        else:
            self.value = halves[0]

    def finish(self):
        self.quarters = [*self.quarters, self.sl.flip(self.quarters[1], CORE)]


def add_low_kernel(one, two, out):
    out[...] = (one[...].astype(f32) + two[...].astype(f32)).astype(bf16)


def add_split_kernel(side, *refs):
    *parts, kept, sent = refs
    for at, out in ((side[0], kept), (1 - side[0], sent)):
        total = parts[0][:, pl.ds(at, 1)].astype(f32)
        for other in parts[1:]:
            total = total + other[:, pl.ds(at, 1)].astype(f32)
        out[...] = total.astype(bf16)[:, 0]


class Scatter:
    def __init__(self, sl, quarters, lead):
        self.sl, self.quarters, self.value, self.lead = sl, quarters, None, lead
        self.have = sl.high[1:] + sl.deep
        self.steps = [sl.high[:1], sl.high[1:] + sl.deep[-1:], sl.deep[-2::-1]]

    def cross(self):
        own, top, core, both = self.quarters
        top_other = self.sl.flip(both, CORE)
        core_other = self.sl.flip(core, CORE)
        (send,) = call(
            add_low_kernel, [(top.shape, bf16)], [top, top_other], [VMEM] * 2, name="add_low"
        )
        self.quarters = [[own, core_other], send]

    def split(self, other, bit):
        parts = [*self.quarters[0], other]
        if bit is None:
            self.value = sum(part.astype(f32) for part in parts)
            self.quarters = None
            return
        order = self.sl.high + self.sl.deep
        before = 1 << sum(order.index(b) < order.index(bit) for b in self.have)
        before = before * (1 if bit in self.sl.high else self.lead)
        self.have.remove(bit)
        rows, n = other.shape
        shape = (before, 2, rows // 2 // before, n)
        half = ((before, rows // 2 // before, n), bf16)
        keep, send = call(
            add_split_kernel,
            [half, half],
            [mine(bit)[None], *(part.reshape(shape) for part in parts)],
            [SMEM] + [VMEM] * len(parts),
            name="add_split",
        )
        self.quarters = [[keep.reshape(-1, n)], send.reshape(-1, n)]

    def start(self):
        bits = self.steps.pop(0)
        for n, bit in enumerate(bits):
            self.air = self.sl.flip(self.quarters[1], bit)
            if n < len(bits) - 1:
                self.split(self.air, bits[n + 1])
        self.next = self.steps[0][0] if self.steps else None

    def land(self):
        other, self.air = self.air, None
        self.split(other, self.next)


class Live:
    def __init__(self, **values):
        self.flows = []
        self.values = values

    def flow(self, made):
        self.flows.append(made)
        return made

    def __getattr__(self, name):
        return self.values[name]

    def put(self, **values):
        self.values.update(values)

    def drop(self, *names):
        for name in names:
            del self.values[name]

    def seal(self, *landing):
        for made in landing:
            made.land()
        kept = (self.values, [(made.value, made.quarters) for made in self.flows])
        self.values, flown = lax.optimization_barrier(kept)
        for made, (made.value, made.quarters) in zip(self.flows, flown):
            pass


def dot(left, right):
    return jnp.dot(left, right, preferred_element_type=f32)


def dot_t(left, right):
    return lax.dot_general(left, right, (((1,), (1,)), ((), ())), preferred_element_type=f32)


def t_dot(left, right):
    return lax.dot_general(left, right, (((0,), (0,)), ((), ())), preferred_element_type=f32)


def fetch(place, quarters, whole, lead, sems):
    width = whole.shape[1]
    block = whole.shape[0] // (4 * lead)
    copies = []
    for n, part in enumerate(quarters):
        top = place[0] if n % 2 == 0 else 1 - place[0]
        core = place[1] if n < 2 else 1 - place[1]
        for a in range(lead):
            at = pl.multiple_of(((top * lead + a) * 2 + core) * block, block)
            source = part.at[pl.ds(a * block, block), pl.ds(0, width)]
            copies.append(
                pltpu.make_async_copy(source, whole.at[pl.ds(at, block)], sems.at[n * lead + a])
            )
    for copy in copies:
        copy.start()
    return copies


def norm(hidden):
    centred = hidden - jnp.mean(hidden, axis=-1, keepdims=True)
    scale = lax.rsqrt(jnp.mean(centred * centred, axis=-1, keepdims=True) + 1e-05)
    return centred * scale, scale


def norm_kernel(which, base, gains, out):
    rows = base.shape[0] // 2
    for r in range(2):
        block = pl.ds(r * rows, rows)
        g = gains[r, pl.ds(2 * which, 1)]
        b = gains[r, pl.ds(2 * which + 1, 1)]
        out[block] = (norm(base[block])[0] * g + b).astype(bf16)


def add_norm_kernel(which, base, keep, other, gains, total, out):
    rows = base.shape[0] // 2
    for r in range(2):
        block = pl.ds(r * rows, rows)
        back = pl.ds((1 - r) * rows, rows)
        value = base[block] + (keep[block] + other[back].astype(f32))
        total[block] = value
        g = gains[r, pl.ds(2 * which, 1)]
        b = gains[r, pl.ds(2 * which + 1, 1)]
        out[block] = (norm(value)[0] * g + b).astype(bf16)


def norm_back_kernel(which, d_out, keep, other, hidden, gains, total, low, d_gain, d_shift):
    rows = d_out.shape[0] // 2
    for r in range(2):
        block = pl.ds(r * rows, rows)
        back = pl.ds((1 - r) * rows, rows)
        grad = keep[block] + other[back].astype(f32)
        normed, scale = norm(hidden[block])
        if r == 0:
            d_gain[...] = jnp.sum(grad * normed, axis=0, keepdims=True)
            d_shift[...] = jnp.sum(grad, axis=0, keepdims=True)
        e = grad * gains[r, pl.ds(2 * which, 1)]
        part = e - jnp.mean(e, axis=-1, keepdims=True)
        part = part - normed * jnp.mean(e * normed, axis=-1, keepdims=True)
        value = d_out[block] + scale * part
        total[block] = value
        low[block] = value.astype(bf16)


def score(q, k, allowed, size):
    scores = jnp.where(allowed, dot_t(q, k) * size, -1e30)
    exponent = jnp.exp(scores - jnp.max(scores, axis=-1, keepdims=True))
    return exponent / jnp.sum(exponent, axis=-1, keepdims=True)


def lanes_of(which, shape):
    lane = lax.broadcasted_iota(jnp.int32, shape, 1)
    return (lane < shape[1] // 2) if which == 0 else (lane >= shape[1] // 2)


def out_block(weight, k, block, at):
    count = weight.shape[0] // (2 * block)
    wide = weight.shape[1] - at
    return jnp.concatenate([weight[pl.ds((2 * h + k) * block, block), pl.ds(at, wide)] for h in range(count)], 0)


def attend_kernel(size, lead, block, place, f, q0, q1, q2, q3, allow, qkv, mixed, keep, low, weight, sems):
    for copy in fetch(place, (q0, q1, q2, q3), weight, lead, sems):
        copy.wait()
    length = allow.shape[-1]
    third = qkv.shape[1] // 3
    for n in range(3):
        cols = pl.ds(n * third, third)
        qkv[:, cols] = dot(f[...], weight[:, cols]).astype(bf16)

    def one_row(r, carry):
        at = pl.ds(pl.multiple_of(r * length, length), length)
        allowed = allow[r] > 0
        for p in range(third // 128):
            q = qkv[at, pl.ds(p * 128, 128)]
            k = qkv[at, pl.ds(third + p * 128, 128)]
            v = qkv[at, pl.ds(2 * third + p * 128, 128)]
            parts = []
            for h in range(2):
                probs = score(jnp.where(lanes_of(h, q.shape), q, 0), k, allowed, size)
                parts.append(dot(probs.astype(bf16), v))
            mixed[at, pl.ds(p * 128, 128)] = jnp.where(
                lanes_of(0, q.shape), parts[0], parts[1]
            ).astype(bf16)
        return carry

    lax.fori_loop(0, f.shape[0] // length, one_row, 0)
    for k in range(2):
        cols = pl.ds(k * third, third)
        value = dot(mixed[...], out_block(weight, k, block, 3 * third))
        keep[:, cols] = value
        low[:, cols] = value.astype(bf16)


def attend_back_kernel(size, lead, block, place, d, q0, q1, q2, q3, allow, qkv, d_qkv, keep, low, weight, d_mixed, sems):
    for copy in fetch(place, (q0, q1, q2, q3), weight, lead, sems):
        copy.wait()
    length = allow.shape[-1]
    third = qkv.shape[1] // 3
    value = dot_t(d[:, pl.ds(0, third)], out_block(weight, 0, block, 3 * third))
    value = value + dot_t(d[:, pl.ds(third, third)], out_block(weight, 1, block, 3 * third))
    d_mixed[...] = value.astype(bf16)

    def one_row(r, carry):
        at = pl.ds(pl.multiple_of(r * length, length), length)
        allowed = allow[r] > 0
        for p in range(third // 128):
            q = qkv[at, pl.ds(p * 128, 128)]
            k = qkv[at, pl.ds(third + p * 128, 128)]
            v = qkv[at, pl.ds(2 * third + p * 128, 128)]
            dm = d_mixed[at, pl.ds(p * 128, 128)]
            d_q, d_k, d_v = [], [], []
            for h in range(2):
                pick = lanes_of(h, q.shape)
                probs = score(jnp.where(pick, q, 0), k, allowed, size)
                d_probs = dot_t(jnp.where(pick, dm, 0), v)
                d_v.append(t_dot(probs.astype(bf16), dm))
                inner = jnp.sum(probs * d_probs, axis=-1, keepdims=True)
                d_scores = (probs * (d_probs - inner)).astype(bf16)
                d_q.append(dot(d_scores, k))
                d_k.append(t_dot(d_scores, q))
            pick = lanes_of(0, q.shape)
            for n, (parts, scale) in enumerate(((d_q, size), (d_k, size), (d_v, 1.0))):
                value = jnp.where(pick, parts[0], parts[1]) * scale
                d_qkv[at, pl.ds(n * third + p * 128, 128)] = value.astype(bf16)
        return carry

    lax.fori_loop(0, d.shape[0] // length, one_row, 0)
    for n in range(keep.shape[1] // 256):
        cols = pl.ds(n * 256, 256)
        value = dot_t(d_qkv[...], weight[cols, pl.ds(0, 3 * third)])
        keep[:, cols] = value
        low[:, cols] = value.astype(bf16)


def up_kernel(lead, place, f, q0, q1, q2, q3, pre, active, weight, sems):
    for copy in fetch(place, (q0, q1, q2, q3), weight, lead, sems):
        copy.wait()
    for n in range(pre.shape[1] // 256):
        cols = pl.ds(n * 256, 256)
        value = dot(f[...], weight[:, cols])
        pre[:, cols] = value
        active[:, cols] = jax.nn.gelu(value).astype(bf16)


def down_kernel(lead, place, active, q0, q1, q2, q3, keep, low, weight, sems):
    for copy in fetch(place, (q0, q1, q2, q3), weight, lead, sems):
        copy.wait()
    for n in range(keep.shape[1] // 256):
        cols = pl.ds(n * 256, 256)
        value = dot(active[...], weight[:, cols])
        keep[:, cols] = value
        low[:, cols] = value.astype(bf16)


def gelu_slope(x):
    c = 0.7978845608028654
    t = jnp.tanh(c * (x + 0.044715 * (x * x * x)))
    return 0.5 * (1.0 + t) + 0.5 * x * (1.0 - t * t) * (c * (1.0 + 3 * 0.044715 * (x * x)))


def feed_back_kernel(lead, up_place, dn_place, d, pre, u0, u1, u2, u3, n0, n1, n2, n3, d_pre, keep, low, w_up, w_dn, up_sems, dn_sems):
    dn_copies = fetch(dn_place, (n0, n1, n2, n3), w_dn, lead // 2, dn_sems)
    up_copies = fetch(up_place, (u0, u1, u2, u3), w_up, lead, up_sems)
    for copy in dn_copies:
        copy.wait()
    for n in range(pre.shape[1] // 256):
        cols = pl.ds(n * 256, 256)
        d_pre[:, cols] = (gelu_slope(pre[:, cols]) * dot_t(d[...], w_dn[cols])).astype(bf16)
    for copy in up_copies:
        copy.wait()
    for n in range(keep.shape[1] // 256):
        cols = pl.ds(n * 256, 256)
        value = dot_t(d_pre[...], w_up[cols])
        keep[:, cols] = value
        low[:, cols] = value.astype(bf16)


def columns_of(place, value, lead):
    block = value.shape[1] // (4 * lead)
    parts = []
    for n in range(4):
        top = place[0] if n % 2 == 0 else 1 - place[0]
        core = place[1] if n < 2 else 1 - place[1]
        starts = [((top * lead + a) * 2 + core) * block for a in range(lead)]
        if block % 128 == 0:
            starts = [pl.multiple_of(at, 128) for at in starts]
        parts.append(jnp.concatenate([value[:, pl.ds(at, block)] for at in starts], 1))
    return parts


def weight_grad_kernel(lead, aligned, place, left, right, *outs):
    place = place if aligned else (0, 0)
    for part, out in zip(columns_of(place, left, lead), outs):
        out[...] = t_dot(part, right[...]).astype(bf16)


def attend_grad_kernel(lead, aligned, place, left, mixed, d_qkv, d, *outs):
    width = d_qkv.shape[1]
    third = width // 3
    place = place if aligned else (0, 0)
    block = left.shape[1] // (4 * lead)
    lefts, inners = columns_of(place, left, lead), columns_of(place, mixed, lead // 2)
    for part, inner, out in zip(lefts, inners, outs):
        out[:, pl.ds(0, width)] = t_dot(part, d_qkv[...]).astype(bf16)
        value = t_dot(inner, d[...]).astype(bf16)
        for h in range(inner.shape[1] // block):
            for k in range(2):
                out[pl.ds((2 * h + k) * block, block), pl.ds(width, third)] = value[
                    h * block : (h + 1) * block, k * third : (k + 1) * third
                ]


def turn(sl, value, lead):
    tokens, width = value.shape
    value = value.reshape(tokens, 2, lead, 2, width // (4 * lead))
    value = jnp.stack(split(value, sl.high[0], 1), 1)
    return jnp.stack(split(value, CORE, 3), 3).reshape(tokens, width)


def finish_kernel(span, chunk, side, keep, other, out, m, v, *refs):
    grad, new_m, step = refs[-3:]
    third = out.shape[-1]
    part = 3 * third
    rows = keep.shape[0]
    for source, x in ((keep, side[0]), (other, 1 - side[0])):
        for first, base, width, total in ((0, 0, span, part), (part, 8 * third, chunk, keep.shape[1] - part)):
            for n in range(total // width):
                at = pl.multiple_of(base + (2 * n + x) * width, 128)
                grad[0, :, pl.ds(at, width)] = source[:, pl.ds(first + n * width, width)]
    for k in range(2):
        grad[0, :, pl.ds((6 + k) * third, third)] = out[k]
    for n in range(grad.shape[2] // 1024):
        cols = pl.ds(n * 1024, 1024)
        new_m[0, :, cols], step[0, :, cols] = adam_update(m[0, :, cols], v[0, :, cols], grad[0, :, cols])


def finish_down_kernel(value, m, v, *refs):
    grad, new_m, step = refs[-3:]
    grad[0] = value[...]
    new_m[0], step[0] = adam_update(m[0], v[0], value[...])


def update(kernel, layer, shape, parts, specs, moments, before, name):
    one = pl.BlockSpec((1, *shape[1:]), lambda i: (layer, 0, 0))
    count = len(parts) + 2
    return pl.pallas_call(
        kernel,
        grid=(1,),
        out_shape=[jax.ShapeDtypeStruct(shape, f32)] * 3,
        in_specs=[*specs, one, one, *len(before) * [ANY]],
        out_specs=[one] * 3,
        input_output_aliases={count + n: n for n in range(len(before))},
        compiler_params=pltpu.CompilerParams(vmem_limit_bytes=20 << 20),
        name=name,
    )(*parts, *moments, *before)


def adam_update(moment, square, gradient):
    moment = beta_one * moment + (1.0 - beta_one) * gradient
    square = beta_two * square + (1.0 - beta_two) * gradient * gradient
    update = moment / first_fix / (jnp.sqrt(square / second_fix) + 1e-08)
    return (moment, update)


def dma(count):
    return pltpu.SemaphoreType.DMA((count,))


def body(
    dp,
    fsdp,
    inputs,
    cotangent,
    segment_ids,
    section_ids,
    w_big,
    w_down,
    norm_table,
    m_big,
    m_down,
    m_table,
    v_big,
    v_down,
    v_table,
):
    sl = Slice(dp, fsdp)
    length, width = inputs.shape[1:]
    rows = w_big.shape[1]
    feeds = w_down.shape[1]
    feed = w_big.shape[2] - 4 * width
    high = dp // 4
    lead = high
    half, part = width // 2, 3 * width // 2
    block = fsdp * rows
    count = norm_table.shape[0]
    size = (width // HEADS) ** -0.5
    two_f, two_b = ((2 * length, width), f32), ((2 * length, width), bf16)
    wide_b = ((2 * length, feed // 2), bf16)
    quarter = ((width // 4, 2 * width), bf16)
    gain_row = ((1, width), f32)
    place = jnp.stack([mine(sl.high[0]), mine(CORE)])
    w_attn = pltpu.VMEM((width, 2 * width), bf16)
    w_upper = pltpu.VMEM((width, feed // 2), bf16)
    w_lower = pltpu.VMEM((feed // 2, width), bf16)

    qkv = w_big[:, :, : 3 * width].reshape(2, rows, 3, high, 2, 2 * block)
    up = w_big[:, :, 4 * width :].reshape(2, rows, high, 2, 2 * fsdp * feeds)
    qkv_keep, qkv_send = [v.reshape(2, rows, part) for v in split(qkv, SIDE, 4)]
    up_keep, up_send = [v.reshape(2, rows, feed // 2) for v in split(up, SIDE, 3)]
    table_part = norm_table.reshape(-1)
    table_part = jnp.pad(table_part, (0, rows * 128 - table_part.shape[0])).reshape(rows, 128)
    out_proj = w_big[:, :, 3 * width : 4 * width].reshape(2, rows, 2, half)
    out_proj = jnp.swapaxes(out_proj, 1, 2)
    extra = jnp.zeros((16, width), bf16)
    extra = extra.at[0, :length].set(segment_ids[0].astype(bf16))
    extra = extra.at[1, 0].set(section_ids[0].astype(bf16))

    live = Live()
    downs = [live.flow(Gather(sl, w_down[n], 1)) for n in range(2)]

    send = jnp.concatenate([qkv_send[0], table_part], -1)
    keep = jnp.concatenate([qkv_keep[0], table_part], -1)
    own = merge(keep, sl.flip(send, SIDE), SIDE, 0)
    own = jnp.concatenate([own[..., :part], out_proj[0], own[..., part:]], -1)
    attns = [live.flow(Gather(sl, own.reshape(2 * rows, -1), 2))]
    live.put(
        up_keep=up_keep,
        up_send=up_send,
        next_keep=jnp.concatenate([qkv_keep[1], up_keep[1]], -1),
        next_send=jnp.concatenate([qkv_send[1], up_send[1]], -1),
        pack=jnp.concatenate([inputs[0], cotangent[0], extra], 0),
    )
    live.seal()

    attns[0].start()
    other = sl.flip(live.up_send[0], SIDE)
    own = merge(live.up_keep[0], other, SIDE, 0).reshape(2 * rows, -1)
    ups = [live.flow(Gather(sl, own, 2))]
    live.drop("up_keep", "up_send")
    live.seal(attns[0])

    attns[0].start()
    ups[0].start()
    own = merge(live.next_keep, sl.flip(live.next_send, SIDE), SIDE, 0)
    live.put(next=own)
    live.drop("next_keep", "next_send")
    live.seal(attns[0], ups[0])

    attns[0].start()
    ups[0].start()
    downs[0].start()
    packed = jnp.stack([live.pack, sl.flip(live.pack, SIDE)])
    extras = packed[:, 2 * length :]
    segments = extras[:, 0, :length].astype(f32)
    same = segments[:, :, None] == segments[:, None, :]
    position = jnp.arange(length)
    live.put(
        hidden=packed[:, :length].reshape(2 * length, width).astype(f32),
        d_low=packed[:, length : 2 * length].reshape(2 * length, width),
        sections=extras[:, 1, 0].astype(jnp.int32),
        allows=[
            (same & (position[:, None] >= position[None, :])).astype(f32),
            same.astype(f32),
        ],
    )
    live.drop("pack")
    own = jnp.concatenate([live.next[..., :part], out_proj[1]], -1)
    attns.append(live.flow(Gather(sl, own.reshape(2 * rows, -1), 2)))
    ups.append(live.flow(Gather(sl, live.next[..., part:].reshape(2 * rows, -1), 2)))
    live.drop("next")
    live.seal(attns[0], ups[0], downs[0])

    def gains_of(quarters, sections):
        wide = norm_table.shape[1]
        parts = jnp.stack([q[:, 2 * width :] for q in quarters])
        parts = parts.reshape(4, lead // 2, 2, fsdp, rows, 128)
        if wide == 128:
            parts = parts[..., :count, :]
        else:
            parts = parts.reshape(4, lead // 2, 2, fsdp, rows * 128)[..., : count * wide]
            parts = parts.reshape(4, lead // 2, 2, fsdp, count, wide)
        pick = jnp.concatenate([jnp.zeros((2,), jnp.int32), 1 + sections])
        pick = (pick[:, None] == jnp.arange(count)[None, :]).astype(bf16)
        picked = jnp.einsum("sr,qhxdrj->qshxdj", pick, parts, preferred_element_type=f32)
        own, top, core, both = picked
        both = merge(merge(own, core, CORE, 3), merge(top, both, CORE, 3), sl.high[0], 1)
        both = both.reshape(2, 2, 4, width)
        return [both[0], both[1]]

    def attend(layer):
        sems = dma(4 * lead)
        qkv, mixed, keep, low = call(
            partial(attend_kernel, size, lead, 2 * block),
            [((2 * length, part), bf16), ((2 * length, half), bf16), two_f, two_b],
            [attns[layer].place, live.first, *attns[layer].quarters, live.allows[layer]],
            [SMEM, VMEM, ANY, ANY, ANY, ANY, VMEM],
            [w_attn, sems],
            name="attend",
        )
        live.put(**{f"attn{layer}": (live.hidden, live.first, qkv, mixed)})
        live.put(keep=keep, other=sl.flip(low, SIDE))

    def add_norm(which, layer, base):
        return call(
            partial(add_norm_kernel, which),
            [two_f, two_b],
            [base, live.keep, live.other, live.gains[layer]],
            [VMEM] * 4,
            name="add_norm",
        )

    def feed_up(layer):
        attended, second = add_norm(1, layer, live.hidden)
        pre, active = call(
            partial(up_kernel, lead),
            [(wide_b[0], f32), wide_b],
            [ups[layer].place, second, *ups[layer].quarters],
            [SMEM, VMEM, ANY, ANY, ANY, ANY],
            [w_upper, dma(4 * lead)],
            name="up",
        )
        live.put(**{f"feed{layer}": (attended, second, pre, active)})

    def feed_down(layer):
        keep, low = call(
            partial(down_kernel, lead // 2),
            [two_f, two_b],
            [downs[layer].place, live.values[f"feed{layer}"][3], *downs[layer].quarters],
            [SMEM, VMEM, ANY, ANY, ANY, ANY],
            [w_lower, dma(2 * lead)],
            name="down",
        )
        return keep, sl.flip(low, SIDE)

    def feed_back(layer):
        pre = live.values[f"feed{layer}"][2]
        d_pre, keep, low = call(
            partial(feed_back_kernel, lead),
            [wide_b, two_f, two_b],
            [
                ups[layer].place,
                downs[layer].place,
                live.d_low,
                pre,
                *ups[layer].quarters,
                *downs[layer].quarters,
            ],
            [SMEM, SMEM, VMEM, VMEM] + [ANY] * 8,
            [w_upper, w_lower, dma(4 * lead), dma(2 * lead)],
            name="feed_back",
        )
        live.put(d_pre=d_pre, keep=keep, other=sl.flip(low, SIDE))

    def down_grad(layer):
        aligned = feed // 4 // lead % 128 == 0
        active = live.values[f"feed{layer}"][3]
        parts = call(
            partial(weight_grad_kernel, lead // 2, aligned),
            [((feed // 8, width), bf16)] * 4,
            [place, active if aligned else turn(sl, active, lead // 2), live.d_low],
            [SMEM, VMEM, VMEM],
            name="down_grad",
        )
        return live.flow(Scatter(sl, parts, 1))

    def up_grad(layer):
        aligned = block % 128 == 0
        second = live.values[f"feed{layer}"][1]
        parts = call(
            partial(weight_grad_kernel, lead, aligned),
            [quarter] * 4,
            [place, second if aligned else turn(sl, second, lead), live.d_pre],
            [SMEM, VMEM, VMEM],
            name="up_grad",
        )
        return live.flow(Scatter(sl, parts, 2))

    def norm_back(which, layer, hidden):
        grad, d_low, d_gain, d_shift = call(
            partial(norm_back_kernel, which),
            [two_f, two_b, gain_row, gain_row],
            [live.grad, live.keep, live.other, hidden, live.gains[layer]],
            [VMEM] * 5,
            name="norm_back",
        )
        live.put(grad=grad, d_low=d_low)
        live.put(**{f"gains{layer}{which}": jnp.concatenate([d_gain, d_shift], 1)})

    def attend_back(layer):
        norm_back(1, layer, live.values[f"feed{layer}"][0])
        d_qkv, keep, low = call(
            partial(attend_back_kernel, size, lead, 2 * block),
            [((2 * length, part), bf16), two_f, two_b],
            [
                attns[layer].place,
                live.d_low,
                *attns[layer].quarters,
                live.allows[layer],
                live.values[f"attn{layer}"][2],
            ],
            [SMEM, VMEM, ANY, ANY, ANY, ANY, VMEM, VMEM],
            [w_attn, pltpu.VMEM((2 * length, half), bf16), dma(4 * lead)],
            name="attend_back",
        )
        live.put(d_qkv=d_qkv, keep=keep, other=sl.flip(low, SIDE))

    def attend_grad(layer):
        hidden, first, qkv, mixed = live.values[f"attn{layer}"]
        aligned = block % 128 == 0
        if not aligned:
            first, mixed = turn(sl, first, lead), turn(sl, mixed, lead // 2)
        parts = call(
            partial(attend_grad_kernel, lead, aligned),
            [quarter] * 4,
            [place, first, mixed, live.d_qkv, live.d_low],
            [SMEM] + [VMEM] * 4,
            name="attend_grad",
        )
        return live.flow(Scatter(sl, parts, 2))

    def finish(layer, g_attn, g_up, before):
        g_attn = g_attn.value.reshape(2, rows, 2 * width)
        g_up = g_up.value.reshape(2, rows, feed // 2)
        keep, send = split(jnp.concatenate([g_attn[..., :part], g_up], -1), SIDE, 0)
        return update(
            partial(finish_kernel, 2 * block, 2 * fsdp * feeds),
            layer,
            w_big.shape,
            [mine(SIDE)[None], keep, sl.flip(send, SIDE), g_attn[..., part:]],
            [SMEM, VMEM, VMEM, VMEM],
            [m_big, v_big],
            before,
            "finish",
        )

    def finish_down(layer, flow, before):
        return update(
            finish_down_kernel,
            layer,
            w_down.shape,
            [flow.value],
            [VMEM],
            [m_down, v_down],
            before,
            "finish_down",
        )

    def table_grad(layer):
        g_table = jnp.concatenate([live.values[f"gains{layer}0"], live.values[f"gains{layer}1"]], 1)
        if layer == 1:
            hit = jnp.arange(count - 1) == section_ids[0]
            g_table = jnp.where(hit[:, None], g_table, 0.0)
        g_table = g_table.reshape(g_table.shape[0], high, 2, 2, fsdp, norm_table.shape[1])
        g_table = jnp.moveaxis(g_table, 0, 4)
        keep, send = split(g_table, CORE, 2)
        g_table = keep + sl.flip(send, CORE)
        keep, send = split(g_table, SIDE, 1)
        g_table = keep + sl.flip(send, SIDE)
        g_table = g_table.reshape(*(len(sl.high) + len(sl.deep)) * [2], *g_table.shape[-2:])
        for bit in sl.high + sl.deep:
            keep, send = split(g_table, bit, 0)
            g_table = keep + sl.flip(send, bit)
        return g_table

    ups[0].start()
    downs[0].start()
    attns[1].start()
    attns[0].finish()
    live.put(gains=gains_of(attns[0].quarters, live.sections))
    (first,) = call(
        partial(norm_kernel, 0), [two_b], [live.hidden, live.gains[0]], [VMEM] * 2, name="norm"
    )
    live.put(first=first)
    attend(0)
    live.seal(ups[0], downs[0], attns[1])

    downs[0].start()
    attns[1].start()
    ups[1].start()
    ups[0].finish()
    feed_up(0)
    live.seal(downs[0], attns[1], ups[1])

    attns[1].start()
    ups[1].start()
    downs[1].start()
    downs[0].finish()
    keep, other = feed_down(0)
    live.put(keep=keep, other=other)
    live.seal(attns[1], ups[1], downs[1])

    ups[1].start()
    downs[1].start()
    attns[1].finish()
    hidden, first = add_norm(0, 1, live.feed0[0])
    live.put(hidden=hidden, first=first)
    attend(1)
    live.seal(ups[1], downs[1])

    downs[1].start()
    ups[1].finish()
    feed_up(1)
    live.put(grad=live.d_low.astype(f32))
    g_down1 = down_grad(1)
    g_down1.cross()
    live.seal(downs[1])

    g_down1.start()
    downs[1].finish()
    feed_back(1)
    g_up1 = up_grad(1)
    g_up1.cross()
    live.seal(g_down1)

    g_up1.start()
    g_down1.start()
    attend_back(1)
    g_attn1 = attend_grad(1)
    g_attn1.cross()
    live.seal(g_up1, g_down1)

    g_attn1.start()
    g_up1.start()
    g_down1.start()
    norm_back(0, 1, live.attn1[0])
    feed_back(0)
    g_down0, g_up0 = down_grad(0), up_grad(0)
    g_down0.cross()
    g_up0.cross()
    live.seal(g_attn1, g_up1, g_down1)

    g_down0.start()
    g_attn1.start()
    g_up1.start()
    attend_back(0)
    g_attn0 = attend_grad(0)
    g_attn0.cross()
    live.seal(g_down0, g_attn1, g_up1)

    g_up0.start()
    g_down0.start()
    g_attn1.start()
    norm_back(0, 0, live.attn0[0])
    out_keep, out_other = feed_down(1)
    out_act = live.feed1[0][:length] + (out_keep[:length] + out_other[length:].astype(f32))
    live.put(out_act=out_act.astype(bf16), down=finish_down(1, g_down1, []))
    live.seal(g_up0, g_down0, g_attn1)

    g_attn0.start()
    g_up0.start()
    g_down0.start()
    live.put(big=finish(1, g_attn1, g_up1, []), table1=table_grad(1), table0=table_grad(0))
    live.seal(g_attn0, g_up0, g_down0)

    g_attn0.start()
    g_up0.start()
    live.seal(g_attn0, g_up0)

    g_attn0.start()
    live.put(down=finish_down(0, g_down0, live.down))
    live.seal(g_attn0)

    grad_big, new_m_big, step_big = finish(0, g_attn0, g_up0, live.big)
    grad_down, new_m_down, step_down = live.down
    grad_table = jnp.concatenate([live.table0, live.table1], 0)
    new_m_table, step_table = adam_update(m_table, v_table, grad_table)
    return (
        live.out_act[None],
        live.d_low[:length][None],
        grad_big,
        grad_down,
        grad_table,
        new_m_big,
        new_m_down,
        new_m_table,
        step_big,
        step_down,
        step_table,
    )


def solution(mesh):
    both = ("dp", "fsdp")
    rows, middle, last = P(both, None, None), P(None, both, None), P(None, both)
    return jax.shard_map(
        partial(body, mesh.shape["dp"], mesh.shape["fsdp"]),
        mesh=mesh,
        in_specs=(rows, rows, P(both, None), P(both), middle, middle, last)
        + 2 * (middle, middle, last),
        out_specs=(rows, rows) + 3 * (middle, middle, last),
        check_vma=False,
    )
```

```python
import itertools
import math
from functools import partial

import jax
import jax.numpy as jnp
from jax import lax
from jax.experimental import pallas as pl
from jax.experimental.pallas import tpu as pltpu
from jax.sharding import PartitionSpec as P

HEADS = 16

beta_one = 0.9
beta_two = 0.999
first_fix = 1.0 - 0.9**10
second_fix = 1.0 - 0.999**10

f32 = jnp.float32
bf16 = jnp.bfloat16

VMEM = pl.BlockSpec(memory_space=pltpu.VMEM)
SMEM = pl.BlockSpec(memory_space=pltpu.SMEM)
ANY = pl.BlockSpec(memory_space=pl.ANY)

CORE = ("dp", 1)
SIDE = ("dp", 2)


def masks(size):
    return [1 << k for k in reversed(range(size.bit_length() - 1))]


class Slice:
    def __init__(self, dp, fsdp):
        self.high = [("dp", m) for m in masks(dp) if m > 2]
        self.deep = [("fsdp", m) for m in masks(fsdp)]
        self.size = {"dp": dp, "fsdp": fsdp}

    def flip(self, value, bit):
        axis, mask = bit
        return lax.ppermute(value, axis, [(i, i ^ mask) for i in range(self.size[axis])])


def mine(bit):
    axis, mask = bit
    return (lax.axis_index(axis) // mask) % 2


def call(kernel, outs, operands, specs, scratch=(), flops=0, name=None):
    held = [(v.shape, v.dtype) for v, spec in zip(operands, specs) if spec is VMEM] + list(outs)
    held += [(s.shape, s.dtype) for s in scratch if hasattr(s, "memory_space") and s.memory_space == pltpu.VMEM]
    held = sum(math.prod(shape) * jnp.dtype(kind).itemsize for shape, kind in held)
    return pl.pallas_call(
        kernel,
        out_shape=[jax.ShapeDtypeStruct(shape, kind) for shape, kind in outs],
        in_specs=specs,
        out_specs=[VMEM] * len(outs),
        scratch_shapes=list(scratch),
        compiler_params=pltpu.CompilerParams(vmem_limit_bytes=held + (8 << 20)),
        name=name,
    )(*operands)


def merge(own, other, bit, pos):
    side = mine(bit)
    return jnp.where(side == 0, jnp.stack([own, other], pos), jnp.stack([other, own], pos))


def split(value, bit, pos):
    side = mine(bit)
    keep = lax.dynamic_index_in_dim(value, side, pos, keepdims=False)
    send = lax.dynamic_index_in_dim(value, 1 - side, pos, keepdims=False)
    return keep, send


def interleave_kernel(side, own, other, *outs):
    each = own.shape[0] // len(outs)
    for n, out in enumerate(outs):
        part = pl.ds(n * each, each)
        out[:, pl.ds(side[0], 1)] = own[part][:, None]
        out[:, pl.ds(1 - side[0], 1)] = other[part][:, None]


def interleave(own, other, bit, before, outs=1):
    rows, n = own.shape
    shape = (before, rows // before, n)
    whole = (before // outs, 2, rows // before, n)
    result = call(
        interleave_kernel,
        outs * [(whole, own.dtype)],
        [mine(bit)[None], own.reshape(shape), other.reshape(shape)],
        [SMEM, VMEM, VMEM],
        name="interleave",
    )
    return [part.reshape(-1, n) for part in result]


def prepare_kernel(side, big, table, first, first_sent, up0, up0_sent, after, after_sent, out, sems):
    width = out.shape[-1] * 2
    span, chunk = first.shape[1] // 6 // 128 * 128, up0.shape[1] // 2
    third = 3 * width
    copies = []
    for layer, qkv, up in ((0, (first, first_sent), (up0, up0_sent)), (1, (after, after_sent), (after, after_sent))):
        for x, target, upper in ((side[0], qkv[0], up[0]), (1 - side[0], qkv[1], up[1])):
            for n in range(third // (2 * span)):
                at = pl.multiple_of((2 * n + x) * span, 128)
                copies.append((big.at[layer, :, pl.ds(at, span)], target.at[:, pl.ds(n * span, span)]))
            base = 0 if layer == 0 else third // 2
            for n in range(2):
                at = pl.multiple_of(4 * width + (2 * n + x) * chunk, 128)
                copies.append((big.at[layer, :, pl.ds(at, chunk)], upper.at[:, pl.ds(base + n * chunk, chunk)]))
        for k in range(2):
            copies.append((big.at[layer, :, pl.ds(third + k * width // 2, width // 2)], out.at[layer, k]))
    for target in (first, first_sent):
        copies.append((table, target.at[:, pl.ds(third // 2, 128)]))
    copies = [pltpu.make_async_copy(a, b, sems.at[n]) for n, (a, b) in enumerate(copies)]
    for copy in copies:
        copy.start()
    for copy in copies:
        copy.wait()


def place_first_kernel(side, keep, other, out, own):
    part = keep.shape[1] - 128
    wide = out.shape[-1]
    for source, x in ((keep, side[0]), (other, 1 - side[0])):
        own[pl.ds(x, 1), :, pl.ds(0, part)] = source[:, pl.ds(0, part)][None]
        own[pl.ds(x, 1), :, pl.ds(part + wide, 128)] = source[:, pl.ds(part, 128)][None]
    own[:, :, pl.ds(part, wide)] = out[...]


def place_next_kernel(side, keep, other, out, own):
    wide = out.shape[-1]
    part = 3 * wide
    for source, x in ((keep, side[0]), (other, 1 - side[0])):
        own[pl.ds(x, 1), :, pl.ds(0, part)] = source[:, pl.ds(0, part)][None]
        own[pl.ds(2 + x, 1)] = source[:, pl.ds(part, part + wide)][None]
    own[pl.ds(0, 2), :, pl.ds(part, wide)] = out[...]


class Gather:
    def __init__(self, sl, own, lead, top_first=False, twins=False):
        self.sl, self.value, self.lead, self.top_first, self.twins = sl, own, lead, top_first, twins
        self.have, self.air, self.quarters = [], None, None
        near = sl.high[:0:-1]
        if top_first:
            self.steps = [sl.high[:1], near + sl.deep[:-1], sl.deep[-1:]]
        else:
            self.steps = [sl.deep[:-1], sl.deep[-1:] + near]
        core = mine(CORE)
        self.place = jnp.stack([jnp.zeros_like(core) if top_first else mine(sl.high[0]), core])

    def before(self, bit):
        order = self.sl.high + self.sl.deep
        count = sum(order.index(b) < order.index(bit) for b in self.have)
        return (1 + self.twins) * (1 << count) * (1 if bit in self.sl.high else self.lead)

    def start(self):
        if not self.steps:
            self.air = self.sl.flip(self.value, self.sl.high[0]), self.sl.flip(self.value, CORE)
            return
        *others, self.bit = self.steps.pop(0)
        for bit in others:
            other = self.sl.flip(self.value, bit)
            self.value = interleave(self.value, other, bit, self.before(bit))[0]
            self.have.append(bit)
        self.air = self.sl.flip(self.value, self.bit)

    def land(self):
        air, self.air = self.air, None
        if isinstance(air, tuple):
            self.quarters, self.value = [self.value, *air], None
            return
        last = (self.top_first or self.twins) and not self.steps
        halves = interleave(self.value, air, self.bit, self.before(self.bit), 1 + last)
        self.have.append(self.bit)
        if last and self.twins:
            self.value = halves
        elif last:
            self.quarters = [*halves, self.sl.flip(halves[0], CORE)]
            self.value = None
        else:
            self.value = halves[0]

    def part(self, n):
        made = Gather(self.sl, self.value[n], self.lead)
        made.steps = []
        return made

    def finish(self):
        self.quarters = [*self.quarters, self.sl.flip(self.quarters[1], CORE)]


def add_low_kernel(one, two, out):
    out[...] = (one[...].astype(f32) + two[...].astype(f32)).astype(bf16)


def add_split_kernel(side, *refs):
    *parts, kept, sent = refs
    for at, out in ((side[0], kept), (1 - side[0], sent)):
        total = parts[0][:, pl.ds(at, 1)].astype(f32)
        for other in parts[1:]:
            total = total + other[:, pl.ds(at, 1)].astype(f32)
        out[...] = total.astype(bf16)[:, 0]


def cross_split_kernel(side, own, own_other, top, top_other, kept, sent):
    for n, (one, two) in enumerate(((own, own_other), (top, top_other))):
        for at, out in ((side[0], kept), (1 - side[0], sent)):
            total = one[:, pl.ds(at, 1)].astype(f32) + two[:, pl.ds(at, 1)].astype(f32)
            out[n] = total.astype(bf16)[:, 0]


class Scatter:
    def __init__(self, sl, quarters, lead, top_last=False):
        self.sl, self.quarters, self.value, self.lead, self.top_last = sl, quarters, None, lead, top_last
        top, near, deep = sl.high[:1], sl.high[1:], sl.deep
        self.have = sl.high + deep
        if top_last:
            self.steps = [deep[-1:], deep[-2::-1] + near, top]
        else:
            self.steps = [top, near + deep[-1:], deep[-2::-1]]

    def before(self, bit):
        order = self.sl.high + self.sl.deep
        count = sum(order.index(b) < order.index(bit) for b in self.have)
        return (1 << count) * (1 if bit in self.sl.high else self.lead)

    def side(self, bit):
        return jnp.zeros((1,), jnp.int32) if bit == self.sl.high[0] else mine(bit)[None]

    def cross(self):
        own, top, core, both = self.quarters
        top_other = self.sl.flip(both, CORE)
        core_other = self.sl.flip(core, CORE)
        rows, n = top.shape
        if not self.top_last:
            (send,) = call(
                add_low_kernel, [(top.shape, bf16)], [top, top_other], [VMEM] * 2, name="add_low"
            )
            self.quarters = [[own, core_other], send]
            return
        bit = self.steps[0][0]
        before = self.before(bit) // 2
        shape = (before, 2, rows // 2 // before, n)
        half = ((2, before, rows // 2 // before, n), bf16)
        keep, send = call(
            cross_split_kernel,
            [half, half],
            [self.side(bit), *(v.reshape(shape) for v in (own, core_other, top, top_other))],
            [SMEM] + [VMEM] * 4,
            name="cross_split",
        )
        self.quarters = [[keep.reshape(-1, n)], send.reshape(-1, n)]

    def split(self, other, bit):
        parts = [*self.quarters[0], other]
        if bit is None:
            self.value = sum(part.astype(f32) for part in parts)
            self.quarters = None
            return
        before = self.before(bit)
        rows, n = other.shape
        shape = (before, 2, rows // 2 // before, n)
        half = ((before, rows // 2 // before, n), bf16)
        keep, send = call(
            add_split_kernel,
            [half, half],
            [self.side(bit), *(part.reshape(shape) for part in parts)],
            [SMEM] + [VMEM] * len(parts),
            name="add_split",
        )
        self.quarters = [[keep.reshape(-1, n)], send.reshape(-1, n)]

    def start(self):
        bits = self.steps.pop(0)
        for n, bit in enumerate(bits):
            self.air = self.sl.flip(self.quarters[1], bit)
            self.have.remove(bit)
            if n < len(bits) - 1:
                self.split(self.air, bits[n + 1])
        self.next = self.steps[0][0] if self.steps else None

    def land(self):
        other, self.air = self.air, None
        self.split(other, self.next)


class Live:
    def __init__(self, **values):
        self.flows = []
        self.values = values

    def flow(self, made):
        self.flows.append(made)
        return made

    def __getattr__(self, name):
        return self.values[name]

    def put(self, **values):
        self.values.update(values)

    def drop(self, *names):
        for name in names:
            del self.values[name]

    def seal(self, *landing):
        kept = (
            self.values,
            [(made.value, made.quarters) for made in self.flows],
            [made.air for made in landing],
        )
        self.values, flown, airs = lax.optimization_barrier(kept)
        for made, (made.value, made.quarters) in zip(self.flows, flown):
            pass
        for made, made.air in zip(landing, airs):
            made.land()


def dot(left, right):
    return jnp.dot(left, right, preferred_element_type=f32)


def dot_t(left, right):
    return lax.dot_general(left, right, (((1,), (1,)), ((), ())), preferred_element_type=f32)


def t_dot(left, right):
    return lax.dot_general(left, right, (((0,), (0,)), ((), ())), preferred_element_type=f32)


def fetch(place, quarters, whole, lead, sems):
    width = whole.shape[1]
    block = whole.shape[0] // (4 * lead)
    copies = []
    for n, part in enumerate(quarters):
        top = place[0] if n % 2 == 0 else 1 - place[0]
        core = place[1] if n < 2 else 1 - place[1]
        for a in range(lead):
            at = pl.multiple_of(((top * lead + a) * 2 + core) * block, block)
            source = part.at[pl.ds(a * block, block), pl.ds(0, width)]
            copies.append(
                pltpu.make_async_copy(source, whole.at[pl.ds(at, block)], sems.at[n * lead + a])
            )
    for copy in copies:
        copy.start()
    return copies


def norm(hidden):
    centred = hidden - jnp.mean(hidden, axis=-1, keepdims=True)
    scale = lax.rsqrt(jnp.mean(centred * centred, axis=-1, keepdims=True) + 1e-05)
    return centred * scale, scale


def put_rows(outs, cols, value):
    rows = value.shape[0] // len(outs)
    for r, out in enumerate(outs):
        out[:, cols] = value[r * rows : (r + 1) * rows].astype(bf16)


def theirs(others, r, rows):
    if len(others) == 2:
        return others[1 - r][...].astype(f32)
    return others[0][pl.ds((1 - r) * rows, rows)].astype(f32)


def gains_at(gains, r, place, width):
    return gains[pl.ds(r, 1), pl.ds(place * width, width)]


def add_norm(which, parts, gains, total, out):
    base, *shares = parts
    rows, width = out.shape[0] // 2, out.shape[1]
    for r in range(2):
        block = pl.ds(r * rows, rows)
        value = base[block]
        if shares:
            value = value + (shares[0][block] + theirs(shares[1:], r, rows))
            total[block] = value
        gain, bias = [gains_at(gains, r, 2 * which + n, width) for n in range(2)]
        out[block] = (norm(value)[0] * gain + bias).astype(bf16)


def norm_back(which, d_out, keep, others, hidden, gains, total, low, d_gain, d_shift):
    rows, width = d_out.shape[0] // 2, d_out.shape[1]
    for r in range(2):
        block = pl.ds(r * rows, rows)
        grad = keep[block] + theirs(others, r, rows)
        normed, scale = norm(hidden[block])
        if r == 0:
            d_gain[...] = jnp.sum(grad * normed, axis=0, keepdims=True)
            d_shift[...] = jnp.sum(grad, axis=0, keepdims=True)
        e = grad * gains_at(gains, r, 2 * which, width)
        part = e - jnp.mean(e, axis=-1, keepdims=True)
        part = part - normed * jnp.mean(e * normed, axis=-1, keepdims=True)
        value = d_out[block] + scale * part
        total[block] = value
        low[block] = value.astype(bf16)


def norm_back_kernel(which, d_out, keep, *refs):
    norm_back(which, d_out, keep, refs[:-6], *refs[-6:])


def gains_kernel(lead, count, rows, place, pick, q0, q1, q2, q3, first, second, held, wide, sems):
    copies = []
    for n, part in enumerate((q0, q1, q2, q3)):
        source = part.at[:, pl.ds(part.shape[1] - 128, 128)]
        copies.append(pltpu.make_async_copy(source, held.at[n], sems.at[n]))
    for copy in copies:
        copy.start()
    for copy in copies:
        copy.wait()
    wide[...] = held[...].astype(f32)
    deep = wide.shape[1] // (lead * rows)
    for n in range(4):
        top = place[0] if n % 2 == 0 else 1 - place[0]
        core = place[1] if n < 2 else 1 - place[1]
        for a in range(lead):
            for z in range(deep):
                cols = pl.multiple_of((((top * lead + a) * 2 + core) * deep + z) * 128, 128)
                base = (a * deep + z) * rows
                for r in range(2):
                    first[pl.ds(r, 1), pl.ds(cols, 128)] = wide[n, pl.ds(base, 1)]
                    second[pl.ds(r, 1), pl.ds(cols, 128)] = wide[n, pl.ds(base + 1 + pick[r], 1)]


def score(q, k, allowed, size):
    scores = jnp.where(allowed, dot_t(q, k) * size, -1e30)
    exponent = jnp.exp(scores - jnp.max(scores, axis=-1, keepdims=True))
    return exponent / jnp.sum(exponent, axis=-1, keepdims=True)


def lanes_of(which, shape):
    lane = lax.broadcasted_iota(jnp.int32, shape, 1)
    return (lane < shape[1] // 2) if which == 0 else (lane >= shape[1] // 2)


def out_block(weight, k, block, at):
    count = weight.shape[0] // (2 * block)
    wide = weight.shape[1] - at
    return jnp.concatenate([weight[pl.ds((2 * h + k) * block, block), pl.ds(at, wide)] for h in range(count)], 0)


def attend_kernel(ways, size, lead, block, place, *refs):
    refs, (weight, sems) = refs[:-2], refs[-2:]
    refs, lows = refs[:-ways], refs[-ways:]
    *parts, gains, q0, q1, q2, q3, allow, total, f, qkv, mixed, keep = refs
    copies = fetch(place, (q0, q1, q2, q3), weight, lead, sems)
    add_norm(0, parts, gains, total, f)
    for copy in copies:
        copy.wait()
    length = allow.shape[-1]
    third = qkv.shape[1] // 3
    for n in range(3):
        cols = pl.ds(n * third, third)
        qkv[:, cols] = dot(f[...], weight[:, cols]).astype(bf16)

    def one_row(r, carry):
        at = pl.ds(pl.multiple_of(r * length, length), length)
        allowed = allow[r] > 0
        for p in range(third // 128):
            q = qkv[at, pl.ds(p * 128, 128)]
            k = qkv[at, pl.ds(third + p * 128, 128)]
            v = qkv[at, pl.ds(2 * third + p * 128, 128)]
            halves = []
            for h in range(2):
                probs = score(jnp.where(lanes_of(h, q.shape), q, 0), k, allowed, size)
                halves.append(dot(probs.astype(bf16), v))
            mixed[at, pl.ds(p * 128, 128)] = jnp.where(
                lanes_of(0, q.shape), halves[0], halves[1]
            ).astype(bf16)
        return carry

    lax.fori_loop(0, f.shape[0] // length, one_row, 0)
    for k in range(2):
        cols = pl.ds(k * third, third)
        value = dot(mixed[...], out_block(weight, k, block, 3 * third))
        keep[:, cols] = value
        put_rows(lows, cols, value)


def attend_back_kernel(ways, size, lead, block, place, d_out, part, *refs):
    refs, (weight, d_mixed, sems) = refs[:-3], refs[-3:]
    refs, lows = refs[:-ways], refs[-ways:]
    *others, attended, gains, q0, q1, q2, q3, allow, qkv, total, d, d_gain, d_shift, d_qkv, keep = refs
    copies = fetch(place, (q0, q1, q2, q3), weight, lead, sems)
    norm_back(1, d_out, part, others, attended, gains, total, d, d_gain, d_shift)
    for copy in copies:
        copy.wait()
    length = allow.shape[-1]
    third = qkv.shape[1] // 3
    value = dot_t(d[:, pl.ds(0, third)], out_block(weight, 0, block, 3 * third))
    value = value + dot_t(d[:, pl.ds(third, third)], out_block(weight, 1, block, 3 * third))
    d_mixed[...] = value.astype(bf16)

    def one_row(r, carry):
        at = pl.ds(pl.multiple_of(r * length, length), length)
        allowed = allow[r] > 0
        for p in range(third // 128):
            q = qkv[at, pl.ds(p * 128, 128)]
            k = qkv[at, pl.ds(third + p * 128, 128)]
            v = qkv[at, pl.ds(2 * third + p * 128, 128)]
            dm = d_mixed[at, pl.ds(p * 128, 128)]
            d_q, d_k, d_v = [], [], []
            for h in range(2):
                pick = lanes_of(h, q.shape)
                probs = score(jnp.where(pick, q, 0), k, allowed, size)
                d_probs = dot_t(jnp.where(pick, dm, 0), v)
                d_v.append(t_dot(probs.astype(bf16), dm))
                inner = jnp.sum(probs * d_probs, axis=-1, keepdims=True)
                d_scores = (probs * (d_probs - inner)).astype(bf16)
                d_q.append(dot(d_scores, k))
                d_k.append(t_dot(d_scores, q))
            pick = lanes_of(0, q.shape)
            for n, (halves, scale) in enumerate(((d_q, size), (d_k, size), (d_v, 1.0))):
                value = jnp.where(pick, halves[0], halves[1]) * scale
                d_qkv[at, pl.ds(n * third + p * 128, 128)] = value.astype(bf16)
        return carry

    lax.fori_loop(0, d.shape[0] // length, one_row, 0)
    for n in range(keep.shape[1] // 256):
        cols = pl.ds(n * 256, 256)
        value = dot_t(d_qkv[...], weight[cols, pl.ds(0, 3 * third)])
        keep[:, cols] = value
        put_rows(lows, cols, value)


def up(f, weight, pre, active):
    for n in range(pre.shape[1] // 256):
        cols = pl.ds(n * 256, 256)
        value = dot(f[...], weight[:, cols])
        pre[:, cols] = value
        active[:, cols] = jax.nn.gelu(value).astype(bf16)


def down(active, weight, keep, lows):
    for n in range(keep.shape[1] // 256):
        cols = pl.ds(n * 256, 256)
        value = dot(active[...], weight[:, cols])
        keep[:, cols] = value
        put_rows(lows, cols, value)


def feed_kernel(ways, lead, up_place, dn_place, *refs):
    refs, (w_up, w_dn, up_sems, dn_sems) = refs[:-4], refs[-4:]
    refs, lows = refs[:-ways], refs[-ways:]
    *parts, gains, u0, u1, u2, u3, n0, n1, n2, n3, total, f, pre, active, keep = refs
    up_copies = fetch(up_place, (u0, u1, u2, u3), w_up, lead, up_sems)
    dn_copies = fetch(dn_place, (n0, n1, n2, n3), w_dn, lead // 2, dn_sems)
    add_norm(1, parts, gains, total, f)
    for copy in up_copies:
        copy.wait()
    up(f, w_up, pre, active)
    for copy in dn_copies:
        copy.wait()
    down(active, w_dn, keep, lows)


def down_kernel(lead, place, active, q0, q1, q2, q3, keep, low, weight, sems):
    for copy in fetch(place, (q0, q1, q2, q3), weight, lead, sems):
        copy.wait()
    down(active, weight, keep, (low,))


def gelu_slope(x):
    c = 0.7978845608028654
    t = jnp.tanh(c * (x + 0.044715 * (x * x * x)))
    return 0.5 * (1.0 + t) + 0.5 * x * (1.0 - t * t) * (c * (1.0 + 3 * 0.044715 * (x * x)))


def feed_back(d, pre, w_up, w_dn, d_pre, keep, lows):
    for n in range(pre.shape[1] // 256):
        cols = pl.ds(n * 256, 256)
        d_pre[:, cols] = (gelu_slope(pre[:, cols]) * dot_t(d[...], w_dn[cols])).astype(bf16)
    for n in range(keep.shape[1] // 256):
        cols = pl.ds(n * 256, 256)
        value = dot_t(d_pre[...], w_up[cols])
        keep[:, cols] = value
        put_rows(lows, cols, value)


def feed_back_kernel(ways, lead, up_place, dn_place, d_out, part, *refs):
    refs, (w_up, w_dn, up_sems, dn_sems) = refs[:-4], refs[-4:]
    refs, lows = refs[:-ways], refs[-ways:]
    *others, hidden, gains, pre, u0, u1, u2, u3, n0, n1, n2, n3, total, d, d_gain, d_shift, d_pre, keep = refs
    copies = fetch(dn_place, (n0, n1, n2, n3), w_dn, lead // 2, dn_sems)
    copies += fetch(up_place, (u0, u1, u2, u3), w_up, lead, up_sems)
    norm_back(0, d_out, part, others, hidden, gains, total, d, d_gain, d_shift)
    for copy in copies:
        copy.wait()
    feed_back(d, pre, w_up, w_dn, d_pre, keep, lows)


def feed_turn_kernel(ways, lead, up_place, dn_place, *refs):
    refs, (w_up, w_dn, pre, up_sems, dn_sems) = refs[:-5], refs[-5:]
    refs, lows = refs[:-ways], refs[-ways:]
    *parts, gains, d, u0, u1, u2, u3, n0, n1, n2, n3, total, f, active, d_pre, keep = refs
    up_copies = fetch(up_place, (u0, u1, u2, u3), w_up, lead, up_sems)
    dn_copies = fetch(dn_place, (n0, n1, n2, n3), w_dn, lead // 2, dn_sems)
    add_norm(1, parts, gains, total, f)
    for copy in up_copies:
        copy.wait()
    up(f, w_up, pre, active)
    for copy in dn_copies:
        copy.wait()
    feed_back(d, pre, w_up, w_dn, d_pre, keep, lows)


def columns_of(place, value, lead):
    block = value.shape[1] // (4 * lead)
    parts = []
    for n in range(4):
        top = place[0] if n % 2 == 0 else 1 - place[0]
        core = place[1] if n < 2 else 1 - place[1]
        starts = [((top * lead + a) * 2 + core) * block for a in range(lead)]
        if block % 128 == 0:
            starts = [pl.multiple_of(at, 128) for at in starts]
        parts.append(jnp.concatenate([value[:, pl.ds(at, block)] for at in starts], 1))
    return parts


def weight_grad_kernel(lead, aligned, place, left, right, *outs):
    place = place if aligned else (0, 0)
    for part, out in zip(columns_of(place, left, lead), outs):
        out[...] = t_dot(part, right[...]).astype(bf16)


def attend_grad_kernel(lead, aligned, place, left, mixed, d_qkv, d, *outs):
    width = d_qkv.shape[1]
    third = width // 3
    place = place if aligned else (0, 0)
    block = left.shape[1] // (4 * lead)
    lefts, inners = columns_of(place, left, lead), columns_of(place, mixed, lead // 2)
    for part, inner, out in zip(lefts, inners, outs):
        out[:, pl.ds(0, width)] = t_dot(part, d_qkv[...]).astype(bf16)
        value = t_dot(inner, d[...]).astype(bf16)
        for h in range(inner.shape[1] // block):
            for k in range(2):
                out[pl.ds((2 * h + k) * block, block), pl.ds(width, third)] = value[
                    h * block : (h + 1) * block, k * third : (k + 1) * third
                ]


def turn(sl, value, lead):
    tokens, width = value.shape
    value = value.reshape(tokens, 2, lead, 2, width // (4 * lead))
    value = jnp.stack(split(value, sl.high[0], 1), 1)
    return jnp.stack(split(value, CORE, 3), 3).reshape(tokens, width)


def finish_kernel(span, chunk, side, keep, other, out, *refs):
    grad, new_m, step = refs[-3:]
    third = out.shape[-1]
    total = grad.shape[-1] - 8 * third
    pieces, (m, v) = [], refs[:2]
    base, filled = 8 * third, 0
    while 2 * filled < total:
        one, two, *refs = refs
        (m, v) = refs[:2]
        pieces.append((one, two, base + 2 * filled, chunk))
        filled += one.shape[1]
    for one, two, base, width in [(keep, other, 0, span)] + pieces:
        for source, x in ((one, side[0]), (two, 1 - side[0])):
            for n in range(source.shape[1] // width):
                at = pl.multiple_of(base + (2 * n + x) * width, 128)
                grad[0, :, pl.ds(at, width)] = source[:, pl.ds(n * width, width)]
    for k in range(2):
        grad[0, :, pl.ds((6 + k) * third, third)] = out[k]
    for n in range(grad.shape[2] // 1024):
        cols = pl.ds(n * 1024, 1024)
        new_m[0, :, cols], step[0, :, cols] = adam_update(m[0, :, cols], v[0, :, cols], grad[0, :, cols])


def finish_down_kernel(value, m, v, *refs):
    grad, new_m, step = refs[-3:]
    grad[0] = value[...]
    new_m[0], step[0] = adam_update(m[0], v[0], value[...])


def update(kernel, layer, shape, parts, specs, moments, before, name):
    one = pl.BlockSpec((1, *shape[1:]), lambda i: (layer, 0, 0))
    count = len(parts) + 2
    return pl.pallas_call(
        kernel,
        grid=(1,),
        out_shape=[jax.ShapeDtypeStruct(shape, f32)] * 3,
        in_specs=[*specs, one, one, *len(before) * [ANY]],
        out_specs=[one] * 3,
        input_output_aliases={count + n: n for n in range(len(before))},
        compiler_params=pltpu.CompilerParams(vmem_limit_bytes=20 << 20),
        name=name,
    )(*parts, *moments, *before)


def adam_update(moment, square, gradient):
    moment = beta_one * moment + (1.0 - beta_one) * gradient
    square = beta_two * square + (1.0 - beta_two) * gradient * gradient
    update = moment / first_fix / (jnp.sqrt(square / second_fix) + 1e-08)
    return (moment, update)


def dma(count):
    return pltpu.SemaphoreType.DMA((count,))


def body(
    dp,
    fsdp,
    inputs,
    cotangent,
    segment_ids,
    section_ids,
    w_big,
    w_down,
    norm_table,
    m_big,
    m_down,
    m_table,
    v_big,
    v_down,
    v_table,
):
    sl = Slice(dp, fsdp)
    length, width = inputs.shape[1:]
    rows = w_big.shape[1]
    feeds = w_down.shape[1]
    feed = w_big.shape[2] - 4 * width
    high = dp // 4
    lead = high
    half, part = width // 2, 3 * width // 2
    block = fsdp * rows
    count = norm_table.shape[0]
    size = (width // HEADS) ** -0.5
    two_f, two_b = ((2 * length, width), f32), ((2 * length, width), bf16)
    wide_b = ((2 * length, feed // 2), bf16)

    def lows(ways):
        return ways * [((2 // ways * length, width), bf16)]

    quarter = ((width // 4, 2 * width), bf16)
    gain_row = ((1, width), f32)
    place = jnp.stack([mine(sl.high[0]), mine(CORE)])
    w_attn = pltpu.VMEM((width, 2 * width), bf16)
    w_upper = pltpu.VMEM((width, feed // 2), bf16)
    w_lower = pltpu.VMEM((feed // 2, width), bf16)

    def qkv_sides(layer):
        value = w_big[layer, :, : 3 * width].reshape(rows, 3, high, 2, 2 * block)
        return [v.reshape(rows, part) for v in split(value, SIDE, 3)]

    def up_sides(layer):
        value = w_big[layer, :, 4 * width :].reshape(rows, high, 2, 2 * fsdp * feeds)
        return [v.reshape(rows, feed // 2) for v in split(value, SIDE, 2)]

    def prepare(table_part):
        shapes = 2 * [(rows, part + 128)] + 2 * [(rows, feed // 2)] + 2 * [(rows, part + feed // 2)]
        shapes.append((2, 2, rows, half))
        if rows % 16 == 0:
            return call(
                prepare_kernel,
                [(shape, bf16) for shape in shapes],
                [mine(SIDE)[None], w_big, table_part],
                [SMEM, ANY, ANY],
                [dma(2 * (6 * high + 6) + 2)],
                name="prepare",
            )
        first = [jnp.concatenate([v, table_part], -1) for v in qkv_sides(0)]
        after = [jnp.concatenate([a, b], -1) for a, b in zip(qkv_sides(1), up_sides(1))]
        out = w_big[:, :, 3 * width : 4 * width].reshape(2, rows, 2, half)
        return [*first, *up_sides(0), *after, jnp.swapaxes(out, 1, 2)]

    def place_sides(kernel, shape, keep, other, out, name):
        return call(
            kernel,
            [(shape, bf16)],
            [mine(SIDE)[None], keep, other, out],
            [SMEM, VMEM, VMEM, VMEM],
            name=name,
        )[0]

    live = Live()
    downs = [live.flow(Gather(sl, w_down[n], 1, n == 1)) for n in range(2)]

    downs[0].start()
    downs[1].start()
    table_part = norm_table.reshape(-1)
    table_part = jnp.pad(table_part, (0, rows * 128 - table_part.shape[0])).reshape(rows, 128)
    first, first_sent, up0, up0_sent, after, after_sent, out_proj = prepare(table_part)
    live.put(
        first=[first, sl.flip(first_sent, SIDE)],
        up=[up0, up0_sent],
        after=[after, after_sent],
        out=out_proj,
    )
    live.seal(downs[0], downs[1])

    own = place_sides(
        place_first_kernel, (2, rows, 2 * width + 128), *live.first, live.out[0], "place_first"
    )
    attns = [live.flow(Gather(sl, own.reshape(2 * rows, -1), 2))]
    attns[0].start()
    downs[0].start()
    extra = jnp.zeros((16, width), bf16)
    extra = extra.at[0, :length].set(segment_ids[0].astype(bf16))
    extra = extra.at[1, 0].set(section_ids[0].astype(bf16))
    pack = jnp.concatenate([inputs[0], cotangent[0], extra], 0)
    live.put(
        up=[live.up[0], sl.flip(live.up[1], SIDE)],
        after=[live.after[0], sl.flip(live.after[1], SIDE)],
        pack=[pack, sl.flip(pack, SIDE)],
    )
    live.drop("first")
    live.seal(attns[0], downs[0])

    ups = [live.flow(Gather(sl, interleave(*live.up, SIDE, 1)[0], 2))]
    downs[0].start()
    attns[0].start()
    ups[0].start()
    own = place_sides(
        place_next_kernel, (4, rows, 2 * width), *live.after, live.out[1], "place_next"
    )
    live.put(own=own)
    live.drop("up", "after", "out")
    packed = jnp.stack(live.pack)
    extras = packed[:, 2 * length :]
    segments = extras[:, 0, :length].astype(f32)
    same = segments[:, :, None] == segments[:, None, :]
    position = jnp.arange(length)
    live.put(
        hidden=packed[:, :length].reshape(2 * length, width).astype(f32),
        d_low=packed[:, length : 2 * length].reshape(2 * length, width),
        sections=extras[:, 1, 0].astype(jnp.int32),
        allows=[
            (same & (position[:, None] >= position[None, :])).astype(f32),
            same.astype(f32),
        ],
    )
    live.drop("pack")
    live.seal(attns[0], ups[0], downs[0])

    twins = live.flow(Gather(sl, live.own.reshape(4 * rows, -1), 2, twins=True))
    live.drop("own")
    attns[0].start()
    twins.start()
    ups[0].start()
    downs[0].finish()
    live.seal(attns[0], ups[0], twins)

    def gains_of(quarters, sections):
        wide = norm_table.shape[1]
        if wide == 128:
            return call(
                partial(gains_kernel, lead, count, rows),
                2 * [((2, 4 * width), f32)],
                [place, sections, *quarters],
                [SMEM, SMEM] + [ANY] * 4,
                [
                    pltpu.VMEM((4, width // 4, 128), bf16),
                    pltpu.VMEM((4, width // 4, 128), f32),
                    dma(4),
                ],
                name="gains",
            )
        parts = jnp.stack([q[:, 2 * width :] for q in quarters])
        parts = parts.reshape(4, lead // 2, 2, fsdp, rows * 128)[..., : count * wide]
        parts = parts.reshape(4, lead // 2, 2, fsdp, count, wide)
        pick = jnp.concatenate([jnp.zeros((2,), jnp.int32), 1 + sections])
        pick = (pick[:, None] == jnp.arange(count)[None, :]).astype(bf16)
        picked = jnp.einsum("sr,qhxdrj->qshxdj", pick, parts, preferred_element_type=f32)
        own, top, core, both = picked
        both = merge(merge(own, core, CORE, 3), merge(top, both, CORE, 3), sl.high[0], 1)
        return list(both.reshape(2, 2, 4 * width))

    def cross():
        live.put(other=[sl.flip(row, SIDE) for row in live.low])

    def shares():
        return [live.keep, *live.other]

    def attend(layer, base, ways=2):
        parts = [base] if layer == 0 else [base, *shares()]
        total, first, qkv, mixed, keep, *low = call(
            partial(attend_kernel, ways, size, lead, 2 * block),
            [two_f, two_b, ((2 * length, part), bf16), ((2 * length, half), bf16), two_f, *lows(ways)],
            [
                attns[layer].place,
                *parts,
                live.gains[layer],
                *attns[layer].quarters,
                live.allows[layer],
            ],
            [SMEM] + [VMEM] * (len(parts) + 1) + [ANY] * 4 + [VMEM],
            [w_attn, dma(4 * lead)],
            name="attend",
        )
        hidden = base if layer == 0 else total
        live.put(**{f"attn{layer}": (hidden, first, qkv, mixed)}, keep=keep, low=low)

    def feed_forward(layer, ways=2):
        attended, second, pre, active, keep, *low = call(
            partial(feed_kernel, ways, lead),
            [two_f, two_b, (wide_b[0], f32), wide_b, two_f, *lows(ways)],
            [
                ups[layer].place,
                downs[layer].place,
                live.values[f"attn{layer}"][0],
                *shares(),
                live.gains[layer],
                *ups[layer].quarters,
                *downs[layer].quarters,
            ],
            [SMEM, SMEM] + [VMEM] * (3 + len(live.other)) + [ANY] * 8,
            [w_upper, w_lower, dma(4 * lead), dma(2 * lead)],
            name="feed",
        )
        live.put(**{f"feed{layer}": (attended, second, pre, active)}, keep=keep, low=low)

    def feed_turn(layer, ways=2):
        attended, second, active, d_pre, keep, *low = call(
            partial(feed_turn_kernel, ways, lead),
            [two_f, two_b, wide_b, wide_b, two_f, *lows(ways)],
            [
                ups[layer].place,
                downs[layer].place,
                live.values[f"attn{layer}"][0],
                *shares(),
                live.gains[layer],
                live.d_low,
                *ups[layer].quarters,
                *downs[layer].quarters,
            ],
            [SMEM, SMEM] + [VMEM] * (4 + len(live.other)) + [ANY] * 8,
            [w_upper, w_lower, pltpu.VMEM(wide_b[0], f32), dma(4 * lead), dma(2 * lead)],
            name="feed_turn",
        )
        live.put(**{f"feed{layer}": (attended, second, None, active)}, d_pre=d_pre, keep=keep, low=low)

    def feed_down(layer):
        keep, *low = call(
            partial(down_kernel, lead // 2),
            [two_f, *lows(1)],
            [downs[layer].place, live.values[f"feed{layer}"][3], *downs[layer].quarters],
            [SMEM, VMEM, ANY, ANY, ANY, ANY],
            [w_lower, dma(2 * lead)],
            name="down",
        )
        live.put(keep=keep, low=low)

    def feed_back(layer, ways=1):
        grad, d_low, d_gain, d_shift, d_pre, keep, *low = call(
            partial(feed_back_kernel, ways, lead),
            [two_f, two_b, gain_row, gain_row, wide_b, two_f, *lows(ways)],
            [
                ups[layer].place,
                downs[layer].place,
                live.grad,
                *shares(),
                live.values[f"attn{layer + 1}"][0],
                live.gains[layer + 1],
                live.values[f"feed{layer}"][2],
                *ups[layer].quarters,
                *downs[layer].quarters,
            ],
            [SMEM, SMEM] + [VMEM] * (5 + len(live.other)) + [ANY] * 8,
            [w_upper, w_lower, dma(4 * lead), dma(2 * lead)],
            name="feed_back",
        )
        live.put(grad=grad, d_low=d_low, d_pre=d_pre, keep=keep, low=low)
        live.put(**{f"gains{layer + 1}0": jnp.concatenate([d_gain, d_shift], 1)})

    def down_grad(layer, top_last=False):
        aligned = feed // 4 // lead % 128 == 0
        active = live.values[f"feed{layer}"][3]
        parts = call(
            partial(weight_grad_kernel, lead // 2, aligned),
            [((feed // 8, width), bf16)] * 4,
            [place, active if aligned else turn(sl, active, lead // 2), live.d_low],
            [SMEM, VMEM, VMEM],
            name="down_grad",
        )
        return live.flow(Scatter(sl, parts, 1, top_last))

    def up_grad(layer, piece=None):
        aligned = block % 128 == 0
        second, right = live.values[f"feed{layer}"][1], live.d_pre
        columns = feed // 2
        if piece is not None:
            columns = feed // 4
            right = right[:, piece * columns : (piece + 1) * columns]
        parts = call(
            partial(weight_grad_kernel, lead, aligned),
            [((width // 4, columns), bf16)] * 4,
            [place, second if aligned else turn(sl, second, lead), right],
            [SMEM, VMEM, VMEM],
            name="up_grad",
        )
        return live.flow(Scatter(sl, parts, 2, piece == 1))

    def norm_back(which, layer, hidden):
        grad, d_low, d_gain, d_shift = call(
            partial(norm_back_kernel, which),
            [two_f, two_b, gain_row, gain_row],
            [live.grad, *shares(), hidden, live.gains[layer]],
            [VMEM] * (4 + len(live.other)),
            name="norm_back",
        )
        live.put(grad=grad, d_low=d_low)
        live.put(**{f"gains{layer}{which}": jnp.concatenate([d_gain, d_shift], 1)})

    def attend_back(layer, ways=1):
        grad, d_low, d_gain, d_shift, d_qkv, keep, *low = call(
            partial(attend_back_kernel, ways, size, lead, 2 * block),
            [two_f, two_b, gain_row, gain_row, ((2 * length, part), bf16), two_f, *lows(ways)],
            [
                attns[layer].place,
                live.grad,
                *shares(),
                live.values[f"feed{layer}"][0],
                live.gains[layer],
                *attns[layer].quarters,
                live.allows[layer],
                live.values[f"attn{layer}"][2],
            ],
            [SMEM] + [VMEM] * (4 + len(live.other)) + [ANY] * 4 + [VMEM] * 2,
            [w_attn, pltpu.VMEM((2 * length, half), bf16), dma(4 * lead)],
            name="attend_back",
        )
        live.put(grad=grad, d_low=d_low, d_qkv=d_qkv, keep=keep, low=low)
        live.put(**{f"gains{layer}1": jnp.concatenate([d_gain, d_shift], 1)})

    def attend_grad(layer):
        hidden, first, qkv, mixed = live.values[f"attn{layer}"]
        aligned = block % 128 == 0
        if not aligned:
            first, mixed = turn(sl, first, lead), turn(sl, mixed, lead // 2)
        parts = call(
            partial(attend_grad_kernel, lead, aligned),
            [quarter] * 4,
            [place, first, mixed, live.d_qkv, live.d_low],
            [SMEM] + [VMEM] * 4,
            name="attend_grad",
        )
        return live.flow(Scatter(sl, parts, 2))

    def sides(flow, wide, columns):
        value = flow.value.reshape(2, rows, wide)
        keep, send = split(value[..., :columns], SIDE, 0)
        return keep, sl.flip(send, SIDE), value[..., columns:]

    def finish(layer, g_attn, g_ups, before):
        keep, other, out = g_attn
        return update(
            partial(finish_kernel, 2 * block, 2 * fsdp * feeds),
            layer,
            w_big.shape,
            [mine(SIDE)[None], keep, other, out, *itertools.chain(*g_ups)],
            [SMEM] + [VMEM] * (3 + 2 * len(g_ups)),
            [m_big, v_big],
            before,
            "finish",
        )

    def finish_down(layer, flow, before):
        return update(
            finish_down_kernel,
            layer,
            w_down.shape,
            [flow.value],
            [VMEM],
            [m_down, v_down],
            before,
            "finish_down",
        )

    def table_terms():
        first, second = [
            jnp.concatenate([live.values[f"gains{n}0"], live.values[f"gains{n}1"]], 1) for n in range(2)
        ]
        hit = jnp.arange(count - 1) == section_ids[0]
        terms = jnp.concatenate([first, jnp.where(hit[:, None], second, 0.0)], 0)
        terms = terms.reshape(count, high, 2, 2, fsdp, norm_table.shape[1])
        return jnp.moveaxis(terms, 0, 4)

    def table_step(pos, bits):
        value = live.table
        for bit in bits:
            keep, send = split(value, bit, pos)
            value = keep + sl.flip(send, bit)
        live.put(table=value)

    ups[0].start()
    twins.start()
    attns[0].finish()
    live.put(gains=gains_of(attns[0].quarters, live.sections))
    attend(0, live.hidden)
    cross()
    live.seal(ups[0], twins)

    attns.append(live.flow(twins.part(0)))
    ups.append(live.flow(twins.part(1)))
    live.flows.remove(twins)
    attns[1].start()
    downs[1].start()
    ups[0].finish()
    feed_forward(0)
    cross()
    live.seal(attns[1], downs[1])

    ups[1].start()
    downs[1].start()
    attns[1].finish()
    attend(1, live.feed0[0])
    cross()
    live.seal(ups[1], downs[1])

    ups[1].finish()
    downs[1].finish()
    live.put(grad=live.d_low.astype(f32))
    feed_turn(1)
    g_down1 = down_grad(1, True)
    g_down1.cross()
    g_down1.start()
    live.seal()

    g_up1 = up_grad(1)
    g_up1.cross()
    g_up1.start()
    cross()
    attend_back(1)
    live.seal(g_down1, g_up1)

    g_down1.start()
    g_up1.start()
    g_attn1 = attend_grad(1)
    g_attn1.cross()
    g_attn1.start()
    cross()
    feed_back(0)
    g_down0 = down_grad(0)
    live.seal(g_down1, g_up1, g_attn1)

    cross()
    g_down0.cross()
    g_down0.start()
    g_down1.start()
    g_up1.start()
    g_attn1.start()
    g_up0b = up_grad(0, 1)
    g_up0b.cross()
    attend_back(0)
    live.seal(g_down0, g_down1, g_up1, g_attn1)

    cross()
    g_attn0 = attend_grad(0)
    g_attn0.cross()
    g_attn0.start()
    g_up0b.start()
    g_attn1.start()
    g_down0.start()
    g_up0a = up_grad(0, 0)
    norm_back(0, 0, live.attn0[0])
    live.put(down=finish_down(1, g_down1, []), up1=sides(g_up1, feed // 2, feed // 2)[:2])
    live.seal(g_attn0, g_attn1, g_down0, g_up0b)

    g_up0a.cross()
    g_up0a.start()
    g_attn0.start()
    g_up0b.start()
    g_down0.start()
    live.put(table=table_terms())
    table_step(2, [CORE])
    table_step(1, [SIDE])
    table = live.table.reshape(*(len(sl.high) + len(sl.deep)) * [2], count, -1)
    live.put(table=table)
    attn1 = sides(g_attn1, 2 * width, part)
    live.put(big=finish(1, attn1, [live.up1], []))
    feed_down(1)
    live.seal(g_up0a, g_attn0, g_up0b, g_down0)

    g_up0a.start()
    g_attn0.start()
    g_up0b.start()
    cross()
    out_act = live.feed1[0][:length] + (live.keep[:length] + live.other[0][length:].astype(f32))
    table_step(0, sl.high)
    table_step(-3, sl.deep[-1:])
    live.put(out_act=out_act.astype(bf16), down=finish_down(0, g_down0, live.down))
    live.seal(g_up0a, g_attn0, g_up0b)

    g_up0a.start()
    live.put(attn0=sides(g_attn0, 2 * width, part), up0b=sides(g_up0b, feed // 4, feed // 4)[:2])
    live.seal(g_up0a)

    table_step(0, sl.deep[:-1])
    up0a = sides(g_up0a, feed // 4, feed // 4)[:2]
    grad_big, new_m_big, step_big = finish(0, live.attn0, [up0a, live.up0b], live.big)
    grad_down, new_m_down, step_down = live.down
    grad_table = live.table
    new_m_table, step_table = adam_update(m_table, v_table, grad_table)
    return (
        live.out_act[None],
        live.d_low[:length][None],
        grad_big,
        grad_down,
        grad_table,
        new_m_big,
        new_m_down,
        new_m_table,
        step_big,
        step_down,
        step_table,
    )


def solution(mesh):
    both = ("dp", "fsdp")
    rows, middle, last = P(both, None, None), P(None, both, None), P(None, both)
    return jax.shard_map(
        partial(body, mesh.shape["dp"], mesh.shape["fsdp"]),
        mesh=mesh,
        in_specs=(rows, rows, P(both, None), P(both), middle, middle, last)
        + 2 * (middle, middle, last),
        out_specs=(rows, rows) + 3 * (middle, middle, last),
        check_vma=False,
    )
```

```python
import itertools
import math
from functools import partial

import jax
import jax.numpy as jnp
from jax import lax
from jax.experimental import pallas as pl
from jax.experimental.pallas import tpu as pltpu
from jax.sharding import PartitionSpec as P

HEADS = 16

beta_one = 0.9
beta_two = 0.999
first_fix = 1.0 - 0.9**10
second_fix = 1.0 - 0.999**10

f32 = jnp.float32
bf16 = jnp.bfloat16

VMEM = pl.BlockSpec(memory_space=pltpu.VMEM)
SMEM = pl.BlockSpec(memory_space=pltpu.SMEM)
ANY = pl.BlockSpec(memory_space=pl.ANY)

CORE = ("dp", 1)
SIDE = ("dp", 2)


def masks(size):
    return [1 << k for k in reversed(range(size.bit_length() - 1))]


class Slice:
    def __init__(self, dp, fsdp):
        self.high = [("dp", m) for m in masks(dp) if m > 2]
        self.deep = [("fsdp", m) for m in masks(fsdp)]
        self.size = {"dp": dp, "fsdp": fsdp}

    def flip(self, value, bit):
        axis, mask = bit
        return lax.ppermute(value, axis, [(i, i ^ mask) for i in range(self.size[axis])])


def mine(bit):
    axis, mask = bit
    return (lax.axis_index(axis) // mask) % 2


def call(kernel, outs, operands, specs, scratch=(), flops=0, name=None):
    held = [(v.shape, v.dtype) for v, spec in zip(operands, specs) if spec is VMEM] + list(outs)
    held += [(s.shape, s.dtype) for s in scratch if hasattr(s, "memory_space") and s.memory_space == pltpu.VMEM]
    held = sum(math.prod(shape) * jnp.dtype(kind).itemsize for shape, kind in held)
    return pl.pallas_call(
        kernel,
        out_shape=[jax.ShapeDtypeStruct(shape, kind) for shape, kind in outs],
        in_specs=specs,
        out_specs=[VMEM] * len(outs),
        scratch_shapes=list(scratch),
        compiler_params=pltpu.CompilerParams(vmem_limit_bytes=held + (3 << 20)),
        name=name,
    )(*operands)


def merge(own, other, bit, pos):
    side = mine(bit)
    return jnp.where(side == 0, jnp.stack([own, other], pos), jnp.stack([other, own], pos))


def split(value, bit, pos):
    side = mine(bit)
    keep = lax.dynamic_index_in_dim(value, side, pos, keepdims=False)
    send = lax.dynamic_index_in_dim(value, 1 - side, pos, keepdims=False)
    return keep, send


def interleave_kernel(count, side, *refs):
    owns, others, outs = refs[:count], refs[count : 2 * count], refs[2 * count :]
    each = count * owns[0].shape[0] // len(outs)
    for n, (own, other) in enumerate(zip(owns, others)):
        for m in range(own.shape[0]):
            out, at = outs[(n * own.shape[0] + m) // each], (n * own.shape[0] + m) % each
            out[pl.ds(at, 1), pl.ds(side[0], 1)] = own[pl.ds(m, 1)][:, None]
            out[pl.ds(at, 1), pl.ds(1 - side[0], 1)] = other[pl.ds(m, 1)][:, None]


def interleave(owns, others, bit, before, outs=1):
    rows, n = owns[0].shape
    count = len(owns)
    shape = (before, rows // before, n)
    whole = (count * before // outs, 2, rows // before, n)
    result = call(
        partial(interleave_kernel, count),
        outs * [(whole, owns[0].dtype)],
        [mine(bit)[None], *(v.reshape(shape) for v in (*owns, *others))],
        [SMEM] + [VMEM] * (2 * count),
        name="interleave",
    )
    return [part.reshape(-1, n) for part in result]


def prepare_kernel(side, big, table, first, first_sent, up0, up0_sent, after, after_sent, out, sems):
    width = out.shape[-1] * 2
    span, chunk = first.shape[1] // 6 // 128 * 128, up0.shape[1] // 2
    third = 3 * width
    copies = []
    for layer, qkv, up in ((0, (first, first_sent), (up0, up0_sent)), (1, (after, after_sent), (after, after_sent))):
        for x, target, upper in ((side[0], qkv[0], up[0]), (1 - side[0], qkv[1], up[1])):
            for n in range(third // (2 * span)):
                at = pl.multiple_of((2 * n + x) * span, 128)
                copies.append((big.at[layer, :, pl.ds(at, span)], target.at[:, pl.ds(n * span, span)]))
            base = 0 if layer == 0 else third // 2
            for n in range(2):
                at = pl.multiple_of(4 * width + (2 * n + x) * chunk, 128)
                copies.append((big.at[layer, :, pl.ds(at, chunk)], upper.at[:, pl.ds(base + n * chunk, chunk)]))
        for k in range(2):
            copies.append((big.at[layer, :, pl.ds(third + k * width // 2, width // 2)], out.at[layer, k]))
    for target in (first, first_sent):
        copies.append((table, target.at[:, pl.ds(third // 2, 128)]))
    copies = [pltpu.make_async_copy(a, b, sems.at[n]) for n, (a, b) in enumerate(copies)]
    for copy in copies:
        copy.start()
    for copy in copies:
        copy.wait()


def place_first_kernel(side, keep, other, out, own):
    part = keep.shape[1] - 128
    wide = out.shape[-1]
    for source, x in ((keep, side[0]), (other, 1 - side[0])):
        own[pl.ds(x, 1), :, pl.ds(0, part)] = source[:, pl.ds(0, part)][None]
        own[pl.ds(x, 1), :, pl.ds(part + wide, 128)] = source[:, pl.ds(part, 128)][None]
    own[:, :, pl.ds(part, wide)] = out[...]


def place_next_kernel(side, keep, other, out, own):
    wide = out.shape[-1]
    part = 3 * wide
    for source, x in ((keep, side[0]), (other, 1 - side[0])):
        own[pl.ds(x, 1), :, pl.ds(0, part)] = source[:, pl.ds(0, part)][None]
        own[pl.ds(2 + x, 1)] = source[:, pl.ds(part, part + wide)][None]
    own[pl.ds(0, 2), :, pl.ds(part, wide)] = out[...]


class Gather:
    def __init__(self, sl, own, lead, top_first=False, twins=False):
        self.sl, self.value, self.lead, self.top_first, self.twins = sl, own, lead, top_first, twins
        self.have, self.air, self.quarters = [], None, None
        near = sl.high[:0:-1]
        if top_first:
            self.steps = [sl.high[:1], near + sl.deep[:-1], sl.deep[-1:]]
        else:
            self.steps = [sl.deep[:-1], sl.deep[-1:] + near]
        core = mine(CORE)
        self.place = jnp.stack([jnp.zeros_like(core) if top_first else mine(sl.high[0]), core])

    def before(self, bit):
        order = self.sl.high + self.sl.deep
        count = sum(order.index(b) < order.index(bit) for b in self.have)
        return (1 + self.twins) * (1 << count) * (1 if bit in self.sl.high else self.lead)

    def start(self):
        if not self.steps:
            self.air = self.sl.flip(self.value, self.sl.high[0]), self.sl.flip(self.value, CORE)
            return
        *others, self.bit = self.steps.pop(0)
        for bit in others:
            other = self.sl.flip(self.value, bit)
            self.value = interleave([self.value], [other], bit, self.before(bit))[0]
            self.have.append(bit)
        self.air = self.sl.flip(self.value, self.bit)

    def land(self):
        air, self.air = self.air, None
        if isinstance(air, tuple):
            self.quarters, self.value = [self.value, *air], None
            return
        last = (self.top_first or self.twins) and not self.steps
        halves = interleave([self.value], [air], self.bit, self.before(self.bit), 1 + last)
        self.have.append(self.bit)
        if last and self.twins:
            self.value = halves
        elif last:
            self.quarters = [*halves, self.sl.flip(halves[0], CORE)]
            self.value = None
        else:
            self.value = halves[0]

    def join(self, other):
        made = Gather(self.sl, None, self.lead, twins=True)
        airs = self.air, other.air
        made.value = interleave([self.value, other.value], airs, self.bit, self.before(self.bit))[0]
        made.have, made.steps = self.have + [self.bit], self.steps
        return made

    def part(self, n):
        made = Gather(self.sl, self.value[n], self.lead)
        made.steps = []
        return made

    def finish(self):
        self.quarters = [*self.quarters, self.sl.flip(self.quarters[1], CORE)]


def add_low_kernel(one, two, out):
    out[...] = (one[...].astype(f32) + two[...].astype(f32)).astype(bf16)


def add_split_kernel(side, *refs):
    *parts, kept, sent = refs
    for at, out in ((side[0], kept), (1 - side[0], sent)):
        total = parts[0][:, pl.ds(at, 1)].astype(f32)
        for other in parts[1:]:
            total = total + other[:, pl.ds(at, 1)].astype(f32)
        out[...] = total.astype(bf16)[:, 0]


def cross_split_kernel(side, own, own_other, top, top_other, kept, sent):
    for n, (one, two) in enumerate(((own, own_other), (top, top_other))):
        for at, out in ((side[0], kept), (1 - side[0], sent)):
            total = one[:, pl.ds(at, 1)].astype(f32) + two[:, pl.ds(at, 1)].astype(f32)
            out[n] = total.astype(bf16)[:, 0]


class Scatter:
    def __init__(self, sl, quarters, lead, top_last=False):
        self.sl, self.quarters, self.value, self.lead, self.top_last = sl, quarters, None, lead, top_last
        top, near, deep = sl.high[:1], sl.high[1:], sl.deep
        self.have = sl.high + deep
        if top_last:
            self.steps = [deep[-1:], deep[-2::-1] + near, top]
        else:
            self.steps = [top, near + deep[-1:], deep[-2::-1]]

    def before(self, bit):
        order = self.sl.high + self.sl.deep
        count = sum(order.index(b) < order.index(bit) for b in self.have)
        return (1 << count) * (1 if bit in self.sl.high else self.lead)

    def side(self, bit):
        return jnp.zeros((1,), jnp.int32) if bit == self.sl.high[0] else mine(bit)[None]

    def cross(self):
        own, top, core, both = self.quarters
        top_other = self.sl.flip(both, CORE)
        core, _ = lax.optimization_barrier((core, top_other))
        core_other = self.sl.flip(core, CORE)
        rows, n = top.shape
        if not self.top_last:
            (send,) = call(
                add_low_kernel, [(top.shape, bf16)], [top, top_other], [VMEM] * 2, name="add_low"
            )
            self.quarters = [[own, core_other], send]
            return
        bit = self.steps[0][0]
        before = self.before(bit) // 2
        shape = (before, 2, rows // 2 // before, n)
        half = ((2, before, rows // 2 // before, n), bf16)
        keep, send = call(
            cross_split_kernel,
            [half, half],
            [self.side(bit), *(v.reshape(shape) for v in (own, core_other, top, top_other))],
            [SMEM] + [VMEM] * 4,
            name="cross_split",
        )
        self.quarters = [[keep.reshape(-1, n)], send.reshape(-1, n)]

    def split(self, other, bit):
        parts = [*self.quarters[0], other]
        if bit is None:
            self.value = sum(part.astype(f32) for part in parts)
            self.quarters = None
            return
        before = self.before(bit)
        rows, n = other.shape
        shape = (before, 2, rows // 2 // before, n)
        half = ((before, rows // 2 // before, n), bf16)
        keep, send = call(
            add_split_kernel,
            [half, half],
            [self.side(bit), *(part.reshape(shape) for part in parts)],
            [SMEM] + [VMEM] * len(parts),
            name="add_split",
        )
        self.quarters = [[keep.reshape(-1, n)], send.reshape(-1, n)]

    def start(self):
        bits = self.steps.pop(0)
        for n, bit in enumerate(bits):
            self.air = self.sl.flip(self.quarters[1], bit)
            self.have.remove(bit)
            if n < len(bits) - 1:
                self.split(self.air, bits[n + 1])
        self.next = self.steps[0][0] if self.steps else None

    def land(self):
        other, self.air = self.air, None
        self.split(other, self.next)


class Live:
    def __init__(self, **values):
        self.flows = []
        self.values = values

    def flow(self, made):
        self.flows.append(made)
        return made

    def __getattr__(self, name):
        return self.values[name]

    def put(self, **values):
        self.values.update(values)

    def drop(self, *names):
        for name in names:
            del self.values[name]

    def seal(self, *landing, keep=()):
        landing = [*keep, *landing]
        kept = (
            self.values,
            [(made.value, made.quarters) for made in self.flows],
            [made.air for made in landing],
        )
        self.values, flown, airs = lax.optimization_barrier(kept)
        for made, (made.value, made.quarters) in zip(self.flows, flown):
            pass
        for n, (made, made.air) in enumerate(zip(landing, airs)):
            if n >= len(keep):
                made.land()


def dot(left, right):
    return jnp.dot(left, right, preferred_element_type=f32)


def dot_t(left, right):
    return lax.dot_general(left, right, (((1,), (1,)), ((), ())), preferred_element_type=f32)


def t_dot(left, right):
    return lax.dot_general(left, right, (((0,), (0,)), ((), ())), preferred_element_type=f32)


def fetch(place, quarters, whole, lead, sems):
    width = whole.shape[1]
    block = whole.shape[0] // (4 * lead)
    copies = []
    for n, part in enumerate(quarters):
        top = place[0] if n % 2 == 0 else 1 - place[0]
        core = place[1] if n < 2 else 1 - place[1]
        for a in range(lead):
            at = pl.multiple_of(((top * lead + a) * 2 + core) * block, block)
            source = part.at[pl.ds(a * block, block), pl.ds(0, width)]
            copies.append(
                pltpu.make_async_copy(source, whole.at[pl.ds(at, block)], sems.at[n * lead + a])
            )
    for copy in copies:
        copy.start()
    return copies


def norm(hidden):
    centred = hidden - jnp.mean(hidden, axis=-1, keepdims=True)
    scale = lax.rsqrt(jnp.mean(centred * centred, axis=-1, keepdims=True) + 1e-05)
    return centred * scale, scale


def put_rows(outs, cols, value):
    rows = value.shape[0] // len(outs)
    for r, out in enumerate(outs):
        out[:, cols] = value[r * rows : (r + 1) * rows].astype(bf16)


def theirs(others, r, rows):
    if len(others) == 2:
        return others[1 - r][...].astype(f32)
    return others[0][pl.ds((1 - r) * rows, rows)].astype(f32)


def gains_at(gains, r, place, width):
    return gains[pl.ds(r, 1), pl.ds(place * width, width)]


def add_norm(which, parts, gains, total, out):
    base, *shares = parts
    rows, width = out.shape[0] // 2, out.shape[1]
    for r in range(2):
        block = pl.ds(r * rows, rows)
        value = base[block]
        if shares:
            value = value + (shares[0][block] + theirs(shares[1:], r, rows))
            total[block] = value
        gain, bias = [gains_at(gains, r, 2 * which + n, width) for n in range(2)]
        out[block] = (norm(value)[0] * gain + bias).astype(bf16)


def norm_back(which, d_out, keep, others, hidden, gains, total, low, d_gain, d_shift):
    rows, width = d_out.shape[0] // 2, d_out.shape[1]
    for r in range(2):
        block = pl.ds(r * rows, rows)
        grad = keep[block] + theirs(others, r, rows)
        normed, scale = norm(hidden[block])
        if r == 0:
            d_gain[...] = jnp.sum(grad * normed, axis=0, keepdims=True)
            d_shift[...] = jnp.sum(grad, axis=0, keepdims=True)
        e = grad * gains_at(gains, r, 2 * which, width)
        part = e - jnp.mean(e, axis=-1, keepdims=True)
        part = part - normed * jnp.mean(e * normed, axis=-1, keepdims=True)
        value = d_out[block] + scale * part
        total[block] = value
        low[block] = value.astype(bf16)


def norm_back_kernel(which, d_out, keep, *refs):
    norm_back(which, d_out, keep, refs[:-6], *refs[-6:])


def gains_kernel(lead, count, rows, place, pick, q0, q1, q2, q3, first, second, held, wide, sems):
    copies = []
    for n, part in enumerate((q0, q1, q2, q3)):
        source = part.at[:, pl.ds(part.shape[1] - 128, 128)]
        copies.append(pltpu.make_async_copy(source, held.at[n], sems.at[n]))
    for copy in copies:
        copy.start()
    for copy in copies:
        copy.wait()
    wide[...] = held[...].astype(f32)
    deep = wide.shape[1] // (lead * rows)
    for n in range(4):
        top = place[0] if n % 2 == 0 else 1 - place[0]
        core = place[1] if n < 2 else 1 - place[1]
        for a in range(lead):
            for z in range(deep):
                cols = pl.multiple_of((((top * lead + a) * 2 + core) * deep + z) * 128, 128)
                base = (a * deep + z) * rows
                for r in range(2):
                    first[pl.ds(r, 1), pl.ds(cols, 128)] = wide[n, pl.ds(base, 1)]
                    second[pl.ds(r, 1), pl.ds(cols, 128)] = wide[n, pl.ds(base + 1 + pick[r], 1)]


def score(q, k, allowed, size):
    scores = jnp.where(allowed, dot_t(q, k) * size, -1e30)
    exponent = jnp.exp(scores - jnp.max(scores, axis=-1, keepdims=True))
    return exponent / jnp.sum(exponent, axis=-1, keepdims=True)


def lanes_of(which, shape):
    lane = lax.broadcasted_iota(jnp.int32, shape, 1)
    return (lane < shape[1] // 2) if which == 0 else (lane >= shape[1] // 2)


def out_block(weight, k, block, at):
    count = weight.shape[0] // (2 * block)
    wide = weight.shape[1] - at
    return jnp.concatenate([weight[pl.ds((2 * h + k) * block, block), pl.ds(at, wide)] for h in range(count)], 0)


def attend_kernel(ways, size, lead, block, place, *refs):
    refs, (weight, sems) = refs[:-2], refs[-2:]
    refs, lows = refs[:-ways], refs[-ways:]
    *parts, gains, q0, q1, q2, q3, allow, total, f, qkv, mixed, keep = refs
    copies = fetch(place, (q0, q1, q2, q3), weight, lead, sems)
    add_norm(0, parts, gains, total, f)
    for copy in copies:
        copy.wait()
    length = allow.shape[-1]
    third = qkv.shape[1] // 3
    for n in range(3):
        cols = pl.ds(n * third, third)
        qkv[:, cols] = dot(f[...], weight[:, cols]).astype(bf16)

    def one_row(r, carry):
        at = pl.ds(pl.multiple_of(r * length, length), length)
        allowed = allow[r] > 0
        for p in range(third // 128):
            q = qkv[at, pl.ds(p * 128, 128)]
            k = qkv[at, pl.ds(third + p * 128, 128)]
            v = qkv[at, pl.ds(2 * third + p * 128, 128)]
            halves = []
            for h in range(2):
                probs = score(jnp.where(lanes_of(h, q.shape), q, 0), k, allowed, size)
                halves.append(dot(probs.astype(bf16), v))
            mixed[at, pl.ds(p * 128, 128)] = jnp.where(
                lanes_of(0, q.shape), halves[0], halves[1]
            ).astype(bf16)
        return carry

    lax.fori_loop(0, f.shape[0] // length, one_row, 0)
    for k in range(2):
        cols = pl.ds(k * third, third)
        value = dot(mixed[...], out_block(weight, k, block, 3 * third))
        keep[:, cols] = value
        put_rows(lows, cols, value)


def attend_back_kernel(ways, size, lead, block, place, d_out, part, *refs):
    refs, (weight, d_mixed, sems) = refs[:-3], refs[-3:]
    refs, lows = refs[:-ways], refs[-ways:]
    *others, attended, gains, q0, q1, q2, q3, allow, qkv, total, d, d_gain, d_shift, d_qkv, keep = refs
    copies = fetch(place, (q0, q1, q2, q3), weight, lead, sems)
    norm_back(1, d_out, part, others, attended, gains, total, d, d_gain, d_shift)
    for copy in copies:
        copy.wait()
    length = allow.shape[-1]
    third = qkv.shape[1] // 3
    value = dot_t(d[:, pl.ds(0, third)], out_block(weight, 0, block, 3 * third))
    value = value + dot_t(d[:, pl.ds(third, third)], out_block(weight, 1, block, 3 * third))
    d_mixed[...] = value.astype(bf16)

    def one_row(r, carry):
        at = pl.ds(pl.multiple_of(r * length, length), length)
        allowed = allow[r] > 0
        for p in range(third // 128):
            q = qkv[at, pl.ds(p * 128, 128)]
            k = qkv[at, pl.ds(third + p * 128, 128)]
            v = qkv[at, pl.ds(2 * third + p * 128, 128)]
            dm = d_mixed[at, pl.ds(p * 128, 128)]
            d_q, d_k, d_v = [], [], []
            for h in range(2):
                pick = lanes_of(h, q.shape)
                probs = score(jnp.where(pick, q, 0), k, allowed, size)
                d_probs = dot_t(jnp.where(pick, dm, 0), v)
                d_v.append(t_dot(probs.astype(bf16), dm))
                inner = jnp.sum(probs * d_probs, axis=-1, keepdims=True)
                d_scores = (probs * (d_probs - inner)).astype(bf16)
                d_q.append(dot(d_scores, k))
                d_k.append(t_dot(d_scores, q))
            pick = lanes_of(0, q.shape)
            for n, (halves, scale) in enumerate(((d_q, size), (d_k, size), (d_v, 1.0))):
                value = jnp.where(pick, halves[0], halves[1]) * scale
                d_qkv[at, pl.ds(n * third + p * 128, 128)] = value.astype(bf16)
        return carry

    lax.fori_loop(0, d.shape[0] // length, one_row, 0)
    for n in range(keep.shape[1] // 256):
        cols = pl.ds(n * 256, 256)
        value = dot_t(d_qkv[...], weight[cols, pl.ds(0, 3 * third)])
        keep[:, cols] = value
        put_rows(lows, cols, value)


def up(f, weight, pre, active):
    for n in range(pre.shape[1] // 256):
        cols = pl.ds(n * 256, 256)
        value = dot(f[...], weight[:, cols])
        pre[:, cols] = value
        active[:, cols] = jax.nn.gelu(value).astype(bf16)


def down(active, weight, keep, lows):
    for n in range(keep.shape[1] // 256):
        cols = pl.ds(n * 256, 256)
        value = dot(active[...], weight[:, cols])
        keep[:, cols] = value
        put_rows(lows, cols, value)


def feed_kernel(ways, lead, up_place, dn_place, *refs):
    refs, (w_up, w_dn, up_sems, dn_sems) = refs[:-4], refs[-4:]
    refs, lows = refs[:-ways], refs[-ways:]
    *parts, gains, u0, u1, u2, u3, n0, n1, n2, n3, total, f, pre, active, keep = refs
    up_copies = fetch(up_place, (u0, u1, u2, u3), w_up, lead, up_sems)
    dn_copies = fetch(dn_place, (n0, n1, n2, n3), w_dn, lead // 2, dn_sems)
    add_norm(1, parts, gains, total, f)
    for copy in up_copies:
        copy.wait()
    up(f, w_up, pre, active)
    for copy in dn_copies:
        copy.wait()
    down(active, w_dn, keep, lows)


def down_kernel(lead, place, active, q0, q1, q2, q3, keep, low, weight, sems):
    for copy in fetch(place, (q0, q1, q2, q3), weight, lead, sems):
        copy.wait()
    down(active, weight, keep, (low,))


def gelu_slope(x):
    c = 0.7978845608028654
    t = jnp.tanh(c * (x + 0.044715 * (x * x * x)))
    return 0.5 * (1.0 + t) + 0.5 * x * (1.0 - t * t) * (c * (1.0 + 3 * 0.044715 * (x * x)))


def feed_back(d, pre, w_up, w_dn, d_pre, keep, lows):
    for n in range(pre.shape[1] // 256):
        cols = pl.ds(n * 256, 256)
        d_pre[:, cols] = (gelu_slope(pre[:, cols]) * dot_t(d[...], w_dn[cols])).astype(bf16)
    for n in range(keep.shape[1] // 256):
        cols = pl.ds(n * 256, 256)
        value = dot_t(d_pre[...], w_up[cols])
        keep[:, cols] = value
        put_rows(lows, cols, value)


def feed_back_kernel(ways, lead, up_place, dn_place, d_out, part, *refs):
    refs, (w_up, w_dn, up_sems, dn_sems) = refs[:-4], refs[-4:]
    refs, lows = refs[:-ways], refs[-ways:]
    *others, hidden, gains, pre, u0, u1, u2, u3, n0, n1, n2, n3, total, d, d_gain, d_shift, d_pre, keep = refs
    copies = fetch(dn_place, (n0, n1, n2, n3), w_dn, lead // 2, dn_sems)
    copies += fetch(up_place, (u0, u1, u2, u3), w_up, lead, up_sems)
    norm_back(0, d_out, part, others, hidden, gains, total, d, d_gain, d_shift)
    for copy in copies:
        copy.wait()
    feed_back(d, pre, w_up, w_dn, d_pre, keep, lows)


def feed_turn_kernel(ways, lead, up_place, dn_place, *refs):
    refs, (w_up, w_dn, pre, up_sems, dn_sems) = refs[:-5], refs[-5:]
    refs, lows = refs[:-ways], refs[-ways:]
    *parts, gains, d, u0, u1, u2, u3, n0, n1, n2, n3, total, f, active, d_pre, keep = refs
    up_copies = fetch(up_place, (u0, u1, u2, u3), w_up, lead, up_sems)
    dn_copies = fetch(dn_place, (n0, n1, n2, n3), w_dn, lead // 2, dn_sems)
    add_norm(1, parts, gains, total, f)
    for copy in up_copies:
        copy.wait()
    up(f, w_up, pre, active)
    for copy in dn_copies:
        copy.wait()
    feed_back(d, pre, w_up, w_dn, d_pre, keep, lows)


def columns_of(place, value, lead):
    block = value.shape[1] // (4 * lead)
    parts = []
    for n in range(4):
        top = place[0] if n % 2 == 0 else 1 - place[0]
        core = place[1] if n < 2 else 1 - place[1]
        starts = [((top * lead + a) * 2 + core) * block for a in range(lead)]
        if block % 128 == 0:
            starts = [pl.multiple_of(at, 128) for at in starts]
        parts.append(jnp.concatenate([value[:, pl.ds(at, block)] for at in starts], 1))
    return parts


def weight_grad_kernel(lead, aligned, place, left, right, *outs):
    place = place if aligned else (0, 0)
    for part, out in zip(columns_of(place, left, lead), outs):
        out[...] = t_dot(part, right[...]).astype(bf16)


def attend_grad_kernel(lead, aligned, place, left, mixed, d_qkv, d, *outs):
    width = d_qkv.shape[1]
    third = width // 3
    place = place if aligned else (0, 0)
    block = left.shape[1] // (4 * lead)
    lefts, inners = columns_of(place, left, lead), columns_of(place, mixed, lead // 2)
    for part, inner, out in zip(lefts, inners, outs):
        out[:, pl.ds(0, width)] = t_dot(part, d_qkv[...]).astype(bf16)
        value = t_dot(inner, d[...]).astype(bf16)
        for h in range(inner.shape[1] // block):
            for k in range(2):
                out[pl.ds((2 * h + k) * block, block), pl.ds(width, third)] = value[
                    h * block : (h + 1) * block, k * third : (k + 1) * third
                ]


def turn(sl, value, lead):
    tokens, width = value.shape
    value = value.reshape(tokens, 2, lead, 2, width // (4 * lead))
    value = jnp.stack(split(value, sl.high[0], 1), 1)
    return jnp.stack(split(value, CORE, 3), 3).reshape(tokens, width)


def finish_kernel(span, chunk, part, side, keep, other, out, *refs):
    grad, new_m, step = refs[-3:]
    third = out.shape[-1]
    total = (grad.shape[-1] - 8 * third) // 2
    late = total - (keep.shape[1] - part)
    m, v = refs[2:4] if late else refs[:2]
    pieces = [(keep, other, 0, 0, part, span), (keep, other, part, 8 * third + 2 * late, total - late, chunk)]
    if late:
        pieces.append((refs[0], refs[1], 0, 8 * third, late, chunk))
    for one, two, first, base, count, width in pieces:
        for source, x in ((one, side[0]), (two, 1 - side[0])):
            for n in range(count // width):
                at = pl.multiple_of(base + (2 * n + x) * width, 128)
                grad[0, :, pl.ds(at, width)] = source[:, pl.ds(first + n * width, width)]
    for k in range(2):
        grad[0, :, pl.ds((6 + k) * third, third)] = out[k]
    for n in range(grad.shape[2] // 1024):
        cols = pl.ds(n * 1024, 1024)
        new_m[0, :, cols], step[0, :, cols] = adam_update(m[0, :, cols], v[0, :, cols], grad[0, :, cols])


def finish_down_kernel(value, m, v, *refs):
    grad, new_m, step = refs[-3:]
    grad[0] = value[...]
    new_m[0], step[0] = adam_update(m[0], v[0], value[...])


def update(kernel, layer, shape, parts, specs, moments, before, name):
    one = pl.BlockSpec((1, *shape[1:]), lambda i: (layer, 0, 0))
    count = len(parts) + 2
    return pl.pallas_call(
        kernel,
        grid=(1,),
        out_shape=[jax.ShapeDtypeStruct(shape, f32)] * 3,
        in_specs=[*specs, one, one, *len(before) * [ANY]],
        out_specs=[one] * 3,
        input_output_aliases={count + n: n for n in range(len(before))},
        compiler_params=pltpu.CompilerParams(vmem_limit_bytes=20 << 20),
        name=name,
    )(*parts, *moments, *before)


def adam_update(moment, square, gradient):
    moment = beta_one * moment + (1.0 - beta_one) * gradient
    square = beta_two * square + (1.0 - beta_two) * gradient * gradient
    update = moment / first_fix / (jnp.sqrt(square / second_fix) + 1e-08)
    return (moment, update)


def dma(count):
    return pltpu.SemaphoreType.DMA((count,))


def body(
    dp,
    fsdp,
    inputs,
    cotangent,
    segment_ids,
    section_ids,
    w_big,
    w_down,
    norm_table,
    m_big,
    m_down,
    m_table,
    v_big,
    v_down,
    v_table,
):
    sl = Slice(dp, fsdp)
    length, width = inputs.shape[1:]
    rows = w_big.shape[1]
    feeds = w_down.shape[1]
    feed = w_big.shape[2] - 4 * width
    high = dp // 4
    lead = high
    half, part = width // 2, 3 * width // 2
    block = fsdp * rows
    count = norm_table.shape[0]
    size = (width // HEADS) ** -0.5
    two_f, two_b = ((2 * length, width), f32), ((2 * length, width), bf16)
    wide_b = ((2 * length, feed // 2), bf16)

    def lows(ways):
        return ways * [((2 // ways * length, width), bf16)]

    quarter = ((width // 4, 2 * width), bf16)
    gain_row = ((1, width), f32)
    place = jnp.stack([mine(sl.high[0]), mine(CORE)])
    w_attn = pltpu.VMEM((width, 2 * width), bf16)
    w_upper = pltpu.VMEM((width, feed // 2), bf16)
    w_lower = pltpu.VMEM((feed // 2, width), bf16)

    def qkv_sides(layer):
        value = w_big[layer, :, : 3 * width].reshape(rows, 3, high, 2, 2 * block)
        return [v.reshape(rows, part) for v in split(value, SIDE, 3)]

    def up_sides(layer):
        value = w_big[layer, :, 4 * width :].reshape(rows, high, 2, 2 * fsdp * feeds)
        return [v.reshape(rows, feed // 2) for v in split(value, SIDE, 2)]

    def prepare(table_part):
        shapes = 2 * [(rows, part + 128)] + 2 * [(rows, feed // 2)] + 2 * [(rows, part + feed // 2)]
        shapes.append((2, 2, rows, half))
        if rows % 16 == 0:
            return call(
                prepare_kernel,
                [(shape, bf16) for shape in shapes],
                [mine(SIDE)[None], w_big, table_part],
                [SMEM, ANY, ANY],
                [dma(2 * (6 * high + 6) + 2)],
                name="prepare",
            )
        first = [jnp.concatenate([v, table_part], -1) for v in qkv_sides(0)]
        after = [jnp.concatenate([a, b], -1) for a, b in zip(qkv_sides(1), up_sides(1))]
        out = w_big[:, :, 3 * width : 4 * width].reshape(2, rows, 2, half)
        return [*first, *up_sides(0), *after, jnp.swapaxes(out, 1, 2)]

    def place_sides(kernel, shape, keep, other, out, name):
        return call(
            kernel,
            [(shape, bf16)],
            [mine(SIDE)[None], keep, other, out],
            [SMEM, VMEM, VMEM, VMEM],
            name=name,
        )[0]

    live = Live()
    downs = [live.flow(Gather(sl, w_down[n], 1, n == 1)) for n in range(2)]

    downs[0].start()
    downs[1].start()
    table_part = norm_table.reshape(-1)
    table_part = jnp.pad(table_part, (0, rows * 128 - table_part.shape[0])).reshape(rows, 128)
    first, first_sent, up0, up0_sent, after, after_sent, out_proj = prepare(table_part)
    live.put(
        first=[first, sl.flip(first_sent, SIDE)],
        up=[up0, up0_sent],
        after=[after, after_sent],
        out=out_proj,
    )
    live.seal(downs[0], downs[1])

    own = place_sides(
        place_first_kernel, (2, rows, 2 * width + 128), *live.first, live.out[0], "place_first"
    )
    attns = [live.flow(Gather(sl, own.reshape(2 * rows, -1), 2))]
    attns[0].start()
    downs[0].start()
    extra = jnp.zeros((16, width), bf16)
    extra = extra.at[0, :length].set(segment_ids[0].astype(bf16))
    extra = extra.at[1, 0].set(section_ids[0].astype(bf16))
    pack = jnp.concatenate([inputs[0], cotangent[0], extra], 0)
    live.put(
        up=[live.up[0], sl.flip(live.up[1], SIDE)],
        after=[live.after[0], sl.flip(live.after[1], SIDE)],
        pack=[pack, sl.flip(pack, SIDE)],
    )
    live.drop("first")
    live.seal(attns[0], downs[0])

    ups = [live.flow(Gather(sl, interleave(live.up[:1], live.up[1:], SIDE, 1)[0], 2))]
    downs[0].start()
    attns[0].start()
    ups[0].start()
    own = place_sides(
        place_next_kernel, (4, rows, 2 * width), *live.after, live.out[1], "place_next"
    )
    live.put(own=own)
    live.drop("up", "after", "out")
    packed = jnp.stack(live.pack)
    extras = packed[:, 2 * length :]
    segments = extras[:, 0, :length].astype(f32)
    same = segments[:, :, None] == segments[:, None, :]
    position = jnp.arange(length)
    live.put(
        hidden=packed[:, :length].reshape(2 * length, width).astype(f32),
        d_low=packed[:, length : 2 * length].reshape(2 * length, width),
        sections=extras[:, 1, 0].astype(jnp.int32),
        allows=[
            (same & (position[:, None] >= position[None, :])).astype(f32),
            same.astype(f32),
        ],
    )
    live.drop("pack")
    live.seal(attns[0], ups[0], downs[0])

    own = live.own.reshape(2, 2 * rows, -1)
    attns.append(live.flow(Gather(sl, own[0], 2)))
    ups.append(live.flow(Gather(sl, own[1], 2)))
    live.drop("own")
    attns[0].start()
    attns[1].start()
    ups[0].start()
    downs[0].finish()
    live.seal(attns[0], ups[0], attns[1])

    def gate(*made):
        airs = [flow.air for flow in made]
        other, airs = lax.optimization_barrier((live.other, airs))
        live.put(other=other)
        for flow, flow.air in zip(made, airs):
            pass

    def gains_of(quarters, sections):
        wide = norm_table.shape[1]
        if wide == 128:
            return call(
                partial(gains_kernel, lead, count, rows),
                2 * [((2, 4 * width), f32)],
                [place, sections, *quarters],
                [SMEM, SMEM] + [ANY] * 4,
                [
                    pltpu.VMEM((4, width // 4, 128), bf16),
                    pltpu.VMEM((4, width // 4, 128), f32),
                    dma(4),
                ],
                name="gains",
            )
        parts = jnp.stack([q[:, 2 * width :] for q in quarters])
        parts = parts.reshape(4, lead // 2, 2, fsdp, rows * 128)[..., : count * wide]
        parts = parts.reshape(4, lead // 2, 2, fsdp, count, wide)
        pick = jnp.concatenate([jnp.zeros((2,), jnp.int32), 1 + sections])
        pick = (pick[:, None] == jnp.arange(count)[None, :]).astype(bf16)
        picked = jnp.einsum("sr,qhxdrj->qshxdj", pick, parts, preferred_element_type=f32)
        own, top, core, both = picked
        both = merge(merge(own, core, CORE, 3), merge(top, both, CORE, 3), sl.high[0], 1)
        return list(both.reshape(2, 2, 4 * width))

    def cross():
        live.put(other=[sl.flip(row, SIDE) for row in live.low])

    def shares():
        return [live.keep, *live.other]

    def attend(layer, base, ways=2):
        parts = [base] if layer == 0 else [base, *shares()]
        total, first, qkv, mixed, keep, *low = call(
            partial(attend_kernel, ways, size, lead, 2 * block),
            [two_f, two_b, ((2 * length, part), bf16), ((2 * length, half), bf16), two_f, *lows(ways)],
            [
                attns[layer].place,
                *parts,
                live.gains[layer],
                *attns[layer].quarters,
                live.allows[layer],
            ],
            [SMEM] + [VMEM] * (len(parts) + 1) + [ANY] * 4 + [VMEM],
            [w_attn, dma(4 * lead)],
            name="attend",
        )
        hidden = base if layer == 0 else total
        live.put(**{f"attn{layer}": (hidden, first, qkv, mixed)}, keep=keep, low=low)

    def feed_forward(layer, ways=2):
        attended, second, pre, active, keep, *low = call(
            partial(feed_kernel, ways, lead),
            [two_f, two_b, (wide_b[0], f32), wide_b, two_f, *lows(ways)],
            [
                ups[layer].place,
                downs[layer].place,
                live.values[f"attn{layer}"][0],
                *shares(),
                live.gains[layer],
                *ups[layer].quarters,
                *downs[layer].quarters,
            ],
            [SMEM, SMEM] + [VMEM] * (3 + len(live.other)) + [ANY] * 8,
            [w_upper, w_lower, dma(4 * lead), dma(2 * lead)],
            name="feed",
        )
        live.put(**{f"feed{layer}": (attended, second, pre, active)}, keep=keep, low=low)

    def feed_turn(layer, ways=2):
        attended, second, active, d_pre, keep, *low = call(
            partial(feed_turn_kernel, ways, lead),
            [two_f, two_b, wide_b, wide_b, two_f, *lows(ways)],
            [
                ups[layer].place,
                downs[layer].place,
                live.values[f"attn{layer}"][0],
                *shares(),
                live.gains[layer],
                live.d_low,
                *ups[layer].quarters,
                *downs[layer].quarters,
            ],
            [SMEM, SMEM] + [VMEM] * (4 + len(live.other)) + [ANY] * 8,
            [w_upper, w_lower, pltpu.VMEM(wide_b[0], f32), dma(4 * lead), dma(2 * lead)],
            name="feed_turn",
        )
        live.put(**{f"feed{layer}": (attended, second, None, active)}, d_pre=d_pre, keep=keep, low=low)

    def feed_down(layer):
        keep, *low = call(
            partial(down_kernel, lead // 2),
            [two_f, *lows(1)],
            [downs[layer].place, live.values[f"feed{layer}"][3], *downs[layer].quarters],
            [SMEM, VMEM, ANY, ANY, ANY, ANY],
            [w_lower, dma(2 * lead)],
            name="down",
        )
        live.put(keep=keep, low=low)

    def feed_back(layer, ways=1):
        grad, d_low, d_gain, d_shift, d_pre, keep, *low = call(
            partial(feed_back_kernel, ways, lead),
            [two_f, two_b, gain_row, gain_row, wide_b, two_f, *lows(ways)],
            [
                ups[layer].place,
                downs[layer].place,
                live.grad,
                *shares(),
                live.values[f"attn{layer + 1}"][0],
                live.gains[layer + 1],
                live.values[f"feed{layer}"][2],
                *ups[layer].quarters,
                *downs[layer].quarters,
            ],
            [SMEM, SMEM] + [VMEM] * (5 + len(live.other)) + [ANY] * 8,
            [w_upper, w_lower, dma(4 * lead), dma(2 * lead)],
            name="feed_back",
        )
        live.put(grad=grad, d_low=d_low, d_pre=d_pre, keep=keep, low=low)
        live.put(**{f"gains{layer + 1}0": jnp.concatenate([d_gain, d_shift], 1)})

    def down_grad(layer, top_last=False):
        aligned = feed // 4 // lead % 128 == 0
        active = live.values[f"feed{layer}"][3]
        parts = call(
            partial(weight_grad_kernel, lead // 2, aligned),
            [((feed // 8, width), bf16)] * 4,
            [place, active if aligned else turn(sl, active, lead // 2), live.d_low],
            [SMEM, VMEM, VMEM],
            name="down_grad",
        )
        return live.flow(Scatter(sl, parts, 1, top_last))

    def up_grad(layer, piece=None):
        aligned = block % 128 == 0
        second, right = live.values[f"feed{layer}"][1], live.d_pre
        columns = feed // 2
        if piece is not None:
            columns = feed // 4
            right = right[:, piece * columns : (piece + 1) * columns]
        parts = call(
            partial(weight_grad_kernel, lead, aligned),
            [((width // 4, columns), bf16)] * 4,
            [place, second if aligned else turn(sl, second, lead), right],
            [SMEM, VMEM, VMEM],
            name="up_grad",
        )
        return live.flow(Scatter(sl, parts, 2, piece == 1))

    def norm_back(which, layer, hidden):
        grad, d_low, d_gain, d_shift = call(
            partial(norm_back_kernel, which),
            [two_f, two_b, gain_row, gain_row],
            [live.grad, *shares(), hidden, live.gains[layer]],
            [VMEM] * (4 + len(live.other)),
            name="norm_back",
        )
        live.put(grad=grad, d_low=d_low)
        live.put(**{f"gains{layer}{which}": jnp.concatenate([d_gain, d_shift], 1)})

    def attend_back(layer, ways=1):
        grad, d_low, d_gain, d_shift, d_qkv, keep, *low = call(
            partial(attend_back_kernel, ways, size, lead, 2 * block),
            [two_f, two_b, gain_row, gain_row, ((2 * length, part), bf16), two_f, *lows(ways)],
            [
                attns[layer].place,
                live.grad,
                *shares(),
                live.values[f"feed{layer}"][0],
                live.gains[layer],
                *attns[layer].quarters,
                live.allows[layer],
                live.values[f"attn{layer}"][2],
            ],
            [SMEM] + [VMEM] * (4 + len(live.other)) + [ANY] * 4 + [VMEM] * 2,
            [w_attn, pltpu.VMEM((2 * length, half), bf16), dma(4 * lead)],
            name="attend_back",
        )
        live.put(grad=grad, d_low=d_low, d_qkv=d_qkv, keep=keep, low=low)
        live.put(**{f"gains{layer}1": jnp.concatenate([d_gain, d_shift], 1)})

    def attend_grad(layer):
        hidden, first, qkv, mixed = live.values[f"attn{layer}"]
        aligned = block % 128 == 0
        if not aligned:
            first, mixed = turn(sl, first, lead), turn(sl, mixed, lead // 2)
        parts = call(
            partial(attend_grad_kernel, lead, aligned),
            [quarter] * 4,
            [place, first, mixed, live.d_qkv, live.d_low],
            [SMEM] + [VMEM] * 4,
            name="attend_grad",
        )
        return live.flow(Scatter(sl, parts, 2))

    def two_sides(flows, wides, counts):
        values = [flow.value.reshape(2, rows, wide) for flow, wide in zip(flows, wides)]
        both = jnp.concatenate([v[..., :n] for v, n in zip(values, counts)], -1)
        keep, send = split(both, SIDE, 0)
        return keep, sl.flip(send, SIDE), values[0][..., counts[0] :]

    def finish(layer, big, before, more=None):
        keep, other, out = big
        more = [] if more is None else list(more[:2])
        return update(
            partial(finish_kernel, 2 * block, 2 * fsdp * feeds, part),
            layer,
            w_big.shape,
            [mine(SIDE)[None], keep, other, out, *more],
            [SMEM] + [VMEM] * (3 + len(more)),
            [m_big, v_big],
            before,
            "finish",
        )

    def finish_down(layer, flow, before):
        return update(
            finish_down_kernel,
            layer,
            w_down.shape,
            [flow.value],
            [VMEM],
            [m_down, v_down],
            before,
            "finish_down",
        )

    def table_terms():
        first, second = [
            jnp.concatenate([live.values[f"gains{n}0"], live.values[f"gains{n}1"]], 1) for n in range(2)
        ]
        hit = jnp.arange(count - 1) == section_ids[0]
        terms = jnp.concatenate([first, jnp.where(hit[:, None], second, 0.0)], 0)
        terms = terms.reshape(count, high, 2, 2, fsdp, norm_table.shape[1])
        return jnp.moveaxis(terms, 0, 4)

    def table_step(pos, bits):
        value = live.table
        for bit in bits:
            keep, send = split(value, bit, pos)
            value = keep + sl.flip(send, bit)
        live.put(table=value)

    ups[0].start()
    attns[1].start()
    ups[1].start()
    attns[0].finish()
    live.put(gains=gains_of(attns[0].quarters, live.sections))
    attend(0, live.hidden, 1)
    cross()
    live.seal(ups[0], attns[1], ups[1])

    attns[1].start()
    ups[1].start()
    downs[1].start()
    ups[0].finish()
    feed_forward(0, 1)
    cross()
    live.seal(attns[1], ups[1], downs[1])

    ups[1].start()
    downs[1].start()
    attns[1].finish()
    attend(1, live.feed0[0])
    cross()
    live.seal(ups[1], downs[1])

    ups[1].finish()
    downs[1].finish()
    live.put(grad=live.d_low.astype(f32))
    feed_turn(1)
    live.seal()

    cross()
    g_up1 = up_grad(1)
    g_up1.cross()
    g_up1.start()
    g_down1 = down_grad(1, True)
    g_down1.cross()
    g_down1.start()
    attend_back(1)
    live.seal(g_down1, g_up1)

    g_down1.start()
    g_up1.start()
    g_attn1 = attend_grad(1)
    g_attn1.cross()
    g_attn1.start()
    cross()
    feed_back(0)
    g_down0 = down_grad(0)
    live.seal(g_down1, g_up1, g_attn1)

    cross()
    g_down0.cross()
    g_down0.start()
    g_up0b = up_grad(0, 1)
    g_up0b.cross()
    g_up0b.start()
    g_up1.start()
    g_attn1.start()
    attend_back(0)
    live.seal(g_down0, g_up1, g_attn1, g_up0b)

    cross()
    g_attn0 = attend_grad(0)
    g_attn0.cross()
    g_attn0.start()
    g_up0b.start()
    g_attn1.start()
    g_down0.start()
    gate(g_up0b, g_attn1, g_down0)
    norm_back(0, 0, live.attn0[0])
    live.seal(g_attn0, g_attn1, g_down0, g_up0b)

    g_up0a = up_grad(0, 0)
    g_up0a.cross()
    g_up0a.start()
    g_attn0.start()
    g_down0.start()
    g_up0b.start()
    feed_down(1)
    big1 = two_sides([g_attn1, g_up1], [2 * width, feed // 2], [part, feed // 2])
    live.put(big=finish(1, big1, []))
    live.put(table=table_terms())
    live.seal(g_up0a, g_attn0, g_down0, g_up0b)

    g_up0a.start()
    g_attn0.start()
    g_down1.start()
    cross()
    table_step(2, [CORE])
    table_step(1, [SIDE])
    table = live.table.reshape(*(len(sl.high) + len(sl.deep)) * [2], count, -1)
    live.put(table=table, down=finish_down(0, g_down0, []))
    live.seal(g_up0a, g_attn0, g_down1)

    g_up0a.start()
    out_act = live.feed1[0][:length] + (live.keep[:length] + live.other[0][length:].astype(f32))
    big0 = two_sides([g_attn0, g_up0b], [2 * width, feed // 4], [part, feed // 4])
    table_step(0, sl.high)
    table_step(-3, sl.deep[-1:])
    live.put(out_act=out_act.astype(bf16), down=finish_down(1, g_down1, live.down), big0=big0)
    live.seal(g_up0a)

    table_step(0, sl.deep[:-1])
    up0a = two_sides([g_up0a], [feed // 4], [feed // 4])
    grad_big, new_m_big, step_big = finish(0, live.big0, live.big, up0a)
    grad_down, new_m_down, step_down = live.down
    grad_table = live.table
    new_m_table, step_table = adam_update(m_table, v_table, grad_table)
    return (
        live.out_act[None],
        live.d_low[:length][None],
        grad_big,
        grad_down,
        grad_table,
        new_m_big,
        new_m_down,
        new_m_table,
        step_big,
        step_down,
        step_table,
    )


def solution(mesh):
    both = ("dp", "fsdp")
    rows, middle, last = P(both, None, None), P(None, both, None), P(None, both)
    return jax.shard_map(
        partial(body, mesh.shape["dp"], mesh.shape["fsdp"]),
        mesh=mesh,
        in_specs=(rows, rows, P(both, None), P(both), middle, middle, last)
        + 2 * (middle, middle, last),
        out_specs=(rows, rows) + 3 * (middle, middle, last),
        check_vma=False,
    )
```

```python
import itertools
import math
from functools import partial

import jax
import jax.numpy as jnp
from jax import lax
from jax.experimental import pallas as pl
from jax.experimental.pallas import tpu as pltpu
from jax.sharding import PartitionSpec as P

HEADS = 16

beta_one = 0.9
beta_two = 0.999
first_fix = 1.0 - 0.9**10
second_fix = 1.0 - 0.999**10

f32 = jnp.float32
bf16 = jnp.bfloat16

VMEM = pl.BlockSpec(memory_space=pltpu.VMEM)
SMEM = pl.BlockSpec(memory_space=pltpu.SMEM)
ANY = pl.BlockSpec(memory_space=pl.ANY)

CORE = ("dp", 1)
SIDE = ("dp", 2)


def masks(size):
    return [1 << k for k in reversed(range(size.bit_length() - 1))]


class Slice:
    def __init__(self, dp, fsdp):
        self.high = [("dp", m) for m in masks(dp) if m > 2]
        self.deep = [("fsdp", m) for m in masks(fsdp)]
        self.size = {"dp": dp, "fsdp": fsdp}

    def flip(self, value, bit):
        axis, mask = bit
        return lax.ppermute(value, axis, [(i, i ^ mask) for i in range(self.size[axis])])


def mine(bit):
    axis, mask = bit
    return (lax.axis_index(axis) // mask) % 2


def call(kernel, outs, operands, specs, scratch=(), flops=0, name=None):
    held = [(v.shape, v.dtype) for v, spec in zip(operands, specs) if spec is VMEM] + list(outs)
    held += [(s.shape, s.dtype) for s in scratch if hasattr(s, "memory_space") and s.memory_space == pltpu.VMEM]
    held = sum(math.prod(shape) * jnp.dtype(kind).itemsize for shape, kind in held)
    return pl.pallas_call(
        kernel,
        out_shape=[jax.ShapeDtypeStruct(shape, kind) for shape, kind in outs],
        in_specs=specs,
        out_specs=[VMEM] * len(outs),
        scratch_shapes=list(scratch),
        compiler_params=pltpu.CompilerParams(vmem_limit_bytes=held + (3 << 20)),
        name=name,
    )(*operands)


def merge(own, other, bit, pos):
    side = mine(bit)
    return jnp.where(side == 0, jnp.stack([own, other], pos), jnp.stack([other, own], pos))


def split(value, bit, pos):
    side = mine(bit)
    keep = lax.dynamic_index_in_dim(value, side, pos, keepdims=False)
    send = lax.dynamic_index_in_dim(value, 1 - side, pos, keepdims=False)
    return keep, send


def interleave_kernel(count, side, *refs):
    owns, others, outs = refs[:count], refs[count : 2 * count], refs[2 * count :]
    each = count * owns[0].shape[0] // len(outs)
    for n, (own, other) in enumerate(zip(owns, others)):
        for m in range(own.shape[0]):
            out, at = outs[(n * own.shape[0] + m) // each], (n * own.shape[0] + m) % each
            out[pl.ds(at, 1), pl.ds(side[0], 1)] = own[pl.ds(m, 1)][:, None]
            out[pl.ds(at, 1), pl.ds(1 - side[0], 1)] = other[pl.ds(m, 1)][:, None]


def interleave(owns, others, bit, before, outs=1):
    rows, n = owns[0].shape
    count = len(owns)
    shape = (before, rows // before, n)
    whole = (count * before // outs, 2, rows // before, n)
    result = call(
        partial(interleave_kernel, count),
        outs * [(whole, owns[0].dtype)],
        [mine(bit)[None], *(v.reshape(shape) for v in (*owns, *others))],
        [SMEM] + [VMEM] * (2 * count),
        name="interleave",
    )
    return [part.reshape(-1, n) for part in result]


def prepare_kernel(side, big, table, first, first_sent, up0, up0_sent, after, after_sent, out, sems):
    width = out.shape[-1] * 2
    span, chunk = first.shape[1] // 6 // 128 * 128, up0.shape[1] // 2
    third = 3 * width
    copies = []
    for layer, qkv, up in ((0, (first, first_sent), (up0, up0_sent)), (1, (after, after_sent), (after, after_sent))):
        for x, target, upper in ((side[0], qkv[0], up[0]), (1 - side[0], qkv[1], up[1])):
            for n in range(third // (2 * span)):
                at = pl.multiple_of((2 * n + x) * span, 128)
                copies.append((big.at[layer, :, pl.ds(at, span)], target.at[:, pl.ds(n * span, span)]))
            base = 0 if layer == 0 else third // 2
            for n in range(2):
                at = pl.multiple_of(4 * width + (2 * n + x) * chunk, 128)
                copies.append((big.at[layer, :, pl.ds(at, chunk)], upper.at[:, pl.ds(base + n * chunk, chunk)]))
        for k in range(2):
            copies.append((big.at[layer, :, pl.ds(third + k * width // 2, width // 2)], out.at[layer, k]))
    for target in (first, first_sent):
        copies.append((table, target.at[:, pl.ds(third // 2, 128)]))
    copies = [pltpu.make_async_copy(a, b, sems.at[n]) for n, (a, b) in enumerate(copies)]
    for copy in copies:
        copy.start()
    for copy in copies:
        copy.wait()


def place_first_kernel(side, keep, other, out, own):
    part = keep.shape[1] - 128
    wide = out.shape[-1]
    for source, x in ((keep, side[0]), (other, 1 - side[0])):
        own[pl.ds(x, 1), :, pl.ds(0, part)] = source[:, pl.ds(0, part)][None]
        own[pl.ds(x, 1), :, pl.ds(part + wide, 128)] = source[:, pl.ds(part, 128)][None]
    own[:, :, pl.ds(part, wide)] = out[...]


def place_next_kernel(side, keep, other, out, own):
    wide = out.shape[-1]
    part = 3 * wide
    for source, x in ((keep, side[0]), (other, 1 - side[0])):
        own[pl.ds(x, 1), :, pl.ds(0, part)] = source[:, pl.ds(0, part)][None]
        own[pl.ds(2 + x, 1)] = source[:, pl.ds(part, part + wide)][None]
    own[pl.ds(0, 2), :, pl.ds(part, wide)] = out[...]


class Gather:
    def __init__(self, sl, own, lead, top_first=False, twins=False):
        self.sl, self.value, self.lead, self.top_first, self.twins = sl, own, lead, top_first, twins
        self.have, self.air, self.quarters = [], None, None
        near = sl.high[:0:-1]
        if top_first:
            self.steps = [sl.high[:1], near + sl.deep[:-1], sl.deep[-1:]]
        else:
            self.steps = [sl.deep[:-1], sl.deep[-1:] + near]
        core = mine(CORE)
        self.place = jnp.stack([jnp.zeros_like(core) if top_first else mine(sl.high[0]), core])

    def before(self, bit):
        order = self.sl.high + self.sl.deep
        count = sum(order.index(b) < order.index(bit) for b in self.have)
        return (1 + self.twins) * (1 << count) * (1 if bit in self.sl.high else self.lead)

    def start(self):
        if not self.steps:
            self.air = self.sl.flip(self.value, self.sl.high[0]), self.sl.flip(self.value, CORE)
            return
        *others, self.bit = self.steps.pop(0)
        for bit in others:
            other = self.sl.flip(self.value, bit)
            self.value = interleave([self.value], [other], bit, self.before(bit))[0]
            self.have.append(bit)
        self.air = self.sl.flip(self.value, self.bit)

    def land(self):
        air, self.air = self.air, None
        if isinstance(air, tuple):
            self.quarters, self.value = [self.value, *air], None
            return
        last = (self.top_first or self.twins) and not self.steps
        halves = interleave([self.value], [air], self.bit, self.before(self.bit), 1 + last)
        self.have.append(self.bit)
        if last and self.twins:
            self.value = halves
        elif last:
            self.quarters = [*halves, self.sl.flip(halves[0], CORE)]
            self.value = None
        else:
            self.value = halves[0]

    def join(self, other):
        made = Gather(self.sl, None, self.lead, twins=True)
        airs = self.air, other.air
        made.value = interleave([self.value, other.value], airs, self.bit, self.before(self.bit))[0]
        made.have, made.steps = self.have + [self.bit], self.steps
        return made

    def part(self, n):
        made = Gather(self.sl, self.value[n], self.lead)
        made.steps = []
        return made

    def finish(self):
        self.quarters = [*self.quarters, self.sl.flip(self.quarters[1], CORE)]


def add_low_kernel(one, two, out):
    out[...] = (one[...].astype(f32) + two[...].astype(f32)).astype(bf16)


def add_split_kernel(side, *refs):
    *parts, kept, sent = refs
    for at, out in ((side[0], kept), (1 - side[0], sent)):
        total = parts[0][:, pl.ds(at, 1)].astype(f32)
        for other in parts[1:]:
            total = total + other[:, pl.ds(at, 1)].astype(f32)
        out[...] = total.astype(bf16)[:, 0]


def cross_split_kernel(side, own, own_other, top, top_other, kept, sent):
    for n, (one, two) in enumerate(((own, own_other), (top, top_other))):
        for at, out in ((side[0], kept), (1 - side[0], sent)):
            total = one[:, pl.ds(at, 1)].astype(f32) + two[:, pl.ds(at, 1)].astype(f32)
            out[n] = total.astype(bf16)[:, 0]


class Scatter:
    def __init__(self, sl, quarters, lead, top_last=False):
        self.sl, self.quarters, self.value, self.lead, self.top_last = sl, quarters, None, lead, top_last
        top, near, deep = sl.high[:1], sl.high[1:], sl.deep
        self.have = sl.high + deep
        if top_last:
            self.steps = [deep[-1:], deep[-2::-1] + near, top]
        else:
            self.steps = [top, near + deep[-1:], deep[-2::-1]]

    def before(self, bit):
        order = self.sl.high + self.sl.deep
        count = sum(order.index(b) < order.index(bit) for b in self.have)
        return (1 << count) * (1 if bit in self.sl.high else self.lead)

    def side(self, bit):
        return jnp.zeros((1,), jnp.int32) if bit == self.sl.high[0] else mine(bit)[None]

    def cross(self):
        own, top, core, both = self.quarters
        top_other = self.sl.flip(both, CORE)
        core, _ = lax.optimization_barrier((core, top_other))
        core_other = self.sl.flip(core, CORE)
        rows, n = top.shape
        if not self.top_last:
            (send,) = call(
                add_low_kernel, [(top.shape, bf16)], [top, top_other], [VMEM] * 2, name="add_low"
            )
            self.quarters = [[own, core_other], send]
            return
        bit = self.steps[0][0]
        before = self.before(bit) // 2
        shape = (before, 2, rows // 2 // before, n)
        half = ((2, before, rows // 2 // before, n), bf16)
        keep, send = call(
            cross_split_kernel,
            [half, half],
            [self.side(bit), *(v.reshape(shape) for v in (own, core_other, top, top_other))],
            [SMEM] + [VMEM] * 4,
            name="cross_split",
        )
        self.quarters = [[keep.reshape(-1, n)], send.reshape(-1, n)]

    def split(self, other, bit):
        parts = [*self.quarters[0], other]
        if bit is None:
            self.value = sum(part.astype(f32) for part in parts)
            self.quarters = None
            return
        before = self.before(bit)
        rows, n = other.shape
        shape = (before, 2, rows // 2 // before, n)
        half = ((before, rows // 2 // before, n), bf16)
        keep, send = call(
            add_split_kernel,
            [half, half],
            [self.side(bit), *(part.reshape(shape) for part in parts)],
            [SMEM] + [VMEM] * len(parts),
            name="add_split",
        )
        self.quarters = [[keep.reshape(-1, n)], send.reshape(-1, n)]

    def start(self):
        bits = self.steps.pop(0)
        for n, bit in enumerate(bits):
            self.air = self.sl.flip(self.quarters[1], bit)
            self.have.remove(bit)
            if n < len(bits) - 1:
                self.split(self.air, bits[n + 1])
        self.next = self.steps[0][0] if self.steps else None

    def land(self):
        other, self.air = self.air, None
        self.split(other, self.next)


class Live:
    def __init__(self, **values):
        self.flows = []
        self.values = values

    def flow(self, made):
        self.flows.append(made)
        return made

    def __getattr__(self, name):
        return self.values[name]

    def put(self, **values):
        self.values.update(values)

    def drop(self, *names):
        for name in names:
            del self.values[name]

    def seal(self, *landing, keep=()):
        landing = [*keep, *landing]
        kept = (
            self.values,
            [(made.value, made.quarters) for made in self.flows],
            [made.air for made in landing],
        )
        self.values, flown, airs = lax.optimization_barrier(kept)
        for made, (made.value, made.quarters) in zip(self.flows, flown):
            pass
        for n, (made, made.air) in enumerate(zip(landing, airs)):
            if n >= len(keep):
                made.land()


def dot(left, right):
    return jnp.dot(left, right, preferred_element_type=f32)


def dot_t(left, right):
    return lax.dot_general(left, right, (((1,), (1,)), ((), ())), preferred_element_type=f32)


def t_dot(left, right):
    return lax.dot_general(left, right, (((0,), (0,)), ((), ())), preferred_element_type=f32)


def fetch(place, quarters, whole, lead, sems):
    width = whole.shape[1]
    block = whole.shape[0] // (4 * lead)
    copies = []
    for n, part in enumerate(quarters):
        top = place[0] if n % 2 == 0 else 1 - place[0]
        core = place[1] if n < 2 else 1 - place[1]
        for a in range(lead):
            at = pl.multiple_of(((top * lead + a) * 2 + core) * block, block)
            source = part.at[pl.ds(a * block, block), pl.ds(0, width)]
            copies.append(
                pltpu.make_async_copy(source, whole.at[pl.ds(at, block)], sems.at[n * lead + a])
            )
    for copy in copies:
        copy.start()
    return copies


def norm(hidden):
    centred = hidden - jnp.mean(hidden, axis=-1, keepdims=True)
    scale = lax.rsqrt(jnp.mean(centred * centred, axis=-1, keepdims=True) + 1e-05)
    return centred * scale, scale


def put_rows(outs, cols, value):
    rows = value.shape[0] // len(outs)
    for r, out in enumerate(outs):
        out[:, cols] = value[r * rows : (r + 1) * rows].astype(bf16)


def theirs(others, r, rows):
    if len(others) == 2:
        return others[1 - r][...].astype(f32)
    return others[0][pl.ds((1 - r) * rows, rows)].astype(f32)


def gains_at(gains, r, place, width):
    return gains[pl.ds(r, 1), pl.ds(place * width, width)]


def add_norm(which, parts, gains, total, out):
    base, *shares = parts
    rows, width = out.shape[0] // 2, out.shape[1]
    for r in range(2):
        block = pl.ds(r * rows, rows)
        value = base[block]
        if shares:
            value = value + (shares[0][block] + theirs(shares[1:], r, rows))
            total[block] = value
        gain, bias = [gains_at(gains, r, 2 * which + n, width) for n in range(2)]
        out[block] = (norm(value)[0] * gain + bias).astype(bf16)


def norm_back(which, d_out, keep, others, hidden, gains, total, low, d_gain, d_shift):
    rows, width = d_out.shape[0] // 2, d_out.shape[1]
    for r in range(2):
        block = pl.ds(r * rows, rows)
        grad = keep[block] + theirs(others, r, rows)
        normed, scale = norm(hidden[block])
        if r == 0:
            d_gain[...] = jnp.sum(grad * normed, axis=0, keepdims=True)
            d_shift[...] = jnp.sum(grad, axis=0, keepdims=True)
        e = grad * gains_at(gains, r, 2 * which, width)
        part = e - jnp.mean(e, axis=-1, keepdims=True)
        part = part - normed * jnp.mean(e * normed, axis=-1, keepdims=True)
        value = d_out[block] + scale * part
        total[block] = value
        low[block] = value.astype(bf16)


def norm_back_kernel(which, d_out, keep, *refs):
    norm_back(which, d_out, keep, refs[:-6], *refs[-6:])


def gains_kernel(lead, count, rows, place, pick, q0, q1, q2, q3, first, second, held, wide, sems):
    copies = []
    for n, part in enumerate((q0, q1, q2, q3)):
        source = part.at[:, pl.ds(part.shape[1] - 128, 128)]
        copies.append(pltpu.make_async_copy(source, held.at[n], sems.at[n]))
    for copy in copies:
        copy.start()
    for copy in copies:
        copy.wait()
    wide[...] = held[...].astype(f32)
    deep = wide.shape[1] // (lead * rows)
    for n in range(4):
        top = place[0] if n % 2 == 0 else 1 - place[0]
        core = place[1] if n < 2 else 1 - place[1]
        for a in range(lead):
            for z in range(deep):
                cols = pl.multiple_of((((top * lead + a) * 2 + core) * deep + z) * 128, 128)
                base = (a * deep + z) * rows
                for r in range(2):
                    first[pl.ds(r, 1), pl.ds(cols, 128)] = wide[n, pl.ds(base, 1)]
                    second[pl.ds(r, 1), pl.ds(cols, 128)] = wide[n, pl.ds(base + 1 + pick[r], 1)]


def score(q, k, allowed, size):
    scores = jnp.where(allowed, dot_t(q, k) * size, -1e30)
    exponent = jnp.exp(scores - jnp.max(scores, axis=-1, keepdims=True))
    return exponent / jnp.sum(exponent, axis=-1, keepdims=True)


def lanes_of(which, shape):
    lane = lax.broadcasted_iota(jnp.int32, shape, 1)
    return (lane < shape[1] // 2) if which == 0 else (lane >= shape[1] // 2)


def out_block(weight, k, block, at):
    count = weight.shape[0] // (2 * block)
    wide = weight.shape[1] - at
    return jnp.concatenate([weight[pl.ds((2 * h + k) * block, block), pl.ds(at, wide)] for h in range(count)], 0)


def attend_kernel(ways, size, lead, block, place, *refs):
    refs, (weight, sems) = refs[:-2], refs[-2:]
    refs, lows = refs[:-ways], refs[-ways:]
    *parts, gains, q0, q1, q2, q3, allow, total, f, qkv, mixed, keep = refs
    copies = fetch(place, (q0, q1, q2, q3), weight, lead, sems)
    add_norm(0, parts, gains, total, f)
    for copy in copies:
        copy.wait()
    length = allow.shape[-1]
    third = qkv.shape[1] // 3
    for n in range(3):
        cols = pl.ds(n * third, third)
        qkv[:, cols] = dot(f[...], weight[:, cols]).astype(bf16)

    def one_row(r, carry):
        at = pl.ds(pl.multiple_of(r * length, length), length)
        allowed = allow[r] > 0
        for p in range(third // 128):
            q = qkv[at, pl.ds(p * 128, 128)]
            k = qkv[at, pl.ds(third + p * 128, 128)]
            v = qkv[at, pl.ds(2 * third + p * 128, 128)]
            halves = []
            for h in range(2):
                probs = score(jnp.where(lanes_of(h, q.shape), q, 0), k, allowed, size)
                halves.append(dot(probs.astype(bf16), v))
            mixed[at, pl.ds(p * 128, 128)] = jnp.where(
                lanes_of(0, q.shape), halves[0], halves[1]
            ).astype(bf16)
        return carry

    lax.fori_loop(0, f.shape[0] // length, one_row, 0)
    for k in range(2):
        cols = pl.ds(k * third, third)
        value = dot(mixed[...], out_block(weight, k, block, 3 * third))
        keep[:, cols] = value
        put_rows(lows, cols, value)


def attend_back_kernel(ways, size, lead, block, grads, place, *refs):
    if grads:
        (first, mixed), refs = refs[:2], refs[2:]
    (d_out, part), refs = refs[:2], refs[2:]
    refs, (weight, d_mixed, sems) = refs[:-3], refs[-3:]
    if grads:
        refs, outs = refs[:-4], refs[-4:]
    refs, lows = refs[:-ways], refs[-ways:]
    *others, attended, gains, q0, q1, q2, q3, allow, qkv, total, d, d_gain, d_shift, d_qkv, keep = refs
    copies = fetch(place, (q0, q1, q2, q3), weight, lead, sems)
    norm_back(1, d_out, part, others, attended, gains, total, d, d_gain, d_shift)
    for copy in copies:
        copy.wait()
    length = allow.shape[-1]
    third = qkv.shape[1] // 3
    value = dot_t(d[:, pl.ds(0, third)], out_block(weight, 0, block, 3 * third))
    value = value + dot_t(d[:, pl.ds(third, third)], out_block(weight, 1, block, 3 * third))
    d_mixed[...] = value.astype(bf16)

    def one_row(r, carry):
        at = pl.ds(pl.multiple_of(r * length, length), length)
        allowed = allow[r] > 0
        for p in range(third // 128):
            q = qkv[at, pl.ds(p * 128, 128)]
            k = qkv[at, pl.ds(third + p * 128, 128)]
            v = qkv[at, pl.ds(2 * third + p * 128, 128)]
            dm = d_mixed[at, pl.ds(p * 128, 128)]
            d_q, d_k, d_v = [], [], []
            for h in range(2):
                pick = lanes_of(h, q.shape)
                probs = score(jnp.where(pick, q, 0), k, allowed, size)
                d_probs = dot_t(jnp.where(pick, dm, 0), v)
                d_v.append(t_dot(probs.astype(bf16), dm))
                inner = jnp.sum(probs * d_probs, axis=-1, keepdims=True)
                d_scores = (probs * (d_probs - inner)).astype(bf16)
                d_q.append(dot(d_scores, k))
                d_k.append(t_dot(d_scores, q))
            pick = lanes_of(0, q.shape)
            for n, (halves, scale) in enumerate(((d_q, size), (d_k, size), (d_v, 1.0))):
                value = jnp.where(pick, halves[0], halves[1]) * scale
                d_qkv[at, pl.ds(n * third + p * 128, 128)] = value.astype(bf16)
        return carry

    lax.fori_loop(0, d.shape[0] // length, one_row, 0)
    for n in range(keep.shape[1] // 256):
        cols = pl.ds(n * 256, 256)
        value = dot_t(d_qkv[...], weight[cols, pl.ds(0, 3 * third)])
        keep[:, cols] = value
        put_rows(lows, cols, value)
    if grads:
        attend_grad(lead, place, first, mixed, d_qkv, d, outs)


def up(f, weight, pre, active):
    for n in range(pre.shape[1] // 256):
        cols = pl.ds(n * 256, 256)
        value = dot(f[...], weight[:, cols])
        pre[:, cols] = value
        active[:, cols] = jax.nn.gelu(value).astype(bf16)


def down(active, weight, keep, lows):
    for n in range(keep.shape[1] // 256):
        cols = pl.ds(n * 256, 256)
        value = dot(active[...], weight[:, cols])
        keep[:, cols] = value
        put_rows(lows, cols, value)


def feed_kernel(ways, lead, up_place, dn_place, *refs):
    refs, (w_up, w_dn, up_sems, dn_sems) = refs[:-4], refs[-4:]
    refs, lows = refs[:-ways], refs[-ways:]
    *parts, gains, u0, u1, u2, u3, n0, n1, n2, n3, total, f, pre, active, keep = refs
    up_copies = fetch(up_place, (u0, u1, u2, u3), w_up, lead, up_sems)
    dn_copies = fetch(dn_place, (n0, n1, n2, n3), w_dn, lead // 2, dn_sems)
    add_norm(1, parts, gains, total, f)
    for copy in up_copies:
        copy.wait()
    up(f, w_up, pre, active)
    for copy in dn_copies:
        copy.wait()
    down(active, w_dn, keep, lows)


def down_kernel(lead, place, active, q0, q1, q2, q3, keep, low, weight, sems):
    for copy in fetch(place, (q0, q1, q2, q3), weight, lead, sems):
        copy.wait()
    down(active, weight, keep, (low,))


def gelu_slope(x):
    c = 0.7978845608028654
    t = jnp.tanh(c * (x + 0.044715 * (x * x * x)))
    return 0.5 * (1.0 + t) + 0.5 * x * (1.0 - t * t) * (c * (1.0 + 3 * 0.044715 * (x * x)))


def feed_back(d, pre, w_up, w_dn, d_pre, keep, lows):
    for n in range(pre.shape[1] // 256):
        cols = pl.ds(n * 256, 256)
        d_pre[:, cols] = (gelu_slope(pre[:, cols]) * dot_t(d[...], w_dn[cols])).astype(bf16)
    for n in range(keep.shape[1] // 256):
        cols = pl.ds(n * 256, 256)
        value = dot_t(d_pre[...], w_up[cols])
        keep[:, cols] = value
        put_rows(lows, cols, value)


def feed_back_kernel(ways, lead, up_place, dn_place, d_out, part, *refs):
    refs, (w_up, w_dn, up_sems, dn_sems) = refs[:-4], refs[-4:]
    refs, lows = refs[:-ways], refs[-ways:]
    *others, hidden, gains, pre, u0, u1, u2, u3, n0, n1, n2, n3, total, d, d_gain, d_shift, d_pre, keep = refs
    copies = fetch(dn_place, (n0, n1, n2, n3), w_dn, lead // 2, dn_sems)
    copies += fetch(up_place, (u0, u1, u2, u3), w_up, lead, up_sems)
    norm_back(0, d_out, part, others, hidden, gains, total, d, d_gain, d_shift)
    for copy in copies:
        copy.wait()
    feed_back(d, pre, w_up, w_dn, d_pre, keep, lows)


def feed_turn_kernel(ways, lead, grads, place, up_place, dn_place, *refs):
    refs, (w_up, w_dn, pre, up_sems, dn_sems) = refs[:-5], refs[-5:]
    if grads:
        refs, up_outs, dn_outs = refs[:-8], refs[-8:-4], refs[-4:]
    refs, lows = refs[:-ways], refs[-ways:]
    *parts, gains, d, u0, u1, u2, u3, n0, n1, n2, n3, total, f, active, d_pre, keep = refs
    up_copies = fetch(up_place, (u0, u1, u2, u3), w_up, lead, up_sems)
    dn_copies = fetch(dn_place, (n0, n1, n2, n3), w_dn, lead // 2, dn_sems)
    add_norm(1, parts, gains, total, f)
    for copy in up_copies:
        copy.wait()
    up(f, w_up, pre, active)
    for copy in dn_copies:
        copy.wait()
    feed_back(d, pre, w_up, w_dn, d_pre, keep, lows)
    if grads:
        weight_grad(lead, place, f, d_pre, up_outs)
        weight_grad(lead // 2, place, active, d, dn_outs)


def columns_of(place, value, lead):
    block = value.shape[1] // (4 * lead)
    parts = []
    for n in range(4):
        top = place[0] if n % 2 == 0 else 1 - place[0]
        core = place[1] if n < 2 else 1 - place[1]
        starts = [((top * lead + a) * 2 + core) * block for a in range(lead)]
        if block % 128 == 0:
            starts = [pl.multiple_of(at, 128) for at in starts]
        parts.append(jnp.concatenate([value[:, pl.ds(at, block)] for at in starts], 1))
    return parts


def weight_grad(lead, place, left, right, outs):
    for part, out in zip(columns_of(place, left, lead), outs):
        out[...] = t_dot(part, right[...]).astype(bf16)


def weight_grad_kernel(lead, aligned, place, left, right, *outs):
    weight_grad(lead, place if aligned else (0, 0), left, right, outs)


def attend_grad_kernel(lead, aligned, place, left, mixed, d_qkv, d, *outs):
    attend_grad(lead, place if aligned else (0, 0), left, mixed, d_qkv, d, outs)


def attend_grad(lead, place, left, mixed, d_qkv, d, outs):
    width = d_qkv.shape[1]
    third = width // 3
    block = left.shape[1] // (4 * lead)
    lefts, inners = columns_of(place, left, lead), columns_of(place, mixed, lead // 2)
    for part, inner, out in zip(lefts, inners, outs):
        out[:, pl.ds(0, width)] = t_dot(part, d_qkv[...]).astype(bf16)
        value = t_dot(inner, d[...]).astype(bf16)
        for h in range(inner.shape[1] // block):
            for k in range(2):
                out[pl.ds((2 * h + k) * block, block), pl.ds(width, third)] = value[
                    h * block : (h + 1) * block, k * third : (k + 1) * third
                ]


def turn(sl, value, lead):
    tokens, width = value.shape
    value = value.reshape(tokens, 2, lead, 2, width // (4 * lead))
    value = jnp.stack(split(value, sl.high[0], 1), 1)
    return jnp.stack(split(value, CORE, 3), 3).reshape(tokens, width)


def finish_kernel(span, chunk, part, side, keep, other, out, *refs):
    grad, new_m, step = refs[-3:]
    third = out.shape[-1]
    total = (grad.shape[-1] - 8 * third) // 2
    late = total - (keep.shape[1] - part)
    m, v = refs[2:4] if late else refs[:2]
    pieces = [(keep, other, 0, 0, part, span), (keep, other, part, 8 * third + 2 * late, total - late, chunk)]
    if late:
        pieces.append((refs[0], refs[1], 0, 8 * third, late, chunk))
    for one, two, first, base, count, width in pieces:
        for source, x in ((one, side[0]), (two, 1 - side[0])):
            for n in range(count // width):
                at = pl.multiple_of(base + (2 * n + x) * width, 128)
                grad[0, :, pl.ds(at, width)] = source[:, pl.ds(first + n * width, width)]
    for k in range(2):
        grad[0, :, pl.ds((6 + k) * third, third)] = out[k]
    for n in range(grad.shape[2] // 1024):
        cols = pl.ds(n * 1024, 1024)
        new_m[0, :, cols], step[0, :, cols] = adam_update(m[0, :, cols], v[0, :, cols], grad[0, :, cols])


def finish_down_kernel(value, m, v, *refs):
    grad, new_m, step = refs[-3:]
    grad[0] = value[...]
    new_m[0], step[0] = adam_update(m[0], v[0], value[...])


def update(kernel, layer, shape, parts, specs, moments, before, name):
    one = pl.BlockSpec((1, *shape[1:]), lambda i: (layer, 0, 0))
    count = len(parts) + 2
    return pl.pallas_call(
        kernel,
        grid=(1,),
        out_shape=[jax.ShapeDtypeStruct(shape, f32)] * 3,
        in_specs=[*specs, one, one, *len(before) * [ANY]],
        out_specs=[one] * 3,
        input_output_aliases={count + n: n for n in range(len(before))},
        compiler_params=pltpu.CompilerParams(vmem_limit_bytes=20 << 20),
        name=name,
    )(*parts, *moments, *before)


def adam_update(moment, square, gradient):
    moment = beta_one * moment + (1.0 - beta_one) * gradient
    square = beta_two * square + (1.0 - beta_two) * gradient * gradient
    update = moment / first_fix / (jnp.sqrt(square / second_fix) + 1e-08)
    return (moment, update)


def dma(count):
    return pltpu.SemaphoreType.DMA((count,))


def body(
    dp,
    fsdp,
    inputs,
    cotangent,
    segment_ids,
    section_ids,
    w_big,
    w_down,
    norm_table,
    m_big,
    m_down,
    m_table,
    v_big,
    v_down,
    v_table,
):
    sl = Slice(dp, fsdp)
    length, width = inputs.shape[1:]
    rows = w_big.shape[1]
    feeds = w_down.shape[1]
    feed = w_big.shape[2] - 4 * width
    high = dp // 4
    lead = high
    half, part = width // 2, 3 * width // 2
    block = fsdp * rows
    count = norm_table.shape[0]
    size = (width // HEADS) ** -0.5
    two_f, two_b = ((2 * length, width), f32), ((2 * length, width), bf16)
    wide_b = ((2 * length, feed // 2), bf16)

    def lows(ways):
        return ways * [((2 // ways * length, width), bf16)]

    quarter = ((width // 4, 2 * width), bf16)
    gain_row = ((1, width), f32)
    place = jnp.stack([mine(sl.high[0]), mine(CORE)])
    w_attn = pltpu.VMEM((width, 2 * width), bf16)
    w_upper = pltpu.VMEM((width, feed // 2), bf16)
    w_lower = pltpu.VMEM((feed // 2, width), bf16)

    def qkv_sides(layer):
        value = w_big[layer, :, : 3 * width].reshape(rows, 3, high, 2, 2 * block)
        return [v.reshape(rows, part) for v in split(value, SIDE, 3)]

    def up_sides(layer):
        value = w_big[layer, :, 4 * width :].reshape(rows, high, 2, 2 * fsdp * feeds)
        return [v.reshape(rows, feed // 2) for v in split(value, SIDE, 2)]

    def prepare(table_part):
        shapes = 2 * [(rows, part + 128)] + 2 * [(rows, feed // 2)] + 2 * [(rows, part + feed // 2)]
        shapes.append((2, 2, rows, half))
        if rows % 16 == 0:
            return call(
                prepare_kernel,
                [(shape, bf16) for shape in shapes],
                [mine(SIDE)[None], w_big, table_part],
                [SMEM, ANY, ANY],
                [dma(2 * (6 * high + 6) + 2)],
                name="prepare",
            )
        first = [jnp.concatenate([v, table_part], -1) for v in qkv_sides(0)]
        after = [jnp.concatenate([a, b], -1) for a, b in zip(qkv_sides(1), up_sides(1))]
        out = w_big[:, :, 3 * width : 4 * width].reshape(2, rows, 2, half)
        return [*first, *up_sides(0), *after, jnp.swapaxes(out, 1, 2)]

    def place_sides(kernel, shape, keep, other, out, name):
        return call(
            kernel,
            [(shape, bf16)],
            [mine(SIDE)[None], keep, other, out],
            [SMEM, VMEM, VMEM, VMEM],
            name=name,
        )[0]

    live = Live()
    downs = [live.flow(Gather(sl, w_down[n], 1, n == 1)) for n in range(2)]

    downs[0].start()
    downs[1].start()
    table_part = norm_table.reshape(-1)
    table_part = jnp.pad(table_part, (0, rows * 128 - table_part.shape[0])).reshape(rows, 128)
    first, first_sent, up0, up0_sent, after, after_sent, out_proj = prepare(table_part)
    live.put(
        first=[first, sl.flip(first_sent, SIDE)],
        up=[up0, up0_sent],
        after=[after, after_sent],
        out=out_proj,
    )
    live.seal(downs[0], downs[1])

    own = place_sides(
        place_first_kernel, (2, rows, 2 * width + 128), *live.first, live.out[0], "place_first"
    )
    attns = [live.flow(Gather(sl, own.reshape(2 * rows, -1), 2))]
    attns[0].start()
    downs[0].start()
    extra = jnp.zeros((16, width), bf16)
    extra = extra.at[0, :length].set(segment_ids[0].astype(bf16))
    extra = extra.at[1, 0].set(section_ids[0].astype(bf16))
    pack = jnp.concatenate([inputs[0], cotangent[0], extra], 0)
    live.put(
        up=[live.up[0], sl.flip(live.up[1], SIDE)],
        after=[live.after[0], sl.flip(live.after[1], SIDE)],
        pack=[pack, sl.flip(pack, SIDE)],
    )
    live.drop("first")
    live.seal(attns[0], downs[0])

    ups = [live.flow(Gather(sl, interleave(live.up[:1], live.up[1:], SIDE, 1)[0], 2))]
    downs[0].start()
    attns[0].start()
    ups[0].start()
    own = place_sides(
        place_next_kernel, (4, rows, 2 * width), *live.after, live.out[1], "place_next"
    )
    live.put(own=own)
    live.drop("up", "after", "out")
    packed = jnp.stack(live.pack)
    extras = packed[:, 2 * length :]
    segments = extras[:, 0, :length].astype(f32)
    same = segments[:, :, None] == segments[:, None, :]
    position = jnp.arange(length)
    live.put(
        hidden=packed[:, :length].reshape(2 * length, width).astype(f32),
        d_low=packed[:, length : 2 * length].reshape(2 * length, width),
        sections=extras[:, 1, 0].astype(jnp.int32),
        allows=[
            (same & (position[:, None] >= position[None, :])).astype(f32),
            same.astype(f32),
        ],
    )
    live.drop("pack")
    live.seal(attns[0], ups[0], downs[0])

    own = live.own.reshape(2, 2 * rows, -1)
    attns.append(live.flow(Gather(sl, own[0], 2)))
    ups.append(live.flow(Gather(sl, own[1], 2)))
    live.drop("own")
    attns[0].start()
    attns[1].start()
    ups[0].start()
    downs[0].finish()
    live.seal(attns[0], ups[0], attns[1])

    def after(made, value):
        (keep, send), _ = lax.optimization_barrier((made.quarters, value))
        made.quarters = [keep, send]

    def gate(*made):
        airs = [flow.air for flow in made]
        other, airs = lax.optimization_barrier((live.other, airs))
        live.put(other=other)
        for flow, flow.air in zip(made, airs):
            pass

    def gains_of(quarters, sections):
        wide = norm_table.shape[1]
        if wide == 128:
            return call(
                partial(gains_kernel, lead, count, rows),
                2 * [((2, 4 * width), f32)],
                [place, sections, *quarters],
                [SMEM, SMEM] + [ANY] * 4,
                [
                    pltpu.VMEM((4, width // 4, 128), bf16),
                    pltpu.VMEM((4, width // 4, 128), f32),
                    dma(4),
                ],
                name="gains",
            )
        parts = jnp.stack([q[:, 2 * width :] for q in quarters])
        parts = parts.reshape(4, lead // 2, 2, fsdp, rows * 128)[..., : count * wide]
        parts = parts.reshape(4, lead // 2, 2, fsdp, count, wide)
        pick = jnp.concatenate([jnp.zeros((2,), jnp.int32), 1 + sections])
        pick = (pick[:, None] == jnp.arange(count)[None, :]).astype(bf16)
        picked = jnp.einsum("sr,qhxdrj->qshxdj", pick, parts, preferred_element_type=f32)
        own, top, core, both = picked
        both = merge(merge(own, core, CORE, 3), merge(top, both, CORE, 3), sl.high[0], 1)
        return list(both.reshape(2, 2, 4 * width))

    def cross():
        live.put(other=[sl.flip(row, SIDE) for row in live.low])

    def shares():
        return [live.keep, *live.other]

    def attend(layer, base, ways=2):
        parts = [base] if layer == 0 else [base, *shares()]
        total, first, qkv, mixed, keep, *low = call(
            partial(attend_kernel, ways, size, lead, 2 * block),
            [two_f, two_b, ((2 * length, part), bf16), ((2 * length, half), bf16), two_f, *lows(ways)],
            [
                attns[layer].place,
                *parts,
                live.gains[layer],
                *attns[layer].quarters,
                live.allows[layer],
            ],
            [SMEM] + [VMEM] * (len(parts) + 1) + [ANY] * 4 + [VMEM],
            [w_attn, dma(4 * lead)],
            name="attend",
        )
        hidden = base if layer == 0 else total
        live.put(**{f"attn{layer}": (hidden, first, qkv, mixed)}, keep=keep, low=low)

    def feed_forward(layer, ways=2):
        attended, second, pre, active, keep, *low = call(
            partial(feed_kernel, ways, lead),
            [two_f, two_b, (wide_b[0], f32), wide_b, two_f, *lows(ways)],
            [
                ups[layer].place,
                downs[layer].place,
                live.values[f"attn{layer}"][0],
                *shares(),
                live.gains[layer],
                *ups[layer].quarters,
                *downs[layer].quarters,
            ],
            [SMEM, SMEM] + [VMEM] * (3 + len(live.other)) + [ANY] * 8,
            [w_upper, w_lower, dma(4 * lead), dma(2 * lead)],
            name="feed",
        )
        live.put(**{f"feed{layer}": (attended, second, pre, active)}, keep=keep, low=low)

    def feed_turn(layer, ways=2):
        grads = False
        quarters = 4 * [quarter] + 4 * [((feed // 8, width), bf16)]
        attended, second, active, d_pre, keep, *low = call(
            partial(feed_turn_kernel, ways, lead, grads),
            [two_f, two_b, wide_b, wide_b, two_f, *lows(ways), *(quarters if grads else [])],
            [
                place,
                ups[layer].place,
                downs[layer].place,
                live.values[f"attn{layer}"][0],
                *shares(),
                live.gains[layer],
                live.d_low,
                *ups[layer].quarters,
                *downs[layer].quarters,
            ],
            [SMEM] * 3 + [VMEM] * (4 + len(live.other)) + [ANY] * 8,
            [w_upper, w_lower, pltpu.VMEM(wide_b[0], f32), dma(4 * lead), dma(2 * lead)],
            name="feed_turn",
        )
        live.put(**{f"feed{layer}": (attended, second, None, active)}, d_pre=d_pre, keep=keep, low=low)

    def feed_down(layer):
        keep, *low = call(
            partial(down_kernel, lead // 2),
            [two_f, *lows(1)],
            [downs[layer].place, live.values[f"feed{layer}"][3], *downs[layer].quarters],
            [SMEM, VMEM, ANY, ANY, ANY, ANY],
            [w_lower, dma(2 * lead)],
            name="down",
        )
        live.put(keep=keep, low=low)

    def feed_back(layer, ways=1):
        grad, d_low, d_gain, d_shift, d_pre, keep, *low = call(
            partial(feed_back_kernel, ways, lead),
            [two_f, two_b, gain_row, gain_row, wide_b, two_f, *lows(ways)],
            [
                ups[layer].place,
                downs[layer].place,
                live.grad,
                *shares(),
                live.values[f"attn{layer + 1}"][0],
                live.gains[layer + 1],
                live.values[f"feed{layer}"][2],
                *ups[layer].quarters,
                *downs[layer].quarters,
            ],
            [SMEM, SMEM] + [VMEM] * (5 + len(live.other)) + [ANY] * 8,
            [w_upper, w_lower, dma(4 * lead), dma(2 * lead)],
            name="feed_back",
        )
        live.put(grad=grad, d_low=d_low, d_pre=d_pre, keep=keep, low=low)
        live.put(**{f"gains{layer + 1}0": jnp.concatenate([d_gain, d_shift], 1)})

    def down_grad(layer, top_last=False):
        aligned = feed // 4 // lead % 128 == 0
        active = live.values[f"feed{layer}"][3]
        parts = call(
            partial(weight_grad_kernel, lead // 2, aligned),
            [((feed // 8, width), bf16)] * 4,
            [place, active if aligned else turn(sl, active, lead // 2), live.d_low],
            [SMEM, VMEM, VMEM],
            name="down_grad",
        )
        return live.flow(Scatter(sl, parts, 1, top_last))

    def up_grad(layer, piece=None):
        aligned = block % 128 == 0
        second, right = live.values[f"feed{layer}"][1], live.d_pre
        columns = feed // 2
        if piece is not None:
            columns = feed // 4
            right = right[:, piece * columns : (piece + 1) * columns]
        parts = call(
            partial(weight_grad_kernel, lead, aligned),
            [((width // 4, columns), bf16)] * 4,
            [place, second if aligned else turn(sl, second, lead), right],
            [SMEM, VMEM, VMEM],
            name="up_grad",
        )
        return live.flow(Scatter(sl, parts, 2, piece == 1))

    def norm_back(which, layer, hidden):
        grad, d_low, d_gain, d_shift = call(
            partial(norm_back_kernel, which),
            [two_f, two_b, gain_row, gain_row],
            [live.grad, *shares(), hidden, live.gains[layer]],
            [VMEM] * (4 + len(live.other)),
            name="norm_back",
        )
        live.put(grad=grad, d_low=d_low)
        live.put(**{f"gains{layer}{which}": jnp.concatenate([d_gain, d_shift], 1)})

    def attend_back(layer, ways=1):
        grads = block % 128 == 0
        hidden, first, qkv, mixed = live.values[f"attn{layer}"]
        grad, d_low, d_gain, d_shift, d_qkv, keep, *low = call(
            partial(attend_back_kernel, ways, size, lead, 2 * block, grads),
            [
                *(two_f, two_b, gain_row, gain_row, ((2 * length, part), bf16), two_f, *lows(ways)),
                *(4 * [quarter] if grads else []),
            ],
            [
                attns[layer].place,
                *([first, mixed] if grads else []),
                live.grad,
                *shares(),
                live.values[f"feed{layer}"][0],
                live.gains[layer],
                *attns[layer].quarters,
                live.allows[layer],
                live.values[f"attn{layer}"][2],
            ],
            [SMEM] + [VMEM] * (4 + 2 * grads + len(live.other)) + [ANY] * 4 + [VMEM] * 2,
            [w_attn, pltpu.VMEM((2 * length, half), bf16), dma(4 * lead)],
            name="attend_back",
        )
        low, made = low[:ways], low[ways:]
        live.put(grad=grad, d_low=d_low, d_qkv=d_qkv, keep=keep, low=low)
        live.put(**{f"gains{layer}1": jnp.concatenate([d_gain, d_shift], 1)})
        return live.flow(Scatter(sl, made, 2)) if grads else attend_grad(layer)

    def attend_grad(layer):
        hidden, first, qkv, mixed = live.values[f"attn{layer}"]
        aligned = block % 128 == 0
        if not aligned:
            first, mixed = turn(sl, first, lead), turn(sl, mixed, lead // 2)
        parts = call(
            partial(attend_grad_kernel, lead, aligned),
            [quarter] * 4,
            [place, first, mixed, live.d_qkv, live.d_low],
            [SMEM] + [VMEM] * 4,
            name="attend_grad",
        )
        return live.flow(Scatter(sl, parts, 2))

    def two_sides(flows, wides, counts):
        values = [flow.value.reshape(2, rows, wide) for flow, wide in zip(flows, wides)]
        both = jnp.concatenate([v[..., :n] for v, n in zip(values, counts)], -1)
        keep, send = split(both, SIDE, 0)
        return keep, sl.flip(send, SIDE), values[0][..., counts[0] :]

    def finish(layer, big, before, more=None):
        keep, other, out = big
        more = [] if more is None else list(more[:2])
        return update(
            partial(finish_kernel, 2 * block, 2 * fsdp * feeds, part),
            layer,
            w_big.shape,
            [mine(SIDE)[None], keep, other, out, *more],
            [SMEM] + [VMEM] * (3 + len(more)),
            [m_big, v_big],
            before,
            "finish",
        )

    def finish_down(layer, flow, before):
        return update(
            finish_down_kernel,
            layer,
            w_down.shape,
            [flow.value],
            [VMEM],
            [m_down, v_down],
            before,
            "finish_down",
        )

    def table_terms():
        first, second = [
            jnp.concatenate([live.values[f"gains{n}0"], live.values[f"gains{n}1"]], 1) for n in range(2)
        ]
        hit = jnp.arange(count - 1) == section_ids[0]
        terms = jnp.concatenate([first, jnp.where(hit[:, None], second, 0.0)], 0)
        terms = terms.reshape(count, high, 2, 2, fsdp, norm_table.shape[1])
        return jnp.moveaxis(terms, 0, 4)

    def table_step(pos, bits):
        value = live.table
        for bit in bits:
            keep, send = split(value, bit, pos)
            value = keep + sl.flip(send, bit)
        live.put(table=value)

    ups[0].start()
    attns[1].start()
    ups[1].start()
    attns[0].finish()
    live.put(gains=gains_of(attns[0].quarters, live.sections))
    attend(0, live.hidden, 1)
    cross()
    live.seal(ups[0], attns[1], ups[1])

    attns[1].start()
    ups[1].start()
    downs[1].start()
    ups[0].finish()
    feed_forward(0, 1)
    cross()
    live.seal(attns[1], ups[1], downs[1])

    ups[1].start()
    downs[1].start()
    attns[1].finish()
    attend(1, live.feed0[0])
    cross()
    live.seal(ups[1], downs[1])

    ups[1].finish()
    downs[1].finish()
    live.put(grad=live.d_low.astype(f32))
    feed_turn(1)
    live.seal()

    cross()
    g_up1 = up_grad(1)
    g_up1.cross()
    g_up1.start()
    g_down1 = down_grad(1, True)
    g_down1.cross()
    g_down1.start()
    g_attn1 = attend_back(1)
    live.seal(g_down1, g_up1)

    g_down1.start()
    g_up1.start()
    g_attn1.cross()
    g_attn1.start()
    cross()
    feed_back(0)
    g_down0, g_up0b, g_up0a = down_grad(0), up_grad(0, 1), up_grad(0, 0)
    live.seal(g_down1, g_up1, g_attn1)

    cross()
    g_down0.cross()
    g_down0.start()
    g_up0b.cross()
    g_up0b.start()
    g_up0a.cross()
    after(g_up1, g_down0.quarters[0][1])
    g_up1.start()
    g_attn1.start()
    g_attn0 = attend_back(0)
    live.seal(g_down0, g_up1, g_attn1, g_up0b)

    cross()
    g_attn0.cross()
    g_attn0.start()
    g_up0b.start()
    g_down0.start()
    after(g_attn1, g_attn0.quarters[0][1])
    g_attn1.start()
    gate(g_up0b, g_attn1, g_down0)
    norm_back(0, 0, live.attn0[0])
    live.seal(g_attn0, g_attn1, g_down0, g_up0b)

    g_up0a.start()
    after(g_down0, g_attn0.quarters[1])
    (g_attn1.value, g_up1.value), g_attn0.quarters[1] = lax.optimization_barrier(
        ((g_attn1.value, g_up1.value), g_attn0.quarters[1])
    )
    g_attn0.start()
    g_down0.start()
    g_up0b.start()
    feed_down(1)
    big1 = two_sides([g_attn1, g_up1], [2 * width, feed // 2], [part, feed // 2])
    live.put(big=finish(1, big1, []))
    live.put(table=table_terms())
    live.seal(g_up0a, g_attn0, g_down0, g_up0b)

    g_up0a.start()
    g_attn0.start()
    g_down1.start()
    cross()
    table_step(2, [CORE])
    table_step(1, [SIDE])
    table = live.table.reshape(*(len(sl.high) + len(sl.deep)) * [2], count, -1)
    live.put(table=table, down=finish_down(0, g_down0, []))
    live.seal(g_up0a, g_attn0, g_down1)

    g_up0a.start()
    out_act = live.feed1[0][:length] + (live.keep[:length] + live.other[0][length:].astype(f32))
    big0 = two_sides([g_attn0, g_up0b], [2 * width, feed // 4], [part, feed // 4])
    table_step(0, sl.high)
    table_step(-3, sl.deep[-1:])
    live.put(out_act=out_act.astype(bf16), down=finish_down(1, g_down1, live.down), big0=big0)
    live.seal(g_up0a)

    table_step(0, sl.deep[:-1])
    up0a = two_sides([g_up0a], [feed // 4], [feed // 4])
    grad_big, new_m_big, step_big = finish(0, live.big0, live.big, up0a)
    grad_down, new_m_down, step_down = live.down
    grad_table = live.table
    new_m_table, step_table = adam_update(m_table, v_table, grad_table)
    return (
        live.out_act[None],
        live.d_low[:length][None],
        grad_big,
        grad_down,
        grad_table,
        new_m_big,
        new_m_down,
        new_m_table,
        step_big,
        step_down,
        step_table,
    )


def solution(mesh):
    both = ("dp", "fsdp")
    rows, middle, last = P(both, None, None), P(None, both, None), P(None, both)
    return jax.shard_map(
        partial(body, mesh.shape["dp"], mesh.shape["fsdp"]),
        mesh=mesh,
        in_specs=(rows, rows, P(both, None), P(both), middle, middle, last)
        + 2 * (middle, middle, last),
        out_specs=(rows, rows) + 3 * (middle, middle, last),
        check_vma=False,
    )
```

```python
import itertools
import math
from functools import partial

import jax
import jax.numpy as jnp
from jax import lax
from jax.experimental import pallas as pl
from jax.experimental.pallas import tpu as pltpu
from jax.sharding import PartitionSpec as P

HEADS = 16

beta_one = 0.9
beta_two = 0.999
first_fix = 1.0 - 0.9**10
second_fix = 1.0 - 0.999**10

f32 = jnp.float32
bf16 = jnp.bfloat16

VMEM = pl.BlockSpec(memory_space=pltpu.VMEM)
SMEM = pl.BlockSpec(memory_space=pltpu.SMEM)
ANY = pl.BlockSpec(memory_space=pl.ANY)

CORE = ("dp", 1)
SIDE = ("dp", 2)


def masks(size):
    return [1 << k for k in reversed(range(size.bit_length() - 1))]


class Slice:
    def __init__(self, dp, fsdp):
        self.high = [("dp", m) for m in masks(dp) if m > 2]
        self.deep = [("fsdp", m) for m in masks(fsdp)]
        self.size = {"dp": dp, "fsdp": fsdp}

    def flip(self, value, bit):
        axis, mask = bit
        return lax.ppermute(value, axis, [(i, i ^ mask) for i in range(self.size[axis])])


def mine(bit):
    axis, mask = bit
    return (lax.axis_index(axis) // mask) % 2


def call(kernel, outs, operands, specs, scratch=(), flops=0, name=None):
    held = [(v.shape, v.dtype) for v, spec in zip(operands, specs) if spec is VMEM] + list(outs)
    held += [(s.shape, s.dtype) for s in scratch if hasattr(s, "memory_space") and s.memory_space == pltpu.VMEM]
    held = sum(math.prod(shape) * jnp.dtype(kind).itemsize for shape, kind in held)
    return pl.pallas_call(
        kernel,
        out_shape=[jax.ShapeDtypeStruct(shape, kind) for shape, kind in outs],
        in_specs=specs,
        out_specs=[VMEM] * len(outs),
        scratch_shapes=list(scratch),
        compiler_params=pltpu.CompilerParams(vmem_limit_bytes=held + (3 << 20)),
        name=name,
    )(*operands)


def merge(own, other, bit, pos):
    side = mine(bit)
    return jnp.where(side == 0, jnp.stack([own, other], pos), jnp.stack([other, own], pos))


def split(value, bit, pos):
    side = mine(bit)
    keep = lax.dynamic_index_in_dim(value, side, pos, keepdims=False)
    send = lax.dynamic_index_in_dim(value, 1 - side, pos, keepdims=False)
    return keep, send


def interleave_kernel(count, side, *refs):
    owns, others, outs = refs[:count], refs[count : 2 * count], refs[2 * count :]
    each = count * owns[0].shape[0] // len(outs)
    for n, (own, other) in enumerate(zip(owns, others)):
        for m in range(own.shape[0]):
            out, at = outs[(n * own.shape[0] + m) // each], (n * own.shape[0] + m) % each
            out[pl.ds(at, 1), pl.ds(side[0], 1)] = own[pl.ds(m, 1)][:, None]
            out[pl.ds(at, 1), pl.ds(1 - side[0], 1)] = other[pl.ds(m, 1)][:, None]


def interleave(owns, others, bit, before, outs=1):
    rows, n = owns[0].shape
    count = len(owns)
    shape = (before, rows // before, n)
    whole = (count * before // outs, 2, rows // before, n)
    result = call(
        partial(interleave_kernel, count),
        outs * [(whole, owns[0].dtype)],
        [mine(bit)[None], *(v.reshape(shape) for v in (*owns, *others))],
        [SMEM] + [VMEM] * (2 * count),
        name="interleave",
    )
    return [part.reshape(-1, n) for part in result]


def prepare_kernel(span, chunk, side, big, table, first, first_sent, up0, up0_sent, after, after_sent, out, sems):
    width = out.shape[-1] * 2
    third = 3 * width
    copies = []
    for layer, qkv, up in ((0, (first, first_sent), (up0, up0_sent)), (1, (after, after_sent), (after, after_sent))):
        for x, target, upper in ((side[0], qkv[0], up[0]), (1 - side[0], qkv[1], up[1])):
            for n in range(third // (2 * span)):
                at = pl.multiple_of((2 * n + x) * span, 128)
                copies.append((big.at[layer, :, pl.ds(at, span)], target.at[:, pl.ds(n * span, span)]))
            base = 0 if layer == 0 else third // 2
            for n in range(up0.shape[1] // chunk):
                at = pl.multiple_of(4 * width + (2 * n + x) * chunk, 128)
                copies.append((big.at[layer, :, pl.ds(at, chunk)], upper.at[:, pl.ds(base + n * chunk, chunk)]))
        for k in range(2):
            copies.append((big.at[layer, :, pl.ds(third + k * width // 2, width // 2)], out.at[layer, k]))
    for target in (first, first_sent):
        copies.append((table, target.at[:, pl.ds(third // 2, 128)]))
    copies = [pltpu.make_async_copy(a, b, sems.at[n]) for n, (a, b) in enumerate(copies)]
    for copy in copies:
        copy.start()
    for copy in copies:
        copy.wait()


def place_first_kernel(side, keep, other, out, own):
    part = keep.shape[1] - 128
    wide = out.shape[-1]
    for source, x in ((keep, side[0]), (other, 1 - side[0])):
        own[pl.ds(x, 1), :, pl.ds(0, part)] = source[:, pl.ds(0, part)][None]
        own[pl.ds(x, 1), :, pl.ds(part + wide, 128)] = source[:, pl.ds(part, 128)][None]
    own[:, :, pl.ds(part, wide)] = out[...]


def place_next_kernel(side, keep, other, out, own):
    wide = out.shape[-1]
    part = 3 * wide
    for source, x in ((keep, side[0]), (other, 1 - side[0])):
        own[pl.ds(x, 1), :, pl.ds(0, part)] = source[:, pl.ds(0, part)][None]
        own[pl.ds(2 + x, 1)] = source[:, pl.ds(part, part + wide)][None]
    own[pl.ds(0, 2), :, pl.ds(part, wide)] = out[...]


class Gather:
    def __init__(self, sl, own, lead, top_first=False, twins=False):
        self.sl, self.value, self.lead, self.top_first, self.twins = sl, own, lead, top_first, twins
        self.have, self.air, self.quarters = [], None, None
        near = sl.high[:0:-1]
        if top_first:
            self.steps = [sl.high[:1], near + sl.deep[:-1], sl.deep[-1:]]
        else:
            self.steps = [sl.deep[:-1], sl.deep[-1:] + near]
        core = mine(CORE)
        self.place = jnp.stack([jnp.zeros_like(core) if top_first else mine(sl.high[0]), core])

    def before(self, bit):
        order = self.sl.high + self.sl.deep
        count = sum(order.index(b) < order.index(bit) for b in self.have)
        return (1 + self.twins) * (1 << count) * (1 if bit in self.sl.high else self.lead)

    def start(self):
        if not self.steps:
            self.air = self.sl.flip(self.value, self.sl.high[0]), self.sl.flip(self.value, CORE)
            return
        *others, self.bit = self.steps.pop(0)
        for bit in others:
            other = self.sl.flip(self.value, bit)
            self.value = interleave([self.value], [other], bit, self.before(bit))[0]
            self.have.append(bit)
        self.air = self.sl.flip(self.value, self.bit)

    def land(self):
        air, self.air = self.air, None
        if isinstance(air, tuple):
            self.quarters, self.value = [self.value, *air], None
            return
        last = (self.top_first or self.twins) and not self.steps
        halves = interleave([self.value], [air], self.bit, self.before(self.bit), 1 + last)
        self.have.append(self.bit)
        if last and self.twins:
            self.value = halves
        elif last:
            self.quarters = [*halves, self.sl.flip(halves[0], CORE)]
            self.value = None
        else:
            self.value = halves[0]

    def join(self, other):
        made = Gather(self.sl, None, self.lead, twins=True)
        airs = self.air, other.air
        made.value = interleave([self.value, other.value], airs, self.bit, self.before(self.bit))[0]
        made.have, made.steps = self.have + [self.bit], self.steps
        return made

    def part(self, n):
        made = Gather(self.sl, self.value[n], self.lead)
        made.steps = []
        return made

    def finish(self):
        self.quarters = [*self.quarters, self.sl.flip(self.quarters[1], CORE)]


def add_low_kernel(one, two, out):
    out[...] = (one[...].astype(f32) + two[...].astype(f32)).astype(bf16)


def add_split_kernel(side, *refs):
    *parts, kept, sent = refs
    for at, out in ((side[0], kept), (1 - side[0], sent)):
        total = parts[0][:, pl.ds(at, 1)].astype(f32)
        for other in parts[1:]:
            total = total + other[:, pl.ds(at, 1)].astype(f32)
        out[...] = total.astype(bf16)[:, 0]


def cross_split_kernel(side, own, own_other, top, top_other, kept, sent):
    for n, (one, two) in enumerate(((own, own_other), (top, top_other))):
        for at, out in ((side[0], kept), (1 - side[0], sent)):
            total = one[:, pl.ds(at, 1)].astype(f32) + two[:, pl.ds(at, 1)].astype(f32)
            out[n] = total.astype(bf16)[:, 0]


class Scatter:
    def __init__(self, sl, quarters, lead, top_last=False):
        self.sl, self.quarters, self.value, self.lead, self.top_last = sl, quarters, None, lead, top_last
        top, near, deep = sl.high[:1], sl.high[1:], sl.deep
        self.have = sl.high + deep
        if top_last:
            self.steps = [deep[-1:], deep[-2::-1] + near, top]
        else:
            self.steps = [top, near + deep[-1:], deep[-2::-1]]

    def before(self, bit):
        order = self.sl.high + self.sl.deep
        count = sum(order.index(b) < order.index(bit) for b in self.have)
        return (1 << count) * (1 if bit in self.sl.high else self.lead)

    def side(self, bit):
        return jnp.zeros((1,), jnp.int32) if bit == self.sl.high[0] else mine(bit)[None]

    def cross(self):
        own, top, core, both = self.quarters
        top_other = self.sl.flip(both, CORE)
        core, _ = lax.optimization_barrier((core, top_other))
        core_other = self.sl.flip(core, CORE)
        rows, n = top.shape
        if not self.top_last:
            (send,) = call(
                add_low_kernel, [(top.shape, bf16)], [top, top_other], [VMEM] * 2, name="add_low"
            )
            self.quarters = [[own, core_other], send]
            return
        bit = self.steps[0][0]
        before = self.before(bit) // 2
        shape = (before, 2, rows // 2 // before, n)
        half = ((2, before, rows // 2 // before, n), bf16)
        keep, send = call(
            cross_split_kernel,
            [half, half],
            [self.side(bit), *(v.reshape(shape) for v in (own, core_other, top, top_other))],
            [SMEM] + [VMEM] * 4,
            name="cross_split",
        )
        self.quarters = [[keep.reshape(-1, n)], send.reshape(-1, n)]

    def split(self, other, bit):
        parts = [*self.quarters[0], other]
        if bit is None:
            self.value = sum(part.astype(f32) for part in parts)
            self.quarters = None
            return
        before = self.before(bit)
        rows, n = other.shape
        shape = (before, 2, rows // 2 // before, n)
        half = ((before, rows // 2 // before, n), bf16)
        keep, send = call(
            add_split_kernel,
            [half, half],
            [self.side(bit), *(part.reshape(shape) for part in parts)],
            [SMEM] + [VMEM] * len(parts),
            name="add_split",
        )
        self.quarters = [[keep.reshape(-1, n)], send.reshape(-1, n)]

    def start(self):
        bits = self.steps.pop(0)
        for n, bit in enumerate(bits):
            self.air = self.sl.flip(self.quarters[1], bit)
            self.have.remove(bit)
            if n < len(bits) - 1:
                self.split(self.air, bits[n + 1])
        self.next = self.steps[0][0] if self.steps else None

    def land(self):
        other, self.air = self.air, None
        self.split(other, self.next)


class Live:
    def __init__(self, **values):
        self.flows = []
        self.values = values

    def flow(self, made):
        self.flows.append(made)
        return made

    def __getattr__(self, name):
        return self.values[name]

    def put(self, **values):
        self.values.update(values)

    def drop(self, *names):
        for name in names:
            del self.values[name]

    def seal(self, *landing, keep=()):
        landing = [*keep, *landing]
        kept = (
            self.values,
            [(made.value, made.quarters) for made in self.flows],
            [made.air for made in landing],
        )
        self.values, flown, airs = lax.optimization_barrier(kept)
        for made, (made.value, made.quarters) in zip(self.flows, flown):
            pass
        for n, (made, made.air) in enumerate(zip(landing, airs)):
            if n >= len(keep):
                made.land()


def dot(left, right):
    return jnp.dot(left, right, preferred_element_type=f32)


def dot_t(left, right):
    return lax.dot_general(left, right, (((1,), (1,)), ((), ())), preferred_element_type=f32)


def t_dot(left, right):
    return lax.dot_general(left, right, (((0,), (0,)), ((), ())), preferred_element_type=f32)


def fetch(place, quarters, whole, lead, sems):
    width = whole.shape[1]
    block = whole.shape[0] // (4 * lead)
    copies = []
    for n, part in enumerate(quarters):
        top = place[0] if n % 2 == 0 else 1 - place[0]
        core = place[1] if n < 2 else 1 - place[1]
        for a in range(lead):
            at = pl.multiple_of(((top * lead + a) * 2 + core) * block, block)
            source = part.at[pl.ds(a * block, block), pl.ds(0, width)]
            copies.append(
                pltpu.make_async_copy(source, whole.at[pl.ds(at, block)], sems.at[n * lead + a])
            )
    for copy in copies:
        copy.start()
    return copies


def norm(hidden):
    centred = hidden - jnp.mean(hidden, axis=-1, keepdims=True)
    scale = lax.rsqrt(jnp.mean(centred * centred, axis=-1, keepdims=True) + 1e-05)
    return centred * scale, scale


def put_rows(outs, cols, value):
    rows = value.shape[0] // len(outs)
    for r, out in enumerate(outs):
        out[:, cols] = value[r * rows : (r + 1) * rows].astype(bf16)


def theirs(others, r, rows):
    if len(others) == 2:
        return others[1 - r][...].astype(f32)
    return others[0][pl.ds((1 - r) * rows, rows)].astype(f32)


def gains_at(gains, r, place, width):
    return gains[pl.ds(r, 1), pl.ds(place * width, width)]


def add_norm(which, parts, gains, total, out):
    base, *shares = parts
    rows, width = out.shape[0] // 2, out.shape[1]
    for r in range(2):
        block = pl.ds(r * rows, rows)
        value = base[block]
        if shares:
            value = value + (shares[0][block] + theirs(shares[1:], r, rows))
            total[block] = value
        gain, bias = [gains_at(gains, r, 2 * which + n, width) for n in range(2)]
        out[block] = (norm(value)[0] * gain + bias).astype(bf16)


def norm_back(which, d_out, keep, others, hidden, gains, total, low, d_gain, d_shift):
    rows, width = d_out.shape[0] // 2, d_out.shape[1]
    for r in range(2):
        block = pl.ds(r * rows, rows)
        grad = keep[block] + theirs(others, r, rows)
        normed, scale = norm(hidden[block])
        if r == 0:
            d_gain[...] = jnp.sum(grad * normed, axis=0, keepdims=True)
            d_shift[...] = jnp.sum(grad, axis=0, keepdims=True)
        e = grad * gains_at(gains, r, 2 * which, width)
        part = e - jnp.mean(e, axis=-1, keepdims=True)
        part = part - normed * jnp.mean(e * normed, axis=-1, keepdims=True)
        value = d_out[block] + scale * part
        total[block] = value
        low[block] = value.astype(bf16)


def norm_back_kernel(which, d_out, keep, *refs):
    norm_back(which, d_out, keep, refs[:-6], *refs[-6:])


def gains_kernel(lead, count, rows, place, pick, q0, q1, q2, q3, first, second, held, wide, sems):
    copies = []
    for n, part in enumerate((q0, q1, q2, q3)):
        source = part.at[:, pl.ds(part.shape[1] - 128, 128)]
        copies.append(pltpu.make_async_copy(source, held.at[n], sems.at[n]))
    for copy in copies:
        copy.start()
    for copy in copies:
        copy.wait()
    wide[...] = held[...].astype(f32)
    deep = wide.shape[1] // (lead * rows)
    for n in range(4):
        top = place[0] if n % 2 == 0 else 1 - place[0]
        core = place[1] if n < 2 else 1 - place[1]
        for a in range(lead):
            for z in range(deep):
                cols = pl.multiple_of((((top * lead + a) * 2 + core) * deep + z) * 128, 128)
                base = (a * deep + z) * rows
                for r in range(2):
                    first[pl.ds(r, 1), pl.ds(cols, 128)] = wide[n, pl.ds(base, 1)]
                    second[pl.ds(r, 1), pl.ds(cols, 128)] = wide[n, pl.ds(base + 1 + pick[r], 1)]


def score(q, k, allowed, size):
    scores = jnp.where(allowed, dot_t(q, k) * size, -1e30)
    exponent = jnp.exp(scores - jnp.max(scores, axis=-1, keepdims=True))
    return exponent / jnp.sum(exponent, axis=-1, keepdims=True)


def lanes_of(which, shape):
    lane = lax.broadcasted_iota(jnp.int32, shape, 1)
    return (lane < shape[1] // 2) if which == 0 else (lane >= shape[1] // 2)


def out_block(weight, k, block, at):
    count = weight.shape[0] // (2 * block)
    wide = weight.shape[1] - at
    return jnp.concatenate([weight[pl.ds((2 * h + k) * block, block), pl.ds(at, wide)] for h in range(count)], 0)


def attend_kernel(ways, size, lead, block, place, *refs):
    refs, (weight, sems) = refs[:-2], refs[-2:]
    refs, lows = refs[:-ways], refs[-ways:]
    *parts, gains, q0, q1, q2, q3, allow, total, f, qkv, mixed, keep = refs
    copies = fetch(place, (q0, q1, q2, q3), weight, lead, sems)
    add_norm(0, parts, gains, total, f)
    for copy in copies:
        copy.wait()
    length = allow.shape[-1]
    third = qkv.shape[1] // 3
    for n in range(3):
        cols = pl.ds(n * third, third)
        qkv[:, cols] = dot(f[...], weight[:, cols]).astype(bf16)

    def one_row(r, carry):
        at = pl.ds(pl.multiple_of(r * length, length), length)
        allowed = allow[r] > 0
        for p in range(third // 128):
            q = qkv[at, pl.ds(p * 128, 128)]
            k = qkv[at, pl.ds(third + p * 128, 128)]
            v = qkv[at, pl.ds(2 * third + p * 128, 128)]
            halves = []
            for h in range(2):
                probs = score(jnp.where(lanes_of(h, q.shape), q, 0), k, allowed, size)
                halves.append(dot(probs.astype(bf16), v))
            mixed[at, pl.ds(p * 128, 128)] = jnp.where(
                lanes_of(0, q.shape), halves[0], halves[1]
            ).astype(bf16)
        return carry

    lax.fori_loop(0, f.shape[0] // length, one_row, 0)
    for k in range(2):
        cols = pl.ds(k * third, third)
        value = dot(mixed[...], out_block(weight, k, block, 3 * third))
        keep[:, cols] = value
        put_rows(lows, cols, value)


def attend_back_kernel(ways, size, lead, block, grads, place, *refs):
    if grads:
        (first, mixed), refs = refs[:2], refs[2:]
    (d_out, part), refs = refs[:2], refs[2:]
    refs, (weight, d_mixed, sems) = refs[:-3], refs[-3:]
    if grads:
        refs, outs = refs[:-4], refs[-4:]
    refs, lows = refs[:-ways], refs[-ways:]
    *others, attended, gains, q0, q1, q2, q3, allow, qkv, total, d, d_gain, d_shift, d_qkv, keep = refs
    copies = fetch(place, (q0, q1, q2, q3), weight, lead, sems)
    norm_back(1, d_out, part, others, attended, gains, total, d, d_gain, d_shift)
    for copy in copies:
        copy.wait()
    length = allow.shape[-1]
    third = qkv.shape[1] // 3
    value = dot_t(d[:, pl.ds(0, third)], out_block(weight, 0, block, 3 * third))
    value = value + dot_t(d[:, pl.ds(third, third)], out_block(weight, 1, block, 3 * third))
    d_mixed[...] = value.astype(bf16)

    def one_row(r, carry):
        at = pl.ds(pl.multiple_of(r * length, length), length)
        allowed = allow[r] > 0
        for p in range(third // 128):
            q = qkv[at, pl.ds(p * 128, 128)]
            k = qkv[at, pl.ds(third + p * 128, 128)]
            v = qkv[at, pl.ds(2 * third + p * 128, 128)]
            dm = d_mixed[at, pl.ds(p * 128, 128)]
            d_q, d_k, d_v = [], [], []
            for h in range(2):
                pick = lanes_of(h, q.shape)
                probs = score(jnp.where(pick, q, 0), k, allowed, size)
                d_probs = dot_t(jnp.where(pick, dm, 0), v)
                d_v.append(t_dot(probs.astype(bf16), dm))
                inner = jnp.sum(probs * d_probs, axis=-1, keepdims=True)
                d_scores = (probs * (d_probs - inner)).astype(bf16)
                d_q.append(dot(d_scores, k))
                d_k.append(t_dot(d_scores, q))
            pick = lanes_of(0, q.shape)
            for n, (halves, scale) in enumerate(((d_q, size), (d_k, size), (d_v, 1.0))):
                value = jnp.where(pick, halves[0], halves[1]) * scale
                d_qkv[at, pl.ds(n * third + p * 128, 128)] = value.astype(bf16)
        return carry

    lax.fori_loop(0, d.shape[0] // length, one_row, 0)
    for n in range(keep.shape[1] // 256):
        cols = pl.ds(n * 256, 256)
        value = dot_t(d_qkv[...], weight[cols, pl.ds(0, 3 * third)])
        keep[:, cols] = value
        put_rows(lows, cols, value)
    if grads:
        attend_grad(lead, place, first, mixed, d_qkv, d, outs)


def up(f, weight, pre, active):
    for n in range(pre.shape[1] // 256):
        cols = pl.ds(n * 256, 256)
        value = dot(f[...], weight[:, cols])
        pre[:, cols] = value
        active[:, cols] = jax.nn.gelu(value).astype(bf16)


def down(active, weight, keep, lows):
    for n in range(keep.shape[1] // 256):
        cols = pl.ds(n * 256, 256)
        value = dot(active[...], weight[:, cols])
        keep[:, cols] = value
        put_rows(lows, cols, value)


def feed_kernel(ways, lead, up_place, dn_place, *refs):
    refs, (w_up, w_dn, up_sems, dn_sems) = refs[:-4], refs[-4:]
    refs, lows = refs[:-ways], refs[-ways:]
    *parts, gains, u0, u1, u2, u3, n0, n1, n2, n3, total, f, pre, active, keep = refs
    up_copies = fetch(up_place, (u0, u1, u2, u3), w_up, lead, up_sems)
    dn_copies = fetch(dn_place, (n0, n1, n2, n3), w_dn, lead // 2, dn_sems)
    add_norm(1, parts, gains, total, f)
    for copy in up_copies:
        copy.wait()
    up(f, w_up, pre, active)
    for copy in dn_copies:
        copy.wait()
    down(active, w_dn, keep, lows)


def down_kernel(lead, place, active, q0, q1, q2, q3, keep, low, weight, sems):
    for copy in fetch(place, (q0, q1, q2, q3), weight, lead, sems):
        copy.wait()
    down(active, weight, keep, (low,))


def gelu_slope(x):
    c = 0.7978845608028654
    t = jnp.tanh(c * (x + 0.044715 * (x * x * x)))
    return 0.5 * (1.0 + t) + 0.5 * x * (1.0 - t * t) * (c * (1.0 + 3 * 0.044715 * (x * x)))


def feed_back(d, pre, w_up, w_dn, d_pre, keep, lows):
    for n in range(pre.shape[1] // 256):
        cols = pl.ds(n * 256, 256)
        d_pre[:, cols] = (gelu_slope(pre[:, cols]) * dot_t(d[...], w_dn[cols])).astype(bf16)
    for n in range(keep.shape[1] // 256):
        cols = pl.ds(n * 256, 256)
        value = dot_t(d_pre[...], w_up[cols])
        keep[:, cols] = value
        put_rows(lows, cols, value)


def feed_back_kernel(ways, lead, up_place, dn_place, d_out, part, *refs):
    refs, (w_up, w_dn, up_sems, dn_sems) = refs[:-4], refs[-4:]
    refs, lows = refs[:-ways], refs[-ways:]
    *others, hidden, gains, pre, u0, u1, u2, u3, n0, n1, n2, n3, total, d, d_gain, d_shift, d_pre, keep = refs
    copies = fetch(dn_place, (n0, n1, n2, n3), w_dn, lead // 2, dn_sems)
    copies += fetch(up_place, (u0, u1, u2, u3), w_up, lead, up_sems)
    norm_back(0, d_out, part, others, hidden, gains, total, d, d_gain, d_shift)
    for copy in copies:
        copy.wait()
    feed_back(d, pre, w_up, w_dn, d_pre, keep, lows)


def feed_turn_kernel(ways, lead, grads, place, up_place, dn_place, *refs):
    refs, (w_up, w_dn, pre, up_sems, dn_sems) = refs[:-5], refs[-5:]
    if grads:
        refs, up_outs, dn_outs = refs[:-8], refs[-8:-4], refs[-4:]
    refs, lows = refs[:-ways], refs[-ways:]
    *parts, gains, d, u0, u1, u2, u3, n0, n1, n2, n3, total, f, active, d_pre, keep = refs
    up_copies = fetch(up_place, (u0, u1, u2, u3), w_up, lead, up_sems)
    dn_copies = fetch(dn_place, (n0, n1, n2, n3), w_dn, lead // 2, dn_sems)
    add_norm(1, parts, gains, total, f)
    for copy in up_copies:
        copy.wait()
    up(f, w_up, pre, active)
    for copy in dn_copies:
        copy.wait()
    feed_back(d, pre, w_up, w_dn, d_pre, keep, lows)
    if grads:
        weight_grad(lead, place, f, d_pre, up_outs)
        weight_grad(lead // 2, place, active, d, dn_outs)


def columns_of(place, value, lead):
    block = value.shape[1] // (4 * lead)
    parts = []
    for n in range(4):
        top = place[0] if n % 2 == 0 else 1 - place[0]
        core = place[1] if n < 2 else 1 - place[1]
        starts = [((top * lead + a) * 2 + core) * block for a in range(lead)]
        if block % 128 == 0:
            starts = [pl.multiple_of(at, 128) for at in starts]
        parts.append(jnp.concatenate([value[:, pl.ds(at, block)] for at in starts], 1))
    return parts


def weight_grad(lead, place, left, right, outs):
    for part, out in zip(columns_of(place, left, lead), outs):
        out[...] = t_dot(part, right[...]).astype(bf16)


def weight_grad_kernel(lead, aligned, place, left, right, *outs):
    weight_grad(lead, place if aligned else (0, 0), left, right, outs)


def attend_grad_kernel(lead, aligned, place, left, mixed, d_qkv, d, *outs):
    attend_grad(lead, place if aligned else (0, 0), left, mixed, d_qkv, d, outs)


def attend_grad(lead, place, left, mixed, d_qkv, d, outs):
    width = d_qkv.shape[1]
    third = width // 3
    block = left.shape[1] // (4 * lead)
    lefts, inners = columns_of(place, left, lead), columns_of(place, mixed, lead // 2)
    for part, inner, out in zip(lefts, inners, outs):
        out[:, pl.ds(0, width)] = t_dot(part, d_qkv[...]).astype(bf16)
        value = t_dot(inner, d[...]).astype(bf16)
        for h in range(inner.shape[1] // block):
            for k in range(2):
                out[pl.ds((2 * h + k) * block, block), pl.ds(width, third)] = value[
                    h * block : (h + 1) * block, k * third : (k + 1) * third
                ]


def turn(sl, value, lead):
    tokens, width = value.shape
    value = value.reshape(tokens, 2, lead, 2, width // (4 * lead))
    value = jnp.stack(split(value, sl.high[0], 1), 1)
    return jnp.stack(split(value, CORE, 3), 3).reshape(tokens, width)


def finish_kernel(span, chunk, part, side, keep, other, out, *refs):
    grad, new_m, step = refs[-3:]
    third = out.shape[-1]
    total = (grad.shape[-1] - 8 * third) // 2
    late = total - (keep.shape[1] - part)
    m, v = refs[2:4] if late else refs[:2]
    pieces = [(keep, other, 0, 0, 0, part, span), (keep, other, part, 8 * third, late, total - late, chunk)]
    if late:
        pieces.append((refs[0], refs[1], 0, 8 * third, 0, late, chunk))
    for one, two, first, base, start, count, width in pieces:
        each = math.gcd(math.gcd(width, start), count)
        for source, x in ((one, side[0]), (two, 1 - side[0])):
            for n in range(count // each):
                block, inside = divmod(start + n * each, width)
                at = pl.multiple_of(base + (2 * block + x) * width + inside, 128)
                grad[0, :, pl.ds(at, each)] = source[:, pl.ds(first + n * each, each)]
    for k in range(2):
        grad[0, :, pl.ds((6 + k) * third, third)] = out[k]
    for n in range(grad.shape[2] // 1024):
        cols = pl.ds(n * 1024, 1024)
        new_m[0, :, cols], step[0, :, cols] = adam_update(m[0, :, cols], v[0, :, cols], grad[0, :, cols])


def finish_down_kernel(value, m, v, *refs):
    grad, new_m, step = refs[-3:]
    grad[0] = value[...]
    new_m[0], step[0] = adam_update(m[0], v[0], value[...])


def update(kernel, layer, shape, parts, specs, moments, before, name):
    one = pl.BlockSpec((1, *shape[1:]), lambda i: (layer, 0, 0))
    count = len(parts) + 2
    return pl.pallas_call(
        kernel,
        grid=(1,),
        out_shape=[jax.ShapeDtypeStruct(shape, f32)] * 3,
        in_specs=[*specs, one, one, *len(before) * [ANY]],
        out_specs=[one] * 3,
        input_output_aliases={count + n: n for n in range(len(before))},
        compiler_params=pltpu.CompilerParams(vmem_limit_bytes=20 << 20),
        name=name,
    )(*parts, *moments, *before)


def adam_update(moment, square, gradient):
    moment = beta_one * moment + (1.0 - beta_one) * gradient
    square = beta_two * square + (1.0 - beta_two) * gradient * gradient
    update = moment / first_fix / (jnp.sqrt(square / second_fix) + 1e-08)
    return (moment, update)


def dma(count):
    return pltpu.SemaphoreType.DMA((count,))


def body(
    dp,
    fsdp,
    inputs,
    cotangent,
    segment_ids,
    section_ids,
    w_big,
    w_down,
    norm_table,
    m_big,
    m_down,
    m_table,
    v_big,
    v_down,
    v_table,
):
    sl = Slice(dp, fsdp)
    length, width = inputs.shape[1:]
    rows = w_big.shape[1]
    feeds = w_down.shape[1]
    feed = w_big.shape[2] - 4 * width
    high = dp // 4
    lead = high
    half, part = width // 2, 3 * width // 2
    block = fsdp * rows
    count = norm_table.shape[0]
    size = (width // HEADS) ** -0.5
    two_f, two_b = ((2 * length, width), f32), ((2 * length, width), bf16)
    wide_b = ((2 * length, feed // 2), bf16)

    def lows(ways):
        return ways * [((2 // ways * length, width), bf16)]

    quarter = ((width // 4, 2 * width), bf16)
    gain_row = ((1, width), f32)
    up_first = feed // 2 - feed // 8
    place = jnp.stack([mine(sl.high[0]), mine(CORE)])
    w_attn = pltpu.VMEM((width, 2 * width), bf16)
    w_upper = pltpu.VMEM((width, feed // 2), bf16)
    w_lower = pltpu.VMEM((feed // 2, width), bf16)

    def qkv_sides(layer):
        value = w_big[layer, :, : 3 * width].reshape(rows, 3, high, 2, 2 * block)
        return [v.reshape(rows, part) for v in split(value, SIDE, 3)]

    def up_sides(layer):
        value = w_big[layer, :, 4 * width :].reshape(rows, high, 2, 2 * fsdp * feeds)
        return [v.reshape(rows, feed // 2) for v in split(value, SIDE, 2)]

    def prepare(table_part):
        shapes = 2 * [(rows, part + 128)] + 2 * [(rows, feed // 2)] + 2 * [(rows, part + feed // 2)]
        shapes.append((2, 2, rows, half))
        if rows % 16 == 0:
            return call(
                partial(prepare_kernel, 2 * block, 2 * fsdp * feeds),
                [(shape, bf16) for shape in shapes],
                [mine(SIDE)[None], w_big, table_part],
                [SMEM, ANY, ANY],
                [dma(2 * (2 * 3 * high + 2 * high + 2) + 2)],
                name="prepare",
            )
        first = [jnp.concatenate([v, table_part], -1) for v in qkv_sides(0)]
        after = [jnp.concatenate([a, b], -1) for a, b in zip(qkv_sides(1), up_sides(1))]
        out = w_big[:, :, 3 * width : 4 * width].reshape(2, rows, 2, half)
        return [*first, *up_sides(0), *after, jnp.swapaxes(out, 1, 2)]

    def place_sides(kernel, shape, keep, other, out, name):
        return call(
            kernel,
            [(shape, bf16)],
            [mine(SIDE)[None], keep, other, out],
            [SMEM, VMEM, VMEM, VMEM],
            name=name,
        )[0]

    live = Live()
    downs = [live.flow(Gather(sl, w_down[n], 1, n == 1)) for n in range(2)]

    downs[0].start()
    downs[1].start()
    table_part = norm_table.reshape(-1)
    table_part = jnp.pad(table_part, (0, rows * 128 - table_part.shape[0])).reshape(rows, 128)
    first, first_sent, up0, up0_sent, after, after_sent, out_proj = prepare(table_part)
    live.put(
        first=[first, sl.flip(first_sent, SIDE)],
        up=[up0, up0_sent],
        after=[after, after_sent],
        out=out_proj,
    )
    live.seal(downs[0], downs[1])

    own = place_sides(
        place_first_kernel, (2, rows, 2 * width + 128), *live.first, live.out[0], "place_first"
    )
    attns = [live.flow(Gather(sl, own.reshape(2 * rows, -1), 2))]
    attns[0].start()
    downs[0].start()
    extra = jnp.zeros((16, width), bf16)
    extra = extra.at[0, :length].set(segment_ids[0].astype(bf16))
    extra = extra.at[1, 0].set(section_ids[0].astype(bf16))
    pack = jnp.concatenate([inputs[0], cotangent[0], extra], 0)
    live.put(
        up=[live.up[0], sl.flip(live.up[1], SIDE)],
        after=[live.after[0], sl.flip(live.after[1], SIDE)],
        pack=[pack, sl.flip(pack, SIDE)],
    )
    live.drop("first")
    live.seal(attns[0], downs[0])

    ups = [live.flow(Gather(sl, interleave(live.up[:1], live.up[1:], SIDE, 1)[0], 2))]
    downs[0].start()
    attns[0].start()
    ups[0].start()
    own = place_sides(
        place_next_kernel, (4, rows, 2 * width), *live.after, live.out[1], "place_next"
    )
    live.put(own=own)
    live.drop("up", "after", "out")
    packed = jnp.stack(live.pack)
    extras = packed[:, 2 * length :]
    segments = extras[:, 0, :length].astype(f32)
    same = segments[:, :, None] == segments[:, None, :]
    position = jnp.arange(length)
    live.put(
        hidden=packed[:, :length].reshape(2 * length, width).astype(f32),
        d_low=packed[:, length : 2 * length].reshape(2 * length, width),
        sections=extras[:, 1, 0].astype(jnp.int32),
        allows=[
            (same & (position[:, None] >= position[None, :])).astype(f32),
            same.astype(f32),
        ],
    )
    live.drop("pack")
    live.seal(attns[0], ups[0], downs[0])

    own = live.own.reshape(2, 2 * rows, -1)
    attns.append(live.flow(Gather(sl, own[0], 2)))
    ups.append(live.flow(Gather(sl, own[1], 2)))
    live.drop("own")
    attns[0].start()
    attns[1].start()
    ups[0].start()
    downs[0].finish()
    live.seal(attns[0], ups[0], attns[1])

    def after(made, value):
        (keep, send), _ = lax.optimization_barrier((made.quarters, value))
        made.quarters = [keep, send]

    def gate(*made):
        airs = [flow.air for flow in made]
        other, airs = lax.optimization_barrier((live.other, airs))
        live.put(other=other)
        for flow, flow.air in zip(made, airs):
            pass

    def gains_of(flow, sections):
        wide = norm_table.shape[1]
        if wide == 128:
            return call(
                partial(gains_kernel, lead, count, rows),
                2 * [((2, 4 * width), f32)],
                [place, sections, *pinned(flow)],
                [SMEM, SMEM] + [ANY] * 4,
                [
                    pltpu.VMEM((4, width // 4, 128), bf16),
                    pltpu.VMEM((4, width // 4, 128), f32),
                    dma(4),
                ],
                name="gains",
            )
        parts = jnp.stack([q[:, 2 * width :] for q in flow.quarters])
        parts = parts.reshape(4, lead // 2, 2, fsdp, rows * 128)[..., : count * wide]
        parts = parts.reshape(4, lead // 2, 2, fsdp, count, wide)
        pick = jnp.concatenate([jnp.zeros((2,), jnp.int32), 1 + sections])
        pick = (pick[:, None] == jnp.arange(count)[None, :]).astype(bf16)
        picked = jnp.einsum("sr,qhxdrj->qshxdj", pick, parts, preferred_element_type=f32)
        own, top, core, both = picked
        both = merge(merge(own, core, CORE, 3), merge(top, both, CORE, 3), sl.high[0], 1)
        return list(both.reshape(2, 2, 4 * width))

    def pinned(flow):
        own, top, core, both = flow.quarters
        if flow is downs[0]:
            both = pltpu.with_memory_space_constraint(both, pltpu.HBM)
        return [own, top, pltpu.with_memory_space_constraint(core, pltpu.HBM), both]

    def cross():
        live.put(other=[sl.flip(row, SIDE) for row in live.low])

    def shares():
        return [live.keep, *live.other]

    def attend(layer, base, ways=2):
        parts = [base] if layer == 0 else [base, *shares()]
        total, first, qkv, mixed, keep, *low = call(
            partial(attend_kernel, ways, size, lead, 2 * block),
            [two_f, two_b, ((2 * length, part), bf16), ((2 * length, half), bf16), two_f, *lows(ways)],
            [
                attns[layer].place,
                *parts,
                live.gains[layer],
                *pinned(attns[layer]),
                live.allows[layer],
            ],
            [SMEM] + [VMEM] * (len(parts) + 1) + [ANY] * 4 + [VMEM],
            [w_attn, dma(4 * lead)],
            name="attend",
        )
        hidden = base if layer == 0 else total
        live.put(**{f"attn{layer}": (hidden, first, qkv, mixed)}, keep=keep, low=low)

    def feed_forward(layer, ways=2):
        attended, second, pre, active, keep, *low = call(
            partial(feed_kernel, ways, lead),
            [two_f, two_b, (wide_b[0], f32), wide_b, two_f, *lows(ways)],
            [
                ups[layer].place,
                downs[layer].place,
                live.values[f"attn{layer}"][0],
                *shares(),
                live.gains[layer],
                *pinned(ups[layer]),
                *pinned(downs[layer]),
            ],
            [SMEM, SMEM] + [VMEM] * (3 + len(live.other)) + [ANY] * 8,
            [w_upper, w_lower, dma(4 * lead), dma(2 * lead)],
            name="feed",
        )
        live.put(**{f"feed{layer}": (attended, second, pre, active)}, keep=keep, low=low)

    def feed_turn(layer, ways=2):
        grads = False
        quarters = 4 * [quarter] + 4 * [((feed // 8, width), bf16)]
        attended, second, active, d_pre, keep, *low = call(
            partial(feed_turn_kernel, ways, lead, grads),
            [two_f, two_b, wide_b, wide_b, two_f, *lows(ways), *(quarters if grads else [])],
            [
                place,
                ups[layer].place,
                downs[layer].place,
                live.values[f"attn{layer}"][0],
                *shares(),
                live.gains[layer],
                live.d_low,
                *pinned(ups[layer]),
                *pinned(downs[layer]),
            ],
            [SMEM] * 3 + [VMEM] * (4 + len(live.other)) + [ANY] * 8,
            [w_upper, w_lower, pltpu.VMEM(wide_b[0], f32), dma(4 * lead), dma(2 * lead)],
            name="feed_turn",
        )
        live.put(**{f"feed{layer}": (attended, second, None, active)}, d_pre=d_pre, keep=keep, low=low)

    def feed_down(layer):
        keep, *low = call(
            partial(down_kernel, lead // 2),
            [two_f, *lows(1)],
            [downs[layer].place, live.values[f"feed{layer}"][3], *pinned(downs[layer])],
            [SMEM, VMEM, ANY, ANY, ANY, ANY],
            [w_lower, dma(2 * lead)],
            name="down",
        )
        live.put(keep=keep, low=low)

    def feed_back(layer, ways=1):
        grad, d_low, d_gain, d_shift, d_pre, keep, *low = call(
            partial(feed_back_kernel, ways, lead),
            [two_f, two_b, gain_row, gain_row, wide_b, two_f, *lows(ways)],
            [
                ups[layer].place,
                downs[layer].place,
                live.grad,
                *shares(),
                live.values[f"attn{layer + 1}"][0],
                live.gains[layer + 1],
                live.values[f"feed{layer}"][2],
                *pinned(ups[layer]),
                *pinned(downs[layer]),
            ],
            [SMEM, SMEM] + [VMEM] * (5 + len(live.other)) + [ANY] * 8,
            [w_upper, w_lower, dma(4 * lead), dma(2 * lead)],
            name="feed_back",
        )
        live.put(grad=grad, d_low=d_low, d_pre=d_pre, keep=keep, low=low)
        live.put(**{f"gains{layer + 1}0": jnp.concatenate([d_gain, d_shift], 1)})

    def down_grad(layer, top_last=False):
        aligned = feed // 4 // lead % 128 == 0
        active = live.values[f"feed{layer}"][3]
        parts = call(
            partial(weight_grad_kernel, lead // 2, aligned),
            [((feed // 8, width), bf16)] * 4,
            [place, active if aligned else turn(sl, active, lead // 2), live.d_low],
            [SMEM, VMEM, VMEM],
            name="down_grad",
        )
        return live.flow(Scatter(sl, parts, 1, top_last))

    def up_grad(layer, piece=None):
        aligned = block % 128 == 0
        second, right = live.values[f"feed{layer}"][1], live.d_pre
        columns = feed // 2
        if piece is not None:
            right = right[:, :up_first] if piece == 0 else right[:, up_first:]
            columns = right.shape[1]
        parts = call(
            partial(weight_grad_kernel, lead, aligned),
            [((width // 4, columns), bf16)] * 4,
            [place, second if aligned else turn(sl, second, lead), right],
            [SMEM, VMEM, VMEM],
            name="up_grad",
        )
        return live.flow(Scatter(sl, parts, 2, piece == 1))

    def norm_back(which, layer, hidden):
        grad, d_low, d_gain, d_shift = call(
            partial(norm_back_kernel, which),
            [two_f, two_b, gain_row, gain_row],
            [live.grad, *shares(), hidden, live.gains[layer]],
            [VMEM] * (4 + len(live.other)),
            name="norm_back",
        )
        live.put(grad=grad, d_low=d_low)
        live.put(**{f"gains{layer}{which}": jnp.concatenate([d_gain, d_shift], 1)})

    def attend_back(layer, ways=1):
        grads = block % 128 == 0
        hidden, first, qkv, mixed = live.values[f"attn{layer}"]
        grad, d_low, d_gain, d_shift, d_qkv, keep, *low = call(
            partial(attend_back_kernel, ways, size, lead, 2 * block, grads),
            [
                *(two_f, two_b, gain_row, gain_row, ((2 * length, part), bf16), two_f, *lows(ways)),
                *(4 * [quarter] if grads else []),
            ],
            [
                attns[layer].place,
                *([first, mixed] if grads else []),
                live.grad,
                *shares(),
                live.values[f"feed{layer}"][0],
                live.gains[layer],
                *pinned(attns[layer]),
                live.allows[layer],
                live.values[f"attn{layer}"][2],
            ],
            [SMEM] + [VMEM] * (4 + 2 * grads + len(live.other)) + [ANY] * 4 + [VMEM] * 2,
            [w_attn, pltpu.VMEM((2 * length, half), bf16), dma(4 * lead)],
            name="attend_back",
        )
        low, made = low[:ways], low[ways:]
        live.put(grad=grad, d_low=d_low, d_qkv=d_qkv, keep=keep, low=low)
        live.put(**{f"gains{layer}1": jnp.concatenate([d_gain, d_shift], 1)})
        return live.flow(Scatter(sl, made, 2)) if grads else attend_grad(layer)

    def attend_grad(layer):
        hidden, first, qkv, mixed = live.values[f"attn{layer}"]
        aligned = block % 128 == 0
        if not aligned:
            first, mixed = turn(sl, first, lead), turn(sl, mixed, lead // 2)
        parts = call(
            partial(attend_grad_kernel, lead, aligned),
            [quarter] * 4,
            [place, first, mixed, live.d_qkv, live.d_low],
            [SMEM] + [VMEM] * 4,
            name="attend_grad",
        )
        return live.flow(Scatter(sl, parts, 2))

    def two_sides(flows, wides, counts):
        values = [flow.value.reshape(2, rows, wide) for flow, wide in zip(flows, wides)]
        both = jnp.concatenate([v[..., :n] for v, n in zip(values, counts)], -1)
        keep, send = split(both, SIDE, 0)
        return keep, sl.flip(send, SIDE), values[0][..., counts[0] :]

    def finish(layer, big, before, more=None):
        keep, other, out = big
        more = [] if more is None else list(more[:2])
        return update(
            partial(finish_kernel, 2 * block, 2 * fsdp * feeds, part),
            layer,
            w_big.shape,
            [mine(SIDE)[None], keep, other, out, *more],
            [SMEM] + [VMEM] * (3 + len(more)),
            [m_big, v_big],
            before,
            "finish",
        )

    def finish_down(layer, flow, before):
        return update(
            finish_down_kernel,
            layer,
            w_down.shape,
            [flow.value],
            [VMEM],
            [m_down, v_down],
            before,
            "finish_down",
        )

    def table_terms():
        first, second = [
            jnp.concatenate([live.values[f"gains{n}0"], live.values[f"gains{n}1"]], 1) for n in range(2)
        ]
        hit = jnp.arange(count - 1) == section_ids[0]
        terms = jnp.concatenate([first, jnp.where(hit[:, None], second, 0.0)], 0)
        terms = terms.reshape(count, high, 2, 2, fsdp, norm_table.shape[1])
        return jnp.moveaxis(terms, 0, 4)

    def table_step(pos, bits):
        value = live.table
        for bit in bits:
            keep, send = split(value, bit, pos)
            value = keep + sl.flip(send, bit)
        live.put(table=value)

    ups[0].start()
    attns[1].start()
    ups[1].start()
    attns[0].finish()
    live.put(gains=gains_of(attns[0], live.sections))
    attend(0, live.hidden, 1)
    cross()
    live.seal(ups[0], attns[1], ups[1])

    attns[1].start()
    ups[1].start()
    downs[1].start()
    ups[0].finish()
    feed_forward(0, 1)
    cross()
    live.seal(attns[1], ups[1], downs[1])

    ups[1].start()
    downs[1].start()
    attns[1].finish()
    attend(1, live.feed0[0])
    cross()
    live.seal(ups[1], downs[1])

    ups[1].finish()
    downs[1].finish()
    live.put(grad=live.d_low.astype(f32))
    feed_turn(1)
    live.seal()

    cross()
    g_up1 = up_grad(1)
    g_up1.cross()
    g_up1.start()
    g_down1 = down_grad(1, True)
    g_down1.cross()
    g_down1.start()
    g_attn1 = attend_back(1)
    live.seal(g_down1, g_up1)

    g_down1.start()
    g_up1.start()
    g_attn1.cross()
    g_attn1.start()
    cross()
    feed_back(0)
    g_down0, g_up0b, g_up0a = down_grad(0), up_grad(0, 1), up_grad(0, 0)
    live.seal(g_down1, g_up1, g_attn1)

    cross()
    g_down0.cross()
    g_down0.start()
    g_up0b.cross()
    g_up0b.start()
    g_up0a.cross()
    after(g_up1, g_down0.quarters[0][1])
    g_up1.start()
    g_attn1.start()
    g_attn0 = attend_back(0)
    live.seal(g_down0, g_up1, g_attn1, g_up0b)

    cross()
    g_attn0.cross()
    g_attn0.start()
    g_up0b.start()
    g_down0.start()
    after(g_attn1, g_attn0.quarters[0][1])
    g_attn1.start()
    gate(g_up0b, g_attn1, g_down0)
    norm_back(0, 0, live.attn0[0])
    live.seal(g_attn0, g_attn1, g_down0, g_up0b)

    g_up0a.start()
    after(g_down0, g_attn0.quarters[1])
    (g_attn1.value, g_up1.value), g_attn0.quarters[1] = lax.optimization_barrier(
        ((g_attn1.value, g_up1.value), g_attn0.quarters[1])
    )
    g_attn0.start()
    g_down0.start()
    g_up0b.start()
    feed_down(1)
    big1 = two_sides([g_attn1, g_up1], [2 * width, feed // 2], [part, feed // 2])
    live.put(big=finish(1, big1, []))
    live.put(table=table_terms())
    live.seal(g_up0a, g_attn0, g_down0, g_up0b)

    g_up0a.start()
    g_attn0.start()
    g_down1.start()
    cross()
    table_step(2, [CORE])
    table_step(1, [SIDE])
    table = live.table.reshape(*(len(sl.high) + len(sl.deep)) * [2], count, -1)
    live.put(table=table, down=finish_down(0, g_down0, []))
    live.seal(g_up0a, g_attn0, g_down1)

    g_up0a.start()
    out_act = live.feed1[0][:length] + (live.keep[:length] + live.other[0][length:].astype(f32))
    rest = feed // 2 - up_first
    big0 = two_sides([g_attn0, g_up0b], [2 * width, rest], [part, rest])
    table_step(0, sl.high)
    table_step(-3, sl.deep[-1:])
    live.put(out_act=out_act.astype(bf16), down=finish_down(1, g_down1, live.down), big0=big0)
    live.seal(g_up0a)

    table_step(0, sl.deep[:-1])
    up0a = two_sides([g_up0a], [up_first], [up_first])
    grad_big, new_m_big, step_big = finish(0, live.big0, live.big, up0a)
    grad_down, new_m_down, step_down = live.down
    grad_table = live.table
    new_m_table, step_table = adam_update(m_table, v_table, grad_table)
    return (
        live.out_act[None],
        live.d_low[:length][None],
        grad_big,
        grad_down,
        grad_table,
        new_m_big,
        new_m_down,
        new_m_table,
        step_big,
        step_down,
        step_table,
    )


def solution(mesh):
    both = ("dp", "fsdp")
    rows, middle, last = P(both, None, None), P(None, both, None), P(None, both)
    return jax.shard_map(
        partial(body, mesh.shape["dp"], mesh.shape["fsdp"]),
        mesh=mesh,
        in_specs=(rows, rows, P(both, None), P(both), middle, middle, last)
        + 2 * (middle, middle, last),
        out_specs=(rows, rows) + 3 * (middle, middle, last),
        check_vma=False,
    )
```

```python
import itertools
import math
from functools import partial

import jax
import jax.numpy as jnp
from jax import lax
from jax.experimental import pallas as pl
from jax.experimental.pallas import tpu as pltpu
from jax.sharding import PartitionSpec as P

HEADS = 16

beta_one = 0.9
beta_two = 0.999
first_fix = 1.0 - 0.9**10
second_fix = 1.0 - 0.999**10

f32 = jnp.float32
bf16 = jnp.bfloat16

VMEM = pl.BlockSpec(memory_space=pltpu.VMEM)
SMEM = pl.BlockSpec(memory_space=pltpu.SMEM)
ANY = pl.BlockSpec(memory_space=pl.ANY)

CORE = ("dp", 1)
SIDE = ("dp", 2)


def masks(size):
    return [1 << k for k in reversed(range(size.bit_length() - 1))]


class Slice:
    def __init__(self, dp, fsdp):
        self.high = [("dp", m) for m in masks(dp) if m > 2]
        self.deep = [("fsdp", m) for m in masks(fsdp)]
        self.size = {"dp": dp, "fsdp": fsdp}

    def flip(self, value, bit):
        axis, mask = bit
        return lax.ppermute(value, axis, [(i, i ^ mask) for i in range(self.size[axis])])


def mine(bit):
    axis, mask = bit
    return (lax.axis_index(axis) // mask) % 2


def call(kernel, outs, operands, specs, scratch=(), flops=0, name=None):
    held = [(v.shape, v.dtype) for v, spec in zip(operands, specs) if spec is VMEM] + list(outs)
    held += [(s.shape, s.dtype) for s in scratch if hasattr(s, "memory_space") and s.memory_space == pltpu.VMEM]
    held = sum(math.prod(shape) * jnp.dtype(kind).itemsize for shape, kind in held)
    return pl.pallas_call(
        kernel,
        out_shape=[jax.ShapeDtypeStruct(shape, kind) for shape, kind in outs],
        in_specs=specs,
        out_specs=[VMEM] * len(outs),
        scratch_shapes=list(scratch),
        compiler_params=pltpu.CompilerParams(vmem_limit_bytes=held + (3 << 20)),
        name=name,
    )(*operands)


def merge(own, other, bit, pos):
    side = mine(bit)
    return jnp.where(side == 0, jnp.stack([own, other], pos), jnp.stack([other, own], pos))


def split(value, bit, pos):
    side = mine(bit)
    keep = lax.dynamic_index_in_dim(value, side, pos, keepdims=False)
    send = lax.dynamic_index_in_dim(value, 1 - side, pos, keepdims=False)
    return keep, send


def interleave_kernel(count, side, *refs):
    owns, others, outs = refs[:count], refs[count : 2 * count], refs[2 * count :]
    each = count * owns[0].shape[0] // len(outs)
    for n, (own, other) in enumerate(zip(owns, others)):
        for m in range(own.shape[0]):
            out, at = outs[(n * own.shape[0] + m) // each], (n * own.shape[0] + m) % each
            out[pl.ds(at, 1), pl.ds(side[0], 1)] = own[pl.ds(m, 1)][:, None]
            out[pl.ds(at, 1), pl.ds(1 - side[0], 1)] = other[pl.ds(m, 1)][:, None]


def interleave(owns, others, bit, before, outs=1):
    rows, n = owns[0].shape
    count = len(owns)
    shape = (before, rows // before, n)
    whole = (count * before // outs, 2, rows // before, n)
    result = call(
        partial(interleave_kernel, count),
        outs * [(whole, owns[0].dtype)],
        [mine(bit)[None], *(v.reshape(shape) for v in (*owns, *others))],
        [SMEM] + [VMEM] * (2 * count),
        name="interleave",
    )
    return [part.reshape(-1, n) for part in result]


def prepare_kernel(span, chunk, side, big, table, first, first_sent, up0, up0_sent, after, after_sent, out, sems):
    width = out.shape[-1] * 2
    third = 3 * width
    copies = []
    for layer, qkv, up in ((0, (first, first_sent), (up0, up0_sent)), (1, (after, after_sent), (after, after_sent))):
        for x, target, upper in ((side[0], qkv[0], up[0]), (1 - side[0], qkv[1], up[1])):
            for n in range(third // (2 * span)):
                at = pl.multiple_of((2 * n + x) * span, 128)
                copies.append((big.at[layer, :, pl.ds(at, span)], target.at[:, pl.ds(n * span, span)]))
            base = 0 if layer == 0 else third // 2
            for n in range(up0.shape[1] // chunk):
                at = pl.multiple_of(4 * width + (2 * n + x) * chunk, 128)
                copies.append((big.at[layer, :, pl.ds(at, chunk)], upper.at[:, pl.ds(base + n * chunk, chunk)]))
        for k in range(2):
            copies.append((big.at[layer, :, pl.ds(third + k * width // 2, width // 2)], out.at[layer, k]))
    for target in (first, first_sent):
        copies.append((table, target.at[:, pl.ds(third // 2, 128)]))
    copies = [pltpu.make_async_copy(a, b, sems.at[n]) for n, (a, b) in enumerate(copies)]
    for copy in copies:
        copy.start()
    for copy in copies:
        copy.wait()


def place_first_kernel(side, keep, other, out, own):
    part = keep.shape[1] - 128
    wide = out.shape[-1]
    for source, x in ((keep, side[0]), (other, 1 - side[0])):
        own[pl.ds(x, 1), :, pl.ds(0, part)] = source[:, pl.ds(0, part)][None]
        own[pl.ds(x, 1), :, pl.ds(part + wide, 128)] = source[:, pl.ds(part, 128)][None]
    own[:, :, pl.ds(part, wide)] = out[...]


def place_next_kernel(side, keep, other, out, own):
    wide = out.shape[-1]
    part = 3 * wide
    for source, x in ((keep, side[0]), (other, 1 - side[0])):
        own[pl.ds(x, 1), :, pl.ds(0, part)] = source[:, pl.ds(0, part)][None]
        own[pl.ds(2 + x, 1)] = source[:, pl.ds(part, part + wide)][None]
    own[pl.ds(0, 2), :, pl.ds(part, wide)] = out[...]


class Gather:
    def __init__(self, sl, own, lead, top_first=False, twins=False):
        self.sl, self.value, self.lead, self.top_first, self.twins = sl, own, lead, top_first, twins
        self.have, self.air, self.quarters = [], None, None
        near = sl.high[:0:-1]
        if top_first:
            self.steps = [sl.high[:1], near + sl.deep[:-1], sl.deep[-1:]]
        else:
            self.steps = [sl.deep[:-1], sl.deep[-1:] + near]
        core = mine(CORE)
        self.place = jnp.stack([jnp.zeros_like(core) if top_first else mine(sl.high[0]), core])

    def before(self, bit):
        order = self.sl.high + self.sl.deep
        count = sum(order.index(b) < order.index(bit) for b in self.have)
        return (1 + self.twins) * (1 << count) * (1 if bit in self.sl.high else self.lead)

    def start(self):
        if not self.steps:
            self.air = self.sl.flip(self.value, self.sl.high[0]), self.sl.flip(self.value, CORE)
            return
        *others, self.bit = self.steps.pop(0)
        for bit in others:
            other = self.sl.flip(self.value, bit)
            self.value = interleave([self.value], [other], bit, self.before(bit))[0]
            self.have.append(bit)
        self.air = self.sl.flip(self.value, self.bit)

    def land(self):
        air, self.air = self.air, None
        if isinstance(air, tuple):
            self.quarters, self.value = [self.value, *air], None
            return
        last = (self.top_first or self.twins) and not self.steps
        halves = interleave([self.value], [air], self.bit, self.before(self.bit), 1 + last)
        self.have.append(self.bit)
        if last and self.twins:
            self.value = halves
        elif last:
            self.quarters = [*halves, self.sl.flip(halves[0], CORE)]
            self.value = None
        else:
            self.value = halves[0]

    def join(self, other):
        made = Gather(self.sl, None, self.lead, twins=True)
        airs = self.air, other.air
        made.value = interleave([self.value, other.value], airs, self.bit, self.before(self.bit))[0]
        made.have, made.steps = self.have + [self.bit], self.steps
        return made

    def part(self, n):
        made = Gather(self.sl, self.value[n], self.lead)
        made.steps = []
        return made

    def finish(self):
        self.quarters = [*self.quarters, self.sl.flip(self.quarters[1], CORE)]


def add_low_kernel(one, two, out):
    out[...] = (one[...].astype(f32) + two[...].astype(f32)).astype(bf16)


def add_split_kernel(side, *refs):
    *parts, kept, sent = refs
    for at, out in ((side[0], kept), (1 - side[0], sent)):
        total = parts[0][:, pl.ds(at, 1)].astype(f32)
        for other in parts[1:]:
            total = total + other[:, pl.ds(at, 1)].astype(f32)
        out[...] = total.astype(bf16)[:, 0]


def cross_split_kernel(side, own, own_other, top, top_other, kept, sent):
    for n, (one, two) in enumerate(((own, own_other), (top, top_other))):
        for at, out in ((side[0], kept), (1 - side[0], sent)):
            total = one[:, pl.ds(at, 1)].astype(f32) + two[:, pl.ds(at, 1)].astype(f32)
            out[n] = total.astype(bf16)[:, 0]


class Scatter:
    def __init__(self, sl, quarters, lead, top_last=False):
        self.sl, self.quarters, self.value, self.lead, self.top_last = sl, quarters, None, lead, top_last
        top, near, deep = sl.high[:1], sl.high[1:], sl.deep
        self.have = sl.high + deep
        if top_last:
            self.steps = [deep[-1:], deep[-2::-1] + near, top]
        else:
            self.steps = [top, near + deep[-1:], deep[-2::-1]]

    def before(self, bit):
        order = self.sl.high + self.sl.deep
        count = sum(order.index(b) < order.index(bit) for b in self.have)
        return (1 << count) * (1 if bit in self.sl.high else self.lead)

    def side(self, bit):
        return jnp.zeros((1,), jnp.int32) if bit == self.sl.high[0] else mine(bit)[None]

    def cross(self):
        own, top, core, both = self.quarters
        top_other = self.sl.flip(both, CORE)
        core, _ = lax.optimization_barrier((core, top_other))
        core_other = self.sl.flip(core, CORE)
        rows, n = top.shape
        if not self.top_last:
            (send,) = call(
                add_low_kernel, [(top.shape, bf16)], [top, top_other], [VMEM] * 2, name="add_low"
            )
            self.quarters = [[own, core_other], send]
            return
        bit = self.steps[0][0]
        before = self.before(bit) // 2
        shape = (before, 2, rows // 2 // before, n)
        half = ((2, before, rows // 2 // before, n), bf16)
        keep, send = call(
            cross_split_kernel,
            [half, half],
            [self.side(bit), *(v.reshape(shape) for v in (own, core_other, top, top_other))],
            [SMEM] + [VMEM] * 4,
            name="cross_split",
        )
        self.quarters = [[keep.reshape(-1, n)], send.reshape(-1, n)]

    def split(self, other, bit):
        parts = [*self.quarters[0], other]
        if bit is None:
            self.value = sum(part.astype(f32) for part in parts)
            self.quarters = None
            return
        before = self.before(bit)
        rows, n = other.shape
        shape = (before, 2, rows // 2 // before, n)
        half = ((before, rows // 2 // before, n), bf16)
        keep, send = call(
            add_split_kernel,
            [half, half],
            [self.side(bit), *(part.reshape(shape) for part in parts)],
            [SMEM] + [VMEM] * len(parts),
            name="add_split",
        )
        self.quarters = [[keep.reshape(-1, n)], send.reshape(-1, n)]

    def start(self):
        bits = self.steps.pop(0)
        for n, bit in enumerate(bits):
            self.air = self.sl.flip(self.quarters[1], bit)
            self.have.remove(bit)
            if n < len(bits) - 1:
                self.split(self.air, bits[n + 1])
        self.next = self.steps[0][0] if self.steps else None

    def land(self):
        other, self.air = self.air, None
        self.split(other, self.next)


class Live:
    def __init__(self, **values):
        self.flows = []
        self.values = values

    def flow(self, made):
        self.flows.append(made)
        return made

    def __getattr__(self, name):
        return self.values[name]

    def put(self, **values):
        self.values.update(values)

    def drop(self, *names):
        for name in names:
            del self.values[name]

    def seal(self, *landing, keep=()):
        landing = [*keep, *landing]
        kept = (
            self.values,
            [(made.value, made.quarters) for made in self.flows],
            [made.air for made in landing],
        )
        self.values, flown, airs = lax.optimization_barrier(kept)
        for made, (made.value, made.quarters) in zip(self.flows, flown):
            pass
        for n, (made, made.air) in enumerate(zip(landing, airs)):
            if n >= len(keep):
                made.land()


def dot(left, right):
    return jnp.dot(left, right, preferred_element_type=f32)


def dot_t(left, right):
    return lax.dot_general(left, right, (((1,), (1,)), ((), ())), preferred_element_type=f32)


def t_dot(left, right):
    return lax.dot_general(left, right, (((0,), (0,)), ((), ())), preferred_element_type=f32)


def fetch(place, quarters, whole, lead, sems):
    width = whole.shape[1]
    block = whole.shape[0] // (4 * lead)
    copies = []
    for n, part in enumerate(quarters):
        top = place[0] if n % 2 == 0 else 1 - place[0]
        core = place[1] if n < 2 else 1 - place[1]
        for a in range(lead):
            at = pl.multiple_of(((top * lead + a) * 2 + core) * block, block)
            source = part.at[pl.ds(a * block, block), pl.ds(0, width)]
            copies.append(
                pltpu.make_async_copy(source, whole.at[pl.ds(at, block)], sems.at[n * lead + a])
            )
    for copy in copies:
        copy.start()
    return copies


def norm(hidden):
    centred = hidden - jnp.mean(hidden, axis=-1, keepdims=True)
    scale = lax.rsqrt(jnp.mean(centred * centred, axis=-1, keepdims=True) + 1e-05)
    return centred * scale, scale


def put_rows(outs, cols, value):
    rows = value.shape[0] // len(outs)
    for r, out in enumerate(outs):
        out[:, cols] = value[r * rows : (r + 1) * rows].astype(bf16)


def theirs(others, r, rows):
    if len(others) == 2:
        return others[1 - r][...].astype(f32)
    return others[0][pl.ds((1 - r) * rows, rows)].astype(f32)


def gains_at(gains, r, place, width):
    return gains[pl.ds(r, 1), pl.ds(place * width, width)]


def add_norm(which, parts, gains, total, out):
    base, *shares = parts
    rows, width = out.shape[0] // 2, out.shape[1]
    for r in range(2):
        block = pl.ds(r * rows, rows)
        value = base[block]
        if shares:
            value = value + (shares[0][block] + theirs(shares[1:], r, rows))
            total[block] = value
        gain, bias = [gains_at(gains, r, 2 * which + n, width) for n in range(2)]
        out[block] = (norm(value)[0] * gain + bias).astype(bf16)


def norm_back(which, d_out, keep, others, hidden, gains, total, low, d_gain, d_shift):
    rows, width = d_out.shape[0] // 2, d_out.shape[1]
    for r in range(2):
        block = pl.ds(r * rows, rows)
        grad = keep[block] + theirs(others, r, rows)
        normed, scale = norm(hidden[block])
        if r == 0:
            d_gain[...] = jnp.sum(grad * normed, axis=0, keepdims=True)
            d_shift[...] = jnp.sum(grad, axis=0, keepdims=True)
        e = grad * gains_at(gains, r, 2 * which, width)
        part = e - jnp.mean(e, axis=-1, keepdims=True)
        part = part - normed * jnp.mean(e * normed, axis=-1, keepdims=True)
        value = d_out[block] + scale * part
        total[block] = value
        low[block] = value.astype(bf16)


def norm_back_kernel(which, d_out, keep, *refs):
    norm_back(which, d_out, keep, refs[:-6], *refs[-6:])


def gains_kernel(lead, count, rows, place, pick, q0, q1, q2, q3, first, second, held, wide, sems):
    copies = []
    for n, part in enumerate((q0, q1, q2, q3)):
        source = part.at[:, pl.ds(part.shape[1] - 128, 128)]
        copies.append(pltpu.make_async_copy(source, held.at[n], sems.at[n]))
    for copy in copies:
        copy.start()
    for copy in copies:
        copy.wait()
    wide[...] = held[...].astype(f32)
    deep = wide.shape[1] // (lead * rows)
    for n in range(4):
        top = place[0] if n % 2 == 0 else 1 - place[0]
        core = place[1] if n < 2 else 1 - place[1]
        for a in range(lead):
            for z in range(deep):
                cols = pl.multiple_of((((top * lead + a) * 2 + core) * deep + z) * 128, 128)
                base = (a * deep + z) * rows
                for r in range(2):
                    first[pl.ds(r, 1), pl.ds(cols, 128)] = wide[n, pl.ds(base, 1)]
                    second[pl.ds(r, 1), pl.ds(cols, 128)] = wide[n, pl.ds(base + 1 + pick[r], 1)]


def score(q, k, allowed, size):
    scores = jnp.where(allowed, dot_t(q, k) * size, -1e30)
    exponent = jnp.exp(scores - jnp.max(scores, axis=-1, keepdims=True))
    return exponent / jnp.sum(exponent, axis=-1, keepdims=True)


def lanes_of(which, shape):
    lane = lax.broadcasted_iota(jnp.int32, shape, 1)
    return (lane < shape[1] // 2) if which == 0 else (lane >= shape[1] // 2)


def out_block(weight, k, block, at):
    count = weight.shape[0] // (2 * block)
    wide = weight.shape[1] - at
    return jnp.concatenate([weight[pl.ds((2 * h + k) * block, block), pl.ds(at, wide)] for h in range(count)], 0)


def attend_kernel(ways, size, lead, block, place, *refs):
    refs, (weight, sems) = refs[:-2], refs[-2:]
    refs, lows = refs[:-ways], refs[-ways:]
    *parts, gains, q0, q1, q2, q3, allow, total, f, qkv, mixed, keep = refs
    copies = fetch(place, (q0, q1, q2, q3), weight, lead, sems)
    add_norm(0, parts, gains, total, f)
    for copy in copies:
        copy.wait()
    length = allow.shape[-1]
    third = qkv.shape[1] // 3
    for n in range(3):
        cols = pl.ds(n * third, third)
        qkv[:, cols] = dot(f[...], weight[:, cols]).astype(bf16)

    def one_row(r, carry):
        at = pl.ds(pl.multiple_of(r * length, length), length)
        allowed = allow[r] > 0
        for p in range(third // 128):
            q = qkv[at, pl.ds(p * 128, 128)]
            k = qkv[at, pl.ds(third + p * 128, 128)]
            v = qkv[at, pl.ds(2 * third + p * 128, 128)]
            halves = []
            for h in range(2):
                probs = score(jnp.where(lanes_of(h, q.shape), q, 0), k, allowed, size)
                halves.append(dot(probs.astype(bf16), v))
            mixed[at, pl.ds(p * 128, 128)] = jnp.where(
                lanes_of(0, q.shape), halves[0], halves[1]
            ).astype(bf16)
        return carry

    lax.fori_loop(0, f.shape[0] // length, one_row, 0)
    for k in range(2):
        cols = pl.ds(k * third, third)
        value = dot(mixed[...], out_block(weight, k, block, 3 * third))
        keep[:, cols] = value
        put_rows(lows, cols, value)


def attend_back_kernel(ways, size, lead, block, grads, place, *refs):
    if grads:
        (first, mixed), refs = refs[:2], refs[2:]
    (d_out, part), refs = refs[:2], refs[2:]
    refs, (weight, d_mixed, sems) = refs[:-3], refs[-3:]
    if grads:
        refs, outs = refs[:-4], refs[-4:]
    refs, lows = refs[:-ways], refs[-ways:]
    *others, attended, gains, q0, q1, q2, q3, allow, qkv, total, d, d_gain, d_shift, d_qkv, keep = refs
    copies = fetch(place, (q0, q1, q2, q3), weight, lead, sems)
    norm_back(1, d_out, part, others, attended, gains, total, d, d_gain, d_shift)
    for copy in copies:
        copy.wait()
    length = allow.shape[-1]
    third = qkv.shape[1] // 3
    value = dot_t(d[:, pl.ds(0, third)], out_block(weight, 0, block, 3 * third))
    value = value + dot_t(d[:, pl.ds(third, third)], out_block(weight, 1, block, 3 * third))
    d_mixed[...] = value.astype(bf16)

    def one_row(r, carry):
        at = pl.ds(pl.multiple_of(r * length, length), length)
        allowed = allow[r] > 0
        for p in range(third // 128):
            q = qkv[at, pl.ds(p * 128, 128)]
            k = qkv[at, pl.ds(third + p * 128, 128)]
            v = qkv[at, pl.ds(2 * third + p * 128, 128)]
            dm = d_mixed[at, pl.ds(p * 128, 128)]
            d_q, d_k, d_v = [], [], []
            for h in range(2):
                pick = lanes_of(h, q.shape)
                probs = score(jnp.where(pick, q, 0), k, allowed, size)
                d_probs = dot_t(jnp.where(pick, dm, 0), v)
                d_v.append(t_dot(probs.astype(bf16), dm))
                inner = jnp.sum(probs * d_probs, axis=-1, keepdims=True)
                d_scores = (probs * (d_probs - inner)).astype(bf16)
                d_q.append(dot(d_scores, k))
                d_k.append(t_dot(d_scores, q))
            pick = lanes_of(0, q.shape)
            for n, (halves, scale) in enumerate(((d_q, size), (d_k, size), (d_v, 1.0))):
                value = jnp.where(pick, halves[0], halves[1]) * scale
                d_qkv[at, pl.ds(n * third + p * 128, 128)] = value.astype(bf16)
        return carry

    lax.fori_loop(0, d.shape[0] // length, one_row, 0)
    for n in range(keep.shape[1] // 256):
        cols = pl.ds(n * 256, 256)
        value = dot_t(d_qkv[...], weight[cols, pl.ds(0, 3 * third)])
        keep[:, cols] = value
        put_rows(lows, cols, value)
    if grads:
        attend_grad(lead, place, first, mixed, d_qkv, d, outs)


def up(f, weight, pre, active):
    for n in range(pre.shape[1] // 256):
        cols = pl.ds(n * 256, 256)
        value = dot(f[...], weight[:, cols])
        pre[:, cols] = value
        active[:, cols] = jax.nn.gelu(value).astype(bf16)


def down(active, weight, keep, lows):
    for n in range(keep.shape[1] // 256):
        cols = pl.ds(n * 256, 256)
        value = dot(active[...], weight[:, cols])
        keep[:, cols] = value
        put_rows(lows, cols, value)


def feed_kernel(ways, lead, up_place, dn_place, *refs):
    refs, (w_up, w_dn, up_sems, dn_sems) = refs[:-4], refs[-4:]
    refs, lows = refs[:-ways], refs[-ways:]
    *parts, gains, u0, u1, u2, u3, n0, n1, n2, n3, total, f, pre, active, keep = refs
    up_copies = fetch(up_place, (u0, u1, u2, u3), w_up, lead, up_sems)
    dn_copies = fetch(dn_place, (n0, n1, n2, n3), w_dn, lead // 2, dn_sems)
    add_norm(1, parts, gains, total, f)
    for copy in up_copies:
        copy.wait()
    up(f, w_up, pre, active)
    for copy in dn_copies:
        copy.wait()
    down(active, w_dn, keep, lows)


def down_kernel(lead, place, active, q0, q1, q2, q3, keep, low, weight, sems):
    for copy in fetch(place, (q0, q1, q2, q3), weight, lead, sems):
        copy.wait()
    down(active, weight, keep, (low,))


def gelu_slope(x):
    c = 0.7978845608028654
    t = jnp.tanh(c * (x + 0.044715 * (x * x * x)))
    return 0.5 * (1.0 + t) + 0.5 * x * (1.0 - t * t) * (c * (1.0 + 3 * 0.044715 * (x * x)))


def feed_back(d, pre, w_up, w_dn, d_pre, keep, lows):
    for n in range(pre.shape[1] // 256):
        cols = pl.ds(n * 256, 256)
        d_pre[:, cols] = (gelu_slope(pre[:, cols]) * dot_t(d[...], w_dn[cols])).astype(bf16)
    for n in range(keep.shape[1] // 256):
        cols = pl.ds(n * 256, 256)
        value = dot_t(d_pre[...], w_up[cols])
        keep[:, cols] = value
        put_rows(lows, cols, value)


def feed_back_kernel(ways, lead, up_place, dn_place, d_out, part, *refs):
    refs, (w_up, w_dn, up_sems, dn_sems) = refs[:-4], refs[-4:]
    refs, lows = refs[:-ways], refs[-ways:]
    *others, hidden, gains, pre, u0, u1, u2, u3, n0, n1, n2, n3, total, d, d_gain, d_shift, d_pre, keep = refs
    copies = fetch(dn_place, (n0, n1, n2, n3), w_dn, lead // 2, dn_sems)
    copies += fetch(up_place, (u0, u1, u2, u3), w_up, lead, up_sems)
    norm_back(0, d_out, part, others, hidden, gains, total, d, d_gain, d_shift)
    for copy in copies:
        copy.wait()
    feed_back(d, pre, w_up, w_dn, d_pre, keep, lows)


def feed_turn_kernel(ways, lead, grads, place, up_place, dn_place, *refs):
    refs, (w_up, w_dn, pre, up_sems, dn_sems) = refs[:-5], refs[-5:]
    if grads:
        refs, up_outs, dn_outs = refs[:-8], refs[-8:-4], refs[-4:]
    refs, lows = refs[:-ways], refs[-ways:]
    *parts, gains, d, u0, u1, u2, u3, n0, n1, n2, n3, total, f, active, d_pre, keep = refs
    up_copies = fetch(up_place, (u0, u1, u2, u3), w_up, lead, up_sems)
    dn_copies = fetch(dn_place, (n0, n1, n2, n3), w_dn, lead // 2, dn_sems)
    add_norm(1, parts, gains, total, f)
    for copy in up_copies:
        copy.wait()
    up(f, w_up, pre, active)
    for copy in dn_copies:
        copy.wait()
    feed_back(d, pre, w_up, w_dn, d_pre, keep, lows)
    if grads:
        weight_grad(lead, place, f, d_pre, up_outs)
        weight_grad(lead // 2, place, active, d, dn_outs)


def columns_of(place, value, lead):
    block = value.shape[1] // (4 * lead)
    parts = []
    for n in range(4):
        top = place[0] if n % 2 == 0 else 1 - place[0]
        core = place[1] if n < 2 else 1 - place[1]
        starts = [((top * lead + a) * 2 + core) * block for a in range(lead)]
        if block % 128 == 0:
            starts = [pl.multiple_of(at, 128) for at in starts]
        parts.append(jnp.concatenate([value[:, pl.ds(at, block)] for at in starts], 1))
    return parts


def weight_grad(lead, place, left, right, outs):
    for part, out in zip(columns_of(place, left, lead), outs):
        out[...] = t_dot(part, right[...]).astype(bf16)


def weight_grad_kernel(lead, aligned, place, left, right, *outs):
    weight_grad(lead, place if aligned else (0, 0), left, right, outs)


def attend_grad_kernel(lead, aligned, place, left, mixed, d_qkv, d, *outs):
    attend_grad(lead, place if aligned else (0, 0), left, mixed, d_qkv, d, outs)


def attend_grad(lead, place, left, mixed, d_qkv, d, outs):
    width = d_qkv.shape[1]
    third = width // 3
    block = left.shape[1] // (4 * lead)
    lefts, inners = columns_of(place, left, lead), columns_of(place, mixed, lead // 2)
    for part, inner, out in zip(lefts, inners, outs):
        out[:, pl.ds(0, width)] = t_dot(part, d_qkv[...]).astype(bf16)
        value = t_dot(inner, d[...]).astype(bf16)
        for h in range(inner.shape[1] // block):
            for k in range(2):
                out[pl.ds((2 * h + k) * block, block), pl.ds(width, third)] = value[
                    h * block : (h + 1) * block, k * third : (k + 1) * third
                ]


def turn(sl, value, lead):
    tokens, width = value.shape
    value = value.reshape(tokens, 2, lead, 2, width // (4 * lead))
    value = jnp.stack(split(value, sl.high[0], 1), 1)
    return jnp.stack(split(value, CORE, 3), 3).reshape(tokens, width)


def finish_kernel(span, side, keep, other, out, m, v, *refs):
    third = out.shape[-1]
    place_sides([(keep, other, 0, 0, 3 * third, span)], side, refs[-3])
    for k in range(2):
        refs[-3][0, :, pl.ds((6 + k) * third, third)] = out[k]
    adam_columns(m, v, *refs[-3:])


def finish_up_kernel(chunk, first, side, keep, other, *refs):
    grad = refs[-3]
    late = grad.shape[-1] // 2 - (keep.shape[1] - first)
    pieces = [(keep, other, first, late, keep.shape[1] - first, chunk)]
    if late:
        pieces.append((refs[0], refs[1], 0, 0, late, chunk))
    place_sides(pieces, side, grad)
    m, v = refs[2:4] if late else refs[:2]
    adam_columns(m, v, *refs[-3:])


def place_sides(pieces, side, grad):
    for one, two, first, start, count, width in pieces:
        each = math.gcd(math.gcd(width, start), count)
        for source, x in ((one, side[0]), (two, 1 - side[0])):
            for n in range(count // each):
                block, inside = divmod(start + n * each, width)
                at = pl.multiple_of((2 * block + x) * width + inside, 128)
                grad[0, :, pl.ds(at, each)] = source[:, pl.ds(first + n * each, each)]


def adam_columns(m, v, grad, new_m, step):
    for n in range(grad.shape[2] // 1024):
        cols = pl.ds(n * 1024, 1024)
        new_m[0, :, cols], step[0, :, cols] = adam_update(m[0, :, cols], v[0, :, cols], grad[0, :, cols])


def finish_down_kernel(value, m, v, *refs):
    grad, new_m, step = refs[-3:]
    grad[0] = value[...]
    new_m[0], step[0] = adam_update(m[0], v[0], value[...])


def update(kernel, layer, shape, parts, specs, moments, before, name, half=None):
    wide = shape[2] if half is None else shape[2] // 2
    one = pl.BlockSpec((1, shape[1], wide), lambda i: (layer, 0, half or 0))
    count = len(parts) + 2
    return pl.pallas_call(
        kernel,
        grid=(1,),
        out_shape=[jax.ShapeDtypeStruct(shape, f32)] * 3,
        in_specs=[*specs, one, one, *len(before) * [ANY]],
        out_specs=[one] * 3,
        input_output_aliases={count + n: n for n in range(len(before))},
        compiler_params=pltpu.CompilerParams(vmem_limit_bytes=20 << 20),
        name=name,
    )(*parts, *moments, *before)


def adam_update(moment, square, gradient):
    moment = beta_one * moment + (1.0 - beta_one) * gradient
    square = beta_two * square + (1.0 - beta_two) * gradient * gradient
    update = moment / first_fix / (jnp.sqrt(square / second_fix) + 1e-08)
    return (moment, update)


def dma(count):
    return pltpu.SemaphoreType.DMA((count,))


def body(
    dp,
    fsdp,
    inputs,
    cotangent,
    segment_ids,
    section_ids,
    w_big,
    w_down,
    norm_table,
    m_big,
    m_down,
    m_table,
    v_big,
    v_down,
    v_table,
):
    sl = Slice(dp, fsdp)
    length, width = inputs.shape[1:]
    rows = w_big.shape[1]
    feeds = w_down.shape[1]
    feed = w_big.shape[2] - 4 * width
    high = dp // 4
    lead = high
    half, part = width // 2, 3 * width // 2
    block = fsdp * rows
    count = norm_table.shape[0]
    size = (width // HEADS) ** -0.5
    two_f, two_b = ((2 * length, width), f32), ((2 * length, width), bf16)
    wide_b = ((2 * length, feed // 2), bf16)

    def lows(ways):
        return ways * [((2 // ways * length, width), bf16)]

    quarter = ((width // 4, 2 * width), bf16)
    gain_row = ((1, width), f32)
    up_first = feed // 2 - feed // 8
    place = jnp.stack([mine(sl.high[0]), mine(CORE)])
    w_attn = pltpu.VMEM((width, 2 * width), bf16)
    w_upper = pltpu.VMEM((width, feed // 2), bf16)
    w_lower = pltpu.VMEM((feed // 2, width), bf16)

    def qkv_sides(layer):
        value = w_big[layer, :, : 3 * width].reshape(rows, 3, high, 2, 2 * block)
        return [v.reshape(rows, part) for v in split(value, SIDE, 3)]

    def up_sides(layer):
        value = w_big[layer, :, 4 * width :].reshape(rows, high, 2, 2 * fsdp * feeds)
        return [v.reshape(rows, feed // 2) for v in split(value, SIDE, 2)]

    def prepare(table_part):
        shapes = 2 * [(rows, part + 128)] + 2 * [(rows, feed // 2)] + 2 * [(rows, part + feed // 2)]
        shapes.append((2, 2, rows, half))
        if rows % 16 == 0:
            return call(
                partial(prepare_kernel, 2 * block, 2 * fsdp * feeds),
                [(shape, bf16) for shape in shapes],
                [mine(SIDE)[None], w_big, table_part],
                [SMEM, ANY, ANY],
                [dma(2 * (2 * 3 * high + 2 * high + 2) + 2)],
                name="prepare",
            )
        first = [jnp.concatenate([v, table_part], -1) for v in qkv_sides(0)]
        after = [jnp.concatenate([a, b], -1) for a, b in zip(qkv_sides(1), up_sides(1))]
        out = w_big[:, :, 3 * width : 4 * width].reshape(2, rows, 2, half)
        return [*first, *up_sides(0), *after, jnp.swapaxes(out, 1, 2)]

    def place_sides(kernel, shape, keep, other, out, name):
        return call(
            kernel,
            [(shape, bf16)],
            [mine(SIDE)[None], keep, other, out],
            [SMEM, VMEM, VMEM, VMEM],
            name=name,
        )[0]

    live = Live()
    downs = [live.flow(Gather(sl, w_down[n], 1, n == 1)) for n in range(2)]

    downs[0].start()
    downs[1].start()
    table_part = norm_table.reshape(-1)
    table_part = jnp.pad(table_part, (0, rows * 128 - table_part.shape[0])).reshape(rows, 128)
    first, first_sent, up0, up0_sent, after, after_sent, out_proj = prepare(table_part)
    live.put(
        first=[first, sl.flip(first_sent, SIDE)],
        up=[up0, up0_sent],
        after=[after, after_sent],
        out=out_proj,
    )
    live.seal(downs[0], downs[1])

    own = place_sides(
        place_first_kernel, (2, rows, 2 * width + 128), *live.first, live.out[0], "place_first"
    )
    attns = [live.flow(Gather(sl, own.reshape(2 * rows, -1), 2))]
    attns[0].start()
    downs[0].start()
    extra = jnp.zeros((16, width), bf16)
    extra = extra.at[0, :length].set(segment_ids[0].astype(bf16))
    extra = extra.at[1, 0].set(section_ids[0].astype(bf16))
    pack = jnp.concatenate([inputs[0], cotangent[0], extra], 0)
    live.put(
        up=[live.up[0], sl.flip(live.up[1], SIDE)],
        after=[live.after[0], sl.flip(live.after[1], SIDE)],
        pack=[pack, sl.flip(pack, SIDE)],
    )
    live.drop("first")
    live.seal(attns[0], downs[0])

    ups = [live.flow(Gather(sl, interleave(live.up[:1], live.up[1:], SIDE, 1)[0], 2))]
    downs[0].start()
    attns[0].start()
    ups[0].start()
    own = place_sides(
        place_next_kernel, (4, rows, 2 * width), *live.after, live.out[1], "place_next"
    )
    live.put(own=own)
    live.drop("up", "after", "out")
    packed = jnp.stack(live.pack)
    extras = packed[:, 2 * length :]
    segments = extras[:, 0, :length].astype(f32)
    same = segments[:, :, None] == segments[:, None, :]
    position = jnp.arange(length)
    live.put(
        hidden=packed[:, :length].reshape(2 * length, width).astype(f32),
        d_low=packed[:, length : 2 * length].reshape(2 * length, width),
        sections=extras[:, 1, 0].astype(jnp.int32),
        allows=[
            (same & (position[:, None] >= position[None, :])).astype(f32),
            same.astype(f32),
        ],
    )
    live.drop("pack")
    live.seal(attns[0], ups[0], downs[0])

    own = live.own.reshape(2, 2 * rows, -1)
    attns.append(live.flow(Gather(sl, own[0], 2)))
    ups.append(live.flow(Gather(sl, own[1], 2)))
    live.drop("own")
    attns[0].start()
    attns[1].start()
    ups[0].start()
    downs[0].finish()
    live.seal(attns[0], ups[0], attns[1])

    def after(made, value):
        (keep, send), _ = lax.optimization_barrier((made.quarters, value))
        made.quarters = [keep, send]

    def gate(*made):
        airs = [flow.air for flow in made]
        other, airs = lax.optimization_barrier((live.other, airs))
        live.put(other=other)
        for flow, flow.air in zip(made, airs):
            pass

    def gains_of(flow, sections):
        wide = norm_table.shape[1]
        if wide == 128:
            return call(
                partial(gains_kernel, lead, count, rows),
                2 * [((2, 4 * width), f32)],
                [place, sections, *pinned(flow)],
                [SMEM, SMEM] + [ANY] * 4,
                [
                    pltpu.VMEM((4, width // 4, 128), bf16),
                    pltpu.VMEM((4, width // 4, 128), f32),
                    dma(4),
                ],
                name="gains",
            )
        parts = jnp.stack([q[:, 2 * width :] for q in flow.quarters])
        parts = parts.reshape(4, lead // 2, 2, fsdp, rows * 128)[..., : count * wide]
        parts = parts.reshape(4, lead // 2, 2, fsdp, count, wide)
        pick = jnp.concatenate([jnp.zeros((2,), jnp.int32), 1 + sections])
        pick = (pick[:, None] == jnp.arange(count)[None, :]).astype(bf16)
        picked = jnp.einsum("sr,qhxdrj->qshxdj", pick, parts, preferred_element_type=f32)
        own, top, core, both = picked
        both = merge(merge(own, core, CORE, 3), merge(top, both, CORE, 3), sl.high[0], 1)
        return list(both.reshape(2, 2, 4 * width))

    def pinned(flow):
        own, top, core, both = flow.quarters
        if flow is downs[0]:
            both = pltpu.with_memory_space_constraint(both, pltpu.HBM)
        return [own, top, pltpu.with_memory_space_constraint(core, pltpu.HBM), both]

    def cross():
        live.put(other=[sl.flip(row, SIDE) for row in live.low])

    def shares():
        return [live.keep, *live.other]

    def attend(layer, base, ways=2):
        parts = [base] if layer == 0 else [base, *shares()]
        total, first, qkv, mixed, keep, *low = call(
            partial(attend_kernel, ways, size, lead, 2 * block),
            [two_f, two_b, ((2 * length, part), bf16), ((2 * length, half), bf16), two_f, *lows(ways)],
            [
                attns[layer].place,
                *parts,
                live.gains[layer],
                *pinned(attns[layer]),
                live.allows[layer],
            ],
            [SMEM] + [VMEM] * (len(parts) + 1) + [ANY] * 4 + [VMEM],
            [w_attn, dma(4 * lead)],
            name="attend",
        )
        hidden = base if layer == 0 else total
        live.put(**{f"attn{layer}": (hidden, first, qkv, mixed)}, keep=keep, low=low)

    def feed_forward(layer, ways=2):
        attended, second, pre, active, keep, *low = call(
            partial(feed_kernel, ways, lead),
            [two_f, two_b, (wide_b[0], f32), wide_b, two_f, *lows(ways)],
            [
                ups[layer].place,
                downs[layer].place,
                live.values[f"attn{layer}"][0],
                *shares(),
                live.gains[layer],
                *pinned(ups[layer]),
                *pinned(downs[layer]),
            ],
            [SMEM, SMEM] + [VMEM] * (3 + len(live.other)) + [ANY] * 8,
            [w_upper, w_lower, dma(4 * lead), dma(2 * lead)],
            name="feed",
        )
        live.put(**{f"feed{layer}": (attended, second, pre, active)}, keep=keep, low=low)

    def feed_turn(layer, ways=2):
        grads = False
        quarters = 4 * [quarter] + 4 * [((feed // 8, width), bf16)]
        attended, second, active, d_pre, keep, *low = call(
            partial(feed_turn_kernel, ways, lead, grads),
            [two_f, two_b, wide_b, wide_b, two_f, *lows(ways), *(quarters if grads else [])],
            [
                place,
                ups[layer].place,
                downs[layer].place,
                live.values[f"attn{layer}"][0],
                *shares(),
                live.gains[layer],
                live.d_low,
                *pinned(ups[layer]),
                *pinned(downs[layer]),
            ],
            [SMEM] * 3 + [VMEM] * (4 + len(live.other)) + [ANY] * 8,
            [w_upper, w_lower, pltpu.VMEM(wide_b[0], f32), dma(4 * lead), dma(2 * lead)],
            name="feed_turn",
        )
        live.put(**{f"feed{layer}": (attended, second, None, active)}, d_pre=d_pre, keep=keep, low=low)

    def feed_down(layer):
        keep, *low = call(
            partial(down_kernel, lead // 2),
            [two_f, *lows(1)],
            [downs[layer].place, live.values[f"feed{layer}"][3], *pinned(downs[layer])],
            [SMEM, VMEM, ANY, ANY, ANY, ANY],
            [w_lower, dma(2 * lead)],
            name="down",
        )
        live.put(keep=keep, low=low)

    def feed_back(layer, ways=1):
        grad, d_low, d_gain, d_shift, d_pre, keep, *low = call(
            partial(feed_back_kernel, ways, lead),
            [two_f, two_b, gain_row, gain_row, wide_b, two_f, *lows(ways)],
            [
                ups[layer].place,
                downs[layer].place,
                live.grad,
                *shares(),
                live.values[f"attn{layer + 1}"][0],
                live.gains[layer + 1],
                live.values[f"feed{layer}"][2],
                *pinned(ups[layer]),
                *pinned(downs[layer]),
            ],
            [SMEM, SMEM] + [VMEM] * (5 + len(live.other)) + [ANY] * 8,
            [w_upper, w_lower, dma(4 * lead), dma(2 * lead)],
            name="feed_back",
        )
        live.put(grad=grad, d_low=d_low, d_pre=d_pre, keep=keep, low=low)
        live.put(**{f"gains{layer + 1}0": jnp.concatenate([d_gain, d_shift], 1)})

    def down_grad(layer, top_last=False):
        aligned = feed // 4 // lead % 128 == 0
        active = live.values[f"feed{layer}"][3]
        parts = call(
            partial(weight_grad_kernel, lead // 2, aligned),
            [((feed // 8, width), bf16)] * 4,
            [place, active if aligned else turn(sl, active, lead // 2), live.d_low],
            [SMEM, VMEM, VMEM],
            name="down_grad",
        )
        return live.flow(Scatter(sl, parts, 1, top_last))

    def up_grad(layer, piece=None):
        aligned = block % 128 == 0
        second, right = live.values[f"feed{layer}"][1], live.d_pre
        columns = feed // 2
        if piece is not None:
            right = right[:, :up_first] if piece == 0 else right[:, up_first:]
            columns = right.shape[1]
        parts = call(
            partial(weight_grad_kernel, lead, aligned),
            [((width // 4, columns), bf16)] * 4,
            [place, second if aligned else turn(sl, second, lead), right],
            [SMEM, VMEM, VMEM],
            name="up_grad",
        )
        return live.flow(Scatter(sl, parts, 2, piece == 1))

    def norm_back(which, layer, hidden):
        grad, d_low, d_gain, d_shift = call(
            partial(norm_back_kernel, which),
            [two_f, two_b, gain_row, gain_row],
            [live.grad, *shares(), hidden, live.gains[layer]],
            [VMEM] * (4 + len(live.other)),
            name="norm_back",
        )
        live.put(grad=grad, d_low=d_low)
        live.put(**{f"gains{layer}{which}": jnp.concatenate([d_gain, d_shift], 1)})

    def attend_back(layer, ways=1):
        grads = block % 128 == 0
        hidden, first, qkv, mixed = live.values[f"attn{layer}"]
        grad, d_low, d_gain, d_shift, d_qkv, keep, *low = call(
            partial(attend_back_kernel, ways, size, lead, 2 * block, grads),
            [
                *(two_f, two_b, gain_row, gain_row, ((2 * length, part), bf16), two_f, *lows(ways)),
                *(4 * [quarter] if grads else []),
            ],
            [
                attns[layer].place,
                *([first, mixed] if grads else []),
                live.grad,
                *shares(),
                live.values[f"feed{layer}"][0],
                live.gains[layer],
                *pinned(attns[layer]),
                live.allows[layer],
                live.values[f"attn{layer}"][2],
            ],
            [SMEM] + [VMEM] * (4 + 2 * grads + len(live.other)) + [ANY] * 4 + [VMEM] * 2,
            [w_attn, pltpu.VMEM((2 * length, half), bf16), dma(4 * lead)],
            name="attend_back",
        )
        low, made = low[:ways], low[ways:]
        live.put(grad=grad, d_low=d_low, d_qkv=d_qkv, keep=keep, low=low)
        live.put(**{f"gains{layer}1": jnp.concatenate([d_gain, d_shift], 1)})
        return live.flow(Scatter(sl, made, 2)) if grads else attend_grad(layer)

    def attend_grad(layer):
        hidden, first, qkv, mixed = live.values[f"attn{layer}"]
        aligned = block % 128 == 0
        if not aligned:
            first, mixed = turn(sl, first, lead), turn(sl, mixed, lead // 2)
        parts = call(
            partial(attend_grad_kernel, lead, aligned),
            [quarter] * 4,
            [place, first, mixed, live.d_qkv, live.d_low],
            [SMEM] + [VMEM] * 4,
            name="attend_grad",
        )
        return live.flow(Scatter(sl, parts, 2))

    def two_sides(flows, wides, counts):
        values = [flow.value.reshape(2, rows, wide) for flow, wide in zip(flows, wides)]
        both = jnp.concatenate([v[..., :n] for v, n in zip(values, counts)], -1)
        keep, send = split(both, SIDE, 0)
        return keep, sl.flip(send, SIDE), values[0][..., counts[0] :]

    def finish(layer, big, before, more=None):
        keep, other, out = big
        side = mine(SIDE)[None]
        before = update(
            partial(finish_kernel, 2 * block),
            layer,
            w_big.shape,
            [side, keep, other, out],
            [SMEM, VMEM, VMEM, VMEM],
            [m_big, v_big],
            before,
            "finish",
            0,
        )
        more = [] if more is None else list(more[:2])
        return update(
            partial(finish_up_kernel, 2 * fsdp * feeds, part),
            layer,
            w_big.shape,
            [side, keep, other, *more],
            [SMEM] + [VMEM] * (2 + len(more)),
            [m_big, v_big],
            before,
            "finish_up",
            1,
        )

    def finish_down(layer, flow, before):
        return update(
            finish_down_kernel,
            layer,
            w_down.shape,
            [flow.value],
            [VMEM],
            [m_down, v_down],
            before,
            "finish_down",
        )

    def table_terms():
        first, second = [
            jnp.concatenate([live.values[f"gains{n}0"], live.values[f"gains{n}1"]], 1) for n in range(2)
        ]
        hit = jnp.arange(count - 1) == section_ids[0]
        terms = jnp.concatenate([first, jnp.where(hit[:, None], second, 0.0)], 0)
        terms = terms.reshape(count, high, 2, 2, fsdp, norm_table.shape[1])
        return jnp.moveaxis(terms, 0, 4)

    def table_step(pos, bits):
        value = live.table
        for bit in bits:
            keep, send = split(value, bit, pos)
            value = keep + sl.flip(send, bit)
        live.put(table=value)

    ups[0].start()
    attns[1].start()
    ups[1].start()
    attns[0].finish()
    live.put(gains=gains_of(attns[0], live.sections))
    attend(0, live.hidden, 1)
    cross()
    live.seal(ups[0], attns[1], ups[1])

    attns[1].start()
    ups[1].start()
    downs[1].start()
    ups[0].finish()
    feed_forward(0, 1)
    cross()
    live.seal(attns[1], ups[1], downs[1])

    ups[1].start()
    downs[1].start()
    attns[1].finish()
    attend(1, live.feed0[0])
    cross()
    live.seal(ups[1], downs[1])

    ups[1].finish()
    downs[1].finish()
    live.put(grad=live.d_low.astype(f32))
    feed_turn(1)
    live.seal()

    cross()
    g_up1 = up_grad(1)
    g_up1.cross()
    g_up1.start()
    g_down1 = down_grad(1, True)
    g_down1.cross()
    g_down1.start()
    g_attn1 = attend_back(1)
    live.seal(g_down1, g_up1)

    g_down1.start()
    g_up1.start()
    g_attn1.cross()
    g_attn1.start()
    cross()
    feed_back(0)
    g_down0, g_up0b, g_up0a = down_grad(0), up_grad(0, 1), up_grad(0, 0)
    live.seal(g_down1, g_up1, g_attn1)

    cross()
    g_down0.cross()
    g_down0.start()
    g_up0b.cross()
    g_up0b.start()
    g_up0a.cross()
    after(g_up1, g_down0.quarters[0][1])
    g_up1.start()
    g_attn1.start()
    g_attn0 = attend_back(0)
    live.seal(g_down0, g_up1, g_attn1, g_up0b)

    cross()
    g_attn0.cross()
    g_attn0.start()
    g_up0b.start()
    g_down0.start()
    after(g_attn1, g_attn0.quarters[0][1])
    g_attn1.start()
    norm_back(0, 0, live.attn0[0])
    live.seal(g_attn0, g_attn1, g_down0, g_up0b)

    g_up0a.start()
    after(g_down0, g_attn0.quarters[1])
    (g_attn1.value, g_up1.value), g_attn0.quarters[1] = lax.optimization_barrier(
        ((g_attn1.value, g_up1.value), g_attn0.quarters[1])
    )
    g_attn0.start()
    g_down0.start()
    g_up0b.start()
    feed_down(1)
    big1 = two_sides([g_attn1, g_up1], [2 * width, feed // 2], [part, feed // 2])
    live.put(big=finish(1, big1, []))
    live.put(table=table_terms())
    table_step(2, [CORE])
    live.seal(g_up0a, g_attn0, g_down0, g_up0b)

    g_up0a.start()
    g_attn0.start()
    g_down1.start()
    cross()
    table_step(1, [SIDE])
    table = live.table.reshape(*(len(sl.high) + len(sl.deep)) * [2], count, -1)
    live.put(table=table, down=finish_down(0, g_down0, []))
    live.seal(g_up0a, g_attn0, g_down1)

    g_up0a.start()
    out_act = live.feed1[0][:length] + (live.keep[:length] + live.other[0][length:].astype(f32))
    rest = feed // 2 - up_first
    big0 = two_sides([g_attn0, g_up0b], [2 * width, rest], [part, rest])
    table_step(0, sl.high)
    table_step(-3, sl.deep[-1:])
    live.put(out_act=out_act.astype(bf16), down=finish_down(1, g_down1, live.down), big0=big0)
    live.seal(g_up0a)

    table_step(0, sl.deep[:-1])
    up0a = two_sides([g_up0a], [up_first], [up_first])
    grad_big, new_m_big, step_big = finish(0, live.big0, live.big, up0a)
    grad_down, new_m_down, step_down = live.down
    grad_table = live.table
    new_m_table, step_table = adam_update(m_table, v_table, grad_table)
    return (
        live.out_act[None],
        live.d_low[:length][None],
        grad_big,
        grad_down,
        grad_table,
        new_m_big,
        new_m_down,
        new_m_table,
        step_big,
        step_down,
        step_table,
    )


def solution(mesh):
    both = ("dp", "fsdp")
    rows, middle, last = P(both, None, None), P(None, both, None), P(None, both)
    return jax.shard_map(
        partial(body, mesh.shape["dp"], mesh.shape["fsdp"]),
        mesh=mesh,
        in_specs=(rows, rows, P(both, None), P(both), middle, middle, last)
        + 2 * (middle, middle, last),
        out_specs=(rows, rows) + 3 * (middle, middle, last),
        check_vma=False,
    )
```

```python
import itertools
import math
from functools import partial

import jax
import jax.numpy as jnp
from jax import lax
from jax.experimental import pallas as pl
from jax.experimental.pallas import tpu as pltpu
from jax.sharding import PartitionSpec as P

HEADS = 16

beta_one = 0.9
beta_two = 0.999
first_fix = 1.0 - 0.9**10
second_fix = 1.0 - 0.999**10

f32 = jnp.float32
bf16 = jnp.bfloat16

VMEM = pl.BlockSpec(memory_space=pltpu.VMEM)
SMEM = pl.BlockSpec(memory_space=pltpu.SMEM)
ANY = pl.BlockSpec(memory_space=pl.ANY)

CORE = ("dp", 1)
SIDE = ("dp", 2)


def masks(size):
    return [1 << k for k in reversed(range(size.bit_length() - 1))]


class Slice:
    def __init__(self, dp, fsdp):
        self.high = [("dp", m) for m in masks(dp) if m > 2]
        self.deep = [("fsdp", m) for m in masks(fsdp)]
        self.size = {"dp": dp, "fsdp": fsdp}

    def flip(self, value, bit):
        axis, mask = bit
        return lax.ppermute(value, axis, [(i, i ^ mask) for i in range(self.size[axis])])


def mine(bit):
    axis, mask = bit
    return (lax.axis_index(axis) // mask) % 2


def call(kernel, outs, operands, specs, scratch=(), flops=0, name=None):
    held = [(v.shape, v.dtype) for v, spec in zip(operands, specs) if spec is VMEM] + list(outs)
    held += [(s.shape, s.dtype) for s in scratch if hasattr(s, "memory_space") and s.memory_space == pltpu.VMEM]
    held = sum(math.prod(shape) * jnp.dtype(kind).itemsize for shape, kind in held)
    return pl.pallas_call(
        kernel,
        out_shape=[jax.ShapeDtypeStruct(shape, kind) for shape, kind in outs],
        in_specs=specs,
        out_specs=[VMEM] * len(outs),
        scratch_shapes=list(scratch),
        compiler_params=pltpu.CompilerParams(vmem_limit_bytes=held + (3 << 20)),
        name=name,
    )(*operands)


def merge(own, other, bit, pos):
    side = mine(bit)
    return jnp.where(side == 0, jnp.stack([own, other], pos), jnp.stack([other, own], pos))


def split(value, bit, pos):
    side = mine(bit)
    keep = lax.dynamic_index_in_dim(value, side, pos, keepdims=False)
    send = lax.dynamic_index_in_dim(value, 1 - side, pos, keepdims=False)
    return keep, send


def interleave_kernel(count, side, *refs):
    owns, others, outs = refs[:count], refs[count : 2 * count], refs[2 * count :]
    each = count * owns[0].shape[0] // len(outs)
    for n, (own, other) in enumerate(zip(owns, others)):
        for m in range(own.shape[0]):
            out, at = outs[(n * own.shape[0] + m) // each], (n * own.shape[0] + m) % each
            out[pl.ds(at, 1), pl.ds(side[0], 1)] = own[pl.ds(m, 1)][:, None]
            out[pl.ds(at, 1), pl.ds(1 - side[0], 1)] = other[pl.ds(m, 1)][:, None]


def interleave(owns, others, bit, before, outs=1):
    rows, n = owns[0].shape
    count = len(owns)
    shape = (before, rows // before, n)
    whole = (count * before // outs, 2, rows // before, n)
    result = call(
        partial(interleave_kernel, count),
        outs * [(whole, owns[0].dtype)],
        [mine(bit)[None], *(v.reshape(shape) for v in (*owns, *others))],
        [SMEM] + [VMEM] * (2 * count),
        name="interleave",
    )
    return [part.reshape(-1, n) for part in result]


def prepare_kernel(span, chunk, side, big, table, first, first_sent, up0, up0_sent, after, after_sent, out, sems):
    width = out.shape[-1] * 2
    third = 3 * width
    copies = []
    for layer, qkv, up in ((0, (first, first_sent), (up0, up0_sent)), (1, (after, after_sent), (after, after_sent))):
        for x, target, upper in ((side[0], qkv[0], up[0]), (1 - side[0], qkv[1], up[1])):
            for n in range(third // (2 * span)):
                at = pl.multiple_of((2 * n + x) * span, 128)
                copies.append((big.at[layer, :, pl.ds(at, span)], target.at[:, pl.ds(n * span, span)]))
            base = 0 if layer == 0 else third // 2
            for n in range(up0.shape[1] // chunk):
                at = pl.multiple_of(4 * width + (2 * n + x) * chunk, 128)
                copies.append((big.at[layer, :, pl.ds(at, chunk)], upper.at[:, pl.ds(base + n * chunk, chunk)]))
        for k in range(2):
            copies.append((big.at[layer, :, pl.ds(third + k * width // 2, width // 2)], out.at[layer, k]))
    for target in (first, first_sent):
        copies.append((table, target.at[:, pl.ds(third // 2, 128)]))
    copies = [pltpu.make_async_copy(a, b, sems.at[n]) for n, (a, b) in enumerate(copies)]
    for copy in copies:
        copy.start()
    for copy in copies:
        copy.wait()


def place_first_kernel(side, keep, other, out, own):
    part = keep.shape[1] - 128
    wide = out.shape[-1]
    for source, x in ((keep, side[0]), (other, 1 - side[0])):
        own[pl.ds(x, 1), :, pl.ds(0, part)] = source[:, pl.ds(0, part)][None]
        own[pl.ds(x, 1), :, pl.ds(part + wide, 128)] = source[:, pl.ds(part, 128)][None]
    own[:, :, pl.ds(part, wide)] = out[...]


def place_next_kernel(side, keep, other, out, own):
    wide = out.shape[-1]
    part = 3 * wide
    for source, x in ((keep, side[0]), (other, 1 - side[0])):
        own[pl.ds(x, 1), :, pl.ds(0, part)] = source[:, pl.ds(0, part)][None]
        own[pl.ds(2 + x, 1)] = source[:, pl.ds(part, part + wide)][None]
    own[pl.ds(0, 2), :, pl.ds(part, wide)] = out[...]


class Gather:
    def __init__(self, sl, own, lead, top_first=False, twins=False):
        self.sl, self.value, self.lead, self.top_first, self.twins = sl, own, lead, top_first, twins
        self.have, self.air, self.quarters = [], None, None
        near = sl.high[:0:-1]
        if top_first:
            self.steps = [sl.high[:1], near + sl.deep[:-1], sl.deep[-1:]]
        else:
            self.steps = [sl.deep[:-1], sl.deep[-1:] + near]
        core = mine(CORE)
        self.place = jnp.stack([jnp.zeros_like(core) if top_first else mine(sl.high[0]), core])

    def before(self, bit):
        order = self.sl.high + self.sl.deep
        count = sum(order.index(b) < order.index(bit) for b in self.have)
        return (1 + self.twins) * (1 << count) * (1 if bit in self.sl.high else self.lead)

    def start(self):
        if not self.steps:
            self.air = self.sl.flip(self.value, self.sl.high[0]), self.sl.flip(self.value, CORE)
            return
        *others, self.bit = self.steps.pop(0)
        for bit in others:
            other = self.sl.flip(self.value, bit)
            self.value = interleave([self.value], [other], bit, self.before(bit))[0]
            self.have.append(bit)
        self.air = self.sl.flip(self.value, self.bit)

    def land(self):
        air, self.air = self.air, None
        if isinstance(air, tuple):
            self.quarters, self.value = [self.value, *air], None
            return
        last = (self.top_first or self.twins) and not self.steps
        halves = interleave([self.value], [air], self.bit, self.before(self.bit), 1 + last)
        self.have.append(self.bit)
        if last and self.twins:
            self.value = halves
        elif last:
            self.quarters = [*halves, self.sl.flip(halves[0], CORE)]
            self.value = None
        else:
            self.value = halves[0]

    def join(self, other):
        made = Gather(self.sl, None, self.lead, twins=True)
        airs = self.air, other.air
        made.value = interleave([self.value, other.value], airs, self.bit, self.before(self.bit))[0]
        made.have, made.steps = self.have + [self.bit], self.steps
        return made

    def part(self, n):
        made = Gather(self.sl, self.value[n], self.lead)
        made.steps = []
        return made

    def finish(self):
        self.quarters = [*self.quarters, self.sl.flip(self.quarters[1], CORE)]


def add_low_kernel(one, two, out):
    out[...] = (one[...].astype(f32) + two[...].astype(f32)).astype(bf16)


def add_split_kernel(side, *refs):
    *parts, kept, sent = refs
    for at, out in ((side[0], kept), (1 - side[0], sent)):
        total = parts[0][:, pl.ds(at, 1)].astype(f32)
        for other in parts[1:]:
            total = total + other[:, pl.ds(at, 1)].astype(f32)
        out[...] = total.astype(bf16)[:, 0]


def cross_split_kernel(side, own, own_other, top, top_other, kept, sent):
    for n, (one, two) in enumerate(((own, own_other), (top, top_other))):
        for at, out in ((side[0], kept), (1 - side[0], sent)):
            total = one[:, pl.ds(at, 1)].astype(f32) + two[:, pl.ds(at, 1)].astype(f32)
            out[n] = total.astype(bf16)[:, 0]


class Scatter:
    def __init__(self, sl, quarters, lead, top_last=False):
        self.sl, self.quarters, self.value, self.lead, self.top_last = sl, quarters, None, lead, top_last
        top, near, deep = sl.high[:1], sl.high[1:], sl.deep
        self.have = sl.high + deep
        if top_last:
            self.steps = [deep[-1:], deep[-2::-1] + near, top]
        else:
            self.steps = [top, near + deep[-1:], deep[-2::-1]]

    def before(self, bit):
        order = self.sl.high + self.sl.deep
        count = sum(order.index(b) < order.index(bit) for b in self.have)
        return (1 << count) * (1 if bit in self.sl.high else self.lead)

    def side(self, bit):
        return jnp.zeros((1,), jnp.int32) if bit == self.sl.high[0] else mine(bit)[None]

    def cross(self):
        own, top, core, both = self.quarters
        top_other = self.sl.flip(both, CORE)
        core, _ = lax.optimization_barrier((core, top_other))
        core_other = self.sl.flip(core, CORE)
        rows, n = top.shape
        if not self.top_last:
            (send,) = call(
                add_low_kernel, [(top.shape, bf16)], [top, top_other], [VMEM] * 2, name="add_low"
            )
            self.quarters = [[own, core_other], send]
            return
        bit = self.steps[0][0]
        before = self.before(bit) // 2
        shape = (before, 2, rows // 2 // before, n)
        half = ((2, before, rows // 2 // before, n), bf16)
        keep, send = call(
            cross_split_kernel,
            [half, half],
            [self.side(bit), *(v.reshape(shape) for v in (own, core_other, top, top_other))],
            [SMEM] + [VMEM] * 4,
            name="cross_split",
        )
        self.quarters = [[keep.reshape(-1, n)], send.reshape(-1, n)]

    def split(self, other, bit):
        parts = [*self.quarters[0], other]
        if bit is None:
            self.value = sum(part.astype(f32) for part in parts)
            self.quarters = None
            return
        before = self.before(bit)
        rows, n = other.shape
        shape = (before, 2, rows // 2 // before, n)
        half = ((before, rows // 2 // before, n), bf16)
        keep, send = call(
            add_split_kernel,
            [half, half],
            [self.side(bit), *(part.reshape(shape) for part in parts)],
            [SMEM] + [VMEM] * len(parts),
            name="add_split",
        )
        self.quarters = [[keep.reshape(-1, n)], send.reshape(-1, n)]

    def start(self):
        bits = self.steps.pop(0)
        for n, bit in enumerate(bits):
            self.air = self.sl.flip(self.quarters[1], bit)
            self.have.remove(bit)
            if n < len(bits) - 1:
                self.split(self.air, bits[n + 1])
        self.next = self.steps[0][0] if self.steps else None

    def land(self):
        other, self.air = self.air, None
        self.split(other, self.next)


class Live:
    def __init__(self, **values):
        self.flows = []
        self.values = values

    def flow(self, made):
        self.flows.append(made)
        return made

    def __getattr__(self, name):
        return self.values[name]

    def put(self, **values):
        self.values.update(values)

    def drop(self, *names):
        for name in names:
            del self.values[name]

    def seal(self, *landing, keep=()):
        landing = [*keep, *landing]
        kept = (
            self.values,
            [(made.value, made.quarters) for made in self.flows],
            [made.air for made in landing],
        )
        self.values, flown, airs = lax.optimization_barrier(kept)
        for made, (made.value, made.quarters) in zip(self.flows, flown):
            pass
        for n, (made, made.air) in enumerate(zip(landing, airs)):
            if n >= len(keep):
                made.land()


def dot(left, right):
    return jnp.dot(left, right, preferred_element_type=f32)


def dot_t(left, right):
    return lax.dot_general(left, right, (((1,), (1,)), ((), ())), preferred_element_type=f32)


def t_dot(left, right):
    return lax.dot_general(left, right, (((0,), (0,)), ((), ())), preferred_element_type=f32)


def fetch(place, quarters, whole, lead, sems):
    width = whole.shape[1]
    block = whole.shape[0] // (4 * lead)
    copies = []
    for n, part in enumerate(quarters):
        top = place[0] if n % 2 == 0 else 1 - place[0]
        core = place[1] if n < 2 else 1 - place[1]
        for a in range(lead):
            at = pl.multiple_of(((top * lead + a) * 2 + core) * block, block)
            source = part.at[pl.ds(a * block, block), pl.ds(0, width)]
            copies.append(
                pltpu.make_async_copy(source, whole.at[pl.ds(at, block)], sems.at[n * lead + a])
            )
    for copy in copies:
        copy.start()
    return copies


def norm(hidden):
    centred = hidden - jnp.mean(hidden, axis=-1, keepdims=True)
    scale = lax.rsqrt(jnp.mean(centred * centred, axis=-1, keepdims=True) + 1e-05)
    return centred * scale, scale


def put_rows(outs, cols, value):
    rows = value.shape[0] // len(outs)
    for r, out in enumerate(outs):
        out[:, cols] = value[r * rows : (r + 1) * rows].astype(bf16)


def theirs(others, r, rows):
    if len(others) == 2:
        return others[1 - r][...].astype(f32)
    return others[0][pl.ds((1 - r) * rows, rows)].astype(f32)


def gains_at(gains, r, place, width):
    return gains[pl.ds(r, 1), pl.ds(place * width, width)]


def add_norm(which, parts, gains, total, out):
    base, *shares = parts
    rows, width = out.shape[0] // 2, out.shape[1]
    for r in range(2):
        block = pl.ds(r * rows, rows)
        value = base[block]
        if shares:
            value = value + (shares[0][block] + theirs(shares[1:], r, rows))
            total[block] = value
        gain, bias = [gains_at(gains, r, 2 * which + n, width) for n in range(2)]
        out[block] = (norm(value)[0] * gain + bias).astype(bf16)


def norm_back(which, d_out, keep, others, hidden, gains, total, low, d_gain, d_shift):
    rows, width = d_out.shape[0] // 2, d_out.shape[1]
    for r in range(2):
        block = pl.ds(r * rows, rows)
        grad = keep[block] + theirs(others, r, rows)
        normed, scale = norm(hidden[block])
        if r == 0:
            d_gain[...] = jnp.sum(grad * normed, axis=0, keepdims=True)
            d_shift[...] = jnp.sum(grad, axis=0, keepdims=True)
        e = grad * gains_at(gains, r, 2 * which, width)
        part = e - jnp.mean(e, axis=-1, keepdims=True)
        part = part - normed * jnp.mean(e * normed, axis=-1, keepdims=True)
        value = d_out[block] + scale * part
        total[block] = value
        low[block] = value.astype(bf16)


def norm_back_kernel(which, d_out, keep, *refs):
    norm_back(which, d_out, keep, refs[:-6], *refs[-6:])


def gains_kernel(lead, count, rows, place, pick, q0, q1, q2, q3, first, second, held, wide, sems):
    copies = []
    for n, part in enumerate((q0, q1, q2, q3)):
        source = part.at[:, pl.ds(part.shape[1] - 128, 128)]
        copies.append(pltpu.make_async_copy(source, held.at[n], sems.at[n]))
    for copy in copies:
        copy.start()
    for copy in copies:
        copy.wait()
    wide[...] = held[...].astype(f32)
    deep = wide.shape[1] // (lead * rows)
    for n in range(4):
        top = place[0] if n % 2 == 0 else 1 - place[0]
        core = place[1] if n < 2 else 1 - place[1]
        for a in range(lead):
            for z in range(deep):
                cols = pl.multiple_of((((top * lead + a) * 2 + core) * deep + z) * 128, 128)
                base = (a * deep + z) * rows
                for r in range(2):
                    first[pl.ds(r, 1), pl.ds(cols, 128)] = wide[n, pl.ds(base, 1)]
                    second[pl.ds(r, 1), pl.ds(cols, 128)] = wide[n, pl.ds(base + 1 + pick[r], 1)]


def score(q, k, allowed, size):
    scores = jnp.where(allowed, dot_t(q, k) * size, -1e30)
    exponent = jnp.exp(scores - jnp.max(scores, axis=-1, keepdims=True))
    return exponent / jnp.sum(exponent, axis=-1, keepdims=True)


def lanes_of(which, shape):
    lane = lax.broadcasted_iota(jnp.int32, shape, 1)
    return (lane < shape[1] // 2) if which == 0 else (lane >= shape[1] // 2)


def out_block(weight, k, block, at):
    count = weight.shape[0] // (2 * block)
    wide = weight.shape[1] - at
    return jnp.concatenate([weight[pl.ds((2 * h + k) * block, block), pl.ds(at, wide)] for h in range(count)], 0)


def attend_kernel(ways, size, lead, block, place, *refs):
    refs, (weight, sems) = refs[:-2], refs[-2:]
    refs, lows = refs[:-ways], refs[-ways:]
    *parts, gains, q0, q1, q2, q3, allow, total, f, qkv, mixed, keep = refs
    copies = fetch(place, (q0, q1, q2, q3), weight, lead, sems)
    add_norm(0, parts, gains, total, f)
    for copy in copies:
        copy.wait()
    length = allow.shape[-1]
    third = qkv.shape[1] // 3
    for n in range(3):
        cols = pl.ds(n * third, third)
        qkv[:, cols] = dot(f[...], weight[:, cols]).astype(bf16)

    def one_row(r):
        at = pl.ds(r * length, length)
        allowed = allow[r] > 0
        for p in range(third // 128):
            q = qkv[at, pl.ds(p * 128, 128)]
            k = qkv[at, pl.ds(third + p * 128, 128)]
            v = qkv[at, pl.ds(2 * third + p * 128, 128)]
            halves = []
            for h in range(2):
                probs = score(jnp.where(lanes_of(h, q.shape), q, 0), k, allowed, size)
                halves.append(dot(probs.astype(bf16), v))
            mixed[at, pl.ds(p * 128, 128)] = jnp.where(
                lanes_of(0, q.shape), halves[0], halves[1]
            ).astype(bf16)

    for r in range(f.shape[0] // length):
        one_row(r)
    for k in range(2):
        cols = pl.ds(k * third, third)
        value = dot(mixed[...], out_block(weight, k, block, 3 * third))
        keep[:, cols] = value
        put_rows(lows, cols, value)


def attend_back_kernel(ways, size, lead, block, grads, place, *refs):
    if grads:
        (first, mixed), refs = refs[:2], refs[2:]
    (d_out, part), refs = refs[:2], refs[2:]
    refs, (weight, d_mixed, sems) = refs[:-3], refs[-3:]
    if grads:
        refs, outs = refs[:-4], refs[-4:]
    refs, lows = refs[:-ways], refs[-ways:]
    *others, attended, gains, q0, q1, q2, q3, allow, qkv, total, d, d_gain, d_shift, d_qkv, keep = refs
    copies = fetch(place, (q0, q1, q2, q3), weight, lead, sems)
    norm_back(1, d_out, part, others, attended, gains, total, d, d_gain, d_shift)
    for copy in copies:
        copy.wait()
    length = allow.shape[-1]
    third = qkv.shape[1] // 3
    value = dot_t(d[:, pl.ds(0, third)], out_block(weight, 0, block, 3 * third))
    value = value + dot_t(d[:, pl.ds(third, third)], out_block(weight, 1, block, 3 * third))
    d_mixed[...] = value.astype(bf16)

    def one_row(r):
        at = pl.ds(r * length, length)
        allowed = allow[r] > 0
        for p in range(third // 128):
            q = qkv[at, pl.ds(p * 128, 128)]
            k = qkv[at, pl.ds(third + p * 128, 128)]
            v = qkv[at, pl.ds(2 * third + p * 128, 128)]
            dm = d_mixed[at, pl.ds(p * 128, 128)]
            d_q, d_k, d_v = [], [], []
            for h in range(2):
                pick = lanes_of(h, q.shape)
                probs = score(jnp.where(pick, q, 0), k, allowed, size)
                d_probs = dot_t(jnp.where(pick, dm, 0), v)
                d_v.append(t_dot(probs.astype(bf16), dm))
                inner = jnp.sum(probs * d_probs, axis=-1, keepdims=True)
                d_scores = (probs * (d_probs - inner)).astype(bf16)
                d_q.append(dot(d_scores, k))
                d_k.append(t_dot(d_scores, q))
            pick = lanes_of(0, q.shape)
            for n, (halves, scale) in enumerate(((d_q, size), (d_k, size), (d_v, 1.0))):
                value = jnp.where(pick, halves[0], halves[1]) * scale
                d_qkv[at, pl.ds(n * third + p * 128, 128)] = value.astype(bf16)

    for r in range(d.shape[0] // length):
        one_row(r)
    for n in range(keep.shape[1] // 256):
        cols = pl.ds(n * 256, 256)
        value = dot_t(d_qkv[...], weight[cols, pl.ds(0, 3 * third)])
        keep[:, cols] = value
        put_rows(lows, cols, value)
    if grads:
        attend_grad(lead, place, first, mixed, d_qkv, d, outs)


def up(f, weight, pre, active):
    for n in range(pre.shape[1] // 256):
        cols = pl.ds(n * 256, 256)
        value = dot(f[...], weight[:, cols])
        pre[:, cols] = value
        active[:, cols] = jax.nn.gelu(value).astype(bf16)


def down(active, weight, keep, lows):
    for n in range(keep.shape[1] // 256):
        cols = pl.ds(n * 256, 256)
        value = dot(active[...], weight[:, cols])
        keep[:, cols] = value
        put_rows(lows, cols, value)


def feed_kernel(ways, lead, up_place, dn_place, *refs):
    refs, (w_up, w_dn, up_sems, dn_sems) = refs[:-4], refs[-4:]
    refs, lows = refs[:-ways], refs[-ways:]
    *parts, gains, u0, u1, u2, u3, n0, n1, n2, n3, total, f, pre, active, keep = refs
    up_copies = fetch(up_place, (u0, u1, u2, u3), w_up, lead, up_sems)
    dn_copies = fetch(dn_place, (n0, n1, n2, n3), w_dn, lead // 2, dn_sems)
    add_norm(1, parts, gains, total, f)
    for copy in up_copies:
        copy.wait()
    up(f, w_up, pre, active)
    for copy in dn_copies:
        copy.wait()
    down(active, w_dn, keep, lows)


def down_kernel(lead, place, active, q0, q1, q2, q3, keep, low, weight, sems):
    for copy in fetch(place, (q0, q1, q2, q3), weight, lead, sems):
        copy.wait()
    down(active, weight, keep, (low,))


def gelu_slope(x):
    c = 0.7978845608028654
    t = jnp.tanh(c * (x + 0.044715 * (x * x * x)))
    return 0.5 * (1.0 + t) + 0.5 * x * (1.0 - t * t) * (c * (1.0 + 3 * 0.044715 * (x * x)))


def feed_back(d, pre, w_up, w_dn, d_pre, keep, lows):
    for n in range(pre.shape[1] // 256):
        cols = pl.ds(n * 256, 256)
        d_pre[:, cols] = (gelu_slope(pre[:, cols]) * dot_t(d[...], w_dn[cols])).astype(bf16)
    for n in range(keep.shape[1] // 256):
        cols = pl.ds(n * 256, 256)
        value = dot_t(d_pre[...], w_up[cols])
        keep[:, cols] = value
        put_rows(lows, cols, value)


def feed_back_kernel(ways, lead, up_place, dn_place, d_out, part, *refs):
    refs, (w_up, w_dn, up_sems, dn_sems) = refs[:-4], refs[-4:]
    refs, lows = refs[:-ways], refs[-ways:]
    *others, hidden, gains, pre, u0, u1, u2, u3, n0, n1, n2, n3, total, d, d_gain, d_shift, d_pre, keep = refs
    copies = fetch(dn_place, (n0, n1, n2, n3), w_dn, lead // 2, dn_sems)
    copies += fetch(up_place, (u0, u1, u2, u3), w_up, lead, up_sems)
    norm_back(0, d_out, part, others, hidden, gains, total, d, d_gain, d_shift)
    for copy in copies:
        copy.wait()
    feed_back(d, pre, w_up, w_dn, d_pre, keep, lows)


def feed_turn_kernel(ways, lead, grads, place, up_place, dn_place, *refs):
    refs, (w_up, w_dn, pre, up_sems, dn_sems) = refs[:-5], refs[-5:]
    if grads:
        refs, up_outs, dn_outs = refs[:-8], refs[-8:-4], refs[-4:]
    refs, lows = refs[:-ways], refs[-ways:]
    *parts, gains, d, u0, u1, u2, u3, n0, n1, n2, n3, total, f, active, d_pre, keep = refs
    up_copies = fetch(up_place, (u0, u1, u2, u3), w_up, lead, up_sems)
    dn_copies = fetch(dn_place, (n0, n1, n2, n3), w_dn, lead // 2, dn_sems)
    add_norm(1, parts, gains, total, f)
    for copy in up_copies:
        copy.wait()
    up(f, w_up, pre, active)
    for copy in dn_copies:
        copy.wait()
    feed_back(d, pre, w_up, w_dn, d_pre, keep, lows)
    if grads:
        weight_grad(lead, place, f, d_pre, up_outs)
        weight_grad(lead // 2, place, active, d, dn_outs)


def columns_of(place, value, lead):
    block = value.shape[1] // (4 * lead)
    parts = []
    for n in range(4):
        top = place[0] if n % 2 == 0 else 1 - place[0]
        core = place[1] if n < 2 else 1 - place[1]
        starts = [((top * lead + a) * 2 + core) * block for a in range(lead)]
        if block % 128 == 0:
            starts = [pl.multiple_of(at, 128) for at in starts]
        parts.append(jnp.concatenate([value[:, pl.ds(at, block)] for at in starts], 1))
    return parts


def weight_grad(lead, place, left, right, outs):
    for part, out in zip(columns_of(place, left, lead), outs):
        out[...] = t_dot(part, right[...]).astype(bf16)


def weight_grad_kernel(lead, aligned, place, left, right, *outs):
    weight_grad(lead, place if aligned else (0, 0), left, right, outs)


def attend_grad_kernel(lead, aligned, place, left, mixed, d_qkv, d, *outs):
    attend_grad(lead, place if aligned else (0, 0), left, mixed, d_qkv, d, outs)


def attend_grad(lead, place, left, mixed, d_qkv, d, outs):
    width = d_qkv.shape[1]
    third = width // 3
    block = left.shape[1] // (4 * lead)
    lefts, inners = columns_of(place, left, lead), columns_of(place, mixed, lead // 2)
    for part, inner, out in zip(lefts, inners, outs):
        out[:, pl.ds(0, width)] = t_dot(part, d_qkv[...]).astype(bf16)
        value = t_dot(inner, d[...]).astype(bf16)
        for h in range(inner.shape[1] // block):
            for k in range(2):
                out[pl.ds((2 * h + k) * block, block), pl.ds(width, third)] = value[
                    h * block : (h + 1) * block, k * third : (k + 1) * third
                ]


def turn(sl, value, lead):
    tokens, width = value.shape
    value = value.reshape(tokens, 2, lead, 2, width // (4 * lead))
    value = jnp.stack(split(value, sl.high[0], 1), 1)
    return jnp.stack(split(value, CORE, 3), 3).reshape(tokens, width)


def finish_kernel(span, side, keep, other, out, m, v, *refs):
    third = out.shape[-1]
    place_sides([(keep, other, 0, 0, 3 * third, span)], side, refs[-3])
    for k in range(2):
        refs[-3][0, :, pl.ds((6 + k) * third, third)] = out[k]
    adam_columns(m, v, *refs[-3:])


def finish_up_kernel(chunk, first, side, keep, other, *refs):
    grad = refs[-3]
    late = grad.shape[-1] // 2 - (keep.shape[1] - first)
    pieces = [(keep, other, first, late, keep.shape[1] - first, chunk)]
    if late:
        pieces.append((refs[0], refs[1], 0, 0, late, chunk))
    place_sides(pieces, side, grad)
    m, v = refs[2:4] if late else refs[:2]
    adam_columns(m, v, *refs[-3:])


def place_sides(pieces, side, grad):
    for one, two, first, start, count, width in pieces:
        each = math.gcd(math.gcd(width, start), count)
        for source, x in ((one, side[0]), (two, 1 - side[0])):
            for n in range(count // each):
                block, inside = divmod(start + n * each, width)
                at = pl.multiple_of((2 * block + x) * width + inside, 128)
                grad[0, :, pl.ds(at, each)] = source[:, pl.ds(first + n * each, each)]


def adam_columns(m, v, grad, new_m, step):
    for n in range(grad.shape[2] // 1024):
        cols = pl.ds(n * 1024, 1024)
        new_m[0, :, cols], step[0, :, cols] = adam_update(m[0, :, cols], v[0, :, cols], grad[0, :, cols])


def finish_down_kernel(value, m, v, *refs):
    grad, new_m, step = refs[-3:]
    grad[0] = value[...]
    new_m[0], step[0] = adam_update(m[0], v[0], value[...])


def update(kernel, layer, shape, parts, specs, moments, before, name, half=None):
    wide = shape[2] if half is None else shape[2] // 2
    one = pl.BlockSpec((1, shape[1], wide), lambda i: (layer, 0, half or 0))
    count = len(parts) + 2
    return pl.pallas_call(
        kernel,
        grid=(1,),
        out_shape=[jax.ShapeDtypeStruct(shape, f32)] * 3,
        in_specs=[*specs, one, one, *len(before) * [ANY]],
        out_specs=[one] * 3,
        input_output_aliases={count + n: n for n in range(len(before))},
        compiler_params=pltpu.CompilerParams(vmem_limit_bytes=20 << 20),
        name=name,
    )(*parts, *moments, *before)


def adam_update(moment, square, gradient):
    moment = beta_one * moment + (1.0 - beta_one) * gradient
    square = beta_two * square + (1.0 - beta_two) * gradient * gradient
    update = moment / first_fix / (jnp.sqrt(square / second_fix) + 1e-08)
    return (moment, update)


def dma(count):
    return pltpu.SemaphoreType.DMA((count,))


def body(
    dp,
    fsdp,
    inputs,
    cotangent,
    segment_ids,
    section_ids,
    w_big,
    w_down,
    norm_table,
    m_big,
    m_down,
    m_table,
    v_big,
    v_down,
    v_table,
):
    sl = Slice(dp, fsdp)
    length, width = inputs.shape[1:]
    rows = w_big.shape[1]
    feeds = w_down.shape[1]
    feed = w_big.shape[2] - 4 * width
    high = dp // 4
    lead = high
    half, part = width // 2, 3 * width // 2
    block = fsdp * rows
    count = norm_table.shape[0]
    size = (width // HEADS) ** -0.5
    two_f, two_b = ((2 * length, width), f32), ((2 * length, width), bf16)
    wide_b = ((2 * length, feed // 2), bf16)

    def lows(ways):
        return ways * [((2 // ways * length, width), bf16)]

    quarter = ((width // 4, 2 * width), bf16)
    gain_row = ((1, width), f32)
    up_first = feed // 2 - feed // 8
    place = jnp.stack([mine(sl.high[0]), mine(CORE)])
    w_attn = pltpu.VMEM((width, 2 * width), bf16)
    w_upper = pltpu.VMEM((width, feed // 2), bf16)
    w_lower = pltpu.VMEM((feed // 2, width), bf16)

    def qkv_sides(layer):
        value = w_big[layer, :, : 3 * width].reshape(rows, 3, high, 2, 2 * block)
        return [v.reshape(rows, part) for v in split(value, SIDE, 3)]

    def up_sides(layer):
        value = w_big[layer, :, 4 * width :].reshape(rows, high, 2, 2 * fsdp * feeds)
        return [v.reshape(rows, feed // 2) for v in split(value, SIDE, 2)]

    def prepare(table_part):
        shapes = 2 * [(rows, part + 128)] + 2 * [(rows, feed // 2)] + 2 * [(rows, part + feed // 2)]
        shapes.append((2, 2, rows, half))
        if rows % 16 == 0:
            return call(
                partial(prepare_kernel, 2 * block, 2 * fsdp * feeds),
                [(shape, bf16) for shape in shapes],
                [mine(SIDE)[None], w_big, table_part],
                [SMEM, ANY, ANY],
                [dma(2 * (2 * 3 * high + 2 * high + 2) + 2)],
                name="prepare",
            )
        first = [jnp.concatenate([v, table_part], -1) for v in qkv_sides(0)]
        after = [jnp.concatenate([a, b], -1) for a, b in zip(qkv_sides(1), up_sides(1))]
        out = w_big[:, :, 3 * width : 4 * width].reshape(2, rows, 2, half)
        return [*first, *up_sides(0), *after, jnp.swapaxes(out, 1, 2)]

    def place_sides(kernel, shape, keep, other, out, name):
        return call(
            kernel,
            [(shape, bf16)],
            [mine(SIDE)[None], keep, other, out],
            [SMEM, VMEM, VMEM, VMEM],
            name=name,
        )[0]

    live = Live()
    downs = [live.flow(Gather(sl, w_down[n], 1, n == 1)) for n in range(2)]

    downs[0].start()
    downs[1].start()
    table_part = norm_table.reshape(-1)
    table_part = jnp.pad(table_part, (0, rows * 128 - table_part.shape[0])).reshape(rows, 128)
    first, first_sent, up0, up0_sent, after, after_sent, out_proj = prepare(table_part)
    live.put(
        first=[first, sl.flip(first_sent, SIDE)],
        up=[up0, up0_sent],
        after=[after, after_sent],
        out=out_proj,
    )
    live.seal(downs[0], downs[1])

    own = place_sides(
        place_first_kernel, (2, rows, 2 * width + 128), *live.first, live.out[0], "place_first"
    )
    attns = [live.flow(Gather(sl, own.reshape(2 * rows, -1), 2))]
    attns[0].start()
    downs[0].start()
    extra = jnp.zeros((16, width), bf16)
    extra = extra.at[0, :length].set(segment_ids[0].astype(bf16))
    extra = extra.at[1, 0].set(section_ids[0].astype(bf16))
    pack = jnp.concatenate([inputs[0], cotangent[0], extra], 0)
    live.put(
        up=[live.up[0], sl.flip(live.up[1], SIDE)],
        after=[live.after[0], sl.flip(live.after[1], SIDE)],
        pack=[pack, sl.flip(pack, SIDE)],
    )
    live.drop("first")
    live.seal(attns[0], downs[0])

    ups = [live.flow(Gather(sl, interleave(live.up[:1], live.up[1:], SIDE, 1)[0], 2))]
    downs[0].start()
    attns[0].start()
    ups[0].start()
    own = place_sides(
        place_next_kernel, (4, rows, 2 * width), *live.after, live.out[1], "place_next"
    )
    live.put(own=own)
    live.drop("up", "after", "out")
    packed = jnp.stack(live.pack)
    extras = packed[:, 2 * length :]
    segments = extras[:, 0, :length].astype(f32)
    same = segments[:, :, None] == segments[:, None, :]
    position = jnp.arange(length)
    live.put(
        hidden=packed[:, :length].reshape(2 * length, width).astype(f32),
        d_low=packed[:, length : 2 * length].reshape(2 * length, width),
        sections=extras[:, 1, 0].astype(jnp.int32),
        allows=[
            (same & (position[:, None] >= position[None, :])).astype(f32),
            same.astype(f32),
        ],
    )
    live.drop("pack")
    live.seal(attns[0], ups[0], downs[0])

    own = live.own.reshape(2, 2 * rows, -1)
    attns.append(live.flow(Gather(sl, own[0], 2)))
    ups.append(live.flow(Gather(sl, own[1], 2)))
    live.drop("own")
    attns[0].start()
    attns[1].start()
    ups[0].start()
    downs[0].finish()
    live.seal(attns[0], ups[0], attns[1])

    def after(made, value):
        (keep, send), _ = lax.optimization_barrier((made.quarters, value))
        made.quarters = [keep, send]

    def gate(*made):
        airs = [flow.air for flow in made]
        other, airs = lax.optimization_barrier((live.other, airs))
        live.put(other=other)
        for flow, flow.air in zip(made, airs):
            pass

    def gains_of(flow, sections):
        wide = norm_table.shape[1]
        if wide == 128:
            return call(
                partial(gains_kernel, lead, count, rows),
                2 * [((2, 4 * width), f32)],
                [place, sections, *pinned(flow)],
                [SMEM, SMEM] + [ANY] * 4,
                [
                    pltpu.VMEM((4, width // 4, 128), bf16),
                    pltpu.VMEM((4, width // 4, 128), f32),
                    dma(4),
                ],
                name="gains",
            )
        parts = jnp.stack([q[:, 2 * width :] for q in flow.quarters])
        parts = parts.reshape(4, lead // 2, 2, fsdp, rows * 128)[..., : count * wide]
        parts = parts.reshape(4, lead // 2, 2, fsdp, count, wide)
        pick = jnp.concatenate([jnp.zeros((2,), jnp.int32), 1 + sections])
        pick = (pick[:, None] == jnp.arange(count)[None, :]).astype(bf16)
        picked = jnp.einsum("sr,qhxdrj->qshxdj", pick, parts, preferred_element_type=f32)
        own, top, core, both = picked
        both = merge(merge(own, core, CORE, 3), merge(top, both, CORE, 3), sl.high[0], 1)
        return list(both.reshape(2, 2, 4 * width))

    def pinned(flow):
        own, top, core, both = flow.quarters
        if flow is downs[0]:
            both = pltpu.with_memory_space_constraint(both, pltpu.HBM)
        return [own, top, pltpu.with_memory_space_constraint(core, pltpu.HBM), both]

    def cross():
        live.put(other=[sl.flip(row, SIDE) for row in live.low])

    def shares():
        return [live.keep, *live.other]

    def attend(layer, base, ways=2):
        parts = [base] if layer == 0 else [base, *shares()]
        total, first, qkv, mixed, keep, *low = call(
            partial(attend_kernel, ways, size, lead, 2 * block),
            [two_f, two_b, ((2 * length, part), bf16), ((2 * length, half), bf16), two_f, *lows(ways)],
            [
                attns[layer].place,
                *parts,
                live.gains[layer],
                *pinned(attns[layer]),
                live.allows[layer],
            ],
            [SMEM] + [VMEM] * (len(parts) + 1) + [ANY] * 4 + [VMEM],
            [w_attn, dma(4 * lead)],
            name="attend",
        )
        hidden = base if layer == 0 else total
        live.put(**{f"attn{layer}": (hidden, first, qkv, mixed)}, keep=keep, low=low)

    def feed_forward(layer, ways=2):
        attended, second, pre, active, keep, *low = call(
            partial(feed_kernel, ways, lead),
            [two_f, two_b, (wide_b[0], f32), wide_b, two_f, *lows(ways)],
            [
                ups[layer].place,
                downs[layer].place,
                live.values[f"attn{layer}"][0],
                *shares(),
                live.gains[layer],
                *pinned(ups[layer]),
                *pinned(downs[layer]),
            ],
            [SMEM, SMEM] + [VMEM] * (3 + len(live.other)) + [ANY] * 8,
            [w_upper, w_lower, dma(4 * lead), dma(2 * lead)],
            name="feed",
        )
        live.put(**{f"feed{layer}": (attended, second, pre, active)}, keep=keep, low=low)

    def feed_turn(layer, ways=2):
        grads = False
        quarters = 4 * [quarter] + 4 * [((feed // 8, width), bf16)]
        attended, second, active, d_pre, keep, *low = call(
            partial(feed_turn_kernel, ways, lead, grads),
            [two_f, two_b, wide_b, wide_b, two_f, *lows(ways), *(quarters if grads else [])],
            [
                place,
                ups[layer].place,
                downs[layer].place,
                live.values[f"attn{layer}"][0],
                *shares(),
                live.gains[layer],
                live.d_low,
                *pinned(ups[layer]),
                *pinned(downs[layer]),
            ],
            [SMEM] * 3 + [VMEM] * (4 + len(live.other)) + [ANY] * 8,
            [w_upper, w_lower, pltpu.VMEM(wide_b[0], f32), dma(4 * lead), dma(2 * lead)],
            name="feed_turn",
        )
        live.put(**{f"feed{layer}": (attended, second, None, active)}, d_pre=d_pre, keep=keep, low=low)

    def feed_down(layer):
        keep, *low = call(
            partial(down_kernel, lead // 2),
            [two_f, *lows(1)],
            [downs[layer].place, live.values[f"feed{layer}"][3], *pinned(downs[layer])],
            [SMEM, VMEM, ANY, ANY, ANY, ANY],
            [w_lower, dma(2 * lead)],
            name="down",
        )
        live.put(keep=keep, low=low)

    def feed_back(layer, ways=1):
        grad, d_low, d_gain, d_shift, d_pre, keep, *low = call(
            partial(feed_back_kernel, ways, lead),
            [two_f, two_b, gain_row, gain_row, wide_b, two_f, *lows(ways)],
            [
                ups[layer].place,
                downs[layer].place,
                live.grad,
                *shares(),
                live.values[f"attn{layer + 1}"][0],
                live.gains[layer + 1],
                live.values[f"feed{layer}"][2],
                *pinned(ups[layer]),
                *pinned(downs[layer]),
            ],
            [SMEM, SMEM] + [VMEM] * (5 + len(live.other)) + [ANY] * 8,
            [w_upper, w_lower, dma(4 * lead), dma(2 * lead)],
            name="feed_back",
        )
        live.put(grad=grad, d_low=d_low, d_pre=d_pre, keep=keep, low=low)
        live.put(**{f"gains{layer + 1}0": jnp.concatenate([d_gain, d_shift], 1)})

    def down_grad(layer, top_last=False):
        aligned = feed // 4 // lead % 128 == 0
        active = live.values[f"feed{layer}"][3]
        parts = call(
            partial(weight_grad_kernel, lead // 2, aligned),
            [((feed // 8, width), bf16)] * 4,
            [place, active if aligned else turn(sl, active, lead // 2), live.d_low],
            [SMEM, VMEM, VMEM],
            name="down_grad",
        )
        return live.flow(Scatter(sl, parts, 1, top_last))

    def up_grad(layer, piece=None):
        aligned = block % 128 == 0
        second, right = live.values[f"feed{layer}"][1], live.d_pre
        columns = feed // 2
        if piece is not None:
            right = right[:, :up_first] if piece == 0 else right[:, up_first:]
            columns = right.shape[1]
        parts = call(
            partial(weight_grad_kernel, lead, aligned),
            [((width // 4, columns), bf16)] * 4,
            [place, second if aligned else turn(sl, second, lead), right],
            [SMEM, VMEM, VMEM],
            name="up_grad",
        )
        return live.flow(Scatter(sl, parts, 2, piece == 1))

    def norm_back(which, layer, hidden):
        grad, d_low, d_gain, d_shift = call(
            partial(norm_back_kernel, which),
            [two_f, two_b, gain_row, gain_row],
            [live.grad, *shares(), hidden, live.gains[layer]],
            [VMEM] * (4 + len(live.other)),
            name="norm_back",
        )
        live.put(grad=grad, d_low=d_low)
        live.put(**{f"gains{layer}{which}": jnp.concatenate([d_gain, d_shift], 1)})

    def attend_back(layer, ways=1):
        grads = block % 128 == 0
        hidden, first, qkv, mixed = live.values[f"attn{layer}"]
        grad, d_low, d_gain, d_shift, d_qkv, keep, *low = call(
            partial(attend_back_kernel, ways, size, lead, 2 * block, grads),
            [
                *(two_f, two_b, gain_row, gain_row, ((2 * length, part), bf16), two_f, *lows(ways)),
                *(4 * [quarter] if grads else []),
            ],
            [
                attns[layer].place,
                *([first, mixed] if grads else []),
                live.grad,
                *shares(),
                live.values[f"feed{layer}"][0],
                live.gains[layer],
                *pinned(attns[layer]),
                live.allows[layer],
                live.values[f"attn{layer}"][2],
            ],
            [SMEM] + [VMEM] * (4 + 2 * grads + len(live.other)) + [ANY] * 4 + [VMEM] * 2,
            [w_attn, pltpu.VMEM((2 * length, half), bf16), dma(4 * lead)],
            name="attend_back",
        )
        low, made = low[:ways], low[ways:]
        live.put(grad=grad, d_low=d_low, d_qkv=d_qkv, keep=keep, low=low)
        live.put(**{f"gains{layer}1": jnp.concatenate([d_gain, d_shift], 1)})
        return live.flow(Scatter(sl, made, 2)) if grads else attend_grad(layer)

    def attend_grad(layer):
        hidden, first, qkv, mixed = live.values[f"attn{layer}"]
        aligned = block % 128 == 0
        if not aligned:
            first, mixed = turn(sl, first, lead), turn(sl, mixed, lead // 2)
        parts = call(
            partial(attend_grad_kernel, lead, aligned),
            [quarter] * 4,
            [place, first, mixed, live.d_qkv, live.d_low],
            [SMEM] + [VMEM] * 4,
            name="attend_grad",
        )
        return live.flow(Scatter(sl, parts, 2))

    def two_sides(flows, wides, counts):
        values = [flow.value.reshape(2, rows, wide) for flow, wide in zip(flows, wides)]
        both = jnp.concatenate([v[..., :n] for v, n in zip(values, counts)], -1)
        keep, send = split(both, SIDE, 0)
        return keep, sl.flip(send, SIDE), values[0][..., counts[0] :]

    def finish(layer, big, before, more=None):
        keep, other, out = big
        side = mine(SIDE)[None]
        before = update(
            partial(finish_kernel, 2 * block),
            layer,
            w_big.shape,
            [side, keep, other, out],
            [SMEM, VMEM, VMEM, VMEM],
            [m_big, v_big],
            before,
            "finish",
            0,
        )
        more = [] if more is None else list(more[:2])
        return update(
            partial(finish_up_kernel, 2 * fsdp * feeds, part),
            layer,
            w_big.shape,
            [side, keep, other, *more],
            [SMEM] + [VMEM] * (2 + len(more)),
            [m_big, v_big],
            before,
            "finish_up",
            1,
        )

    def finish_down(layer, flow, before):
        return update(
            finish_down_kernel,
            layer,
            w_down.shape,
            [flow.value],
            [VMEM],
            [m_down, v_down],
            before,
            "finish_down",
        )

    def table_terms():
        first, second = [
            jnp.concatenate([live.values[f"gains{n}0"], live.values[f"gains{n}1"]], 1) for n in range(2)
        ]
        hit = jnp.arange(count - 1) == section_ids[0]
        terms = jnp.concatenate([first, jnp.where(hit[:, None], second, 0.0)], 0)
        terms = terms.reshape(count, high, 2, 2, fsdp, norm_table.shape[1])
        return jnp.moveaxis(terms, 0, 4)

    def table_step(pos, bits):
        value = live.table
        for bit in bits:
            keep, send = split(value, bit, pos)
            value = keep + sl.flip(send, bit)
        live.put(table=value)

    ups[0].start()
    attns[1].start()
    ups[1].start()
    attns[0].finish()
    live.put(gains=gains_of(attns[0], live.sections))
    attend(0, live.hidden, 1)
    cross()
    live.seal(ups[0], attns[1], ups[1])

    attns[1].start()
    ups[1].start()
    downs[1].start()
    ups[0].finish()
    feed_forward(0, 1)
    cross()
    live.seal(attns[1], ups[1], downs[1])

    ups[1].start()
    downs[1].start()
    attns[1].finish()
    attend(1, live.feed0[0])
    cross()
    live.seal(ups[1], downs[1])

    ups[1].finish()
    downs[1].finish()
    live.put(grad=live.d_low.astype(f32))
    feed_turn(1)
    live.seal()

    cross()
    g_up1 = up_grad(1)
    g_up1.cross()
    g_up1.start()
    g_down1 = down_grad(1, True)
    g_down1.cross()
    g_down1.start()
    g_attn1 = attend_back(1)
    live.seal(g_down1, g_up1)

    g_down1.start()
    g_up1.start()
    g_attn1.cross()
    g_attn1.start()
    cross()
    feed_back(0)
    g_down0, g_up0b, g_up0a = down_grad(0), up_grad(0, 1), up_grad(0, 0)
    live.seal(g_down1, g_up1, g_attn1)

    cross()
    g_down0.cross()
    g_down0.start()
    g_up0b.cross()
    g_up0b.start()
    g_up0a.cross()
    after(g_up1, g_down0.quarters[0][1])
    g_up1.start()
    g_attn1.start()
    g_attn0 = attend_back(0)
    live.seal(g_down0, g_up1, g_attn1, g_up0b)

    cross()
    g_attn0.cross()
    g_attn0.start()
    g_up0b.start()
    g_down0.start()
    after(g_attn1, g_attn0.quarters[0][1])
    g_attn1.start()
    norm_back(0, 0, live.attn0[0])
    live.seal(g_attn0, g_attn1, g_down0, g_up0b)

    g_up0a.start()
    after(g_down0, g_attn0.quarters[1])
    (g_attn1.value, g_up1.value), g_attn0.quarters[1] = lax.optimization_barrier(
        ((g_attn1.value, g_up1.value), g_attn0.quarters[1])
    )
    g_attn0.start()
    g_down0.start()
    g_up0b.start()
    feed_down(1)
    big1 = two_sides([g_attn1, g_up1], [2 * width, feed // 2], [part, feed // 2])
    live.put(big=finish(1, big1, []))
    live.put(table=table_terms())
    table_step(2, [CORE])
    live.seal(g_up0a, g_attn0, g_down0, g_up0b)

    g_up0a.start()
    g_attn0.start()
    g_down1.start()
    cross()
    table_step(1, [SIDE])
    table = live.table.reshape(*(len(sl.high) + len(sl.deep)) * [2], count, -1)
    live.put(table=table, down=finish_down(0, g_down0, []))
    live.seal(g_up0a, g_attn0, g_down1)

    g_up0a.start()
    out_act = live.feed1[0][:length] + (live.keep[:length] + live.other[0][length:].astype(f32))
    rest = feed // 2 - up_first
    big0 = two_sides([g_attn0, g_up0b], [2 * width, rest], [part, rest])
    table_step(0, sl.high)
    table_step(-3, sl.deep[-1:])
    live.put(out_act=out_act.astype(bf16), down=finish_down(1, g_down1, live.down), big0=big0)
    live.seal(g_up0a)

    table_step(0, sl.deep[:-1])
    up0a = two_sides([g_up0a], [up_first], [up_first])
    grad_big, new_m_big, step_big = finish(0, live.big0, live.big, up0a)
    grad_down, new_m_down, step_down = live.down
    grad_table = live.table
    new_m_table, step_table = adam_update(m_table, v_table, grad_table)
    return (
        live.out_act[None],
        live.d_low[:length][None],
        grad_big,
        grad_down,
        grad_table,
        new_m_big,
        new_m_down,
        new_m_table,
        step_big,
        step_down,
        step_table,
    )


def solution(mesh):
    both = ("dp", "fsdp")
    rows, middle, last = P(both, None, None), P(None, both, None), P(None, both)
    return jax.shard_map(
        partial(body, mesh.shape["dp"], mesh.shape["fsdp"]),
        mesh=mesh,
        in_specs=(rows, rows, P(both, None), P(both), middle, middle, last)
        + 2 * (middle, middle, last),
        out_specs=(rows, rows) + 3 * (middle, middle, last),
        check_vma=False,
    )
```

```python
import itertools
import math
from functools import partial

import jax
import jax.numpy as jnp
from jax import lax
from jax.experimental import pallas as pl
from jax.experimental.pallas import tpu as pltpu
from jax.sharding import PartitionSpec as P

HEADS = 16

beta_one = 0.9
beta_two = 0.999
first_fix = 1.0 - 0.9**10
second_fix = 1.0 - 0.999**10

f32 = jnp.float32
bf16 = jnp.bfloat16

VMEM = pl.BlockSpec(memory_space=pltpu.VMEM)
SMEM = pl.BlockSpec(memory_space=pltpu.SMEM)
ANY = pl.BlockSpec(memory_space=pl.ANY)

CORE = ("dp", 1)
SIDE = ("dp", 2)


def masks(size):
    return [1 << k for k in reversed(range(size.bit_length() - 1))]


class Slice:
    def __init__(self, dp, fsdp):
        self.high = [("dp", m) for m in masks(dp) if m > 2]
        self.deep = [("fsdp", m) for m in masks(fsdp)]
        self.size = {"dp": dp, "fsdp": fsdp}

    def flip(self, value, bit):
        axis, mask = bit
        return lax.ppermute(value, axis, [(i, i ^ mask) for i in range(self.size[axis])])


def mine(bit):
    axis, mask = bit
    return (lax.axis_index(axis) // mask) % 2


def call(kernel, outs, operands, specs, scratch=(), flops=0, name=None):
    held = [(v.shape, v.dtype) for v, spec in zip(operands, specs) if spec is VMEM] + list(outs)
    held += [(s.shape, s.dtype) for s in scratch if hasattr(s, "memory_space") and s.memory_space == pltpu.VMEM]
    held = sum(math.prod(shape) * jnp.dtype(kind).itemsize for shape, kind in held)
    return pl.pallas_call(
        kernel,
        out_shape=[jax.ShapeDtypeStruct(shape, kind) for shape, kind in outs],
        in_specs=specs,
        out_specs=[VMEM] * len(outs),
        scratch_shapes=list(scratch),
        compiler_params=pltpu.CompilerParams(vmem_limit_bytes=held + (3 << 20)),
        name=name,
    )(*operands)


def merge(own, other, bit, pos):
    side = mine(bit)
    return jnp.where(side == 0, jnp.stack([own, other], pos), jnp.stack([other, own], pos))


def split(value, bit, pos):
    side = mine(bit)
    keep = lax.dynamic_index_in_dim(value, side, pos, keepdims=False)
    send = lax.dynamic_index_in_dim(value, 1 - side, pos, keepdims=False)
    return keep, send


def interleave_kernel(count, side, *refs):
    owns, others, outs = refs[:count], refs[count : 2 * count], refs[2 * count :]
    each = count * owns[0].shape[0] // len(outs)
    for n, (own, other) in enumerate(zip(owns, others)):
        for m in range(own.shape[0]):
            out, at = outs[(n * own.shape[0] + m) // each], (n * own.shape[0] + m) % each
            out[pl.ds(at, 1), pl.ds(side[0], 1)] = own[pl.ds(m, 1)][:, None]
            out[pl.ds(at, 1), pl.ds(1 - side[0], 1)] = other[pl.ds(m, 1)][:, None]


def interleave(owns, others, bit, before, outs=1):
    rows, n = owns[0].shape
    count = len(owns)
    shape = (before, rows // before, n)
    whole = (count * before // outs, 2, rows // before, n)
    result = call(
        partial(interleave_kernel, count),
        outs * [(whole, owns[0].dtype)],
        [mine(bit)[None], *(v.reshape(shape) for v in (*owns, *others))],
        [SMEM] + [VMEM] * (2 * count),
        name="interleave",
    )
    return [part.reshape(-1, n) for part in result]


def prepare_kernel(span, chunk, side, big, table, first, first_sent, up0, up0_sent, after, after_sent, out, sems):
    width = out.shape[-1] * 2
    third = 3 * width
    copies = []
    for layer, qkv, up in ((0, (first, first_sent), (up0, up0_sent)), (1, (after, after_sent), (after, after_sent))):
        for x, target, upper in ((side[0], qkv[0], up[0]), (1 - side[0], qkv[1], up[1])):
            for n in range(third // (2 * span)):
                at = pl.multiple_of((2 * n + x) * span, 128)
                copies.append((big.at[layer, :, pl.ds(at, span)], target.at[:, pl.ds(n * span, span)]))
            base = 0 if layer == 0 else third // 2
            for n in range(up0.shape[1] // chunk):
                at = pl.multiple_of(4 * width + (2 * n + x) * chunk, 128)
                copies.append((big.at[layer, :, pl.ds(at, chunk)], upper.at[:, pl.ds(base + n * chunk, chunk)]))
        for k in range(2):
            copies.append((big.at[layer, :, pl.ds(third + k * width // 2, width // 2)], out.at[layer, k]))
    for target in (first, first_sent):
        copies.append((table, target.at[:, pl.ds(third // 2, 128)]))
    copies = [pltpu.make_async_copy(a, b, sems.at[n]) for n, (a, b) in enumerate(copies)]
    for copy in copies:
        copy.start()
    for copy in copies:
        copy.wait()


def place_first_kernel(side, keep, other, out, own):
    part = keep.shape[1] - 128
    wide = out.shape[-1]
    for source, x in ((keep, side[0]), (other, 1 - side[0])):
        own[pl.ds(x, 1), :, pl.ds(0, part)] = source[:, pl.ds(0, part)][None]
        own[pl.ds(x, 1), :, pl.ds(part + wide, 128)] = source[:, pl.ds(part, 128)][None]
    own[:, :, pl.ds(part, wide)] = out[...]


def place_next_kernel(side, keep, other, out, own):
    wide = out.shape[-1]
    part = 3 * wide
    for source, x in ((keep, side[0]), (other, 1 - side[0])):
        own[pl.ds(x, 1), :, pl.ds(0, part)] = source[:, pl.ds(0, part)][None]
        own[pl.ds(2 + x, 1)] = source[:, pl.ds(part, part + wide)][None]
    own[pl.ds(0, 2), :, pl.ds(part, wide)] = out[...]


class Gather:
    def __init__(self, sl, own, lead, top_first=False, twins=False):
        self.sl, self.value, self.lead, self.top_first, self.twins = sl, own, lead, top_first, twins
        self.have, self.air, self.quarters = [], None, None
        near = sl.high[:0:-1]
        if top_first:
            self.steps = [sl.high[:1], near + sl.deep[:-1], sl.deep[-1:]]
        else:
            self.steps = [sl.deep[:-1], sl.deep[-1:] + near]
        core = mine(CORE)
        self.place = jnp.stack([jnp.zeros_like(core) if top_first else mine(sl.high[0]), core])

    def before(self, bit):
        order = self.sl.high + self.sl.deep
        count = sum(order.index(b) < order.index(bit) for b in self.have)
        return (1 + self.twins) * (1 << count) * (1 if bit in self.sl.high else self.lead)

    def start(self):
        if not self.steps:
            self.air = self.sl.flip(self.value, self.sl.high[0]), self.sl.flip(self.value, CORE)
            return
        *others, self.bit = self.steps.pop(0)
        for bit in others:
            other = self.sl.flip(self.value, bit)
            self.value = interleave([self.value], [other], bit, self.before(bit))[0]
            self.have.append(bit)
        self.air = self.sl.flip(self.value, self.bit)

    def land(self):
        air, self.air = self.air, None
        if isinstance(air, tuple):
            self.quarters, self.value = [self.value, *air], None
            return
        last = (self.top_first or self.twins) and not self.steps
        halves = interleave([self.value], [air], self.bit, self.before(self.bit), 1 + last)
        self.have.append(self.bit)
        if last and self.twins:
            self.value = halves
        elif last:
            self.quarters = [*halves, self.sl.flip(halves[0], CORE)]
            self.value = None
        else:
            self.value = halves[0]

    def join(self, other):
        made = Gather(self.sl, None, self.lead, twins=True)
        airs = self.air, other.air
        made.value = interleave([self.value, other.value], airs, self.bit, self.before(self.bit))[0]
        made.have, made.steps = self.have + [self.bit], self.steps
        return made

    def part(self, n):
        made = Gather(self.sl, self.value[n], self.lead)
        made.steps = []
        return made

    def finish(self):
        self.quarters = [*self.quarters, self.sl.flip(self.quarters[1], CORE)]


def add_low_kernel(one, two, out):
    out[...] = (one[...].astype(f32) + two[...].astype(f32)).astype(bf16)


def add_split_kernel(side, *refs):
    *parts, kept, sent = refs
    for at, out in ((side[0], kept), (1 - side[0], sent)):
        total = parts[0][:, pl.ds(at, 1)].astype(f32)
        for other in parts[1:]:
            total = total + other[:, pl.ds(at, 1)].astype(f32)
        out[...] = total.astype(bf16)[:, 0]


def cross_split_kernel(side, own, own_other, top, top_other, kept, sent):
    for n, (one, two) in enumerate(((own, own_other), (top, top_other))):
        for at, out in ((side[0], kept), (1 - side[0], sent)):
            total = one[:, pl.ds(at, 1)].astype(f32) + two[:, pl.ds(at, 1)].astype(f32)
            out[n] = total.astype(bf16)[:, 0]


class Scatter:
    def __init__(self, sl, quarters, lead, top_last=False):
        self.sl, self.quarters, self.value, self.lead, self.top_last = sl, quarters, None, lead, top_last
        top, near, deep = sl.high[:1], sl.high[1:], sl.deep
        self.have = sl.high + deep
        if top_last:
            self.steps = [deep[-1:], deep[-2::-1] + near, top]
        else:
            self.steps = [top, near + deep[-1:], deep[-2::-1]]

    def before(self, bit):
        order = self.sl.high + self.sl.deep
        count = sum(order.index(b) < order.index(bit) for b in self.have)
        return (1 << count) * (1 if bit in self.sl.high else self.lead)

    def side(self, bit):
        return jnp.zeros((1,), jnp.int32) if bit == self.sl.high[0] else mine(bit)[None]

    def cross(self):
        own, top, core, both = self.quarters
        top_other = self.sl.flip(both, CORE)
        core, _ = lax.optimization_barrier((core, top_other))
        core_other = self.sl.flip(core, CORE)
        rows, n = top.shape
        if not self.top_last:
            (send,) = call(
                add_low_kernel, [(top.shape, bf16)], [top, top_other], [VMEM] * 2, name="add_low"
            )
            self.quarters = [[own, core_other], send]
            return
        bit = self.steps[0][0]
        before = self.before(bit) // 2
        shape = (before, 2, rows // 2 // before, n)
        half = ((2, before, rows // 2 // before, n), bf16)
        keep, send = call(
            cross_split_kernel,
            [half, half],
            [self.side(bit), *(v.reshape(shape) for v in (own, core_other, top, top_other))],
            [SMEM] + [VMEM] * 4,
            name="cross_split",
        )
        self.quarters = [[keep.reshape(-1, n)], send.reshape(-1, n)]

    def split(self, other, bit):
        parts = [*self.quarters[0], other]
        if bit is None:
            self.value = sum(part.astype(f32) for part in parts)
            self.quarters = None
            return
        before = self.before(bit)
        rows, n = other.shape
        shape = (before, 2, rows // 2 // before, n)
        half = ((before, rows // 2 // before, n), bf16)
        keep, send = call(
            add_split_kernel,
            [half, half],
            [self.side(bit), *(part.reshape(shape) for part in parts)],
            [SMEM] + [VMEM] * len(parts),
            name="add_split",
        )
        self.quarters = [[keep.reshape(-1, n)], send.reshape(-1, n)]

    def start(self):
        bits = self.steps.pop(0)
        for n, bit in enumerate(bits):
            self.air = self.sl.flip(self.quarters[1], bit)
            self.have.remove(bit)
            if n < len(bits) - 1:
                self.split(self.air, bits[n + 1])
        self.next = self.steps[0][0] if self.steps else None

    def land(self):
        other, self.air = self.air, None
        self.split(other, self.next)


class Live:
    def __init__(self, **values):
        self.flows = []
        self.values = values

    def flow(self, made):
        self.flows.append(made)
        return made

    def __getattr__(self, name):
        return self.values[name]

    def put(self, **values):
        self.values.update(values)

    def drop(self, *names):
        for name in names:
            del self.values[name]

    def seal(self, *landing, keep=()):
        landing = [*keep, *landing]
        kept = (
            self.values,
            [(made.value, made.quarters) for made in self.flows],
            [made.air for made in landing],
        )
        self.values, flown, airs = lax.optimization_barrier(kept)
        for made, (made.value, made.quarters) in zip(self.flows, flown):
            pass
        for n, (made, made.air) in enumerate(zip(landing, airs)):
            if n >= len(keep):
                made.land()


def dot(left, right):
    return jnp.dot(left, right, preferred_element_type=f32)


def dot_t(left, right):
    return lax.dot_general(left, right, (((1,), (1,)), ((), ())), preferred_element_type=f32)


def t_dot(left, right):
    return lax.dot_general(left, right, (((0,), (0,)), ((), ())), preferred_element_type=f32)


def fetch(place, quarters, whole, lead, sems):
    width = whole.shape[1]
    block = whole.shape[0] // (4 * lead)
    copies = []
    for n, part in enumerate(quarters):
        top = place[0] if n % 2 == 0 else 1 - place[0]
        core = place[1] if n < 2 else 1 - place[1]
        for a in range(lead):
            at = pl.multiple_of(((top * lead + a) * 2 + core) * block, block)
            source = part.at[pl.ds(a * block, block), pl.ds(0, width)]
            copies.append(
                pltpu.make_async_copy(source, whole.at[pl.ds(at, block)], sems.at[n * lead + a])
            )
    for copy in copies:
        copy.start()
    return copies


def norm(hidden):
    centred = hidden - jnp.mean(hidden, axis=-1, keepdims=True)
    scale = lax.rsqrt(jnp.mean(centred * centred, axis=-1, keepdims=True) + 1e-05)
    return centred * scale, scale


def put_rows(outs, cols, value):
    rows = value.shape[0] // len(outs)
    for r, out in enumerate(outs):
        out[:, cols] = value[r * rows : (r + 1) * rows].astype(bf16)


def theirs(others, r, rows):
    if len(others) == 2:
        return others[1 - r][...].astype(f32)
    return others[0][pl.ds((1 - r) * rows, rows)].astype(f32)


def gains_at(gains, r, place, width):
    return gains[pl.ds(r, 1), pl.ds(place * width, width)]


def add_norm(which, parts, gains, total, out):
    base, *shares = parts
    rows, width = out.shape[0] // 2, out.shape[1]
    for r in range(2):
        block = pl.ds(r * rows, rows)
        value = base[block]
        if shares:
            value = value + (shares[0][block] + theirs(shares[1:], r, rows))
            total[block] = value
        gain, bias = [gains_at(gains, r, 2 * which + n, width) for n in range(2)]
        out[block] = (norm(value)[0] * gain + bias).astype(bf16)


def norm_back(which, d_out, keep, others, hidden, gains, total, low, d_gain, d_shift):
    rows, width = d_out.shape[0] // 2, d_out.shape[1]
    for r in range(2):
        block = pl.ds(r * rows, rows)
        grad = keep[block] + theirs(others, r, rows)
        normed, scale = norm(hidden[block])
        if r == 0:
            d_gain[...] = jnp.sum(grad * normed, axis=0, keepdims=True)
            d_shift[...] = jnp.sum(grad, axis=0, keepdims=True)
        e = grad * gains_at(gains, r, 2 * which, width)
        part = e - jnp.mean(e, axis=-1, keepdims=True)
        part = part - normed * jnp.mean(e * normed, axis=-1, keepdims=True)
        value = d_out[block] + scale * part
        total[block] = value
        low[block] = value.astype(bf16)


def norm_back_kernel(which, d_out, keep, *refs):
    norm_back(which, d_out, keep, refs[:-6], *refs[-6:])


def gains_kernel(lead, count, rows, place, pick, q0, q1, q2, q3, first, second, held, wide, sems):
    copies = []
    for n, part in enumerate((q0, q1, q2, q3)):
        source = part.at[:, pl.ds(part.shape[1] - 128, 128)]
        copies.append(pltpu.make_async_copy(source, held.at[n], sems.at[n]))
    for copy in copies:
        copy.start()
    for copy in copies:
        copy.wait()
    wide[...] = held[...].astype(f32)
    deep = wide.shape[1] // (lead * rows)
    for n in range(4):
        top = place[0] if n % 2 == 0 else 1 - place[0]
        core = place[1] if n < 2 else 1 - place[1]
        for a in range(lead):
            for z in range(deep):
                cols = pl.multiple_of((((top * lead + a) * 2 + core) * deep + z) * 128, 128)
                base = (a * deep + z) * rows
                for r in range(2):
                    first[pl.ds(r, 1), pl.ds(cols, 128)] = wide[n, pl.ds(base, 1)]
                    second[pl.ds(r, 1), pl.ds(cols, 128)] = wide[n, pl.ds(base + 1 + pick[r], 1)]


def score(q, k, allowed, size):
    scores = jnp.where(allowed, dot_t(q, k) * size, -1e30)
    exponent = jnp.exp(scores - jnp.max(scores, axis=-1, keepdims=True))
    return exponent * (1.0 / jnp.sum(exponent, axis=-1, keepdims=True))


def lanes_of(which, shape):
    lane = lax.broadcasted_iota(jnp.int32, shape, 1)
    return (lane < shape[1] // 2) if which == 0 else (lane >= shape[1] // 2)


def out_block(weight, k, block, at):
    count = weight.shape[0] // (2 * block)
    wide = weight.shape[1] - at
    return jnp.concatenate([weight[pl.ds((2 * h + k) * block, block), pl.ds(at, wide)] for h in range(count)], 0)


def attend_kernel(ways, size, lead, block, place, *refs):
    refs, (weight, sems) = refs[:-2], refs[-2:]
    refs, lows = refs[:-ways], refs[-ways:]
    *parts, gains, q0, q1, q2, q3, allow, total, f, qkv, mixed, keep = refs
    copies = fetch(place, (q0, q1, q2, q3), weight, lead, sems)
    add_norm(0, parts, gains, total, f)
    for copy in copies:
        copy.wait()
    length = allow.shape[-1]
    third = qkv.shape[1] // 3
    for n in range(3):
        cols = pl.ds(n * third, third)
        qkv[:, cols] = dot(f[...], weight[:, cols]).astype(bf16)

    def one_row(r):
        at = pl.ds(r * length, length)
        allowed = allow[r] > 0
        for p in range(third // 128):
            q = qkv[at, pl.ds(p * 128, 128)]
            k = qkv[at, pl.ds(third + p * 128, 128)]
            v = qkv[at, pl.ds(2 * third + p * 128, 128)]
            halves = []
            for h in range(2):
                probs = score(jnp.where(lanes_of(h, q.shape), q, 0), k, allowed, size)
                halves.append(dot(probs.astype(bf16), v))
            mixed[at, pl.ds(p * 128, 128)] = jnp.where(
                lanes_of(0, q.shape), halves[0], halves[1]
            ).astype(bf16)

    for r in range(f.shape[0] // length):
        one_row(r)
    for k in range(2):
        cols = pl.ds(k * third, third)
        value = dot(mixed[...], out_block(weight, k, block, 3 * third))
        keep[:, cols] = value
        put_rows(lows, cols, value)


def attend_back_kernel(ways, size, lead, block, grads, place, *refs):
    if grads:
        (first, mixed), refs = refs[:2], refs[2:]
    (d_out, part), refs = refs[:2], refs[2:]
    refs, (weight, d_mixed, sems) = refs[:-3], refs[-3:]
    if grads:
        refs, outs = refs[:-4], refs[-4:]
    refs, lows = refs[:-ways], refs[-ways:]
    *others, attended, gains, q0, q1, q2, q3, allow, qkv, total, d, d_gain, d_shift, d_qkv, keep = refs
    copies = fetch(place, (q0, q1, q2, q3), weight, lead, sems)
    norm_back(1, d_out, part, others, attended, gains, total, d, d_gain, d_shift)
    for copy in copies:
        copy.wait()
    length = allow.shape[-1]
    third = qkv.shape[1] // 3
    value = dot_t(d[:, pl.ds(0, third)], out_block(weight, 0, block, 3 * third))
    value = value + dot_t(d[:, pl.ds(third, third)], out_block(weight, 1, block, 3 * third))
    d_mixed[...] = value.astype(bf16)

    def one_row(r):
        at = pl.ds(r * length, length)
        allowed = allow[r] > 0
        for p in range(third // 128):
            q = qkv[at, pl.ds(p * 128, 128)]
            k = qkv[at, pl.ds(third + p * 128, 128)]
            v = qkv[at, pl.ds(2 * third + p * 128, 128)]
            dm = d_mixed[at, pl.ds(p * 128, 128)]
            d_q, d_k, d_v = [], [], []
            for h in range(2):
                pick = lanes_of(h, q.shape)
                probs = score(jnp.where(pick, q, 0), k, allowed, size)
                d_probs = dot_t(jnp.where(pick, dm, 0), v)
                d_v.append(t_dot(probs.astype(bf16), dm))
                inner = jnp.sum(probs * d_probs, axis=-1, keepdims=True)
                d_scores = (probs * (d_probs - inner)).astype(bf16)
                d_q.append(dot(d_scores, k))
                d_k.append(t_dot(d_scores, q))
            pick = lanes_of(0, q.shape)
            for n, (halves, scale) in enumerate(((d_q, size), (d_k, size), (d_v, 1.0))):
                value = jnp.where(pick, halves[0], halves[1]) * scale
                d_qkv[at, pl.ds(n * third + p * 128, 128)] = value.astype(bf16)

    for r in range(d.shape[0] // length):
        one_row(r)
    for n in range(keep.shape[1] // 256):
        cols = pl.ds(n * 256, 256)
        value = dot_t(d_qkv[...], weight[cols, pl.ds(0, 3 * third)])
        keep[:, cols] = value
        put_rows(lows, cols, value)
    if grads:
        attend_grad(lead, place, first, mixed, d_qkv, d, outs)


def up(f, weight, pre, active):
    for n in range(pre.shape[1] // 256):
        cols = pl.ds(n * 256, 256)
        value = dot(f[...], weight[:, cols])
        pre[:, cols] = value
        active[:, cols] = jax.nn.gelu(value).astype(bf16)


def down(active, weight, keep, lows):
    for n in range(keep.shape[1] // 256):
        cols = pl.ds(n * 256, 256)
        value = dot(active[...], weight[:, cols])
        keep[:, cols] = value
        put_rows(lows, cols, value)


def feed_kernel(ways, lead, up_place, dn_place, *refs):
    refs, (w_up, w_dn, up_sems, dn_sems) = refs[:-4], refs[-4:]
    refs, lows = refs[:-ways], refs[-ways:]
    *parts, gains, u0, u1, u2, u3, n0, n1, n2, n3, total, f, pre, active, keep = refs
    up_copies = fetch(up_place, (u0, u1, u2, u3), w_up, lead, up_sems)
    dn_copies = fetch(dn_place, (n0, n1, n2, n3), w_dn, lead // 2, dn_sems)
    add_norm(1, parts, gains, total, f)
    for copy in up_copies:
        copy.wait()
    up(f, w_up, pre, active)
    for copy in dn_copies:
        copy.wait()
    down(active, w_dn, keep, lows)


def down_kernel(lead, place, active, q0, q1, q2, q3, keep, low, weight, sems):
    for copy in fetch(place, (q0, q1, q2, q3), weight, lead, sems):
        copy.wait()
    down(active, weight, keep, (low,))


def gelu_slope(x):
    c = 0.7978845608028654
    t = jnp.tanh(c * (x + 0.044715 * (x * x * x)))
    return 0.5 * (1.0 + t) + 0.5 * x * (1.0 - t * t) * (c * (1.0 + 3 * 0.044715 * (x * x)))


def feed_back(d, pre, w_up, w_dn, d_pre, keep, lows):
    for n in range(pre.shape[1] // 256):
        cols = pl.ds(n * 256, 256)
        d_pre[:, cols] = (gelu_slope(pre[:, cols]) * dot_t(d[...], w_dn[cols])).astype(bf16)
    for n in range(keep.shape[1] // 256):
        cols = pl.ds(n * 256, 256)
        value = dot_t(d_pre[...], w_up[cols])
        keep[:, cols] = value
        put_rows(lows, cols, value)


def feed_back_kernel(ways, lead, up_place, dn_place, d_out, part, *refs):
    refs, (w_up, w_dn, up_sems, dn_sems) = refs[:-4], refs[-4:]
    refs, lows = refs[:-ways], refs[-ways:]
    *others, hidden, gains, pre, u0, u1, u2, u3, n0, n1, n2, n3, total, d, d_gain, d_shift, d_pre, keep = refs
    copies = fetch(dn_place, (n0, n1, n2, n3), w_dn, lead // 2, dn_sems)
    copies += fetch(up_place, (u0, u1, u2, u3), w_up, lead, up_sems)
    norm_back(0, d_out, part, others, hidden, gains, total, d, d_gain, d_shift)
    for copy in copies:
        copy.wait()
    feed_back(d, pre, w_up, w_dn, d_pre, keep, lows)


def feed_turn_kernel(ways, lead, grads, place, up_place, dn_place, *refs):
    refs, (w_up, w_dn, pre, up_sems, dn_sems) = refs[:-5], refs[-5:]
    if grads:
        refs, up_outs, dn_outs = refs[:-8], refs[-8:-4], refs[-4:]
    refs, lows = refs[:-ways], refs[-ways:]
    *parts, gains, d, u0, u1, u2, u3, n0, n1, n2, n3, total, f, active, d_pre, keep = refs
    up_copies = fetch(up_place, (u0, u1, u2, u3), w_up, lead, up_sems)
    dn_copies = fetch(dn_place, (n0, n1, n2, n3), w_dn, lead // 2, dn_sems)
    add_norm(1, parts, gains, total, f)
    for copy in up_copies:
        copy.wait()
    up(f, w_up, pre, active)
    for copy in dn_copies:
        copy.wait()
    feed_back(d, pre, w_up, w_dn, d_pre, keep, lows)
    if grads:
        weight_grad(lead, place, f, d_pre, up_outs)
        weight_grad(lead // 2, place, active, d, dn_outs)


def columns_of(place, value, lead):
    block = value.shape[1] // (4 * lead)
    parts = []
    for n in range(4):
        top = place[0] if n % 2 == 0 else 1 - place[0]
        core = place[1] if n < 2 else 1 - place[1]
        starts = [((top * lead + a) * 2 + core) * block for a in range(lead)]
        if block % 128 == 0:
            starts = [pl.multiple_of(at, 128) for at in starts]
        parts.append(jnp.concatenate([value[:, pl.ds(at, block)] for at in starts], 1))
    return parts


def weight_grad(lead, place, left, right, outs):
    for part, out in zip(columns_of(place, left, lead), outs):
        out[...] = t_dot(part, right[...]).astype(bf16)


def weight_grad_kernel(lead, aligned, place, left, right, *outs):
    weight_grad(lead, place if aligned else (0, 0), left, right, outs)


def attend_grad_kernel(lead, aligned, place, left, mixed, d_qkv, d, *outs):
    attend_grad(lead, place if aligned else (0, 0), left, mixed, d_qkv, d, outs)


def attend_grad(lead, place, left, mixed, d_qkv, d, outs):
    width = d_qkv.shape[1]
    third = width // 3
    block = left.shape[1] // (4 * lead)
    lefts, inners = columns_of(place, left, lead), columns_of(place, mixed, lead // 2)
    for part, inner, out in zip(lefts, inners, outs):
        out[:, pl.ds(0, width)] = t_dot(part, d_qkv[...]).astype(bf16)
        value = t_dot(inner, d[...]).astype(bf16)
        for h in range(inner.shape[1] // block):
            for k in range(2):
                out[pl.ds((2 * h + k) * block, block), pl.ds(width, third)] = value[
                    h * block : (h + 1) * block, k * third : (k + 1) * third
                ]


def turn(sl, value, lead):
    tokens, width = value.shape
    value = value.reshape(tokens, 2, lead, 2, width // (4 * lead))
    value = jnp.stack(split(value, sl.high[0], 1), 1)
    return jnp.stack(split(value, CORE, 3), 3).reshape(tokens, width)


def finish_kernel(span, side, keep, other, out, m, v, *refs):
    third = out.shape[-1]
    place_sides([(keep, other, 0, 0, 3 * third, span)], side, refs[-3])
    for k in range(2):
        refs[-3][0, :, pl.ds((6 + k) * third, third)] = out[k]
    adam_columns(m, v, *refs[-3:])


def finish_up_kernel(chunk, first, side, keep, other, *refs):
    grad = refs[-3]
    late = grad.shape[-1] // 2 - (keep.shape[1] - first)
    pieces = [(keep, other, first, late, keep.shape[1] - first, chunk)]
    if late:
        pieces.append((refs[0], refs[1], 0, 0, late, chunk))
    place_sides(pieces, side, grad)
    m, v = refs[2:4] if late else refs[:2]
    adam_columns(m, v, *refs[-3:])


def place_sides(pieces, side, grad):
    for one, two, first, start, count, width in pieces:
        each = math.gcd(math.gcd(width, start), count)
        for source, x in ((one, side[0]), (two, 1 - side[0])):
            for n in range(count // each):
                block, inside = divmod(start + n * each, width)
                at = pl.multiple_of((2 * block + x) * width + inside, 128)
                grad[0, :, pl.ds(at, each)] = source[:, pl.ds(first + n * each, each)]


def adam_columns(m, v, grad, new_m, step):
    for n in range(grad.shape[2] // 1024):
        cols = pl.ds(n * 1024, 1024)
        new_m[0, :, cols], step[0, :, cols] = adam_update(m[0, :, cols], v[0, :, cols], grad[0, :, cols])


def finish_down_kernel(value, m, v, *refs):
    grad, new_m, step = refs[-3:]
    grad[0] = value[...]
    new_m[0], step[0] = adam_update(m[0], v[0], value[...])


def update(kernel, layer, shape, parts, specs, moments, before, name, half=None):
    wide = shape[2] if half is None else shape[2] // 2
    one = pl.BlockSpec((1, shape[1], wide), lambda i: (layer, 0, half or 0))
    count = len(parts) + 2
    return pl.pallas_call(
        kernel,
        grid=(1,),
        out_shape=[jax.ShapeDtypeStruct(shape, f32)] * 3,
        in_specs=[*specs, one, one, *len(before) * [ANY]],
        out_specs=[one] * 3,
        input_output_aliases={count + n: n for n in range(len(before))},
        compiler_params=pltpu.CompilerParams(vmem_limit_bytes=20 << 20),
        name=name,
    )(*parts, *moments, *before)


def adam_update(moment, square, gradient):
    moment = beta_one * moment + (1.0 - beta_one) * gradient
    square = beta_two * square + (1.0 - beta_two) * gradient * gradient
    update = moment / first_fix / (jnp.sqrt(square / second_fix) + 1e-08)
    return (moment, update)


def dma(count):
    return pltpu.SemaphoreType.DMA((count,))


def body(
    dp,
    fsdp,
    inputs,
    cotangent,
    segment_ids,
    section_ids,
    w_big,
    w_down,
    norm_table,
    m_big,
    m_down,
    m_table,
    v_big,
    v_down,
    v_table,
):
    sl = Slice(dp, fsdp)
    length, width = inputs.shape[1:]
    rows = w_big.shape[1]
    feeds = w_down.shape[1]
    feed = w_big.shape[2] - 4 * width
    high = dp // 4
    lead = high
    half, part = width // 2, 3 * width // 2
    block = fsdp * rows
    count = norm_table.shape[0]
    size = (width // HEADS) ** -0.5
    two_f, two_b = ((2 * length, width), f32), ((2 * length, width), bf16)
    wide_b = ((2 * length, feed // 2), bf16)

    def lows(ways):
        return ways * [((2 // ways * length, width), bf16)]

    quarter = ((width // 4, 2 * width), bf16)
    gain_row = ((1, width), f32)
    up_first = feed // 2 - feed // 8
    place = jnp.stack([mine(sl.high[0]), mine(CORE)])
    w_attn = pltpu.VMEM((width, 2 * width), bf16)
    w_upper = pltpu.VMEM((width, feed // 2), bf16)
    w_lower = pltpu.VMEM((feed // 2, width), bf16)

    def qkv_sides(layer):
        value = w_big[layer, :, : 3 * width].reshape(rows, 3, high, 2, 2 * block)
        return [v.reshape(rows, part) for v in split(value, SIDE, 3)]

    def up_sides(layer):
        value = w_big[layer, :, 4 * width :].reshape(rows, high, 2, 2 * fsdp * feeds)
        return [v.reshape(rows, feed // 2) for v in split(value, SIDE, 2)]

    def prepare(table_part):
        shapes = 2 * [(rows, part + 128)] + 2 * [(rows, feed // 2)] + 2 * [(rows, part + feed // 2)]
        shapes.append((2, 2, rows, half))
        if rows % 16 == 0:
            return call(
                partial(prepare_kernel, 2 * block, 2 * fsdp * feeds),
                [(shape, bf16) for shape in shapes],
                [mine(SIDE)[None], w_big, table_part],
                [SMEM, ANY, ANY],
                [dma(2 * (2 * 3 * high + 2 * high + 2) + 2)],
                name="prepare",
            )
        first = [jnp.concatenate([v, table_part], -1) for v in qkv_sides(0)]
        after = [jnp.concatenate([a, b], -1) for a, b in zip(qkv_sides(1), up_sides(1))]
        out = w_big[:, :, 3 * width : 4 * width].reshape(2, rows, 2, half)
        return [*first, *up_sides(0), *after, jnp.swapaxes(out, 1, 2)]

    def place_sides(kernel, shape, keep, other, out, name):
        return call(
            kernel,
            [(shape, bf16)],
            [mine(SIDE)[None], keep, other, out],
            [SMEM, VMEM, VMEM, VMEM],
            name=name,
        )[0]

    live = Live()
    downs = [live.flow(Gather(sl, w_down[n], 1, n == 1)) for n in range(2)]

    downs[0].start()
    downs[1].start()
    table_part = norm_table.reshape(-1)
    table_part = jnp.pad(table_part, (0, rows * 128 - table_part.shape[0])).reshape(rows, 128)
    first, first_sent, up0, up0_sent, after, after_sent, out_proj = prepare(table_part)
    live.put(
        first=[first, sl.flip(first_sent, SIDE)],
        up=[up0, up0_sent],
        after=[after, after_sent],
        out=out_proj,
    )
    live.seal(downs[0], downs[1])

    own = place_sides(
        place_first_kernel, (2, rows, 2 * width + 128), *live.first, live.out[0], "place_first"
    )
    attns = [live.flow(Gather(sl, own.reshape(2 * rows, -1), 2))]
    attns[0].start()
    downs[0].start()
    extra = jnp.zeros((16, width), bf16)
    extra = extra.at[0, :length].set(segment_ids[0].astype(bf16))
    extra = extra.at[1, 0].set(section_ids[0].astype(bf16))
    pack = jnp.concatenate([inputs[0], cotangent[0], extra], 0)
    live.put(
        up=[live.up[0], sl.flip(live.up[1], SIDE)],
        after=[live.after[0], sl.flip(live.after[1], SIDE)],
        pack=[pack, sl.flip(pack, SIDE)],
    )
    live.drop("first")
    live.seal(attns[0], downs[0])

    ups = [live.flow(Gather(sl, interleave(live.up[:1], live.up[1:], SIDE, 1)[0], 2))]
    downs[0].start()
    attns[0].start()
    ups[0].start()
    own = place_sides(
        place_next_kernel, (4, rows, 2 * width), *live.after, live.out[1], "place_next"
    )
    live.put(own=own)
    live.drop("up", "after", "out")
    packed = jnp.stack(live.pack)
    extras = packed[:, 2 * length :]
    segments = extras[:, 0, :length].astype(f32)
    same = segments[:, :, None] == segments[:, None, :]
    position = jnp.arange(length)
    live.put(
        hidden=packed[:, :length].reshape(2 * length, width).astype(f32),
        d_low=packed[:, length : 2 * length].reshape(2 * length, width),
        sections=extras[:, 1, 0].astype(jnp.int32),
        allows=[
            (same & (position[:, None] >= position[None, :])).astype(f32),
            same.astype(f32),
        ],
    )
    live.drop("pack")
    live.seal(attns[0], ups[0], downs[0])

    own = live.own.reshape(2, 2 * rows, -1)
    attns.append(live.flow(Gather(sl, own[0], 2)))
    ups.append(live.flow(Gather(sl, own[1], 2)))
    live.drop("own")
    attns[0].start()
    attns[1].start()
    ups[0].start()
    downs[0].finish()
    live.seal(attns[0], ups[0], attns[1])

    def after(made, value):
        (keep, send), _ = lax.optimization_barrier((made.quarters, value))
        made.quarters = [keep, send]

    def gate(*made):
        airs = [flow.air for flow in made]
        other, airs = lax.optimization_barrier((live.other, airs))
        live.put(other=other)
        for flow, flow.air in zip(made, airs):
            pass

    def gains_of(flow, sections):
        wide = norm_table.shape[1]
        if wide == 128:
            return call(
                partial(gains_kernel, lead, count, rows),
                2 * [((2, 4 * width), f32)],
                [place, sections, *pinned(flow)],
                [SMEM, SMEM] + [ANY] * 4,
                [
                    pltpu.VMEM((4, width // 4, 128), bf16),
                    pltpu.VMEM((4, width // 4, 128), f32),
                    dma(4),
                ],
                name="gains",
            )
        parts = jnp.stack([q[:, 2 * width :] for q in flow.quarters])
        parts = parts.reshape(4, lead // 2, 2, fsdp, rows * 128)[..., : count * wide]
        parts = parts.reshape(4, lead // 2, 2, fsdp, count, wide)
        pick = jnp.concatenate([jnp.zeros((2,), jnp.int32), 1 + sections])
        pick = (pick[:, None] == jnp.arange(count)[None, :]).astype(bf16)
        picked = jnp.einsum("sr,qhxdrj->qshxdj", pick, parts, preferred_element_type=f32)
        own, top, core, both = picked
        both = merge(merge(own, core, CORE, 3), merge(top, both, CORE, 3), sl.high[0], 1)
        return list(both.reshape(2, 2, 4 * width))

    def pinned(flow):
        own, top, core, both = flow.quarters
        if flow is downs[0]:
            both = pltpu.with_memory_space_constraint(both, pltpu.HBM)
        return [own, top, pltpu.with_memory_space_constraint(core, pltpu.HBM), both]

    def cross():
        live.put(other=[sl.flip(row, SIDE) for row in live.low])

    def shares():
        return [live.keep, *live.other]

    def attend(layer, base, ways=2):
        parts = [base] if layer == 0 else [base, *shares()]
        total, first, qkv, mixed, keep, *low = call(
            partial(attend_kernel, ways, size, lead, 2 * block),
            [two_f, two_b, ((2 * length, part), bf16), ((2 * length, half), bf16), two_f, *lows(ways)],
            [
                attns[layer].place,
                *parts,
                live.gains[layer],
                *pinned(attns[layer]),
                live.allows[layer],
            ],
            [SMEM] + [VMEM] * (len(parts) + 1) + [ANY] * 4 + [VMEM],
            [w_attn, dma(4 * lead)],
            name="attend",
        )
        hidden = base if layer == 0 else total
        live.put(**{f"attn{layer}": (hidden, first, qkv, mixed)}, keep=keep, low=low)

    def feed_forward(layer, ways=2):
        attended, second, pre, active, keep, *low = call(
            partial(feed_kernel, ways, lead),
            [two_f, two_b, (wide_b[0], f32), wide_b, two_f, *lows(ways)],
            [
                ups[layer].place,
                downs[layer].place,
                live.values[f"attn{layer}"][0],
                *shares(),
                live.gains[layer],
                *pinned(ups[layer]),
                *pinned(downs[layer]),
            ],
            [SMEM, SMEM] + [VMEM] * (3 + len(live.other)) + [ANY] * 8,
            [w_upper, w_lower, dma(4 * lead), dma(2 * lead)],
            name="feed",
        )
        live.put(**{f"feed{layer}": (attended, second, pre, active)}, keep=keep, low=low)

    def feed_turn(layer, ways=2):
        grads = False
        quarters = 4 * [quarter] + 4 * [((feed // 8, width), bf16)]
        attended, second, active, d_pre, keep, *low = call(
            partial(feed_turn_kernel, ways, lead, grads),
            [two_f, two_b, wide_b, wide_b, two_f, *lows(ways), *(quarters if grads else [])],
            [
                place,
                ups[layer].place,
                downs[layer].place,
                live.values[f"attn{layer}"][0],
                *shares(),
                live.gains[layer],
                live.d_low,
                *pinned(ups[layer]),
                *pinned(downs[layer]),
            ],
            [SMEM] * 3 + [VMEM] * (4 + len(live.other)) + [ANY] * 8,
            [w_upper, w_lower, pltpu.VMEM(wide_b[0], f32), dma(4 * lead), dma(2 * lead)],
            name="feed_turn",
        )
        live.put(**{f"feed{layer}": (attended, second, None, active)}, d_pre=d_pre, keep=keep, low=low)

    def feed_down(layer):
        keep, *low = call(
            partial(down_kernel, lead // 2),
            [two_f, *lows(1)],
            [downs[layer].place, live.values[f"feed{layer}"][3], *pinned(downs[layer])],
            [SMEM, VMEM, ANY, ANY, ANY, ANY],
            [w_lower, dma(2 * lead)],
            name="down",
        )
        live.put(keep=keep, low=low)

    def feed_back(layer, ways=1):
        grad, d_low, d_gain, d_shift, d_pre, keep, *low = call(
            partial(feed_back_kernel, ways, lead),
            [two_f, two_b, gain_row, gain_row, wide_b, two_f, *lows(ways)],
            [
                ups[layer].place,
                downs[layer].place,
                live.grad,
                *shares(),
                live.values[f"attn{layer + 1}"][0],
                live.gains[layer + 1],
                live.values[f"feed{layer}"][2],
                *pinned(ups[layer]),
                *pinned(downs[layer]),
            ],
            [SMEM, SMEM] + [VMEM] * (5 + len(live.other)) + [ANY] * 8,
            [w_upper, w_lower, dma(4 * lead), dma(2 * lead)],
            name="feed_back",
        )
        live.put(grad=grad, d_low=d_low, d_pre=d_pre, keep=keep, low=low)
        live.put(**{f"gains{layer + 1}0": jnp.concatenate([d_gain, d_shift], 1)})

    def down_grad(layer, top_last=False):
        aligned = feed // 4 // lead % 128 == 0
        active = live.values[f"feed{layer}"][3]
        parts = call(
            partial(weight_grad_kernel, lead // 2, aligned),
            [((feed // 8, width), bf16)] * 4,
            [place, active if aligned else turn(sl, active, lead // 2), live.d_low],
            [SMEM, VMEM, VMEM],
            name="down_grad",
        )
        return live.flow(Scatter(sl, parts, 1, top_last))

    def up_grad(layer, piece=None):
        aligned = block % 128 == 0
        second, right = live.values[f"feed{layer}"][1], live.d_pre
        columns = feed // 2
        if piece is not None:
            right = right[:, :up_first] if piece == 0 else right[:, up_first:]
            columns = right.shape[1]
        parts = call(
            partial(weight_grad_kernel, lead, aligned),
            [((width // 4, columns), bf16)] * 4,
            [place, second if aligned else turn(sl, second, lead), right],
            [SMEM, VMEM, VMEM],
            name="up_grad",
        )
        return live.flow(Scatter(sl, parts, 2, piece == 1))

    def norm_back(which, layer, hidden):
        grad, d_low, d_gain, d_shift = call(
            partial(norm_back_kernel, which),
            [two_f, two_b, gain_row, gain_row],
            [live.grad, *shares(), hidden, live.gains[layer]],
            [VMEM] * (4 + len(live.other)),
            name="norm_back",
        )
        live.put(grad=grad, d_low=d_low)
        live.put(**{f"gains{layer}{which}": jnp.concatenate([d_gain, d_shift], 1)})

    def attend_back(layer, ways=1):
        grads = block % 128 == 0
        hidden, first, qkv, mixed = live.values[f"attn{layer}"]
        grad, d_low, d_gain, d_shift, d_qkv, keep, *low = call(
            partial(attend_back_kernel, ways, size, lead, 2 * block, grads),
            [
                *(two_f, two_b, gain_row, gain_row, ((2 * length, part), bf16), two_f, *lows(ways)),
                *(4 * [quarter] if grads else []),
            ],
            [
                attns[layer].place,
                *([first, mixed] if grads else []),
                live.grad,
                *shares(),
                live.values[f"feed{layer}"][0],
                live.gains[layer],
                *pinned(attns[layer]),
                live.allows[layer],
                live.values[f"attn{layer}"][2],
            ],
            [SMEM] + [VMEM] * (4 + 2 * grads + len(live.other)) + [ANY] * 4 + [VMEM] * 2,
            [w_attn, pltpu.VMEM((2 * length, half), bf16), dma(4 * lead)],
            name="attend_back",
        )
        low, made = low[:ways], low[ways:]
        live.put(grad=grad, d_low=d_low, d_qkv=d_qkv, keep=keep, low=low)
        live.put(**{f"gains{layer}1": jnp.concatenate([d_gain, d_shift], 1)})
        return live.flow(Scatter(sl, made, 2)) if grads else attend_grad(layer)

    def attend_grad(layer):
        hidden, first, qkv, mixed = live.values[f"attn{layer}"]
        aligned = block % 128 == 0
        if not aligned:
            first, mixed = turn(sl, first, lead), turn(sl, mixed, lead // 2)
        parts = call(
            partial(attend_grad_kernel, lead, aligned),
            [quarter] * 4,
            [place, first, mixed, live.d_qkv, live.d_low],
            [SMEM] + [VMEM] * 4,
            name="attend_grad",
        )
        return live.flow(Scatter(sl, parts, 2))

    def two_sides(flows, wides, counts):
        values = [flow.value.reshape(2, rows, wide) for flow, wide in zip(flows, wides)]
        both = jnp.concatenate([v[..., :n] for v, n in zip(values, counts)], -1)
        keep, send = split(both, SIDE, 0)
        return keep, sl.flip(send, SIDE), values[0][..., counts[0] :]

    def finish(layer, big, before, more=None):
        keep, other, out = big
        side = mine(SIDE)[None]
        before = update(
            partial(finish_kernel, 2 * block),
            layer,
            w_big.shape,
            [side, keep, other, out],
            [SMEM, VMEM, VMEM, VMEM],
            [m_big, v_big],
            before,
            "finish",
            0,
        )
        more = [] if more is None else list(more[:2])
        return update(
            partial(finish_up_kernel, 2 * fsdp * feeds, part),
            layer,
            w_big.shape,
            [side, keep, other, *more],
            [SMEM] + [VMEM] * (2 + len(more)),
            [m_big, v_big],
            before,
            "finish_up",
            1,
        )

    def finish_down(layer, flow, before):
        return update(
            finish_down_kernel,
            layer,
            w_down.shape,
            [flow.value],
            [VMEM],
            [m_down, v_down],
            before,
            "finish_down",
        )

    def table_terms():
        first, second = [
            jnp.concatenate([live.values[f"gains{n}0"], live.values[f"gains{n}1"]], 1) for n in range(2)
        ]
        hit = jnp.arange(count - 1) == section_ids[0]
        terms = jnp.concatenate([first, jnp.where(hit[:, None], second, 0.0)], 0)
        terms = terms.reshape(count, high, 2, 2, fsdp, norm_table.shape[1])
        return jnp.moveaxis(terms, 0, 4)

    def table_step(pos, bits):
        value = live.table
        for bit in bits:
            keep, send = split(value, bit, pos)
            value = keep + sl.flip(send, bit)
        live.put(table=value)

    ups[0].start()
    attns[1].start()
    ups[1].start()
    attns[0].finish()
    live.put(gains=gains_of(attns[0], live.sections))
    attend(0, live.hidden, 1)
    cross()
    live.seal(ups[0], attns[1], ups[1])

    attns[1].start()
    ups[1].start()
    downs[1].start()
    ups[0].finish()
    feed_forward(0, 1)
    cross()
    live.seal(attns[1], ups[1], downs[1])

    ups[1].start()
    downs[1].start()
    attns[1].finish()
    attend(1, live.feed0[0])
    cross()
    live.seal(ups[1], downs[1])

    ups[1].finish()
    downs[1].finish()
    live.put(grad=live.d_low.astype(f32))
    feed_turn(1)
    live.seal()

    cross()
    g_up1 = up_grad(1)
    g_up1.cross()
    g_up1.start()
    g_down1 = down_grad(1, True)
    g_down1.cross()
    g_down1.start()
    g_attn1 = attend_back(1)
    live.seal(g_down1, g_up1)

    g_down1.start()
    g_up1.start()
    g_attn1.cross()
    g_attn1.start()
    cross()
    feed_back(0)
    g_down0, g_up0b, g_up0a = down_grad(0), up_grad(0, 1), up_grad(0, 0)
    live.seal(g_down1, g_up1, g_attn1)

    cross()
    g_down0.cross()
    g_down0.start()
    g_up0b.cross()
    g_up0b.start()
    g_up0a.cross()
    after(g_up1, g_down0.quarters[0][1])
    g_up1.start()
    g_attn1.start()
    g_attn0 = attend_back(0)
    live.seal(g_down0, g_up1, g_attn1, g_up0b)

    cross()
    g_attn0.cross()
    g_attn0.start()
    g_up0b.start()
    g_down0.start()
    after(g_attn1, g_attn0.quarters[0][1])
    g_attn1.start()
    norm_back(0, 0, live.attn0[0])
    live.seal(g_attn0, g_attn1, g_down0, g_up0b)

    g_up0a.start()
    after(g_down0, g_attn0.quarters[1])
    (g_attn1.value, g_up1.value), g_attn0.quarters[1] = lax.optimization_barrier(
        ((g_attn1.value, g_up1.value), g_attn0.quarters[1])
    )
    g_attn0.start()
    g_down0.start()
    g_up0b.start()
    feed_down(1)
    big1 = two_sides([g_attn1, g_up1], [2 * width, feed // 2], [part, feed // 2])
    live.put(big=finish(1, big1, []))
    live.put(table=table_terms())
    table_step(2, [CORE])
    live.seal(g_up0a, g_attn0, g_down0, g_up0b)

    g_up0a.start()
    g_attn0.start()
    g_down1.start()
    cross()
    table_step(1, [SIDE])
    table = live.table.reshape(*(len(sl.high) + len(sl.deep)) * [2], count, -1)
    live.put(table=table, down=finish_down(0, g_down0, []))
    table_step(0, sl.high)
    live.seal(g_up0a, g_attn0, g_down1)

    g_up0a.start()
    out_act = live.feed1[0][:length] + (live.keep[:length] + live.other[0][length:].astype(f32))
    rest = feed // 2 - up_first
    big0 = two_sides([g_attn0, g_up0b], [2 * width, rest], [part, rest])
    table_step(-3, sl.deep[-1:])
    live.put(out_act=out_act.astype(bf16), big0=big0)
    live.seal(g_up0a)

    table_step(0, sl.deep[:-1])
    up0a = two_sides([g_up0a], [up_first], [up_first])
    grad_big, new_m_big, step_big = finish(0, live.big0, live.big, up0a)
    grad_down, new_m_down, step_down = finish_down(1, g_down1, live.down)
    grad_table = live.table
    new_m_table, step_table = adam_update(m_table, v_table, grad_table)
    return (
        live.out_act[None],
        live.d_low[:length][None],
        grad_big,
        grad_down,
        grad_table,
        new_m_big,
        new_m_down,
        new_m_table,
        step_big,
        step_down,
        step_table,
    )


def solution(mesh):
    both = ("dp", "fsdp")
    rows, middle, last = P(both, None, None), P(None, both, None), P(None, both)
    return jax.shard_map(
        partial(body, mesh.shape["dp"], mesh.shape["fsdp"]),
        mesh=mesh,
        in_specs=(rows, rows, P(both, None), P(both), middle, middle, last)
        + 2 * (middle, middle, last),
        out_specs=(rows, rows) + 3 * (middle, middle, last),
        check_vma=False,
    )
```
